128 devices in a mesh: dp: 32 (over x, z, y_hi), tensor: 4 (over y_lo, core).
Axes of the slice: x: 4, y: 4 (y_hi: 2, y_lo: 2; y = y_hi * 2 + y_lo), z: 4, core: 2. Of those that a mesh axis runs over, the one named last changes fastest.
Arguments:
- tokens: bfloat16 [32768, 1536], P(('dp', 'tensor')), may hold values from -6 to 6
- norm_gains: float32 [2, 1536], P(None, ('dp', 'tensor')), may hold values from 0.25 to 1.75
- w_query: bfloat16 [1536, 1536], P('dp', 'tensor'), may hold values from -0.15625 to 0.15625
- w_keyval: bfloat16 [1536, 1536], P('dp', 'tensor'), may hold values from -0.15625 to 0.15625
- w_out: bfloat16 [1536, 1536], P('tensor', 'dp'), may hold values from -2 to 2
- w_gateup: bfloat16 [1536, 2, 4096], P('dp', None, 'tensor'), may hold values from -0.15625 to 0.15625
- w_down: bfloat16 [4096, 1536], P('tensor', 'dp'), may hold values from -0.09375 to 0.09375
- cotangent: bfloat16 [32768, 1536], P(('dp', 'tensor')), may hold values from -6 to 6
Outputs:
- result: bfloat16 [32768, 1536], P(('dp', 'tensor'))
- input_grad: bfloat16 [32768, 1536], P(('dp', 'tensor'))
- grad_query: float32 [1536, 1536], P('dp', 'tensor')
- grad_keyval: float32 [1536, 1536], P('dp', 'tensor')
- grad_out: float32 [1536, 1536], P('tensor', 'dp')
- grad_gateup: float32 [1536, 2, 4096], P('dp', None, 'tensor')
- grad_down: float32 [4096, 1536], P('tensor', 'dp')
- grad_gains: float32 [2, 1536], P(None, ('dp', 'tensor'))
The draws below stay inside these ranges and needn't reach their ends.
All inputs are finite; a program needn't handle non-finite values.
Results may differ from the reference program's by a relative error of at most 0.02.
Values may be sent and summed in bfloat16 or wider, within the bound.
No kernel may reach another device: no remote copies, remote signals or barrier semaphores. Data moves between devices by JAX's collectives and lax.ppermute only.
A program may use at most 128 MiB of HBM per device.

```python
import jax
import jax.numpy as jnp
from jax import lax

D = 1536
H = 16
KV = 8
HD = 96
FF = 4096
SEQ_LEN = 1024
TOKENS = 32768
N_DP = 32


def shard_levels(key, dims, cuts, smallest, top_value):
    loudness = 1.0
    for position, parts in cuts:
        heights = jax.random.uniform(jax.random.fold_in(jax.random.fold_in(key, 6), position), (parts,), jnp.float32, smallest / len(cuts), top_value / len(cuts))
        loudness = loudness * jnp.repeat(jnp.exp(heights), dims[position] // parts).reshape((-1,) + (1,) * (len(dims) - 1 - position))
    return loudness


def normal_values(rng, extent, scale, reach, split=(), kind=jnp.bfloat16):
    array = scale * jax.random.normal(rng, extent, jnp.float32)
    if split:
        array = array * shard_levels(rng, extent, split, -0.22, 0.18)
    return jnp.clip(array, -reach, reach).astype(kind)


def setup_inputs(seed: int = 0) -> dict:
    arg_keys = jax.random.split(jax.random.key(seed), 9)
    return {
        "tokens": normal_values(arg_keys[0], (TOKENS, D), 1.0, 6.0, ((0, 128),)),
        "norm_gains": jnp.clip(1.0 + 0.15 * jax.random.normal(arg_keys[1], (2, D), jnp.float32), 0.25, 1.75),
        "w_query": normal_values(arg_keys[2], (D, H * HD), D ** -0.5, 0.15625, ((0, 32), (1, 4))),
        "w_keyval": normal_values(arg_keys[3], (D, 2 * KV * HD), D ** -0.5, 0.15625, ((0, 32), (1, 4))),
        "w_out": normal_values(arg_keys[4], (H * HD, D), (D * 16 // (3 * SEQ_LEN)) ** -0.5, 2.0, ((0, 4), (1, 32))),
        "w_gateup": normal_values(arg_keys[5], (D, 2, FF), D ** -0.5, 0.15625, ((0, 32), (2, 4))),
        "w_down": normal_values(arg_keys[6], (FF, D), FF ** -0.5, 0.09375, ((0, 4), (1, 32))),
        "cotangent": normal_values(arg_keys[7], (TOKENS, D), 1.0, 6.0, ((0, 128),)),
    }


@jax.custom_vjp
def low(v):
    return lax.optimization_barrier(v.astype(jnp.bfloat16)).astype(jnp.float32)

@jax.custom_vjp
def low_back(v):
    return v

def low_keep(v):
    return (low(v), None)

def low_pass(kept, grad):
    return (grad,)

def back_keep(v):
    return (v, None)

def back_low(kept, grad):
    return (low(grad),)
low.defvjp(low_keep, low_pass)
low_back.defvjp(back_keep, back_low)
norm_eps = 1e-05
rope_base = 100000.0
highest = lax.Precision.HIGHEST

def rope_tables(length):
    positions = jnp.arange(length).astype(jnp.float32)
    freqs = rope_base ** (-(jnp.arange(HD // 2).astype(jnp.float32) * 2.0 / HD))
    angles = positions[:, None] * freqs[None, :]
    return (jnp.cos(angles), jnp.sin(angles))

def rotate(field, cosine, sine_table):
    half_dim = HD // 2
    first = field[..., :half_dim]
    second = field[..., half_dim:]
    cos_rows = cosine[:, None, :]
    sin_rows = sine_table[:, None, :]
    return jnp.concatenate([first * cos_rows - second * sin_rows, second * cos_rows + first * sin_rows], -1)

def rms_normed(values_in):
    return values_in * lax.rsqrt(lax.optimization_barrier(jnp.mean(values_in * values_in, -1, keepdims=True)) + norm_eps)

def decoder_layer(residual, norm_gains, w_query, w_keyval, w_out, w_gateup, w_down):
    length = residual.shape[0]
    cosine, sine_table = rope_tables(length)
    h_first = low(rms_normed(residual) * norm_gains[0])
    q_pre = low_back(jnp.dot(h_first, w_query, precision=highest)).reshape(length, H, HD)
    queries = low(rotate(q_pre, cosine, sine_table)).reshape(length, KV, H // KV, HD)
    kv_pre = low_back(jnp.dot(h_first, w_keyval, precision=highest)).reshape(length, KV, 2, HD)
    key_rows = low(rotate(kv_pre[:, :, 0], cosine, sine_table))
    values = low(kv_pre[:, :, 1])
    scores = low_back(jnp.einsum('skgd,tkd->kgst', queries, key_rows, precision=highest) * HD ** (-0.5))
    allowed = jnp.arange(length)[None, :] <= jnp.arange(length)[:, None]
    scores = jnp.where(allowed, scores, -1e+30)
    row_top = lax.optimization_barrier(jnp.max(scores, -1, keepdims=True))
    expo = jnp.exp(scores - row_top)
    probs = low(expo / lax.optimization_barrier(jnp.sum(expo, -1, keepdims=True)))
    attn = low(low_back(jnp.einsum('kgst,tkd->skgd', probs, values, precision=highest))).reshape(length, H * HD)
    middle = residual + low_back(jnp.dot(attn, w_out, precision=highest))
    h_second = low(rms_normed(middle) * norm_gains[1])
    gate_up = low_back(jnp.einsum('sd,dcf->scf', h_second, w_gateup, precision=highest))
    gate_pre = gate_up[:, 0]
    up_pre = gate_up[:, 1]
    hidden = low(gate_pre / (1.0 + jnp.exp(-gate_pre)) * up_pre)
    return middle + low_back(jnp.dot(hidden, w_down, precision=highest))

def reference(tokens, norm_gains, w_query, w_keyval, w_out, w_gateup, w_down, cotangent):
    params = tuple((a.astype(jnp.float32) for a in (norm_gains, w_query, w_keyval, w_out, w_gateup, w_down)))
    inputs_seq = tokens.astype(jnp.float32).reshape(N_DP, SEQ_LEN, D)
    grads_seq = cotangent.astype(jnp.float32).reshape(N_DP, SEQ_LEN, D)

    def sequence_step(totals, sequence_item):
        seq_in, seq_grad = sequence_item
        layer_out, pull_back = jax.vjp(decoder_layer, seq_in, *params)
        pulled = pull_back(seq_grad)
        return (tuple((t + g for t, g in zip(totals, pulled[1:]))), (layer_out, pulled[0]))
    zero_grads = tuple((jnp.zeros_like(p) for p in params))
    totals, (layer_outs, input_grads) = lax.scan(sequence_step, zero_grads, (inputs_seq, grads_seq))
    return (layer_outs.reshape(TOKENS, D).astype(jnp.bfloat16), input_grads.reshape(TOKENS, D).astype(jnp.bfloat16), totals[1], totals[2], totals[3], totals[4], totals[5], totals[0])
```

```python
import jax
import jax.numpy as jnp
from jax import lax
from jax.sharding import Mesh, PartitionSpec as P

HD = 96
F32 = jnp.float32
BF16 = jnp.bfloat16

norm_eps = 1e-05
rope_base = 100000.0


def rope_tables(length):
    positions = jnp.arange(length).astype(F32)
    freqs = rope_base ** (-(jnp.arange(HD // 2).astype(F32) * 2.0 / HD))
    angles = positions[:, None] * freqs[None, :]
    return (jnp.cos(angles), jnp.sin(angles))


def rotate(field, cosine, sine_table, direction):
    half_dim = HD // 2
    first = field[..., :half_dim]
    second = field[..., half_dim:]
    cos_rows = cosine[:, None, :]
    sin_rows = direction * sine_table[:, None, :]
    return jnp.concatenate(
        [first * cos_rows - second * sin_rows, second * cos_rows + first * sin_rows], -1
    )


def norm_rows(values_in):
    factor = lax.rsqrt(jnp.mean(values_in * values_in, -1, keepdims=True) + norm_eps)
    return (values_in * factor, factor)


def norm_back(grad_in, normed, factor, gain_row):
    grad_normed = grad_in * gain_row
    inner = jnp.mean(grad_normed * normed, -1, keepdims=True)
    return (factor * (grad_normed - normed * inner), jnp.sum(grad_in * normed, 0))


def dot_n(left, right):
    return jnp.dot(left, right, preferred_element_type=F32)


def dot_t(left, right):
    return lax.dot_general(left, right, (((1,), (1,)), ((), ())), preferred_element_type=F32)


def dot_tn(left, right):
    return lax.dot_general(left, right, (((0,), (0,)), ((), ())), preferred_element_type=F32)


def from_offset(v, axis, offset, size):
    return lax.ppermute(v, axis, [((i + offset) % size, i) for i in range(size)])


def other(v, axis):
    return from_offset(v, axis, 1, 2)


def pick(flag, first, second):
    return jnp.where(flag, first, second)


def ring_gather(v, axis, dim):
    me = lax.axis_index(axis)
    shape = list(v.shape)
    shape[dim] = 4
    out = jnp.zeros(shape, v.dtype)
    for offset in (0, 1, 3, 2):
        block = v if offset == 0 else from_offset(v, axis, offset, 4)
        out = lax.dynamic_update_slice_in_dim(out, block, (me + offset) % 4, dim)
    return out


def ring_scatter(v, axis, dim):
    me = lax.axis_index(axis)
    total = lax.dynamic_slice_in_dim(v, me, 1, dim).astype(F32)
    for offset in (1, 3, 2):
        block = lax.dynamic_slice_in_dim(v, (me + 4 - offset) % 4, 1, dim).astype(BF16)
        total = total + from_offset(block, axis, offset, 4).astype(F32)
    return total


def pair_rows(v, axis):
    it = other(v, axis)
    flag = lax.axis_index(axis) == 0
    return jnp.concatenate([pick(flag, v, it), pick(flag, it, v)], 0)


def tensor_gather(v):
    near = pair_rows(v, "core")
    far = pair_rows(other(v, "yl"), "core")
    flag = lax.axis_index("yl") == 0
    return jnp.concatenate([pick(flag, near, far), pick(flag, far, near)], 0)


def tensor_scatter(v):
    rows = v.shape[0] // 4
    core = lax.axis_index("core")
    yl = lax.axis_index("yl")
    blocks = v.reshape(2, 2, rows, v.shape[1])
    mine = lax.dynamic_slice_in_dim(blocks, core, 1, 1)[:, 0]
    theirs = lax.dynamic_slice_in_dim(blocks, 1 - core, 1, 1)[:, 0].astype(BF16)
    both = mine.astype(F32) + other(theirs, "core").astype(F32)
    keep = lax.dynamic_slice_in_dim(both, yl, 1, 0)[0]
    send = lax.dynamic_slice_in_dim(both, 1 - yl, 1, 0)[0].astype(BF16)
    return keep + other(send, "yl").astype(F32)


def sum_everywhere(v):
    for axis in ("core", "yl", "yh"):
        v = v + other(v, axis)
    for axis in ("x", "z"):
        v = v + from_offset(v, axis, 1, 4) + from_offset(v, axis, 3, 4) + from_offset(v, axis, 2, 4)
    return v


def block_scores(query_block, start, key_rows, length):
    block_rows = query_block.shape[0]
    scores = jnp.einsum(
        "bkgd,tkd->bkgt", query_block, key_rows, preferred_element_type=F32
    ) * HD ** (-0.5)
    rows_at = start + jnp.arange(block_rows)
    allowed = jnp.arange(length)[None, :] <= rows_at[:, None]
    return jnp.where(allowed[:, None, None, :], scores, -1e30)


def body(tokens, norm_gains, w_query, w_keyval, w_out, w_gateup, w_down, cotangent):
    ix, iz, iyh = lax.axis_index("x"), lax.axis_index("z"), lax.axis_index("yh")
    place = (((ix * 4 + iz) * 2 + iyh) * 2 + lax.axis_index("yl")) * 2 + lax.axis_index("core")
    D = tokens.shape[1]
    heads_w = w_query.shape[1]
    hidden_w = w_down.shape[0]
    gains_w = norm_gains.shape[1]

    mlp_own = jnp.concatenate([w_gateup[:, 0], w_gateup[:, 1], w_down.T], 1)
    mlp_pair = pair_rows(mlp_own, "yh")
    full_mlp = lax.all_gather(mlp_pair, ("x", "z"), axis=0, tiled=True)

    out_t = w_out.T
    half = heads_w // 2
    attn_own = jnp.concatenate([w_query, out_t[:, :half], w_keyval, out_t[:, half:]], 1)
    attn_pair = pair_rows(attn_own, "yh")
    width = heads_w + half
    first = attn_pair[None, None, :, :width]
    second = attn_pair[None, None, :, width:]
    first = ring_gather(ring_gather(first, "z", 1), "x", 0).reshape(D, width)
    second = ring_gather(ring_gather(second, "x", 0), "z", 1).reshape(D, width)
    full_q, full_kv = first[:, :heads_w], second[:, :heads_w]
    full_ot = jnp.concatenate([first[:, heads_w:], second[:, heads_w:]], 1)

    gain_rows = sum_everywhere(
        lax.dynamic_update_slice(jnp.zeros((2, D), F32), norm_gains, (0, place * gains_w))
    )

    tokens_all = tensor_gather(tokens)
    normed1, factor1 = norm_rows(tokens.astype(F32))
    h_first = (norm_rows(tokens_all.astype(F32))[0] * gain_rows[0]).astype(BF16)
    length = h_first.shape[0]
    head_count = full_q.shape[1] // HD
    kv_count = full_kv.shape[1] // (2 * HD)
    group_size = head_count // kv_count
    cosine, sine_table = rope_tables(length)
    q_pre = dot_n(h_first, full_q).reshape(length, head_count, HD)
    queries = rotate(q_pre, cosine, sine_table, 1.0).astype(BF16)
    kv_pre = dot_n(h_first, full_kv).reshape(length, kv_count, 2, HD)
    key_rows = rotate(kv_pre[:, :, 0], cosine, sine_table, 1.0).astype(BF16)
    values = kv_pre[:, :, 1].astype(BF16)
    block_rows = min(512, length)
    block_count = length // block_rows
    query_blocks = queries.reshape(block_count, block_rows, kv_count, group_size, HD)
    starts = jnp.arange(block_count, dtype=jnp.int32) * block_rows

    def attend(inputs):
        query_block, start = inputs
        scores = block_scores(query_block, start, key_rows, length)
        row_top = jnp.max(scores, -1, keepdims=True)
        expo = jnp.exp(scores - row_top)
        row_total = jnp.sum(expo, -1, keepdims=True)
        probs = (expo / row_total).astype(BF16)
        mixed = jnp.einsum("bkgt,tkd->bkgd", probs, values, preferred_element_type=F32)
        return (mixed.astype(BF16), (row_top + jnp.log(row_total))[..., 0])

    attn_blocks, log_totals = lax.map(attend, (query_blocks, starts))
    attn = attn_blocks.reshape(length, head_count * HD)
    middle = tokens.astype(F32) + tensor_scatter(dot_t(attn, full_ot))
    normed2, factor2 = norm_rows(middle)
    h_second = tensor_gather((normed2 * gain_rows[1]).astype(BF16))
    grad_full = tensor_gather(cotangent)

    full_gate = full_mlp[:, :hidden_w]
    full_up = full_mlp[:, hidden_w : 2 * hidden_w]
    full_dt = full_mlp[:, 2 * hidden_w :]
    gate_pre = dot_n(h_second, full_gate)
    up_pre = dot_n(h_second, full_up)
    sigmoid_gate = jax.nn.sigmoid(gate_pre)
    hidden = (gate_pre * sigmoid_gate * up_pre).astype(BF16)
    result = (middle + tensor_scatter(dot_t(hidden, full_dt))).astype(BF16)

    d_hidden = dot_n(grad_full, full_dt)
    d_gate = (d_hidden * up_pre * sigmoid_gate * (1.0 + gate_pre * (1.0 - sigmoid_gate))).astype(BF16)
    d_up = (d_hidden * gate_pre * sigmoid_gate).astype(BF16)
    d_h2_own = tensor_scatter(dot_t(d_gate, full_gate) + dot_t(d_up, full_up))
    grad_mlp_part = jnp.concatenate(
        [
            dot_tn(h_second, d_gate).astype(BF16),
            dot_tn(h_second, d_up).astype(BF16),
            dot_tn(grad_full, hidden).astype(BF16),
        ],
        1,
    )
    d_norm2, gain_two = norm_back(d_h2_own, normed2, factor2, gain_rows[1])
    d_middle = cotangent.astype(F32) + d_norm2
    d_out_full = tensor_gather(d_middle.astype(BF16))
    d_attn = dot_n(d_out_full, full_ot).astype(BF16)
    grad_ot_part = dot_tn(d_out_full, attn).astype(BF16)

    early = lax.psum_scatter(
        jnp.concatenate([grad_mlp_part, grad_ot_part], 1), ("x", "z"), scatter_dimension=0, tiled=True
    )
    rows = early.shape[0] // 2
    early_keep = lax.dynamic_slice_in_dim(early, iyh * rows, rows, 0)
    early_send = lax.dynamic_slice_in_dim(early, (1 - iyh) * rows, rows, 0)
    early_sum = early_keep.astype(F32) + other(early_send, "yh").astype(F32)

    grad_blocks = d_attn.reshape(block_count, block_rows, kv_count, group_size, HD)

    def attend_back(totals, inputs):
        d_key_total, d_value_total = totals
        query_block, grad_block, log_total, start = inputs
        scores = block_scores(query_block, start, key_rows, length)
        soft = jnp.exp(scores - log_total[..., None])
        probs = soft.astype(BF16)
        d_value_total = d_value_total + jnp.einsum(
            "bkgt,bkgd->tkd", probs, grad_block, preferred_element_type=F32
        )
        d_probs = jnp.einsum("bkgd,tkd->bkgt", grad_block, values, preferred_element_type=F32)
        row_inner = jnp.sum(soft * d_probs, -1, keepdims=True)
        d_scores = (soft * (d_probs - row_inner)).astype(BF16)
        d_query_block = jnp.einsum(
            "bkgt,tkd->bkgd", d_scores, key_rows, preferred_element_type=F32
        ) * HD ** (-0.5)
        d_key_total = d_key_total + jnp.einsum(
            "bkgt,bkgd->tkd", d_scores, query_block, preferred_element_type=F32
        ) * HD ** (-0.5)
        return ((d_key_total, d_value_total), d_query_block)

    zero_rows = jnp.zeros((length, kv_count, HD), F32)
    (d_key_total, d_value_total), d_query_blocks = lax.scan(
        attend_back, (zero_rows, zero_rows), (query_blocks, grad_blocks, log_totals, starts)
    )
    d_q_rot = rotate(d_query_blocks.reshape(length, head_count, HD), cosine, sine_table, -1.0)
    d_q_pre = d_q_rot.astype(BF16).reshape(length, head_count * HD)
    d_k_rot = rotate(d_key_total, cosine, sine_table, -1.0)
    d_kv_pre = (
        jnp.stack([d_k_rot, d_value_total], 2).astype(BF16).reshape(length, kv_count * 2 * HD)
    )
    grad_q_part = dot_tn(h_first, d_q_pre).astype(BF16).reshape(4, 4, D // 16, heads_w)
    grad_kv_part = dot_tn(h_first, d_kv_pre).astype(BF16).reshape(4, 4, D // 16, heads_w)
    q_sum = ring_scatter(ring_scatter(grad_q_part, "x", 0), "z", 1)
    kv_sum = ring_scatter(ring_scatter(grad_kv_part, "z", 1), "x", 0)
    late = jnp.concatenate([q_sum, kv_sum], -1).reshape(D // 16, 2 * heads_w)
    late_keep = lax.dynamic_slice_in_dim(late, iyh * rows, rows, 0)
    late_send = lax.dynamic_slice_in_dim(late, (1 - iyh) * rows, rows, 0).astype(BF16)
    late_sum = late_keep + other(late_send, "yh").astype(F32)

    d_h1_own = tensor_scatter(dot_t(d_q_pre, full_q) + dot_t(d_kv_pre, full_kv))
    d_norm1, gain_one = norm_back(d_h1_own, normed1, factor1, gain_rows[0])
    input_grad = (d_middle + d_norm1).astype(BF16)

    gains_all = sum_everywhere(jnp.stack([gain_one, gain_two]))
    grad_gains = lax.dynamic_slice(gains_all, (0, place * gains_w), (2, gains_w))
    grad_gateup = early_sum[:, : 2 * hidden_w].reshape(rows, 2, hidden_w)
    grad_down = early_sum[:, 2 * hidden_w : 3 * hidden_w].T
    grad_out = early_sum[:, 3 * hidden_w :].T
    return (
        result,
        input_grad,
        late_sum[:, :heads_w],
        late_sum[:, heads_w:],
        grad_out,
        grad_gateup,
        grad_down,
        grad_gains,
    )


def solution(mesh):
    fine = Mesh(mesh.devices.reshape(4, 4, 2, 2, 2), ("x", "z", "yh", "yl", "core"))
    dp = ("x", "z", "yh")
    tensor = ("yl", "core")
    every = dp + tensor
    weights = (P(dp, tensor), P(dp, tensor), P(tensor, dp), P(dp, None, tensor), P(tensor, dp))
    rows = P(every, None)
    gains = P(None, every)
    return jax.shard_map(
        body,
        mesh=fine,
        in_specs=(rows, gains) + weights + (rows,),
        out_specs=(rows, rows) + weights + (gains,),
        check_vma=False,
    )
```

```python
import jax
import jax.numpy as jnp
from jax import lax
from jax.experimental import pallas as pl
from jax.experimental.pallas import tpu as pltpu
from jax.sharding import Mesh, PartitionSpec as P

HD = 96
F32 = jnp.float32
BF16 = jnp.bfloat16
norm_eps = 1e-05
rope_base = 100000.0
LOG2E = 1.4426950408889634
SCALE = HD ** (-0.5)
MIB = 1024 * 1024

QUERY_AT, KEYVAL_AT, OUT_AT, ATTN_WIDTH = 0, 384, 768, 1152


def dot_n(left, right):
    return jnp.dot(left, right, preferred_element_type=F32)


def dot_t(left, right):
    return lax.dot_general(left, right, (((1,), (1,)), ((), ())), preferred_element_type=F32)


def dot_tn(left, right):
    return lax.dot_general(left, right, (((0,), (0,)), ((), ())), preferred_element_type=F32)


def block_at(index, size):
    return pl.ds(pl.multiple_of(index * size, size), size)


def causal_mask(scores, size):
    key_at = lax.broadcasted_iota(jnp.int32, (size, size), 0)
    query_at = lax.broadcasted_iota(jnp.int32, (size, size), 1)
    tail = jnp.where(key_at <= query_at, scores[-size:], -1e30)
    if scores.shape[0] == size:
        return tail
    return jnp.concatenate([scores[:-size], tail], 0)


def project_kernel(place, t0, t1, t2, t3, w_ref, gains_ref, cos_ref, sin_ref,
                   h_ref, qt_ref, q_ref, kt_ref, k_ref, vt_ref, v_ref):
    block = place[0]
    half = HD // 2
    gain_row = gains_ref[0:1, :]
    for step, piece in enumerate((t0, t1, t2, t3)):
        size = piece.shape[0]
        at = block_at(lax.bitwise_xor(block, step), size)
        value = piece[...].astype(F32)
        factor = lax.rsqrt(jnp.mean(value * value, -1, keepdims=True) + norm_eps)
        normed = (value * factor * gain_row).astype(BF16)
        h_ref[at, :] = normed
        cosine = cos_ref[:, at]
        sine = sin_ref[:, at]
        query = dot_n(normed, w_ref[:, QUERY_AT:KEYVAL_AT]).T
        keyval = dot_n(normed, w_ref[:, KEYVAL_AT:OUT_AT]).T

        def rotated(field):
            first, second = field[:half], field[half:]
            return jnp.concatenate(
                [first * cosine - second * sine, second * cosine + first * sine], 0
            )

        for head in range(query.shape[0] // HD):
            turned = rotated(query[head * HD : (head + 1) * HD])
            qt_ref[head, :, at] = turned.astype(BF16)
            q_ref[head, at, :] = turned.T.astype(BF16)
        for head in range(keyval.shape[0] // (2 * HD)):
            turned = rotated(keyval[2 * head * HD : (2 * head + 1) * HD])
            value_t = keyval[(2 * head + 1) * HD : (2 * head + 2) * HD]
            kt_ref[head, :, at] = turned.astype(BF16)
            k_ref[head, at, :] = turned.T.astype(BF16)
            vt_ref[head, :, at] = value_t.astype(BF16)
            v_ref[head, at, :] = value_t.T.astype(BF16)


def whole():
    return pl.BlockSpec(memory_space=pltpu.VMEM)


def scalars():
    return pl.BlockSpec(memory_space=pltpu.SMEM)


def project(place, pieces, weights, gain_rows, cosine, sine):
    length = 4 * pieces[0].shape[0]
    width = pieces[0].shape[1]
    heads = (KEYVAL_AT - QUERY_AT) // HD
    groups = (OUT_AT - KEYVAL_AT) // (2 * HD)
    shapes = [
        ((length, width), BF16),
        ((heads, HD, length), BF16), ((heads, length, HD), BF16),
        ((groups, HD, length), BF16), ((groups, length, HD), BF16),
        ((groups, HD, length), BF16), ((groups, length, HD), BF16),
    ]
    return pl.pallas_call(
        project_kernel,
        out_shape=[jax.ShapeDtypeStruct(*shape) for shape in shapes],
        in_specs=[scalars()] + [whole()] * 8,
        out_specs=[whole()] * len(shapes),
        compiler_params=pltpu.CompilerParams(vmem_limit_bytes=56 * MIB),
        cost_estimate=pl.CostEstimate(
            flops=4 * length * width * 384, bytes_accessed=16 * MIB, transcendentals=0),
        name="project",
    )(place, *pieces, weights, gain_rows, cosine, sine)


def attend_kernel(place, qt_ref, k_ref, vt_ref, w_ref,
                  attn_ref, attnt_ref, lse_ref, keep_ref, send_ref, natural):
    block = place[0]
    heads, _, length = qt_ref.shape
    group_size = heads // k_ref.shape[0]
    size = length // 4

    def one_head(head, carry):
        group = head // group_size
        for step in range(4):
            reach = (step + 1) * size
            columns = slice(step * size, reach)
            scores = causal_mask(dot_n(k_ref[group, :reach, :], qt_ref[head, :, columns]), size)
            top = jnp.max(scores, 0, keepdims=True)
            expo = jnp.exp2((scores - top) * (SCALE * LOG2E))
            total = jnp.sum(expo, 0, keepdims=True)
            probs = (expo * (1.0 / total)).astype(BF16)
            mixed = dot_n(vt_ref[group, :, :reach], probs)
            attnt_ref[head, :, columns] = mixed.astype(BF16)
            lse_ref[head, :, columns] = top * (SCALE * LOG2E) + jnp.log2(total)
        return carry

    lax.fori_loop(0, heads, one_head, 0)
    natural[...] = attnt_ref[...].reshape(heads * HD, length).T
    for step in range(4):
        at = block_at(lax.bitwise_xor(block, step), size)
        rows = natural[at, :]
        attn_ref[step * size : (step + 1) * size, :] = rows
        part = dot_t(rows, w_ref[:, OUT_AT:ATTN_WIDTH]).astype(BF16)
        if step % 2 == 0:
            keep_ref[step // 2] = part
        else:
            send_ref[step // 2] = part


def attend(place, qt, k, vt, weights):
    heads, _, length = qt.shape
    width = weights.shape[0]
    size = length // 4
    shapes = [
        ((length, heads * HD), BF16), ((heads, HD, length), BF16), ((heads, 1, length), F32),
        ((2, size, width), BF16), ((2, size, width), BF16),
    ]
    return pl.pallas_call(
        attend_kernel,
        out_shape=[jax.ShapeDtypeStruct(*shape) for shape in shapes],
        in_specs=[scalars()] + [whole()] * 4,
        out_specs=[whole()] * len(shapes),
        scratch_shapes=[pltpu.VMEM((length, heads * HD), BF16)],
        compiler_params=pltpu.CompilerParams(vmem_limit_bytes=56 * MIB),
        cost_estimate=pl.CostEstimate(
            flops=8 * 1024**3, bytes_accessed=16 * MIB, transcendentals=heads * length * length),
        name="attend",
    )(place, qt, k, vt, weights)


def attend_back_kernel(place, o0, o1, o2, o3, t0, t1, t2, t3, w_ref, qt_ref, q_ref, kt_ref, k_ref,
                       v_ref, attnt_ref, lse_ref, cos_ref, sin_ref,
                       dqkv_ref, keep_ref, send_ref, gain_ref,
                       do_ref, dot_ref, delta_ref, dk_ref, dv_ref, turned_ref):
    block = place[0]
    heads, _, length = qt_ref.shape
    groups = k_ref.shape[0]
    group_size = heads // groups
    size = length // 4
    half = HD // 2
    for step, piece in enumerate((o0, o1, o2, o3)):
        at = block_at(lax.bitwise_xor(block, step), size)
        grad = dot_n(piece[...], w_ref[:, OUT_AT:ATTN_WIDTH]).astype(BF16)
        grad_t = grad.astype(F32).T.astype(BF16)
        for head in range(heads):
            dot_ref[head, :, at] = grad_t[head * HD : (head + 1) * HD]
            do_ref[head, at, :] = grad[:, head * HD : (head + 1) * HD]
    delta_ref[...] = jnp.sum(
        attnt_ref[...].astype(F32) * dot_ref[...].astype(F32), 1, keepdims=True)
    dk_ref[...] = jnp.zeros_like(dk_ref)
    dv_ref[...] = jnp.zeros_like(dv_ref)

    def turned_back(field, cosine, sine):
        first, second = field[:half], field[half:]
        return jnp.concatenate(
            [first * cosine + second * sine, second * cosine - first * sine], 0)

    def one_head(head, carry):
        group = head // group_size
        for step in range(4):
            reach = (step + 1) * size
            columns = slice(step * size, reach)
            scores = causal_mask(dot_n(k_ref[group, :reach, :], qt_ref[head, :, columns]), size)
            soft = jnp.exp2(scores * (SCALE * LOG2E) - lse_ref[head, :, columns])
            d_probs = dot_n(v_ref[group, :reach, :], dot_ref[head, :, columns])
            d_scores = (soft * (d_probs - delta_ref[head, :, columns])).astype(BF16)
            dv_ref[group, :reach, :] += dot_n(soft.astype(BF16), do_ref[head, columns, :])
            dk_ref[group, :reach, :] += dot_n(d_scores, q_ref[head, columns, :])
            d_query = dot_n(kt_ref[group, :, :reach], d_scores) * SCALE
            turned_ref[head, :, columns] = turned_back(
                d_query, cos_ref[:, columns], sin_ref[:, columns])
        return carry

    lax.fori_loop(0, heads, one_head, 0)
    for group in range(groups):
        turned_ref[heads + 2 * group] = turned_back(
            dk_ref[group].T * SCALE, cos_ref[...], sin_ref[...])
        turned_ref[heads + 2 * group + 1] = dv_ref[group].T
    dqkv_ref[...] = turned_ref[...].reshape((heads + 2 * groups) * HD, length).T.astype(BF16)
    gain = jnp.zeros(gain_ref.shape, F32)
    for step, piece in enumerate((t0, t1, t2, t3)):
        at = block_at(lax.bitwise_xor(block, step), size)
        part = dot_t(dqkv_ref[at, :], w_ref[:, QUERY_AT:OUT_AT])
        value = piece[...].astype(F32)
        factor = lax.rsqrt(jnp.mean(value * value, -1, keepdims=True) + norm_eps)
        gain += jnp.sum(part * (value * factor), 0, keepdims=True)
        if step % 2 == 0:
            keep_ref[step // 2] = part.astype(BF16)
        else:
            send_ref[step // 2] = part.astype(BF16)
    gain_ref[...] = gain


def attend_back(place, pieces, token_pieces, weights, qt, q, kt, k, v, attnt, lse, cosine, sine):
    heads, _, length = qt.shape
    groups = k.shape[0]
    width = weights.shape[0]
    size = length // 4
    every = heads + 2 * groups
    shapes = [
        ((length, every * HD), BF16), ((2, size, width), BF16), ((2, size, width), BF16),
        ((1, width), F32),
    ]
    return pl.pallas_call(
        attend_back_kernel,
        out_shape=[jax.ShapeDtypeStruct(*shape) for shape in shapes],
        in_specs=[scalars()] + [whole()] * 18,
        out_specs=[whole()] * len(shapes),
        scratch_shapes=[
            pltpu.VMEM((heads, length, HD), BF16), pltpu.VMEM((heads, HD, length), BF16),
            pltpu.VMEM((heads, 1, length), F32),
            pltpu.VMEM((groups, length, HD), F32), pltpu.VMEM((groups, length, HD), F32),
            pltpu.VMEM((every, HD, length), F32),
        ],
        compiler_params=pltpu.CompilerParams(vmem_limit_bytes=56 * MIB),
        cost_estimate=pl.CostEstimate(
            flops=20 * 1024**3, bytes_accessed=24 * MIB, transcendentals=heads * length * length),
        name="attend_back",
    )(place, *pieces, *token_pieces, weights, qt, q, kt, k, v, attnt, lse, cosine, sine)


def feed_kernel(with_first, with_second, *refs):
    refs = list(refs)
    w_hbm = refs.pop(0)
    if with_first:
        normed_refs, grad_refs = refs[0:2], refs[2:4]
        hidden_ref, dgu_ref = refs[4:6]
        refs = refs[6:]
    else:
        hidden_ref, dgu_ref = refs[0:2]
        refs = refs[2:]
    if with_second:
        back_refs, out_refs = refs[0:2], refs[2:4]
        refs = refs[4:]
    w_ref, sem = refs
    hidden_w = hidden_ref.shape[1]
    size = hidden_ref.shape[0] // 2
    parts = [slice(i * hidden_w, (i + 1) * hidden_w) for i in range(3)]
    copies = [
        pltpu.make_async_copy(w_hbm.at[:, part], w_ref.at[:, part], sem.at[i])
        for i, part in enumerate(parts)
    ]
    for copy in copies:
        copy.start()
    for i in range(2):
        rows = slice(i * size, (i + 1) * size)
        if with_first:
            if i == 0:
                copies[0].wait()
            gate = dot_n(normed_refs[i][...], w_ref[:, parts[0]])
            if i == 0:
                copies[1].wait()
            up = dot_n(normed_refs[i][...], w_ref[:, parts[1]])
            sig = 1.0 / (1.0 + jnp.exp2(gate * (-LOG2E)))
            silu = gate * sig
            hidden = (silu * up).astype(BF16)
            hidden_ref[rows, :] = hidden
            if i == 0:
                copies[2].wait()
            d_hidden = dot_n(grad_refs[i][...], w_ref[:, parts[2]])
            d_gate = (d_hidden * up * (sig * (1.0 + gate * (1.0 - sig)))).astype(BF16)
            d_up = (d_hidden * silu).astype(BF16)
            dgu_ref[rows, :hidden_w] = d_gate
            dgu_ref[rows, hidden_w:] = d_up
        if with_second:
            if not with_first and i == 0:
                copies[0].wait()
                copies[1].wait()
            d_normed = dot_t(dgu_ref[rows, :], w_ref[:, : 2 * hidden_w])
            back_refs[i][...] = d_normed.astype(BF16)
            if not with_first and i == 0:
                copies[2].wait()
            out_refs[i][...] = dot_t(hidden_ref[rows, :], w_ref[:, parts[2]]).astype(BF16)


def feed(weights, normed_pieces, grad_pieces, first=None, with_second=True):
    width = weights.shape[0]
    hidden_w = weights.shape[1] // 3
    with_first = first is None
    size = normed_pieces[0].shape[0]
    piece = jax.ShapeDtypeStruct((size, width), BF16)
    shapes = []
    if with_first:
        shapes += [
            jax.ShapeDtypeStruct((2 * size, hidden_w), BF16),
            jax.ShapeDtypeStruct((2 * size, 2 * hidden_w), BF16),
        ]
    if with_second:
        shapes += [piece] * 4
    operands = (*normed_pieces, *grad_pieces) if with_first else first
    products = 3 * with_first + 3 * with_second
    return pl.pallas_call(
        lambda *refs: feed_kernel(with_first, with_second, *refs),
        out_shape=shapes,
        in_specs=[pl.BlockSpec(memory_space=pl.ANY)] + [whole()] * len(operands),
        out_specs=[whole()] * len(shapes),
        scratch_shapes=[
            pltpu.VMEM((width, 3 * hidden_w), BF16), pltpu.SemaphoreType.DMA((3,)),
        ],
        compiler_params=pltpu.CompilerParams(vmem_limit_bytes=56 * MIB),
        cost_estimate=pl.CostEstimate(
            flops=4 * products * size * width * hidden_w, bytes_accessed=16 * MIB,
            transcendentals=2 * size * hidden_w * with_first),
        name="feed_" + "ab"[with_second] if with_first else "feed_c",
    )(weights, *operands)


def feed_grads_kernel(h0, h1, h2, h3, g0, g1, g2, g3, dgu_a, dgu_b, hidden_a, hidden_b,
                      out_ref, left_ref):
    tile = pl.program_id(0)
    size = h0.shape[0]

    def turn(pieces):
        for i, piece in enumerate(pieces):
            left_ref[:, i * size : (i + 1) * size] = piece[...].T

    @pl.when(tile == 0)
    def _():
        turn((h0, h1, h2, h3))

    gate_up_tiles = 2 * pl.num_programs(0) // 3

    @pl.when(tile == gate_up_tiles)
    def _():
        turn((g0, g1, g2, g3))

    @pl.when(tile < gate_up_tiles)
    def _():
        right = jnp.concatenate([dgu_a[...], dgu_b[...]], 0)
        out_ref[...] = dot_n(left_ref[...], right).astype(BF16)

    @pl.when(tile >= gate_up_tiles)
    def _():
        right = jnp.concatenate([hidden_a[...], hidden_b[...]], 0)
        out_ref[...] = dot_n(left_ref[...], right).astype(BF16)


def feed_grads(normed_pieces, grad_pieces, dgu_a, dgu_b, hidden_a, hidden_b):
    size, width = normed_pieces[0].shape
    half, hidden_w = hidden_a.shape
    column = 512
    tiles = 3 * hidden_w // column
    split = 2 * tiles // 3
    whole_piece = pl.BlockSpec((size, width), lambda i: (0, 0), pipeline_mode=pl.Buffered(1))
    dgu_spec = pl.BlockSpec((half, column), lambda i: (0, jnp.minimum(i, split - 1)))
    hidden_spec = pl.BlockSpec((half, column), lambda i: (0, jnp.maximum(i - split, 0)))
    return pl.pallas_call(
        feed_grads_kernel,
        grid=(tiles,),
        out_shape=jax.ShapeDtypeStruct((width, 3 * hidden_w), BF16),
        in_specs=[whole_piece] * 8 + [dgu_spec] * 2 + [hidden_spec] * 2,
        out_specs=pl.BlockSpec((width, column), lambda i: (0, i)),
        scratch_shapes=[pltpu.VMEM((width, 4 * size), BF16)],
        compiler_params=pltpu.CompilerParams(vmem_limit_bytes=56 * MIB),
        cost_estimate=pl.CostEstimate(
            flops=12 * half * width * hidden_w, bytes_accessed=22 * MIB, transcendentals=0),
        name="feed_grads",
    )(*normed_pieces, *grad_pieces, dgu_a, dgu_b, hidden_a, hidden_b)


LATE_OUT, LATE_WIDTH = 128, 640


def late_grads_kernel(place, h_ref, o0, o1, o2, o3, dqkv_ref, attn_ref, gains_ref, *refs):
    x_refs, y_refs = refs[0:4], refs[4:8]
    left_ref, first_ref, second_ref = refs[8:]
    ix, iz = place[1], place[2]
    width = h_ref.shape[1]
    heads_w = attn_ref.shape[1]
    size = o0.shape[0]
    rows = width // 16
    left_ref[...] = h_ref[...].T
    part = dot_n(left_ref[...], dqkv_ref[...]).astype(BF16)
    first_ref[:, :heads_w] = part[:, :heads_w]
    second_ref[:, LATE_WIDTH - heads_w :] = part[:, heads_w:]
    for i, piece in enumerate((o0, o1, o2, o3)):
        left_ref[:, i * size : (i + 1) * size] = piece[...].T
    part = dot_n(left_ref[...], attn_ref[...]).astype(BF16)
    first_ref[:, heads_w : heads_w + LATE_OUT] = part[:, :LATE_OUT]
    second_ref[:, : heads_w - LATE_OUT] = part[:, LATE_OUT:]
    first_ref[:, heads_w + LATE_OUT :] = gains_ref[...].T.astype(BF16)
    for offset in range(4):
        to_x = lax.rem(ix + 4 - offset, 4)
        to_z = lax.rem(iz + 4 - offset, 4)
        for block in range(4):
            x_refs[offset][block] = first_ref[block_at(to_x * 4 + block, rows), :]
            y_refs[offset][block] = second_ref[block_at(block * 4 + to_z, rows), :]


def late_grads(place, h_first, out_pieces, d_qkv, attn, gains):
    length, width = h_first.shape
    block = jax.ShapeDtypeStruct((4, width // 16, LATE_WIDTH), BF16)
    return pl.pallas_call(
        late_grads_kernel,
        out_shape=[block] * 8,
        in_specs=[scalars()] + [whole()] * 8,
        out_specs=[whole()] * 8,
        scratch_shapes=[
            pltpu.VMEM((width, length), BF16),
            pltpu.VMEM((width, LATE_WIDTH), BF16), pltpu.VMEM((width, LATE_WIDTH), BF16),
        ],
        compiler_params=pltpu.CompilerParams(vmem_limit_bytes=56 * MIB),
        cost_estimate=pl.CostEstimate(
            flops=2 * length * width * 1152, bytes_accessed=16 * MIB, transcendentals=0),
        name="late_grads",
    )(place, h_first, *out_pieces, d_qkv, attn, gains)


def late_middle_kernel(place, *refs):
    x_in, y_in, outs = refs[0:4], refs[4:8], refs[8:]
    ix, iz = place[1], place[2]
    for inputs, at, first in ((x_in, iz, 0), (y_in, ix, 4)):
        for offset in range(4):
            to = lax.rem(at + 4 - offset, 4)
            total = inputs[0][to].astype(F32)
            for ref in inputs[1:]:
                total += ref[to].astype(F32)
            outs[first + offset][...] = total.astype(BF16)


def late_middle(place, along_x, along_z):
    _, rows, width = along_x[0].shape
    block = jax.ShapeDtypeStruct((rows, width), BF16)
    return pl.pallas_call(
        late_middle_kernel,
        out_shape=[block] * 8,
        in_specs=[scalars()] + [whole()] * 8,
        out_specs=[whole()] * 8,
        name="late_middle",
    )(place, *along_x, *along_z)


def late_last_kernel(place, *refs):
    x_in, y_in, keep_ref, send_ref = refs[0:4], refs[4:8], refs[8], refs[9]
    mine = place[3]
    rows = keep_ref.shape[0]
    for inputs, columns in ((x_in, slice(0, LATE_WIDTH)), (y_in, slice(LATE_WIDTH, 2 * LATE_WIDTH))):
        for ref, half in ((keep_ref, mine), (send_ref, 1 - mine)):
            at = block_at(half, rows)
            total = inputs[0][at, :].astype(F32)
            for other_ref in inputs[1:]:
                total += other_ref[at, :].astype(F32)
            ref[:, columns] = total.astype(ref.dtype)


def late_last(place, along_z, along_x):
    rows, width = along_x[0].shape
    return pl.pallas_call(
        late_last_kernel,
        out_shape=[
            jax.ShapeDtypeStruct((rows // 2, 2 * width), F32),
            jax.ShapeDtypeStruct((rows // 2, 2 * width), BF16),
        ],
        in_specs=[scalars()] + [whole()] * 8,
        out_specs=[whole()] * 2,
        name="late_last",
    )(place, *along_z, *along_x)


def norm_rows(values_in):
    factor = lax.rsqrt(jnp.mean(values_in * values_in, -1, keepdims=True) + norm_eps)
    return (values_in * factor, factor)


def norm_back(grad_in, normed, factor, gain_row):
    grad_normed = grad_in * gain_row
    inner = jnp.mean(grad_normed * normed, -1, keepdims=True)
    return (factor * (grad_normed - normed * inner), jnp.sum(grad_in * normed, 0))


def from_offset(v, axis, offset, size):
    return lax.ppermute(v, axis, [((i + offset) % size, i) for i in range(size)])


def other(v, axis):
    return from_offset(v, axis, 1, 2)


def pair_rows(v, axis):
    it = other(v, axis)
    flag = lax.axis_index(axis) == 0
    return jnp.concatenate([jnp.where(flag, v, it), jnp.where(flag, it, v)], 0)


def tensor_pieces(v):
    far = other(v, "yl")
    return [v, other(v, "core"), far, other(far, "core")]


def tensor_sum(own, core, chip, diagonal):
    far = chip.astype(F32) + other(diagonal, "core").astype(F32)
    near = own.astype(F32) + other(core, "core").astype(F32)
    return near + other(far.astype(BF16), "yl").astype(F32)


def from_others(v, axis):
    return [v[0]] + [from_offset(v[i], axis, i, 4) for i in range(1, 4)]


def sum_everywhere(v):
    for axis in ("core", "yl", "yh"):
        v = v + other(v, axis)
    for axis in ("z", "x"):
        v = v + from_offset(v, axis, 1, 4) + from_offset(v, axis, 3, 4) + from_offset(v, axis, 2, 4)
    return v


def gather_rows(v):
    return lax.all_gather(pair_rows(v, "yh"), ("x", "z"), axis=0, tiled=True)


def scatter_rows(v):
    two = lax.psum_scatter(v, ("x", "z"), scatter_dimension=0, tiled=True)
    rows = two.shape[0] // 2
    iyh = lax.axis_index("yh")
    keep = lax.dynamic_slice_in_dim(two, iyh * rows, rows, 0)
    send = lax.dynamic_slice_in_dim(two, (1 - iyh) * rows, rows, 0)
    return keep.astype(F32) + other(send, "yh").astype(F32)


def body(tokens, norm_gains, w_query, w_keyval, w_out, w_gateup, w_down, cotangent):
    D = tokens.shape[1]
    length = 4 * tokens.shape[0]
    hidden_w = w_down.shape[0]
    heads_w = w_query.shape[1]
    gains_w = norm_gains.shape[1]
    block = lax.axis_index("yl") * 2 + lax.axis_index("core")
    row = (lax.axis_index("x") * 4 + lax.axis_index("z")) * 2 + lax.axis_index("yh")
    gains_at = (row * 4 + block) * gains_w
    place = jnp.stack(
        [block, lax.axis_index("x"), lax.axis_index("z"), lax.axis_index("yh")]
    ).astype(jnp.int32)

    attn_w = gather_rows(jnp.concatenate([w_query, w_keyval, w_out.T], 1))
    mlp_w = gather_rows(jnp.concatenate([w_gateup[:, 0], w_gateup[:, 1], w_down.T], 1))
    token_pieces = tensor_pieces(tokens)
    gain_rows = sum_everywhere(
        lax.dynamic_update_slice(jnp.zeros((2, D), F32), norm_gains, (0, gains_at))
    )
    grad_pieces = tensor_pieces(cotangent)
    token_pieces, grad_pieces = lax.optimization_barrier((token_pieces, grad_pieces))

    positions = jnp.arange(length).astype(F32)
    freqs = rope_base ** (-(jnp.arange(HD // 2).astype(F32) * 2.0 / HD))
    angles = freqs[:, None] * positions[None, :]
    cosine, sine = jnp.cos(angles), jnp.sin(angles)

    h_first, qt, q, kt, k, vt, v = project(place, token_pieces, attn_w, gain_rows, cosine, sine)
    attn, attnt, lse, keep, send = attend(place, qt, k, vt, attn_w)
    both = keep.astype(F32) + other(send, "core").astype(F32)
    middle = tokens.astype(F32) + both[0] + other(both[1].astype(BF16), "yl").astype(F32)
    normed2, factor2 = norm_rows(middle)
    h_pieces = tensor_pieces((normed2 * gain_rows[1]).astype(BF16))

    hidden_a, dgu_a = feed(mlp_w, h_pieces[:2], grad_pieces[:2], with_second=False)
    hidden_b, dgu_b, back_chip, back_diag, out_chip, out_diag = feed(
        mlp_w, h_pieces[2:], grad_pieces[2:]
    )
    back_own, back_core, out_own, out_core = feed(
        mlp_w, h_pieces[:2], grad_pieces[:2], first=(hidden_a, dgu_a)
    )
    mlp_grads = feed_grads(h_pieces, grad_pieces, dgu_a, dgu_b, hidden_a, hidden_b)
    early = scatter_rows(mlp_grads)
    d_h2_own = tensor_sum(back_own, back_core, back_chip, back_diag)

    d_norm2, gain_two = norm_back(d_h2_own, normed2, factor2, gain_rows[1])
    d_middle = cotangent.astype(F32) + d_norm2
    out_pieces = tensor_pieces(d_middle.astype(BF16))
    out_pieces, out_parts = lax.optimization_barrier(
        (out_pieces, (out_own, out_core, out_chip, out_diag))
    )
    result = (middle + tensor_sum(*out_parts)).astype(BF16)

    d_qkv, keep, send, gain_one = attend_back(
        place, out_pieces, token_pieces, attn_w, qt, q, kt, k, v, attnt, lse, cosine, sine
    )
    gains = jnp.concatenate([gain_one, gain_two[None], jnp.zeros((126, D), F32)], 0)
    parts = late_grads(place, h_first, out_pieces, d_qkv, attn, gains)
    parts = late_middle(place, from_others(parts[:4], "x"), from_others(parts[4:], "z"))
    late_keep, late_send = late_last(
        place, from_others(parts[:4], "z"), from_others(parts[4:], "x")
    )
    late = late_keep + other(late_send, "yh").astype(F32)

    both = keep.astype(F32) + other(send, "core").astype(F32)
    d_h1_own = both[0] + other(both[1].astype(BF16), "yl").astype(F32)
    normed1, factor1 = norm_rows(tokens.astype(F32))
    d_norm1, _ = norm_back(d_h1_own, normed1, factor1, gain_rows[0])
    input_grad = (d_middle + d_norm1).astype(BF16)

    out_at = heads_w + LATE_OUT
    grad_out = jnp.concatenate([late[:, heads_w:out_at], late[:, LATE_WIDTH : LATE_WIDTH + heads_w - LATE_OUT]], 1)
    gain_sum = late[:, out_at : out_at + 2].T
    for axis in ("core", "yl"):
        gain_sum = gain_sum + other(gain_sum, axis)
    grad_gains = lax.dynamic_slice(gain_sum, (0, block * gains_w), (2, gains_w))
    return (
        result,
        input_grad,
        late[:, :heads_w],
        late[:, 2 * LATE_WIDTH - heads_w :],
        grad_out.T,
        early[:, : 2 * hidden_w].reshape(-1, 2, hidden_w),
        early[:, 2 * hidden_w :].T,
        grad_gains,
    )


def solution(mesh):
    fine = Mesh(mesh.devices.reshape(4, 4, 2, 2, 2), ("x", "z", "yh", "yl", "core"))
    dp = ("x", "z", "yh")
    tensor = ("yl", "core")
    every = dp + tensor
    weights = (P(dp, tensor), P(dp, tensor), P(tensor, dp), P(dp, None, tensor), P(tensor, dp))
    rows = P(every, None)
    gains = P(None, every)
    return jax.shard_map(
        body,
        mesh=fine,
        in_specs=(rows, gains) + weights + (rows,),
        out_specs=(rows, rows) + weights + (gains,),
        check_vma=False,
    )
```

```python
import jax
import jax.numpy as jnp
from jax import lax
from jax.experimental import pallas as pl
from jax.experimental.pallas import tpu as pltpu
from jax.sharding import Mesh, PartitionSpec as P

HD = 96
F32 = jnp.float32
BF16 = jnp.bfloat16
norm_eps = 1e-05
rope_base = 100000.0
LOG2E = 1.4426950408889634
SCALE = HD ** (-0.5)
MIB = 1024 * 1024
SMALL = pl.CostEstimate(flops=1, bytes_accessed=1, transcendentals=0)

QUERY_AT, KEYVAL_AT, OUT_AT, ATTN_WIDTH = 0, 384, 768, 1152


def dot_n(left, right):
    return jnp.dot(left, right, preferred_element_type=F32)


def dot_t(left, right):
    return lax.dot_general(left, right, (((1,), (1,)), ((), ())), preferred_element_type=F32)


def dot_tn(left, right):
    return lax.dot_general(left, right, (((0,), (0,)), ((), ())), preferred_element_type=F32)


def block_at(index, size):
    return pl.ds(pl.multiple_of(index * size, size), size)


def causal_mask(scores, size):
    key_at = lax.broadcasted_iota(jnp.int32, (size, size), 0)
    query_at = lax.broadcasted_iota(jnp.int32, (size, size), 1)
    tail = jnp.where(key_at <= query_at, scores[-size:], -1e30)
    if scores.shape[0] == size:
        return tail
    return jnp.concatenate([scores[:-size], tail], 0)


class Moves:
    def __init__(self, sems):
        self.sems = sems
        self.started = []

    def start(self, source, target):
        copy = pltpu.make_async_copy(source, target, self.sems.at[len(self.started)])
        copy.start()
        self.started.append(copy)
        return copy

    def wait(self):
        for copy in self.started:
            copy.wait()


def vmem(shape, dtype=BF16):
    return pltpu.VMEM(shape, dtype)


def like(shape, dtype=BF16):
    return jax.ShapeDtypeStruct(shape, dtype)


def whole():
    return pl.BlockSpec(memory_space=pltpu.VMEM)


def apart():
    return pl.BlockSpec(memory_space=pl.ANY)


def scalars():
    return pl.BlockSpec(memory_space=pltpu.SMEM)


def kernel_call(kernel, name, place, small, large, outs, small_outs, scratch, fetches, stores, limit):
    return pl.pallas_call(
        kernel,
        out_shape=list(small_outs) + list(outs),
        in_specs=[scalars()] + [whole()] * len(small) + [apart()] * len(large),
        out_specs=[whole()] * len(small_outs) + [apart()] * len(outs),
        scratch_shapes=list(scratch)
        + [pltpu.SemaphoreType.DMA((fetches,)), pltpu.SemaphoreType.DMA((stores,))],
        compiler_params=pltpu.CompilerParams(vmem_limit_bytes=limit * MIB),
        cost_estimate=SMALL,
        name=name,
    )(place, *small, *large)


def attend_kernel(place, gains_ref, cos_ref, sin_ref, t0, t1, t2, t3, w_hbm,
                  lse_ref, h_hbm, qt_hbm, q_hbm, kt_hbm, k_hbm, v_hbm, attn_hbm, attnt_hbm,
                  o0, o1, o2, o3,
                  t_ref, w_ref, h_ref, qt_ref, q_ref, kt_ref, k_ref, vt_ref, v_ref,
                  natural, attn_ref, attnt_ref, part_ref, in_sem, out_sem):
    block = place[0]
    half = HD // 2
    size = t_ref.shape[1]
    heads, _, length = qt_ref.shape
    group_size = heads // k_ref.shape[0]
    fetch, store = Moves(in_sem), Moves(out_sem)
    pieces = (t0, t1, t2, t3)
    came = [fetch.start(pieces[0], t_ref.at[0])]
    proj = pl.ds(0, OUT_AT)
    w_came = fetch.start(w_hbm.at[:, proj], w_ref.at[:, proj])
    came += [fetch.start(pieces[i], t_ref.at[i]) for i in range(1, 4)]
    last = pl.ds(OUT_AT, ATTN_WIDTH - OUT_AT)
    o_came = fetch.start(w_hbm.at[:, last], w_ref.at[:, last])
    gain_row = gains_ref[0:1, :]
    for step in range(4):
        at = block_at(lax.bitwise_xor(block, step), size)
        came[step].wait()
        value = t_ref[step].astype(F32)
        factor = lax.rsqrt(jnp.mean(value * value, -1, keepdims=True) + norm_eps)
        normed = (value * factor * gain_row).astype(BF16)
        h_ref[at, :] = normed
        cosine = cos_ref[:, at]
        sine = sin_ref[:, at]
        if step == 0:
            w_came.wait()
        every = dot_n(normed, w_ref[:, :OUT_AT]).T
        query, keyval = every[:KEYVAL_AT], every[KEYVAL_AT:]

        def rotated(field):
            first, second = field[:half], field[half:]
            return jnp.concatenate(
                [first * cosine - second * sine, second * cosine + first * sine], 0
            )

        for head in range(query.shape[0] // HD):
            turned = rotated(query[head * HD : (head + 1) * HD])
            qt_ref[head, :, at] = turned.astype(BF16)
            q_ref[head, at, :] = turned.T.astype(BF16)
        for head in range(keyval.shape[0] // (2 * HD)):
            turned = rotated(keyval[2 * head * HD : (2 * head + 1) * HD])
            value_t = keyval[(2 * head + 1) * HD : (2 * head + 2) * HD]
            kt_ref[head, :, at] = turned.astype(BF16)
            k_ref[head, at, :] = turned.T.astype(BF16)
            vt_ref[head, :, at] = value_t.astype(BF16)
            v_ref[head, at, :] = value_t.T.astype(BF16)
    for source, target in ((h_ref, h_hbm), (qt_ref, qt_hbm), (q_ref, q_hbm), (kt_ref, kt_hbm),
                           (k_ref, k_hbm), (v_ref, v_hbm)):
        store.start(source, target)

    def one_head(head, carry):
        group = head // group_size
        for step in range(4):
            reach = (step + 1) * size
            columns = slice(step * size, reach)
            scores = causal_mask(dot_n(k_ref[group, :reach, :], qt_ref[head, :, columns]), size)
            top = jnp.max(scores, 0, keepdims=True)
            expo = jnp.exp2((scores - top) * (SCALE * LOG2E))
            total = jnp.sum(expo, 0, keepdims=True)
            probs = (expo * (1.0 / total)).astype(BF16)
            mixed = dot_n(vt_ref[group, :, :reach], probs)
            attnt_ref[head, :, columns] = mixed.astype(BF16)
            lse_ref[head, :, columns] = top * (SCALE * LOG2E) + jnp.log2(total)
        return carry

    lax.fori_loop(0, heads, one_head, 0)
    store.start(attnt_ref, attnt_hbm)
    natural[...] = attnt_ref[...].reshape(heads * HD, length).T
    o_came.wait()
    for step, out in ((1, o1), (3, o3), (2, o2), (0, o0)):
        at = block_at(lax.bitwise_xor(block, step), size)
        rows = natural[at, :]
        attn_ref[step * size : (step + 1) * size, :] = rows
        part_ref[step] = dot_t(rows, w_ref[:, OUT_AT:ATTN_WIDTH]).astype(BF16)
        store.start(part_ref.at[step], out)
    store.start(attn_ref, attn_hbm)
    store.wait()


def attend(place, pieces, weights, gain_rows, cosine, sine):
    size, width = pieces[0].shape
    length = 4 * size
    heads = (KEYVAL_AT - QUERY_AT) // HD
    groups = (OUT_AT - KEYVAL_AT) // (2 * HD)
    columns, rows = (heads, HD, length), (heads, length, HD)
    g_columns, g_rows = (groups, HD, length), (groups, length, HD)
    outs = [(length, width), columns, rows, g_columns, g_rows, g_rows,
            (length, heads * HD), columns] + [(size, width)] * 4
    scratch = [(4, size, width), (width, ATTN_WIDTH), (length, width), columns, rows,
               g_columns, g_rows, g_columns, g_rows,
               (length, heads * HD), (length, heads * HD), columns, (4, size, width)]
    return kernel_call(
        attend_kernel, "attend", place, (gain_rows, cosine, sine), (*pieces, weights),
        [like(s) for s in outs], [like((heads, 1, length), F32)], [vmem(s) for s in scratch],
        6, 12, 52)


def attend_back_kernel(place, lse_ref, cos_ref, sin_ref, gain2_ref,
                       o0, o1, o2, o3, t0, t1, t2, t3, w_hbm, h_hbm, qt_hbm, q_hbm, kt_hbm,
                       k_hbm, v_hbm, attn_hbm, attnt_hbm,
                       c0, c1, c2, c3, x0, x1, x2, x3, y0, y1, y2, y3,
                       o_ref, t_ref, w_ref, h_ref, qt_ref, q_ref, kt_ref, k_ref, v_ref,
                       attn_ref, attnt_ref,
                       do_ref, dot_ref, dqkv_ref, part_ref, first_ref, second_ref,
                       delta_ref, dk_ref, dv_ref, turned_ref, in_sem, out_sem):
    block, ix, iz = place[0], place[1], place[2]
    heads, _, length = qt_ref.shape
    groups = k_ref.shape[0]
    group_size = heads // groups
    size = length // 4
    half = HD // 2
    width = w_ref.shape[0]
    heads_w = heads * HD
    fetch, store = Moves(in_sem), Moves(out_sem)
    last = pl.ds(OUT_AT, ATTN_WIDTH - OUT_AT)
    early = [fetch.start(w_hbm.at[:, last], w_ref.at[:, last])]
    early += [
        fetch.start(piece, o_ref.at[pl.ds(i * size, size), :])
        for i, piece in enumerate((o0, o1, o2, o3))
    ]
    for source, target in ((attnt_hbm, attnt_ref), (qt_hbm, qt_ref), (q_hbm, q_ref),
                           (kt_hbm, kt_ref), (k_hbm, k_ref), (v_hbm, v_ref)):
        early.append(fetch.start(source, target))
    proj = pl.ds(0, OUT_AT)
    later = [
        fetch.start(attn_hbm, attn_ref),
        fetch.start(h_hbm, h_ref),
        fetch.start(w_hbm.at[:, proj], w_ref.at[:, proj]),
    ]
    later += [fetch.start(piece, t_ref.at[i]) for i, piece in enumerate((t0, t1, t2, t3))]
    early[0].wait()
    for step in range(4):
        at = block_at(lax.bitwise_xor(block, step), size)
        early[1 + step].wait()
        grad = dot_n(o_ref[step * size : (step + 1) * size, :], w_ref[:, OUT_AT:ATTN_WIDTH])
        grad_t = grad.T.astype(BF16)
        grad = grad.astype(BF16)
        for head in range(heads):
            dot_ref[head, :, at] = grad_t[head * HD : (head + 1) * HD]
            do_ref[head, at, :] = grad[:, head * HD : (head + 1) * HD]
    for copy in early[5:]:
        copy.wait()
    delta_ref[...] = jnp.sum(
        attnt_ref[...].astype(F32) * dot_ref[...].astype(F32), 1, keepdims=True)
    dk_ref[...] = jnp.zeros_like(dk_ref)
    dv_ref[...] = jnp.zeros_like(dv_ref)

    def turned_back(field, cosine, sine):
        first, second = field[:half], field[half:]
        return jnp.concatenate(
            [first * cosine + second * sine, second * cosine - first * sine], 0)

    def one_head(head, carry):
        group = head // group_size
        for step in range(4):
            reach = (step + 1) * size
            columns = slice(step * size, reach)
            scores = causal_mask(dot_n(k_ref[group, :reach, :], qt_ref[head, :, columns]), size)
            soft = jnp.exp2(scores * (SCALE * LOG2E) - lse_ref[head, :, columns])
            d_probs = dot_n(v_ref[group, :reach, :], dot_ref[head, :, columns])
            d_scores = (soft * (d_probs - delta_ref[head, :, columns])).astype(BF16)
            dv_ref[group, :reach, :] += dot_n(soft.astype(BF16), do_ref[head, columns, :])
            dk_ref[group, :reach, :] += dot_n(d_scores, q_ref[head, columns, :])
            d_query = dot_n(kt_ref[group, :, :reach], d_scores) * SCALE
            turned_ref[head, :, columns] = turned_back(
                d_query, cos_ref[:, columns], sin_ref[:, columns])
        return carry

    lax.fori_loop(0, heads, one_head, 0)
    for group in range(groups):
        turned_ref[heads + 2 * group] = turned_back(
            dk_ref[group].T * SCALE, cos_ref[...], sin_ref[...])
        turned_ref[heads + 2 * group + 1] = dv_ref[group].T
    dqkv_ref[...] = turned_ref[...].reshape((heads + 2 * groups) * HD, length).T.astype(BF16)
    for copy in later:
        copy.wait()

    gain = jnp.zeros((1, width), F32)
    for step, out in ((1, c1), (3, c3), (2, c2), (0, c0)):
        at = block_at(lax.bitwise_xor(block, step), size)
        part = dot_t(dqkv_ref[at, :], w_ref[:, QUERY_AT:OUT_AT])
        value = t_ref[step].astype(F32)
        factor = lax.rsqrt(jnp.mean(value * value, -1, keepdims=True) + norm_eps)
        gain += jnp.sum(part * (value * factor), 0, keepdims=True)
        part_ref[step] = part.astype(BF16)
        store.start(part_ref.at[step], out)

    rows = width // 16
    part = dot_tn(h_ref[...], dqkv_ref[...]).astype(BF16)
    first_ref[:, :heads_w] = part[:, :heads_w]
    second_ref[:, LATE_WIDTH - heads_w :] = part[:, heads_w:]
    part = dot_tn(o_ref[...], attn_ref[...]).astype(BF16)
    first_ref[:, heads_w : heads_w + LATE_OUT] = part[:, :LATE_OUT]
    second_ref[:, : heads_w - LATE_OUT] = part[:, LATE_OUT:]
    gains = jnp.concatenate([gain, gain2_ref[...], jnp.zeros((126, width), F32)], 0)
    first_ref[:, heads_w + LATE_OUT :] = gains.T.astype(BF16)
    for offset, (x_out, y_out) in enumerate(((x0, y0), (x1, y1), (x2, y2), (x3, y3))):
        to_x = lax.rem(ix + 4 - offset, 4)
        to_z = lax.rem(iz + 4 - offset, 4)
        store.start(first_ref.at[block_at(to_x, 4 * rows), :], x_out)
        for i in range(4):
            store.start(second_ref.at[block_at(i * 4 + to_z, rows), :], y_out.at[i])
    store.wait()


def attend_back(place, lse, cosine, sine, gain_two, pieces, token_pieces, weights, h_first,
                qt, q, kt, k, v, attn, attnt):
    size, width = pieces[0].shape
    heads, _, length = qt.shape
    groups = k.shape[0]
    every = heads + 2 * groups
    rows = width // 16
    outs = [(size, width)] * 4 + [(4 * rows, LATE_WIDTH)] * 4 + [(4, rows, LATE_WIDTH)] * 4
    scratch = [
        (length, width), (4, size, width), (width, ATTN_WIDTH), (length, width),
        qt.shape, q.shape, kt.shape, k.shape, v.shape, attn.shape, attnt.shape,
        (heads, length, HD), (heads, HD, length), (length, every * HD), (4, size, width),
        (width, LATE_WIDTH), (width, LATE_WIDTH),
    ]
    wide = [(heads, 1, length), (groups, length, HD), (groups, length, HD), (every, HD, length)]
    return kernel_call(
        attend_back_kernel, "attend_back", place, (lse, cosine, sine, gain_two),
        (*pieces, *token_pieces, weights, h_first, qt, q, kt, k, v, attn, attnt),
        [like(s) for s in outs], [],
        [vmem(s) for s in scratch] + [vmem(s, F32) for s in wide], 18, 24, 56)


def feed_kernel(place, h0, h1, g0, g1, w_hbm, hidden_hbm, dgu_hbm, b0, b1, r0, r1,
                w_ref, h_ref, g_ref, hidden_ref, dgu_ref, back_ref, out_ref, in_sem, out_sem):
    del place
    hidden_w = hidden_ref.shape[1]
    size = h_ref.shape[1]
    parts = [slice(i * hidden_w, (i + 1) * hidden_w) for i in range(3)]
    fetch, store = Moves(in_sem), Moves(out_sem)

    def weight(i):
        at = pl.ds(i * hidden_w, hidden_w)
        return fetch.start(w_hbm.at[:, at], w_ref.at[:, at])

    came = [fetch.start(h0, h_ref.at[0]), weight(0), weight(1), fetch.start(g0, g_ref.at[0]),
            weight(2), fetch.start(h1, h_ref.at[1]), fetch.start(g1, g_ref.at[1])]
    for i, (back, out) in enumerate(((b0, r0), (b1, r1))):
        rows = slice(i * size, (i + 1) * size)
        at = pl.ds(i * size, size)
        for copy in came[0:2] if i == 0 else came[5:7]:
            copy.wait()
        gate = dot_n(h_ref[i], w_ref[:, parts[0]])
        if i == 0:
            came[2].wait()
        up = dot_n(h_ref[i], w_ref[:, parts[1]])
        sig = 1.0 / (1.0 + jnp.exp2(gate * (-LOG2E)))
        silu = gate * sig
        hidden = (silu * up).astype(BF16)
        hidden_ref[rows, :] = hidden
        store.start(hidden_ref.at[at, :], hidden_hbm.at[at, :])
        if i == 0:
            came[3].wait()
            came[4].wait()
        d_hidden = dot_n(g_ref[i], w_ref[:, parts[2]])
        dgu_ref[rows, :hidden_w] = (
            d_hidden * up * (sig * (1.0 + gate * (1.0 - sig)))).astype(BF16)
        dgu_ref[rows, hidden_w:] = (d_hidden * silu).astype(BF16)
        store.start(dgu_ref.at[at, :], dgu_hbm.at[at, :])
        back_ref[i] = dot_t(dgu_ref[rows, :], w_ref[:, : 2 * hidden_w]).astype(BF16)
        store.start(back_ref.at[i], back)
        out_ref[i] = dot_t(hidden_ref[rows, :], w_ref[:, parts[2]]).astype(BF16)
        store.start(out_ref.at[i], out)
    store.wait()


def feed(place, weights, normed_pieces, grad_pieces):
    size, width = normed_pieces[0].shape
    hidden_w = weights.shape[1] // 3
    wide = [(2 * size, hidden_w), (2 * size, 2 * hidden_w)]
    return kernel_call(
        feed_kernel, "feed", place, (), (*normed_pieces, *grad_pieces, weights),
        [like(s) for s in wide + [(size, width)] * 4], [],
        [vmem(s) for s in [weights.shape] + [(2, size, width)] * 2 + wide + [(2, size, width)] * 2],
        7, 8, 40)


def feed_grads_kernel(place, h0, h1, h2, h3, g0, g1, g2, g3, dgu_a, dgu_b, hidden_a, hidden_b,
                      out_hbm, h_ref, g_ref, dgu_ref, hidden_ref, out_ref, in_sem, out_sem):
    del place
    size = h0.shape[0]
    half, hidden_w = hidden_a.shape
    column = 512
    fetch, store = Moves(in_sem), Moves(out_sem)

    def rows_of(pieces, ref):
        return [
            fetch.start(piece, ref.at[pl.ds(i * size, size), :]) for i, piece in enumerate(pieces)
        ]

    def tiles_of(pieces, ref):
        tiles = []
        for tile in range(ref.shape[1] // column):
            at = pl.ds(tile * column, column)
            tiles.append([
                fetch.start(piece.at[:, at], ref.at[pl.ds(i * half, half), at])
                for i, piece in enumerate(pieces)
            ])
        return tiles

    h_came = rows_of((h0, h1, h2, h3), h_ref)
    dgu_came = tiles_of((dgu_a, dgu_b), dgu_ref)
    g_came = rows_of((g0, g1, g2, g3), g_ref)
    hidden_came = tiles_of((hidden_a, hidden_b), hidden_ref)
    at = 0
    for came, left, tiles, right in (
        (h_came, h_ref, dgu_came, dgu_ref), (g_came, g_ref, hidden_came, hidden_ref)
    ):
        for copy in came:
            copy.wait()
        for tile, copies in enumerate(tiles):
            for copy in copies:
                copy.wait()
            columns = pl.ds(at, column)
            out_ref[:, columns] = dot_tn(
                left[...], right[:, tile * column : (tile + 1) * column]).astype(BF16)
            store.start(out_ref.at[:, columns], out_hbm.at[:, columns])
            at += column
    store.wait()


def feed_grads(place, normed_pieces, grad_pieces, dgu_a, dgu_b, hidden_a, hidden_b):
    size, width = normed_pieces[0].shape
    half, hidden_w = hidden_a.shape
    scratch = [(4 * size, width)] * 2 + [(2 * half, 2 * hidden_w), (2 * half, hidden_w),
                                         (width, 3 * hidden_w)]
    return kernel_call(
        feed_grads_kernel, "feed_grads", place, (),
        (*normed_pieces, *grad_pieces, dgu_a, dgu_b, hidden_a, hidden_b),
        [like((width, 3 * hidden_w))], [], [vmem(s) for s in scratch], 20, 6, 36)[0]


LATE_OUT, LATE_WIDTH = 128, 640


def late_middle_kernel(place, *refs):
    x_in, y_in, outs = refs[0:4], refs[4:8], refs[8:]
    ix, iz = place[1], place[2]
    rows = outs[0].shape[0]
    for offset in range(4):
        at = block_at(lax.rem(iz + 4 - offset, 4), rows)
        total = x_in[0][at, :].astype(F32)
        for ref in x_in[1:]:
            total += ref[at, :].astype(F32)
        outs[offset][...] = total.astype(BF16)
        to = lax.rem(ix + 4 - offset, 4)
        total = y_in[0][to].astype(F32)
        for ref in y_in[1:]:
            total += ref[to].astype(F32)
        outs[4 + offset][...] = total.astype(BF16)


def late_middle(place, along_x, along_z):
    _, rows, width = along_z[0].shape
    return pl.pallas_call(
        late_middle_kernel,
        out_shape=[like((rows, width))] * 8,
        in_specs=[scalars()] + [whole()] * 8,
        out_specs=[whole()] * 8,
        cost_estimate=SMALL,
        name="late_middle",
    )(place, *along_x, *along_z)


def late_last_kernel(place, *refs):
    x_in, y_in, keep_ref, send_ref = refs[0:4], refs[4:8], refs[8], refs[9]
    mine = place[3]
    rows = keep_ref.shape[0]
    for inputs, columns in ((x_in, slice(0, LATE_WIDTH)), (y_in, slice(LATE_WIDTH, 2 * LATE_WIDTH))):
        for ref, half in ((keep_ref, mine), (send_ref, 1 - mine)):
            at = block_at(half, rows)
            total = inputs[0][at, :].astype(F32)
            for other_ref in inputs[1:]:
                total += other_ref[at, :].astype(F32)
            ref[:, columns] = total.astype(ref.dtype)


def late_last(place, along_z, along_x):
    rows, width = along_x[0].shape
    return pl.pallas_call(
        late_last_kernel,
        out_shape=[
            jax.ShapeDtypeStruct((rows // 2, 2 * width), F32),
            jax.ShapeDtypeStruct((rows // 2, 2 * width), BF16),
        ],
        in_specs=[scalars()] + [whole()] * 8,
        out_specs=[whole()] * 2,
        cost_estimate=SMALL,
        name="late_last",
    )(place, *along_z, *along_x)


def norm_rows(values_in):
    factor = lax.rsqrt(jnp.mean(values_in * values_in, -1, keepdims=True) + norm_eps)
    return (values_in * factor, factor)


def norm_back(grad_in, normed, factor, gain_row):
    grad_normed = grad_in * gain_row
    inner = jnp.mean(grad_normed * normed, -1, keepdims=True)
    return (factor * (grad_normed - normed * inner), jnp.sum(grad_in * normed, 0))


def from_offset(v, axis, offset, size):
    return lax.ppermute(v, axis, [((i + offset) % size, i) for i in range(size)])


def other(v, axis):
    return from_offset(v, axis, 1, 2)


def pair_rows(v, axis):
    it = other(v, axis)
    flag = lax.axis_index(axis) == 0
    return jnp.concatenate([jnp.where(flag, v, it), jnp.where(flag, it, v)], 0)


def near_sum(own, core):
    return own.astype(F32) + other(core, "core").astype(F32)


def far_sum(chip, diagonal):
    return near_sum(chip, diagonal).astype(BF16)


def after(value, first):
    return lax.optimization_barrier((value, first))


def from_others(v, axis):
    return [v[0]] + [from_offset(v[i], axis, i, 4) for i in range(1, 4)]


def gather_rows(v):
    return lax.all_gather(pair_rows(v, "yh"), ("x", "z"), axis=0, tiled=True)


def scatter_rows(v):
    two = lax.psum_scatter(v, ("x", "z"), scatter_dimension=0, tiled=True)
    rows = two.shape[0] // 2
    iyh = lax.axis_index("yh")
    keep = lax.dynamic_slice_in_dim(two, iyh * rows, rows, 0)
    send = lax.dynamic_slice_in_dim(two, (1 - iyh) * rows, rows, 0)
    return keep.astype(F32) + other(send, "yh").astype(F32)


def body(tokens, norm_gains, w_query, w_keyval, w_out, w_gateup, w_down, cotangent):
    D = tokens.shape[1]
    length = 4 * tokens.shape[0]
    hidden_w = w_down.shape[0]
    heads_w = w_query.shape[1]
    gains_w = norm_gains.shape[1]
    block = lax.axis_index("yl") * 2 + lax.axis_index("core")
    row = (lax.axis_index("x") * 4 + lax.axis_index("z")) * 2 + lax.axis_index("yh")
    gains_at = (row * 4 + block) * gains_w
    place = jnp.stack(
        [block, lax.axis_index("x"), lax.axis_index("z"), lax.axis_index("yh")]
    ).astype(jnp.int32)

    attn_w = gather_rows(jnp.concatenate([w_query, w_keyval, w_out.T], 1))
    mlp_w = gather_rows(jnp.concatenate([w_gateup[:, 0], w_gateup[:, 1], w_down.T], 1))
    gain_rows = lax.dynamic_update_slice(jnp.zeros((2, D), F32), norm_gains, (0, gains_at))
    for axis in ("core", "yl", "yh"):
        gain_rows = gain_rows + other(gain_rows, axis)
    tokens, gain_rows = after(tokens, gain_rows)
    for axis in ("z", "x"):
        gain_rows = gain_rows + sum(from_offset(gain_rows, axis, i, 4) for i in (1, 3, 2))
    token_far = other(tokens, "yl")
    token_pieces = [tokens, other(tokens, "core"), token_far, other(token_far, "core")]
    cotangent, token_far = after(cotangent, token_far)
    grad_far = other(cotangent, "yl")
    grad_pieces = [cotangent, other(cotangent, "core"), grad_far, other(grad_far, "core")]
    token_pieces, grad_pieces = after(token_pieces, grad_pieces)

    positions = jnp.arange(length).astype(F32)
    freqs = rope_base ** (-(jnp.arange(HD // 2).astype(F32) * 2.0 / HD))
    angles = freqs[:, None] * positions[None, :]
    cosine, sine = jnp.cos(angles), jnp.sin(angles)

    lse, h_first, qt, q, kt, k, v, attn, attnt, *parts = attend(
        place, token_pieces, attn_w, gain_rows, cosine, sine
    )
    middle_far = far_sum(parts[2], parts[3])
    middle = (
        tokens.astype(F32) + near_sum(parts[0], parts[1]) + other(middle_far, "yl").astype(F32)
    )
    normed2, factor2 = norm_rows(middle)
    h_own = (normed2 * gain_rows[1]).astype(BF16)

    h_pieces = [h_own, other(h_own, "core")]
    h_far = other(h_own, "yl")
    hidden_a, dgu_a, back_own, back_core, out_own, out_core = feed(
        place, mlp_w, h_pieces, grad_pieces[:2]
    )
    h_far, hidden_a = after(h_far, hidden_a)
    h_pieces += [h_far, other(h_far, "core")]
    hidden_b, dgu_b, back_chip, back_diag, out_chip, out_diag = feed(
        place, mlp_w, h_pieces[2:], grad_pieces[2:]
    )
    back_near = near_sum(back_own, back_core)
    out_near = near_sum(out_own, out_core)

    back_far = far_sum(back_chip, back_diag)
    hidden_b, back_far = after(hidden_b, back_far)
    mlp_grads = feed_grads(place, h_pieces, grad_pieces, dgu_a, dgu_b, hidden_a, hidden_b)
    back_far = other(back_far, "yl").astype(F32)
    mlp_grads, back_far = after(mlp_grads, back_far)
    d_h2_own = back_near + back_far
    early = scatter_rows(mlp_grads)
    out_far = far_sum(out_chip, out_diag)

    d_norm2, gain_two = norm_back(d_h2_own, normed2, factor2, gain_rows[1])
    d_middle = cotangent.astype(F32) + d_norm2
    d_out = d_middle.astype(BF16)
    d_out_far = other(d_out, "yl")
    d_out_far, out_near = after(d_out_far, out_near)
    out_pieces = [d_out, other(d_out, "core"), d_out_far, other(d_out_far, "core")]
    out_far, out_pieces = after(out_far, out_pieces)
    out_far = other(out_far, "yl").astype(F32)

    back = attend_back(
        place, lse, cosine, sine, gain_two[None], out_pieces, token_pieces, attn_w,
        h_first, qt, q, kt, k, v, attn, attnt,
    )
    out_near, back = after(out_near, back)
    result = (middle + out_near + out_far).astype(BF16)
    parts, late_parts = back[:4], back[4:]
    late_parts, result = after(late_parts, result)
    d_far = far_sum(parts[2], parts[3])
    along_x, along_z = from_others(late_parts[:4], "x"), from_others(late_parts[4:], "z")
    along_x, d_far = after(along_x, d_far)
    middle_parts = late_middle(place, along_x, along_z)
    along_z, along_x = from_others(middle_parts[:4], "z"), from_others(middle_parts[4:], "x")
    late_keep, late_send = late_last(place, along_z, along_x)
    d_h1_own = near_sum(parts[0], parts[1]) + other(d_far, "yl").astype(F32)
    late_other, (d_h1_own, early) = after(other(late_send, "yh"), (d_h1_own, early))
    late = late_keep + late_other.astype(F32)

    normed1, factor1 = norm_rows(tokens.astype(F32))
    d_norm1, _ = norm_back(d_h1_own, normed1, factor1, gain_rows[0])
    input_grad = (d_middle + d_norm1).astype(BF16)

    out_at = heads_w + LATE_OUT
    grad_out = jnp.concatenate([late[:, heads_w:out_at], late[:, LATE_WIDTH : LATE_WIDTH + heads_w - LATE_OUT]], 1)
    gain_sum = late[:, out_at : out_at + 2].T
    for axis in ("core", "yl"):
        gain_sum = gain_sum + other(gain_sum, axis)
    grad_gains = lax.dynamic_slice(gain_sum, (0, block * gains_w), (2, gains_w))
    return (
        result,
        input_grad,
        late[:, :heads_w],
        late[:, 2 * LATE_WIDTH - heads_w :],
        grad_out.T,
        early[:, : 2 * hidden_w].reshape(-1, 2, hidden_w),
        early[:, 2 * hidden_w :].T,
        grad_gains,
    )


def solution(mesh):
    fine = Mesh(mesh.devices.reshape(4, 4, 2, 2, 2), ("x", "z", "yh", "yl", "core"))
    dp = ("x", "z", "yh")
    tensor = ("yl", "core")
    every = dp + tensor
    weights = (P(dp, tensor), P(dp, tensor), P(tensor, dp), P(dp, None, tensor), P(tensor, dp))
    rows = P(every, None)
    gains = P(None, every)
    return jax.shard_map(
        body,
        mesh=fine,
        in_specs=(rows, gains) + weights + (rows,),
        out_specs=(rows, rows) + weights + (gains,),
        check_vma=False,
    )
```

```python
import jax
import jax.numpy as jnp
from jax import lax
from jax.experimental import pallas as pl
from jax.experimental.pallas import tpu as pltpu
from jax.sharding import Mesh, PartitionSpec as P

HD = 96
F32 = jnp.float32
BF16 = jnp.bfloat16
norm_eps = 1e-05
rope_base = 100000.0
LOG2E = 1.4426950408889634
SCALE = HD ** (-0.5)
MIB = 1024 * 1024
SMALL = pl.CostEstimate(flops=1, bytes_accessed=1, transcendentals=0)

GAIN_AT, OUT_AT, QUERY_AT, KEYVAL_AT, REST_AT, ATTN_WIDTH = 0, 128, 256, 640, 1024, 1280
HALF_WIDTH = ATTN_WIDTH // 2
OUT_CUT = QUERY_AT - OUT_AT
LIMIT = 60


def dot_n(left, right):
    return jnp.dot(left, right, preferred_element_type=F32)


def dot_t(left, right):
    return lax.dot_general(left, right, (((1,), (1,)), ((), ())), preferred_element_type=F32)


def dot_tn(left, right):
    return lax.dot_general(left, right, (((0,), (0,)), ((), ())), preferred_element_type=F32)


def block_at(index, size):
    return pl.ds(pl.multiple_of(index * size, size), size)


def causal_mask(scores, size):
    key_at = lax.broadcasted_iota(jnp.int32, (size, size), 0)
    query_at = lax.broadcasted_iota(jnp.int32, (size, size), 1)
    tail = jnp.where(key_at <= query_at, scores[-size:], -1e30)
    if scores.shape[0] == size:
        return tail
    return jnp.concatenate([scores[:-size], tail], 0)


class Moves:
    def __init__(self, sems):
        self.sems = sems
        self.started = []

    def start(self, source, target):
        copy = pltpu.make_async_copy(source, target, self.sems.at[len(self.started)])
        copy.start()
        self.started.append(copy)
        return copy

    def wait(self):
        for copy in self.started:
            copy.wait()


def vmem(shape, dtype=BF16):
    return pltpu.VMEM(shape, dtype)


def like(shape, dtype=BF16):
    return jax.ShapeDtypeStruct(shape, dtype)


def whole():
    return pl.BlockSpec(memory_space=pltpu.VMEM)


def apart():
    return pl.BlockSpec(memory_space=pl.ANY)


def scalars():
    return pl.BlockSpec(memory_space=pltpu.SMEM)


def kernel_call(kernel, name, place, small, large, outs, small_outs, scratch, *copies):
    return pl.pallas_call(
        kernel,
        out_shape=list(small_outs) + list(outs),
        in_specs=[scalars()] + [whole()] * len(small) + [apart()] * len(large),
        out_specs=[whole()] * len(small_outs) + [apart()] * len(outs),
        scratch_shapes=list(scratch)
        + [pltpu.SemaphoreType.DMA((count,)) for count in copies],
        compiler_params=pltpu.CompilerParams(vmem_limit_bytes=LIMIT * MIB),
        cost_estimate=SMALL,
        name=name,
    )(place, *small, *large)


def probs_at(step, size):
    return step * (step + 1) // 2 * size, (step + 1) * size


def attend_kernel(place, cos_ref, sin_ref, t0, t1, t2, t3, a0, a1, a2, a3, b0, b1, b2, b3,
                  gains_ref, w_hbm, h_hbm, q_hbm, kt_hbm, v_hbm, attn_hbm, attnt_hbm, probs_hbm,
                  o0, o1, o2, o3,
                  t_ref, w_ref, h_ref, qt_ref, q_ref, kt_ref, k_ref, vt_ref, v_ref,
                  natural, attn_ref, attnt_ref, probs_ref, part_ref, in_sem, out_sem, probs_sem):
    block, ix, iz = place[0], place[1], place[2]
    half = HD // 2
    size = t_ref.shape[1]
    heads, _, length = qt_ref.shape
    group_size = heads // k_ref.shape[0]
    rows = a0.shape[1]
    fetch, store = Moves(in_sem), Moves(out_sem)
    came = []
    for far, (along_x, along_z) in enumerate(zip((a0, a1, a2, a3), (b0, b1, b2, b3))):
        for near in range(4):
            at_a = lax.rem(ix + far, 4) * 4 + lax.rem(iz + near, 4)
            at_b = lax.rem(ix + near, 4) * 4 + lax.rem(iz + far, 4)
            came.append(fetch.start(
                along_x.at[near], w_ref.at[block_at(at_a, rows), pl.ds(0, HALF_WIDTH)]))
            came.append(fetch.start(
                along_z.at[near], w_ref.at[block_at(at_b, rows), pl.ds(HALF_WIDTH, HALF_WIDTH)]))
    tokens_came = [
        fetch.start(piece, t_ref.at[i]) for i, piece in enumerate((t0, t1, t2, t3))
    ]
    for copy in came:
        copy.wait()
    store.start(w_ref, w_hbm)
    gains = w_ref[:, GAIN_AT:OUT_AT].astype(F32).T
    gain_row = gains[0:1] + gains[2:3]
    gains_ref[...] = gains[0:2] + gains[2:4]
    for step in range(4):
        at = block_at(lax.bitwise_xor(block, step), size)
        tokens_came[step].wait()
        value = t_ref[step].astype(F32)
        factor = lax.rsqrt(jnp.mean(value * value, -1, keepdims=True) + norm_eps)
        normed = (value * factor * gain_row).astype(BF16)
        h_ref[at, :] = normed
        cosine = cos_ref[:, at]
        sine = sin_ref[:, at]
        every = dot_n(normed, w_ref[:, QUERY_AT:REST_AT]).T
        query, keyval = every[: KEYVAL_AT - QUERY_AT], every[KEYVAL_AT - QUERY_AT :]

        def rotated(field):
            first, second = field[:half], field[half:]
            return jnp.concatenate(
                [first * cosine - second * sine, second * cosine + first * sine], 0
            )

        for head in range(query.shape[0] // HD):
            turned = rotated(query[head * HD : (head + 1) * HD])
            qt_ref[head, :, at] = turned.astype(BF16)
            q_ref[head, at, :] = turned.T.astype(BF16)
        for head in range(keyval.shape[0] // (2 * HD)):
            turned = rotated(keyval[2 * head * HD : (2 * head + 1) * HD])
            value_t = keyval[(2 * head + 1) * HD : (2 * head + 2) * HD]
            kt_ref[head, :, at] = turned.astype(BF16)
            k_ref[head, at, :] = turned.T.astype(BF16)
            vt_ref[head, :, at] = value_t.astype(BF16)
            v_ref[head, at, :] = value_t.T.astype(BF16)
    for source, target in ((h_ref, h_hbm), (q_ref, q_hbm), (kt_ref, kt_hbm), (v_ref, v_hbm)):
        store.start(source, target)

    def probs_copy(head):
        return pltpu.make_async_copy(probs_ref.at[head], probs_hbm.at[head], probs_sem.at[head])

    def one_head(head, carry):
        group = head // group_size
        for step in range(4):
            first, reach = probs_at(step, size)
            columns = slice(step * size, reach)
            scores = causal_mask(dot_n(k_ref[group, :reach, :], qt_ref[head, :, columns]), size)
            top = jnp.max(scores, 0, keepdims=True)
            expo = jnp.exp2((scores - top) * (SCALE * LOG2E))
            total = jnp.sum(expo, 0, keepdims=True)
            probs = (expo * (1.0 / total)).astype(BF16)
            probs_ref[head, first : first + reach, :] = probs
            mixed = dot_n(vt_ref[group, :, :reach], probs)
            attnt_ref[head, :, columns] = mixed.astype(BF16)
        probs_copy(head).start()
        return carry

    lax.fori_loop(0, heads, one_head, 0)
    store.start(attnt_ref, attnt_hbm)
    natural[...] = attnt_ref[...].reshape(heads * HD, length).T
    for step, out in ((1, o1), (3, o3), (2, o2), (0, o0)):
        at = block_at(lax.bitwise_xor(block, step), size)
        attn = natural[at, :]
        attn_ref[step * size : (step + 1) * size, :] = attn
        part = dot_t(attn[:, :OUT_CUT], w_ref[:, OUT_AT:QUERY_AT])
        part += dot_t(attn[:, OUT_CUT:], w_ref[:, REST_AT:])
        part_ref[step] = part.astype(BF16)
        store.start(part_ref.at[step], out)
    store.start(attn_ref, attn_hbm)
    store.wait()
    for head in range(heads):
        probs_copy(head).wait()


def attend(place, pieces, along_x, along_z, cosine, sine):
    width = pieces[0].shape[1]
    length = cosine.shape[1]
    size = length // 4
    heads = (KEYVAL_AT - QUERY_AT) // HD
    groups = (REST_AT - KEYVAL_AT) // (2 * HD)
    columns, rows = (heads, HD, length), (heads, length, HD)
    g_columns, g_rows = (groups, HD, length), (groups, length, HD)
    probs = (heads, sum(probs_at(3, size)), size)
    outs = [(width, ATTN_WIDTH), (length, width), rows, g_columns, g_rows,
            (length, heads * HD), columns, probs] + [(size, width)] * 4
    scratch = [(4, size, width), (width, ATTN_WIDTH), (length, width), columns, rows,
               g_columns, g_rows, g_columns, g_rows,
               (length, heads * HD), (length, heads * HD), columns, probs, (4, size, width)]
    return kernel_call(
        attend_kernel, "attend", place, (cosine, sine), (*pieces, *along_x, *along_z),
        [like(s) for s in outs], [like((2, width), F32)], [vmem(s) for s in scratch],
        36, 11, heads)


def attend_back_kernel(place, cos_ref, sin_ref, gain2_ref,
                       o0, o1, o2, o3, t0, t1, t2, t3, w_hbm, h_hbm, q_hbm, kt_hbm,
                       v_hbm, attn_hbm, attnt_hbm, probs_hbm,
                       c0, c1, c2, c3, x0, x1, x2, x3, y0, y1, y2, y3,
                       o_ref, t_ref, w_ref, h_ref, q_ref, kt_ref, v_ref,
                       attn_ref, attnt_ref, probs_ref,
                       do_ref, dot_ref, dqkv_ref, part_ref, first_ref, second_ref,
                       delta_ref, dk_ref, dv_ref, turned_ref, in_sem, out_sem, probs_sem):
    block, ix, iz = place[0], place[1], place[2]
    heads, length, _ = q_ref.shape
    groups = v_ref.shape[0]
    group_size = heads // groups
    size = length // 4
    half = HD // 2
    width = w_ref.shape[0]
    heads_w = heads * HD
    fetch, store = Moves(in_sem), Moves(out_sem)
    early = [fetch.start(w_hbm, w_ref)]
    early += [
        fetch.start(piece, o_ref.at[pl.ds(i * size, size), :])
        for i, piece in enumerate((o0, o1, o2, o3))
    ]
    for source, target in ((attnt_hbm, attnt_ref), (v_hbm, v_ref), (q_hbm, q_ref),
                           (kt_hbm, kt_ref)):
        early.append(fetch.start(source, target))

    def probs_copy(head):
        return pltpu.make_async_copy(probs_hbm.at[head], probs_ref.at[head], probs_sem.at[head])

    for head in range(heads):
        probs_copy(head).start()
    later = [fetch.start(attn_hbm, attn_ref), fetch.start(h_hbm, h_ref)]
    later += [fetch.start(piece, t_ref.at[i]) for i, piece in enumerate((t0, t1, t2, t3))]
    early[0].wait()
    for step in range(4):
        at = block_at(lax.bitwise_xor(block, step), size)
        early[1 + step].wait()
        grad_in = o_ref[step * size : (step + 1) * size, :]
        grad = jnp.concatenate(
            [dot_n(grad_in, w_ref[:, OUT_AT:QUERY_AT]), dot_n(grad_in, w_ref[:, REST_AT:])], 1)
        grad_t = grad.T.astype(BF16)
        grad = grad.astype(BF16)
        for head in range(heads):
            dot_ref[head, :, at] = grad_t[head * HD : (head + 1) * HD]
            do_ref[head, at, :] = grad[:, head * HD : (head + 1) * HD]
    for copy in early[5:]:
        copy.wait()
    delta_ref[...] = jnp.sum(
        attnt_ref[...].astype(F32) * dot_ref[...].astype(F32), 1, keepdims=True)
    dk_ref[...] = jnp.zeros_like(dk_ref)
    dv_ref[...] = jnp.zeros_like(dv_ref)

    def turned_back(field, cosine, sine):
        first, second = field[:half], field[half:]
        return jnp.concatenate(
            [first * cosine + second * sine, second * cosine - first * sine], 0)

    def one_head(head, carry):
        group = head // group_size
        probs_copy(head).wait()
        for step in range(4):
            first, reach = probs_at(step, size)
            columns = slice(step * size, reach)
            probs = probs_ref[head, first : first + reach, :]
            d_probs = dot_n(v_ref[group, :reach, :], dot_ref[head, :, columns])
            d_scores = (probs.astype(F32) * (d_probs - delta_ref[head, :, columns])).astype(BF16)
            dv_ref[group, :reach, :] += dot_n(probs, do_ref[head, columns, :])
            dk_ref[group, :reach, :] += dot_n(d_scores, q_ref[head, columns, :])
            d_query = dot_n(kt_ref[group, :, :reach], d_scores) * SCALE
            turned_ref[head, :, columns] = turned_back(
                d_query, cos_ref[:, columns], sin_ref[:, columns])
        return carry

    lax.fori_loop(0, heads, one_head, 0)
    for group in range(groups):
        turned_ref[heads + 2 * group] = turned_back(
            dk_ref[group].T * SCALE, cos_ref[...], sin_ref[...])
        turned_ref[heads + 2 * group + 1] = dv_ref[group].T
    dqkv_ref[...] = turned_ref[...].reshape((heads + 2 * groups) * HD, length).T.astype(BF16)
    for copy in later:
        copy.wait()

    gain = jnp.zeros((1, width), F32)
    for step, out in ((1, c1), (3, c3), (2, c2), (0, c0)):
        at = block_at(lax.bitwise_xor(block, step), size)
        part = dot_t(dqkv_ref[at, :], w_ref[:, QUERY_AT:REST_AT])
        value = t_ref[step].astype(F32)
        factor = lax.rsqrt(jnp.mean(value * value, -1, keepdims=True) + norm_eps)
        gain += jnp.sum(part * (value * factor), 0, keepdims=True)
        part_ref[step] = part.astype(BF16)
        store.start(part_ref.at[step], out)

    rows = width // 16
    part = dot_tn(h_ref[...], dqkv_ref[...]).astype(BF16)
    first_ref[:, :heads_w] = part[:, :heads_w]
    second_ref[:, LATE_WIDTH - heads_w :] = part[:, heads_w:]
    part = dot_tn(o_ref[...], attn_ref[...]).astype(BF16)
    first_ref[:, heads_w : heads_w + LATE_OUT] = part[:, :LATE_OUT]
    second_ref[:, : heads_w - LATE_OUT] = part[:, LATE_OUT:]
    gains = jnp.concatenate([gain, gain2_ref[...], jnp.zeros((126, width), F32)], 0)
    first_ref[:, heads_w + LATE_OUT :] = gains.T.astype(BF16)
    for offset, (x_out, y_out) in enumerate(((x0, y0), (x1, y1), (x2, y2), (x3, y3))):
        to_x = lax.rem(ix + 4 - offset, 4)
        to_z = lax.rem(iz + 4 - offset, 4)
        store.start(first_ref.at[block_at(to_x, 4 * rows), :], x_out)
        for i in range(4):
            store.start(second_ref.at[block_at(i * 4 + to_z, rows), :], y_out.at[i])
    store.wait()


def attend_back(place, cosine, sine, gain_two, pieces, token_pieces, weights, h_first,
                q, kt, v, attn, attnt, probs):
    size, width = pieces[0].shape
    heads, length, _ = q.shape
    groups = v.shape[0]
    every = heads + 2 * groups
    rows = width // 16
    outs = [(size, width)] * 4 + [(4 * rows, LATE_WIDTH)] * 4 + [(4, rows, LATE_WIDTH)] * 4
    scratch = [
        (length, width), (4, size, width), (width, ATTN_WIDTH), (length, width),
        q.shape, kt.shape, v.shape, attn.shape, attnt.shape, probs.shape,
        (heads, length, HD), (heads, HD, length), (length, every * HD), (4, size, width),
        (width, LATE_WIDTH), (width, LATE_WIDTH),
    ]
    wide = [(heads, 1, length), (groups, length, HD), (groups, length, HD), (every, HD, length)]
    return kernel_call(
        attend_back_kernel, "attend_back", place, (cosine, sine, gain_two),
        (*pieces, *token_pieces, weights, h_first, q, kt, v, attn, attnt, probs),
        [like(s) for s in outs], [],
        [vmem(s) for s in scratch] + [vmem(s, F32) for s in wide], 15, 24, heads)


def feed_kernel(place, h0, h1, g0, g1, w_hbm, hidden_hbm, dgu_hbm, b0, b1, r0, r1,
                w_ref, h_ref, g_ref, hidden_ref, dgu_ref, back_ref, out_ref, in_sem, out_sem):
    del place
    hidden_w = hidden_ref.shape[1]
    size = h_ref.shape[1]
    parts = [slice(i * hidden_w, (i + 1) * hidden_w) for i in range(3)]
    fetch, store = Moves(in_sem), Moves(out_sem)

    def weight(i):
        at = pl.ds(i * hidden_w, hidden_w)
        return fetch.start(w_hbm.at[:, at], w_ref.at[:, at])

    came = [fetch.start(h0, h_ref.at[0]), weight(0), weight(1), fetch.start(g0, g_ref.at[0]),
            weight(2), fetch.start(h1, h_ref.at[1]), fetch.start(g1, g_ref.at[1])]
    for i, (back, out) in enumerate(((b0, r0), (b1, r1))):
        rows = slice(i * size, (i + 1) * size)
        at = pl.ds(i * size, size)
        for copy in came[0:2] if i == 0 else came[5:7]:
            copy.wait()
        gate = dot_n(h_ref[i], w_ref[:, parts[0]])
        if i == 0:
            came[2].wait()
        up = dot_n(h_ref[i], w_ref[:, parts[1]])
        sig = 1.0 / (1.0 + jnp.exp2(gate * (-LOG2E)))
        silu = gate * sig
        hidden = (silu * up).astype(BF16)
        hidden_ref[rows, :] = hidden
        store.start(hidden_ref.at[at, :], hidden_hbm.at[at, :])
        if i == 0:
            came[3].wait()
            came[4].wait()
        d_hidden = dot_n(g_ref[i], w_ref[:, parts[2]])
        dgu_ref[rows, :hidden_w] = (
            d_hidden * up * (sig * (1.0 + gate * (1.0 - sig)))).astype(BF16)
        dgu_ref[rows, hidden_w:] = (d_hidden * silu).astype(BF16)
        store.start(dgu_ref.at[at, :], dgu_hbm.at[at, :])
        back_ref[i] = dot_t(dgu_ref[rows, :], w_ref[:, : 2 * hidden_w]).astype(BF16)
        store.start(back_ref.at[i], back)
        out_ref[i] = dot_t(hidden_ref[rows, :], w_ref[:, parts[2]]).astype(BF16)
        store.start(out_ref.at[i], out)
    store.wait()


def feed(place, weights, normed_pieces, grad_pieces):
    size, width = normed_pieces[0].shape
    hidden_w = weights.shape[1] // 3
    wide = [(2 * size, hidden_w), (2 * size, 2 * hidden_w)]
    return kernel_call(
        feed_kernel, "feed", place, (), (*normed_pieces, *grad_pieces, weights),
        [like(s) for s in wide + [(size, width)] * 4], [],
        [vmem(s) for s in [weights.shape] + [(2, size, width)] * 2 + wide + [(2, size, width)] * 2],
        7, 8)


def feed_grads_kernel(place, h0, h1, h2, h3, g0, g1, g2, g3, dgu_a, dgu_b, hidden_a, hidden_b,
                      out_hbm, h_ref, g_ref, dgu_ref, hidden_ref, out_ref, in_sem, out_sem):
    del place
    size = h0.shape[0]
    half, hidden_w = hidden_a.shape
    column = 512
    fetch, store = Moves(in_sem), Moves(out_sem)

    def rows_of(pieces, ref):
        return [
            fetch.start(piece, ref.at[pl.ds(i * size, size), :]) for i, piece in enumerate(pieces)
        ]

    def tiles_of(pieces, ref):
        tiles = []
        for tile in range(ref.shape[1] // column):
            at = pl.ds(tile * column, column)
            tiles.append([
                fetch.start(piece.at[:, at], ref.at[pl.ds(i * half, half), at])
                for i, piece in enumerate(pieces)
            ])
        return tiles

    h_came = rows_of((h0, h1, h2, h3), h_ref)
    dgu_came = tiles_of((dgu_a, dgu_b), dgu_ref)
    g_came = rows_of((g0, g1, g2, g3), g_ref)
    hidden_came = tiles_of((hidden_a, hidden_b), hidden_ref)
    at = 0
    for came, left, tiles, right in (
        (h_came, h_ref, dgu_came, dgu_ref), (g_came, g_ref, hidden_came, hidden_ref)
    ):
        for copy in came:
            copy.wait()
        for tile, copies in enumerate(tiles):
            for copy in copies:
                copy.wait()
            columns = pl.ds(at, column)
            out_ref[:, columns] = dot_tn(
                left[...], right[:, tile * column : (tile + 1) * column]).astype(BF16)
            store.start(out_ref.at[:, columns], out_hbm.at[:, columns])
            at += column
    store.wait()


def feed_grads(place, normed_pieces, grad_pieces, dgu_a, dgu_b, hidden_a, hidden_b):
    size, width = normed_pieces[0].shape
    half, hidden_w = hidden_a.shape
    scratch = [(4 * size, width)] * 2 + [(2 * half, 2 * hidden_w), (2 * half, hidden_w),
                                         (width, 3 * hidden_w)]
    return kernel_call(
        feed_grads_kernel, "feed_grads", place, (),
        (*normed_pieces, *grad_pieces, dgu_a, dgu_b, hidden_a, hidden_b),
        [like((width, 3 * hidden_w))], [], [vmem(s) for s in scratch], 20, 6)[0]


LATE_OUT, LATE_WIDTH = 128, 640


def late_middle_kernel(place, *refs):
    x_in, y_in, outs = refs[0:4], refs[4:8], refs[8:]
    ix, iz = place[1], place[2]
    rows = outs[0].shape[0]
    for offset in range(4):
        at = block_at(lax.rem(iz + 4 - offset, 4), rows)
        total = x_in[0][at, :].astype(F32)
        for ref in x_in[1:]:
            total += ref[at, :].astype(F32)
        outs[offset][...] = total.astype(BF16)
        to = lax.rem(ix + 4 - offset, 4)
        total = y_in[0][to].astype(F32)
        for ref in y_in[1:]:
            total += ref[to].astype(F32)
        outs[4 + offset][...] = total.astype(BF16)


def late_middle(place, along_x, along_z):
    _, rows, width = along_z[0].shape
    return pl.pallas_call(
        late_middle_kernel,
        out_shape=[like((rows, width))] * 8,
        in_specs=[scalars()] + [whole()] * 8,
        out_specs=[whole()] * 8,
        cost_estimate=SMALL,
        name="late_middle",
    )(place, *along_x, *along_z)


def late_last_kernel(place, *refs):
    x_in, y_in, keep_ref, send_ref = refs[0:4], refs[4:8], refs[8], refs[9]
    mine = place[3]
    rows = keep_ref.shape[0]
    for inputs, columns in ((x_in, slice(0, LATE_WIDTH)), (y_in, slice(LATE_WIDTH, 2 * LATE_WIDTH))):
        for ref, half in ((keep_ref, mine), (send_ref, 1 - mine)):
            at = block_at(half, rows)
            total = inputs[0][at, :].astype(F32)
            for other_ref in inputs[1:]:
                total += other_ref[at, :].astype(F32)
            ref[:, columns] = total.astype(ref.dtype)


def late_last(place, along_z, along_x):
    rows, width = along_x[0].shape
    return pl.pallas_call(
        late_last_kernel,
        out_shape=[
            jax.ShapeDtypeStruct((rows // 2, 2 * width), F32),
            jax.ShapeDtypeStruct((rows // 2, 2 * width), BF16),
        ],
        in_specs=[scalars()] + [whole()] * 8,
        out_specs=[whole()] * 2,
        cost_estimate=SMALL,
        name="late_last",
    )(place, *along_z, *along_x)


def norm_rows(values_in):
    factor = lax.rsqrt(jnp.mean(values_in * values_in, -1, keepdims=True) + norm_eps)
    return (values_in * factor, factor)


def norm_back(grad_in, normed, factor, gain_row):
    grad_normed = grad_in * gain_row
    inner = jnp.mean(grad_normed * normed, -1, keepdims=True)
    return (factor * (grad_normed - normed * inner), jnp.sum(grad_in * normed, 0))


def from_offset(v, axis, offset, size):
    return lax.ppermute(v, axis, [((i + offset) % size, i) for i in range(size)])


def other(v, axis):
    return from_offset(v, axis, 1, 2)


def pair_rows(v, axis):
    it = other(v, axis)
    flag = lax.axis_index(axis) == 0
    return jnp.concatenate([jnp.where(flag, v, it), jnp.where(flag, it, v)], 0)


def near_sum(own, core):
    return own.astype(F32) + other(core, "core").astype(F32)


def far_sum(chip, diagonal):
    return near_sum(chip, diagonal).astype(BF16)


def after(value, first):
    return lax.optimization_barrier((value, first))


def from_both(along_first, first_axis, along_second, second_axis):
    near = [
        from_offset(part[i], axis, i, 4)
        for i in (1, 3)
        for part, axis in ((along_first, first_axis), (along_second, second_axis))
    ]
    opposite, near = after((along_first[2], along_second[2]), near)
    first = [along_first[0], near[0], from_offset(opposite[0], first_axis, 2, 4), near[2]]
    second = [along_second[0], near[1], from_offset(opposite[1], second_axis, 2, 4), near[3]]
    return first, second


def gather_rows(v):
    return lax.all_gather(pair_rows(v, "yh"), ("x", "z"), axis=0, tiled=True)


def scatter_rows(v):
    two = lax.psum_scatter(v, ("x", "z"), scatter_dimension=0, tiled=True)
    rows = two.shape[0] // 2
    iyh = lax.axis_index("yh")
    keep = lax.dynamic_slice_in_dim(two, iyh * rows, rows, 0)
    send = lax.dynamic_slice_in_dim(two, (1 - iyh) * rows, rows, 0)
    return keep.astype(F32) + other(send, "yh").astype(F32)


def body(tokens, norm_gains, w_query, w_keyval, w_out, w_gateup, w_down, cotangent):
    D = tokens.shape[1]
    length = 4 * tokens.shape[0]
    hidden_w = w_down.shape[0]
    heads_w = w_query.shape[1]
    gains_w = norm_gains.shape[1]
    block = lax.axis_index("yl") * 2 + lax.axis_index("core")
    place = jnp.stack(
        [block, lax.axis_index("x"), lax.axis_index("z"), lax.axis_index("yh")]
    ).astype(jnp.int32)

    mlp_own = jnp.concatenate([w_gateup[:, 0], w_gateup[:, 1], w_down.T], 1)
    mlp_w = gather_rows(mlp_own)

    out_t = w_out.T
    attn_own = jnp.concatenate(
        [
            jnp.zeros((out_t.shape[0], OUT_AT), BF16),
            out_t[:, :OUT_CUT],
            w_query,
            w_keyval,
            out_t[:, OUT_CUT:],
        ],
        1,
    )
    near = other(tokens, "core")
    attn_pair = pair_rows(attn_own, "yh")

    pair_w = 8 * gains_w
    gain_at = (lax.axis_index("yh") * 4 + block) * gains_w
    gain_part = lax.dynamic_update_slice(jnp.zeros((2, pair_w), F32), norm_gains, (0, gain_at))
    for axis in ("core", "yl", "yh"):
        gain_part = gain_part + other(gain_part, axis)
    gain_part = gain_part.T
    gain_high = gain_part.astype(BF16)
    gain_low = (gain_part - gain_high.astype(F32)).astype(BF16)
    first, second = attn_pair[:, :HALF_WIDTH], attn_pair[:, HALF_WIDTH:]
    first += jnp.pad(gain_high, ((0, 0), (0, HALF_WIDTH - 2)))
    first += jnp.pad(gain_low, ((0, 0), (2, HALF_WIDTH - 4)))

    tokens, (first, near) = after(tokens, (first, near))
    far = other(tokens, "yl")
    along_z, along_x = from_both([first] * 4, "z", [second] * 4, "x")
    along_z, along_x, far = lax.optimization_barrier((jnp.stack(along_z), jnp.stack(along_x), far))
    token_pieces = [tokens, near, far, other(far, "core")]
    cotangent, far = after(cotangent, far)
    grad_far = other(cotangent, "yl")
    along_x, along_z = from_both([along_z] * 4, "x", [along_x] * 4, "z")

    positions = jnp.arange(length).astype(F32)
    freqs = rope_base ** (-(jnp.arange(HD // 2).astype(F32) * 2.0 / HD))
    angles = freqs[:, None] * positions[None, :]
    cosine, sine = jnp.cos(angles), jnp.sin(angles)

    gain_rows, attn_w, h_first, q, kt, v, attn, attnt, probs, *parts = attend(
        place, token_pieces, along_x, along_z, cosine, sine
    )
    grad_far, parts = after(grad_far, parts)
    grad_pieces = [cotangent, other(cotangent, "core"), grad_far, other(grad_far, "core")]
    middle_far = far_sum(parts[2], parts[3])
    middle = (
        tokens.astype(F32) + near_sum(parts[0], parts[1]) + other(middle_far, "yl").astype(F32)
    )
    normed2, factor2 = norm_rows(middle)
    h_own = (normed2 * gain_rows[1]).astype(BF16)

    h_pieces = [h_own, other(h_own, "core")]
    h_far = other(h_own, "yl")
    hidden_a, dgu_a, back_own, back_core, out_own, out_core = feed(
        place, mlp_w, h_pieces, grad_pieces[:2]
    )
    h_far, hidden_a = after(h_far, hidden_a)
    h_pieces += [h_far, other(h_far, "core")]
    hidden_b, dgu_b, back_chip, back_diag, out_chip, out_diag = feed(
        place, mlp_w, h_pieces[2:], grad_pieces[2:]
    )
    back_near = near_sum(back_own, back_core)
    out_near = near_sum(out_own, out_core)

    back_far = far_sum(back_chip, back_diag)
    hidden_b, back_far = after(hidden_b, back_far)
    mlp_grads = feed_grads(place, h_pieces, grad_pieces, dgu_a, dgu_b, hidden_a, hidden_b)
    mlp_grads, back_far = after(mlp_grads, other(back_far, "yl"))
    d_h2_own = back_near + back_far.astype(F32)
    early = scatter_rows(mlp_grads)
    out_far = far_sum(out_chip, out_diag)

    d_norm2, gain_two = norm_back(d_h2_own, normed2, factor2, gain_rows[1])
    d_middle = cotangent.astype(F32) + d_norm2
    d_out = d_middle.astype(BF16)
    d_out_far = other(d_out, "yl")
    d_out_far, out_near = after(d_out_far, out_near)
    out_pieces = [d_out, other(d_out, "core"), d_out_far, other(d_out_far, "core")]
    out_far, out_pieces = after(out_far, out_pieces)
    out_far = other(out_far, "yl")

    back = attend_back(
        place, cosine, sine, gain_two[None], out_pieces, token_pieces, attn_w,
        h_first, q, kt, v, attn, attnt, probs,
    )
    out_near, back = after(out_near, back)
    result = (middle + out_near + out_far.astype(F32)).astype(BF16)
    parts, late_parts = back[:4], back[4:]
    late_parts, result = after(late_parts, result)
    d_far = far_sum(parts[2], parts[3])
    along_x, along_z = from_both(late_parts[:4], "x", late_parts[4:], "z")
    along_x, d_far = after(along_x, d_far)
    middle_parts = late_middle(place, along_x, along_z)
    along_z, along_x = from_both(middle_parts[:4], "z", middle_parts[4:], "x")
    late_keep, late_send = late_last(place, along_z, along_x)
    d_h1_own = near_sum(parts[0], parts[1]) + other(d_far, "yl").astype(F32)
    late_other, (d_h1_own, early) = after(other(late_send, "yh"), (d_h1_own, early))
    late = late_keep + late_other.astype(F32)

    normed1, factor1 = norm_rows(tokens.astype(F32))
    d_norm1, _ = norm_back(d_h1_own, normed1, factor1, gain_rows[0])
    input_grad = (d_middle + d_norm1).astype(BF16)

    out_at = heads_w + LATE_OUT
    grad_out = jnp.concatenate([late[:, heads_w:out_at], late[:, LATE_WIDTH : LATE_WIDTH + heads_w - LATE_OUT]], 1)
    gain_sum = late[:, out_at : out_at + 2].T
    for axis in ("core", "yl"):
        gain_sum = gain_sum + other(gain_sum, axis)
    grad_gains = lax.dynamic_slice(gain_sum, (0, block * gains_w), (2, gains_w))
    return (
        result,
        input_grad,
        late[:, :heads_w],
        late[:, 2 * LATE_WIDTH - heads_w :],
        grad_out.T,
        early[:, : 2 * hidden_w].reshape(-1, 2, hidden_w),
        early[:, 2 * hidden_w :].T,
        grad_gains,
    )


def solution(mesh):
    fine = Mesh(mesh.devices.reshape(4, 4, 2, 2, 2), ("x", "z", "yh", "yl", "core"))
    dp = ("x", "z", "yh")
    tensor = ("yl", "core")
    every = dp + tensor
    weights = (P(dp, tensor), P(dp, tensor), P(tensor, dp), P(dp, None, tensor), P(tensor, dp))
    rows = P(every, None)
    gains = P(None, every)
    return jax.shard_map(
        body,
        mesh=fine,
        in_specs=(rows, gains) + weights + (rows,),
        out_specs=(rows, rows) + weights + (gains,),
        check_vma=False,
    )
```

```python
import jax
import jax.numpy as jnp
from jax import lax
from jax.experimental import pallas as pl
from jax.experimental.pallas import tpu as pltpu
from jax.sharding import Mesh, PartitionSpec as P

HD = 96
F32 = jnp.float32
BF16 = jnp.bfloat16
norm_eps = 1e-05
rope_base = 100000.0
LOG2E = 1.4426950408889634
SCALE = HD ** (-0.5)
MIB = 1024 * 1024
SMALL = pl.CostEstimate(flops=1, bytes_accessed=1, transcendentals=0)

GAIN_AT, OUT_AT, QUERY_AT, KEYVAL_AT, REST_AT, ATTN_WIDTH = 0, 128, 256, 640, 1024, 1280
HALF_WIDTH = ATTN_WIDTH // 2
OUT_CUT = QUERY_AT - OUT_AT
LIMIT = 60


def dot_n(left, right):
    return jnp.dot(left, right, preferred_element_type=F32)


def dot_t(left, right):
    return lax.dot_general(left, right, (((1,), (1,)), ((), ())), preferred_element_type=F32)


def dot_tn(left, right):
    return lax.dot_general(left, right, (((0,), (0,)), ((), ())), preferred_element_type=F32)


def block_at(index, size):
    return pl.ds(pl.multiple_of(index * size, size), size)


def causal_mask(scores, size):
    key_at = lax.broadcasted_iota(jnp.int32, (size, size), 0)
    query_at = lax.broadcasted_iota(jnp.int32, (size, size), 1)
    tail = jnp.where(key_at <= query_at, scores[-size:], -1e30)
    if scores.shape[0] == size:
        return tail
    return jnp.concatenate([scores[:-size], tail], 0)


class Moves:
    def __init__(self, sems):
        self.sems = sems
        self.started = []

    def start(self, source, target):
        copy = pltpu.make_async_copy(source, target, self.sems.at[len(self.started)])
        copy.start()
        self.started.append(copy)
        return copy

    def wait(self):
        for copy in self.started:
            copy.wait()


def vmem(shape, dtype=BF16):
    return pltpu.VMEM(shape, dtype)


def like(shape, dtype=BF16):
    return jax.ShapeDtypeStruct(shape, dtype)


def whole():
    return pl.BlockSpec(memory_space=pltpu.VMEM)


def apart():
    return pl.BlockSpec(memory_space=pl.ANY)


def scalars():
    return pl.BlockSpec(memory_space=pltpu.SMEM)


def kernel_call(kernel, name, place, small, large, outs, small_outs, scratch, *copies):
    return pl.pallas_call(
        kernel,
        out_shape=list(small_outs) + list(outs),
        in_specs=[scalars()] + [whole()] * len(small) + [apart()] * len(large),
        out_specs=[whole()] * len(small_outs) + [apart()] * len(outs),
        scratch_shapes=list(scratch)
        + [pltpu.SemaphoreType.DMA((count,)) for count in copies],
        compiler_params=pltpu.CompilerParams(vmem_limit_bytes=LIMIT * MIB),
        cost_estimate=SMALL,
        name=name,
    )(place, *small, *large)


def probs_at(step, size):
    return step * (step + 1) // 2 * size, (step + 1) * size


def attend_kernel(place, cos_ref, sin_ref, t0, t1, t2, t3, a0, a1, a2, a3, b0, b1, b2, b3,
                  gains_ref, w_hbm, h_hbm, q_hbm, kt_hbm, v_hbm, attn_hbm, attnt_hbm, probs_hbm,
                  o0, o1, o2, o3,
                  t_ref, w_ref, h_ref, qt_ref, q_ref, kt_ref, k_ref, vt_ref, v_ref,
                  natural, attn_ref, attnt_ref, probs_ref, part_ref, in_sem, out_sem, probs_sem):
    block, ix, iz = place[0], place[1], place[2]
    half = HD // 2
    size = t_ref.shape[1]
    heads, _, length = qt_ref.shape
    group_size = heads // k_ref.shape[0]
    rows = a0.shape[1]
    fetch, store = Moves(in_sem), Moves(out_sem)
    came = []
    for far, (along_x, along_z) in enumerate(zip((a0, a1, a2, a3), (b0, b1, b2, b3))):
        for near in range(4):
            at_a = lax.rem(ix + far, 4) * 4 + lax.rem(iz + near, 4)
            at_b = lax.rem(ix + near, 4) * 4 + lax.rem(iz + far, 4)
            came.append(fetch.start(
                along_x.at[near], w_ref.at[block_at(at_a, rows), pl.ds(0, HALF_WIDTH)]))
            came.append(fetch.start(
                along_z.at[near], w_ref.at[block_at(at_b, rows), pl.ds(HALF_WIDTH, HALF_WIDTH)]))
    tokens_came = [
        fetch.start(piece, t_ref.at[i]) for i, piece in enumerate((t0, t1, t2, t3))
    ]
    for copy in came:
        copy.wait()
    store.start(w_ref, w_hbm)
    gains = w_ref[:, GAIN_AT:OUT_AT].astype(F32).T
    gain_row = gains[0:1] + gains[2:3]
    gains_ref[...] = gains[0:2] + gains[2:4]
    for step in range(4):
        at = block_at(lax.bitwise_xor(block, step), size)
        tokens_came[step].wait()
        value = t_ref[step].astype(F32)
        factor = lax.rsqrt(jnp.mean(value * value, -1, keepdims=True) + norm_eps)
        normed = (value * factor * gain_row).astype(BF16)
        h_ref[at, :] = normed
        cosine = cos_ref[:, at]
        sine = sin_ref[:, at]
        every = dot_n(normed, w_ref[:, QUERY_AT:REST_AT]).T
        query, keyval = every[: KEYVAL_AT - QUERY_AT], every[KEYVAL_AT - QUERY_AT :]

        def rotated(field):
            first, second = field[:half], field[half:]
            return jnp.concatenate(
                [first * cosine - second * sine, second * cosine + first * sine], 0
            )

        for head in range(query.shape[0] // HD):
            turned = rotated(query[head * HD : (head + 1) * HD])
            qt_ref[head, :, at] = turned.astype(BF16)
            q_ref[head, at, :] = turned.T.astype(BF16)
        for head in range(keyval.shape[0] // (2 * HD)):
            turned = rotated(keyval[2 * head * HD : (2 * head + 1) * HD])
            value_t = keyval[(2 * head + 1) * HD : (2 * head + 2) * HD]
            kt_ref[head, :, at] = turned.astype(BF16)
            k_ref[head, at, :] = turned.T.astype(BF16)
            vt_ref[head, :, at] = value_t.astype(BF16)
            v_ref[head, at, :] = value_t.T.astype(BF16)
    for source, target in ((h_ref, h_hbm), (q_ref, q_hbm), (kt_ref, kt_hbm), (v_ref, v_hbm)):
        store.start(source, target)

    def probs_copy(head):
        return pltpu.make_async_copy(probs_ref.at[head], probs_hbm.at[head], probs_sem.at[head])

    def one_head(head, carry):
        group = head // group_size
        for step in range(4):
            first, reach = probs_at(step, size)
            columns = slice(step * size, reach)
            scores = causal_mask(dot_n(k_ref[group, :reach, :], qt_ref[head, :, columns]), size)
            top = jnp.max(scores, 0, keepdims=True)
            expo = jnp.exp2((scores - top) * (SCALE * LOG2E))
            total = jnp.sum(expo, 0, keepdims=True)
            probs = (expo * (1.0 / total)).astype(BF16)
            probs_ref[head, first : first + reach, :] = probs
            mixed = dot_n(vt_ref[group, :, :reach], probs)
            attnt_ref[head, :, columns] = mixed.astype(BF16)
        probs_copy(head).start()
        return carry

    lax.fori_loop(0, heads, one_head, 0)
    store.start(attnt_ref, attnt_hbm)
    natural[...] = attnt_ref[...].reshape(heads * HD, length).T
    for step, out in ((1, o1), (3, o3), (2, o2), (0, o0)):
        at = block_at(lax.bitwise_xor(block, step), size)
        attn = natural[at, :]
        attn_ref[step * size : (step + 1) * size, :] = attn
        part = dot_t(attn[:, :OUT_CUT], w_ref[:, OUT_AT:QUERY_AT])
        part += dot_t(attn[:, OUT_CUT:], w_ref[:, REST_AT:])
        part_ref[step] = part.astype(BF16)
        store.start(part_ref.at[step], out)
    store.start(attn_ref, attn_hbm)
    store.wait()
    for head in range(heads):
        probs_copy(head).wait()


def attend(place, pieces, along_x, along_z, cosine, sine):
    width = pieces[0].shape[1]
    length = cosine.shape[1]
    size = length // 4
    heads = (KEYVAL_AT - QUERY_AT) // HD
    groups = (REST_AT - KEYVAL_AT) // (2 * HD)
    columns, rows = (heads, HD, length), (heads, length, HD)
    g_columns, g_rows = (groups, HD, length), (groups, length, HD)
    probs = (heads, sum(probs_at(3, size)), size)
    outs = [(width, ATTN_WIDTH), (length, width), rows, g_columns, g_rows,
            (length, heads * HD), columns, probs] + [(size, width)] * 4
    scratch = [(4, size, width), (width, ATTN_WIDTH), (length, width), columns, rows,
               g_columns, g_rows, g_columns, g_rows,
               (length, heads * HD), (length, heads * HD), columns, probs, (4, size, width)]
    return kernel_call(
        attend_kernel, "attend", place, (cosine, sine), (*pieces, *along_x, *along_z),
        [like(s) for s in outs], [like((2, width), F32)], [vmem(s) for s in scratch],
        36, 11, heads)


def attend_back_kernel(place, cos_ref, sin_ref, gain2_ref,
                       o0, o1, o2, o3, t0, t1, t2, t3, w_hbm, h_hbm, q_hbm, kt_hbm,
                       v_hbm, attn_hbm, attnt_hbm, probs_hbm,
                       c0, c1, c2, c3, x0, x1, x2, x3, y0, y1, y2, y3,
                       o_ref, t_ref, w_ref, h_ref, q_ref, kt_ref, v_ref,
                       attn_ref, attnt_ref, probs_ref,
                       do_ref, dot_ref, dqkv_ref, part_ref, first_ref, second_ref,
                       delta_ref, dk_ref, dv_ref, turned_ref, in_sem, out_sem, probs_sem):
    block, ix, iz = place[0], place[1], place[2]
    heads, length, _ = q_ref.shape
    groups = v_ref.shape[0]
    group_size = heads // groups
    size = length // 4
    half = HD // 2
    width = w_ref.shape[0]
    heads_w = heads * HD
    fetch, store = Moves(in_sem), Moves(out_sem)
    early = [fetch.start(w_hbm, w_ref)]
    early += [
        fetch.start(piece, o_ref.at[pl.ds(i * size, size), :])
        for i, piece in enumerate((o0, o1, o2, o3))
    ]
    for source, target in ((attnt_hbm, attnt_ref), (v_hbm, v_ref), (q_hbm, q_ref),
                           (kt_hbm, kt_ref)):
        early.append(fetch.start(source, target))

    def probs_copy(head):
        return pltpu.make_async_copy(probs_hbm.at[head], probs_ref.at[head], probs_sem.at[head])

    for head in range(heads):
        probs_copy(head).start()
    later = [fetch.start(attn_hbm, attn_ref), fetch.start(h_hbm, h_ref)]
    later += [fetch.start(piece, t_ref.at[i]) for i, piece in enumerate((t0, t1, t2, t3))]
    early[0].wait()
    for step in range(4):
        at = block_at(lax.bitwise_xor(block, step), size)
        early[1 + step].wait()
        grad_in = o_ref[step * size : (step + 1) * size, :]
        grad = jnp.concatenate(
            [dot_n(grad_in, w_ref[:, OUT_AT:QUERY_AT]), dot_n(grad_in, w_ref[:, REST_AT:])], 1)
        grad_t = grad.T.astype(BF16)
        grad = grad.astype(BF16)
        for head in range(heads):
            dot_ref[head, :, at] = grad_t[head * HD : (head + 1) * HD]
            do_ref[head, at, :] = grad[:, head * HD : (head + 1) * HD]
    for copy in early[5:]:
        copy.wait()
    delta_ref[...] = jnp.sum(
        attnt_ref[...].astype(F32) * dot_ref[...].astype(F32), 1, keepdims=True)
    dk_ref[...] = jnp.zeros_like(dk_ref)
    dv_ref[...] = jnp.zeros_like(dv_ref)

    def turned_back(field, cosine, sine):
        first, second = field[:half], field[half:]
        return jnp.concatenate(
            [first * cosine + second * sine, second * cosine - first * sine], 0)

    def one_head(head, carry):
        group = head // group_size
        probs_copy(head).wait()
        for step in range(4):
            first, reach = probs_at(step, size)
            columns = slice(step * size, reach)
            probs = probs_ref[head, first : first + reach, :]
            d_probs = dot_n(v_ref[group, :reach, :], dot_ref[head, :, columns])
            d_scores = (probs.astype(F32) * (d_probs - delta_ref[head, :, columns])).astype(BF16)
            dv_ref[group, :reach, :] += dot_n(probs, do_ref[head, columns, :])
            dk_ref[group, :reach, :] += dot_n(d_scores, q_ref[head, columns, :])
            d_query = dot_n(kt_ref[group, :, :reach], d_scores) * SCALE
            turned_ref[head, :, columns] = turned_back(
                d_query, cos_ref[:, columns], sin_ref[:, columns])
        return carry

    lax.fori_loop(0, heads, one_head, 0)
    for group in range(groups):
        turned_ref[heads + 2 * group] = turned_back(
            dk_ref[group].T * SCALE, cos_ref[...], sin_ref[...])
        turned_ref[heads + 2 * group + 1] = dv_ref[group].T
    dqkv_ref[...] = turned_ref[...].reshape((heads + 2 * groups) * HD, length).T.astype(BF16)
    for copy in later:
        copy.wait()

    gain = jnp.zeros((1, width), F32)
    for step, out in ((1, c1), (3, c3), (2, c2), (0, c0)):
        at = block_at(lax.bitwise_xor(block, step), size)
        part = dot_t(dqkv_ref[at, :], w_ref[:, QUERY_AT:REST_AT])
        value = t_ref[step].astype(F32)
        factor = lax.rsqrt(jnp.mean(value * value, -1, keepdims=True) + norm_eps)
        gain += jnp.sum(part * (value * factor), 0, keepdims=True)
        part_ref[step] = part.astype(BF16)
        store.start(part_ref.at[step], out)

    rows = width // 16
    part = dot_tn(h_ref[...], dqkv_ref[...]).astype(BF16)
    first_ref[:, :heads_w] = part[:, :heads_w]
    second_ref[:, LATE_WIDTH - heads_w :] = part[:, heads_w:]
    part = dot_tn(o_ref[...], attn_ref[...]).astype(BF16)
    first_ref[:, heads_w : heads_w + LATE_OUT] = part[:, :LATE_OUT]
    second_ref[:, : heads_w - LATE_OUT] = part[:, LATE_OUT:]
    gains = jnp.concatenate([gain, gain2_ref[...], jnp.zeros((126, width), F32)], 0)
    first_ref[:, heads_w + LATE_OUT :] = gains.T.astype(BF16)
    for offset, (x_out, y_out) in enumerate(((x0, y0), (x1, y1), (x2, y2), (x3, y3))):
        to_x = lax.rem(ix + 4 - offset, 4)
        to_z = lax.rem(iz + 4 - offset, 4)
        store.start(first_ref.at[block_at(to_x, 4 * rows), :], x_out)
        for i in range(4):
            store.start(second_ref.at[block_at(i * 4 + to_z, rows), :], y_out.at[i])
    store.wait()


def attend_back(place, cosine, sine, gain_two, pieces, token_pieces, weights, h_first,
                q, kt, v, attn, attnt, probs):
    size, width = pieces[0].shape
    heads, length, _ = q.shape
    groups = v.shape[0]
    every = heads + 2 * groups
    rows = width // 16
    outs = [(size, width)] * 4 + [(4 * rows, LATE_WIDTH)] * 4 + [(4, rows, LATE_WIDTH)] * 4
    scratch = [
        (length, width), (4, size, width), (width, ATTN_WIDTH), (length, width),
        q.shape, kt.shape, v.shape, attn.shape, attnt.shape, probs.shape,
        (heads, length, HD), (heads, HD, length), (length, every * HD), (4, size, width),
        (width, LATE_WIDTH), (width, LATE_WIDTH),
    ]
    wide = [(heads, 1, length), (groups, length, HD), (groups, length, HD), (every, HD, length)]
    return kernel_call(
        attend_back_kernel, "attend_back", place, (cosine, sine, gain_two),
        (*pieces, *token_pieces, weights, h_first, q, kt, v, attn, attnt, probs),
        [like(s) for s in outs], [],
        [vmem(s) for s in scratch] + [vmem(s, F32) for s in wide], 15, 24, heads)


def feed_kernel(place, h0, h1, g0, g1, w_hbm, hidden_hbm, dgu_hbm, b0, b1, r0, r1,
                w_ref, h_ref, g_ref, hidden_ref, dgu_ref, back_ref, out_ref, in_sem, out_sem):
    del place
    hidden_w = hidden_ref.shape[1]
    size = h_ref.shape[1]
    parts = [slice(i * hidden_w, (i + 1) * hidden_w) for i in range(3)]
    fetch, store = Moves(in_sem), Moves(out_sem)

    def weight(i):
        at = pl.ds(i * hidden_w, hidden_w)
        return fetch.start(w_hbm.at[:, at], w_ref.at[:, at])

    came = [fetch.start(h0, h_ref.at[0]), weight(0), weight(1), fetch.start(g0, g_ref.at[0]),
            weight(2), fetch.start(h1, h_ref.at[1]), fetch.start(g1, g_ref.at[1])]
    for i, (back, out) in enumerate(((b0, r0), (b1, r1))):
        rows = slice(i * size, (i + 1) * size)
        at = pl.ds(i * size, size)
        for copy in came[0:2] if i == 0 else came[5:7]:
            copy.wait()
        gate = dot_n(h_ref[i], w_ref[:, parts[0]])
        if i == 0:
            came[2].wait()
        up = dot_n(h_ref[i], w_ref[:, parts[1]])
        sig = 1.0 / (1.0 + jnp.exp2(gate * (-LOG2E)))
        silu = gate * sig
        hidden = (silu * up).astype(BF16)
        hidden_ref[rows, :] = hidden
        store.start(hidden_ref.at[at, :], hidden_hbm.at[at, :])
        if i == 0:
            came[3].wait()
            came[4].wait()
        d_hidden = dot_n(g_ref[i], w_ref[:, parts[2]])
        dgu_ref[rows, :hidden_w] = (
            d_hidden * up * (sig * (1.0 + gate * (1.0 - sig)))).astype(BF16)
        dgu_ref[rows, hidden_w:] = (d_hidden * silu).astype(BF16)
        store.start(dgu_ref.at[at, :], dgu_hbm.at[at, :])
        back_ref[i] = dot_t(dgu_ref[rows, :], w_ref[:, : 2 * hidden_w]).astype(BF16)
        store.start(back_ref.at[i], back)
        out_ref[i] = dot_t(hidden_ref[rows, :], w_ref[:, parts[2]]).astype(BF16)
        store.start(out_ref.at[i], out)
    store.wait()


def feed(place, weights, normed_pieces, grad_pieces):
    size, width = normed_pieces[0].shape
    hidden_w = weights.shape[1] // 3
    wide = [(2 * size, hidden_w), (2 * size, 2 * hidden_w)]
    return kernel_call(
        feed_kernel, "feed", place, (), (*normed_pieces, *grad_pieces, weights),
        [like(s) for s in wide + [(size, width)] * 4], [],
        [vmem(s) for s in [weights.shape] + [(2, size, width)] * 2 + wide + [(2, size, width)] * 2],
        7, 8)


def feed_grads_kernel(place, h0, h1, h2, h3, g0, g1, g2, g3, dgu_a, dgu_b, hidden_a, hidden_b,
                      out_hbm, h_ref, g_ref, dgu_ref, hidden_ref, out_ref, in_sem, out_sem):
    del place
    size = h0.shape[0]
    half, hidden_w = hidden_a.shape
    column = 512
    fetch, store = Moves(in_sem), Moves(out_sem)

    def rows_of(pieces, ref):
        return [
            fetch.start(piece, ref.at[pl.ds(i * size, size), :]) for i, piece in enumerate(pieces)
        ]

    def tiles_of(pieces, ref):
        tiles = []
        for tile in range(ref.shape[1] // column):
            at = pl.ds(tile * column, column)
            tiles.append([
                fetch.start(piece.at[:, at], ref.at[pl.ds(i * half, half), at])
                for i, piece in enumerate(pieces)
            ])
        return tiles

    h_came = rows_of((h0, h1, h2, h3), h_ref)
    dgu_came = tiles_of((dgu_a, dgu_b), dgu_ref)
    g_came = rows_of((g0, g1, g2, g3), g_ref)
    hidden_came = tiles_of((hidden_a, hidden_b), hidden_ref)
    at = 0
    for came, left, tiles, right in (
        (h_came, h_ref, dgu_came, dgu_ref), (g_came, g_ref, hidden_came, hidden_ref)
    ):
        for copy in came:
            copy.wait()
        for tile, copies in enumerate(tiles):
            for copy in copies:
                copy.wait()
            columns = pl.ds(at, column)
            out_ref[:, columns] = dot_tn(
                left[...], right[:, tile * column : (tile + 1) * column]).astype(BF16)
            store.start(out_ref.at[:, columns], out_hbm.at[:, columns])
            at += column
    store.wait()


def feed_grads(place, normed_pieces, grad_pieces, dgu_a, dgu_b, hidden_a, hidden_b):
    size, width = normed_pieces[0].shape
    half, hidden_w = hidden_a.shape
    scratch = [(4 * size, width)] * 2 + [(2 * half, 2 * hidden_w), (2 * half, hidden_w),
                                         (width, 3 * hidden_w)]
    return kernel_call(
        feed_grads_kernel, "feed_grads", place, (),
        (*normed_pieces, *grad_pieces, dgu_a, dgu_b, hidden_a, hidden_b),
        [like((width, 3 * hidden_w))], [], [vmem(s) for s in scratch], 20, 6)[0]


LATE_OUT, LATE_WIDTH = 128, 640


def late_middle_kernel(place, *refs):
    x_in, y_in, outs = refs[0:4], refs[4:8], refs[8:]
    ix, iz = place[1], place[2]
    rows = outs[0].shape[0]
    for offset in range(4):
        at = block_at(lax.rem(iz + 4 - offset, 4), rows)
        total = x_in[0][at, :].astype(F32)
        for ref in x_in[1:]:
            total += ref[at, :].astype(F32)
        outs[offset][...] = total.astype(BF16)
        to = lax.rem(ix + 4 - offset, 4)
        total = y_in[0][to].astype(F32)
        for ref in y_in[1:]:
            total += ref[to].astype(F32)
        outs[4 + offset][...] = total.astype(BF16)


def late_middle(place, along_x, along_z):
    _, rows, width = along_z[0].shape
    return pl.pallas_call(
        late_middle_kernel,
        out_shape=[like((rows, width))] * 8,
        in_specs=[scalars()] + [whole()] * 8,
        out_specs=[whole()] * 8,
        cost_estimate=SMALL,
        name="late_middle",
    )(place, *along_x, *along_z)


def late_last_kernel(place, *refs):
    x_in, y_in, keep_ref, send_ref = refs[0:4], refs[4:8], refs[8], refs[9]
    mine = place[3]
    rows = keep_ref.shape[0]
    for inputs, columns in ((x_in, slice(0, LATE_WIDTH)), (y_in, slice(LATE_WIDTH, 2 * LATE_WIDTH))):
        for ref, half in ((keep_ref, mine), (send_ref, 1 - mine)):
            at = block_at(half, rows)
            total = inputs[0][at, :].astype(F32)
            for other_ref in inputs[1:]:
                total += other_ref[at, :].astype(F32)
            ref[:, columns] = total.astype(ref.dtype)


def late_last(place, along_z, along_x):
    rows, width = along_x[0].shape
    return pl.pallas_call(
        late_last_kernel,
        out_shape=[
            jax.ShapeDtypeStruct((rows // 2, 2 * width), F32),
            jax.ShapeDtypeStruct((rows // 2, 2 * width), BF16),
        ],
        in_specs=[scalars()] + [whole()] * 8,
        out_specs=[whole()] * 2,
        cost_estimate=SMALL,
        name="late_last",
    )(place, *along_z, *along_x)


def norm_rows(values_in):
    factor = lax.rsqrt(jnp.mean(values_in * values_in, -1, keepdims=True) + norm_eps)
    return (values_in * factor, factor)


def norm_back(grad_in, normed, factor, gain_row):
    grad_normed = grad_in * gain_row
    inner = jnp.mean(grad_normed * normed, -1, keepdims=True)
    return (factor * (grad_normed - normed * inner), jnp.sum(grad_in * normed, 0))


def from_offset(v, axis, offset, size):
    return lax.ppermute(v, axis, [((i + offset) % size, i) for i in range(size)])


def other(v, axis):
    return from_offset(v, axis, 1, 2)


def pair_rows(v, axis):
    it = other(v, axis)
    mine = jnp.arange(2)[:, None, None] == lax.axis_index(axis)
    return jnp.where(mine, v[None], it[None]).reshape(2 * v.shape[0], v.shape[1])


def side_by_side(parts, width):
    return sum(
        jnp.pad(part, ((0, 0), (at, width - at - part.shape[1]))) for at, part in parts
    )


def near_sum(own, core):
    return own.astype(F32) + other(core, "core").astype(F32)


def far_sum(chip, diagonal):
    return near_sum(chip, diagonal).astype(BF16)


def after(value, first):
    return lax.optimization_barrier((value, first))


def from_both(along_first, first_axis, along_second, second_axis, large):
    near = [
        from_offset(part[i], axis, i, 4)
        for i in (1, 3)
        for part, axis in ((along_first, first_axis), (along_second, second_axis))
    ]
    opposite = along_first[2], along_second[2]
    if large:
        opposite, near = after(opposite, near)
    far = [from_offset(opposite[0], first_axis, 2, 4), from_offset(opposite[1], second_axis, 2, 4)]
    near, far = after(near, far)
    first = [along_first[0], near[0], far[0], near[2]]
    second = [along_second[0], near[1], far[1], near[3]]
    return first, second


def scatter_rows(v):
    two = lax.psum_scatter(v, ("x", "z"), scatter_dimension=0, tiled=True)
    rows = two.shape[0] // 2
    iyh = lax.axis_index("yh")
    keep = lax.dynamic_slice_in_dim(two, iyh * rows, rows, 0)
    send = lax.dynamic_slice_in_dim(two, (1 - iyh) * rows, rows, 0)
    return keep.astype(F32) + other(send, "yh").astype(F32)


def body(tokens, norm_gains, w_query, w_keyval, w_out, w_gateup, w_down, cotangent):
    D = tokens.shape[1]
    length = 4 * tokens.shape[0]
    hidden_w = w_down.shape[0]
    heads_w = w_query.shape[1]
    gains_w = norm_gains.shape[1]
    block = lax.axis_index("yl") * 2 + lax.axis_index("core")
    place = jnp.stack(
        [block, lax.axis_index("x"), lax.axis_index("z"), lax.axis_index("yh")]
    ).astype(jnp.int32)

    out_t = w_out.T
    attn_own = side_by_side(
        [
            (OUT_AT, out_t[:, :OUT_CUT]),
            (QUERY_AT, w_query),
            (KEYVAL_AT, w_keyval),
            (REST_AT, out_t[:, OUT_CUT:]),
        ],
        ATTN_WIDTH,
    )
    near = other(tokens, "core")
    attn_pair = pair_rows(attn_own, "yh")
    mlp_own, attn_pair = after((w_gateup[:, 0], w_gateup[:, 1], w_down.T), attn_pair)
    mlp_own = [(i * hidden_w, part) for i, part in enumerate(mlp_own)]
    mlp_pair = pair_rows(side_by_side(mlp_own, 3 * hidden_w), "yh")

    pair_w = 8 * gains_w
    gain_at = (lax.axis_index("yh") * 4 + block) * gains_w
    gain_part = lax.dynamic_update_slice(jnp.zeros((2, pair_w), F32), norm_gains, (0, gain_at))
    for axis in ("core", "yl", "yh"):
        gain_part = gain_part + other(gain_part, axis)
    gain_part = gain_part.T
    gain_high = gain_part.astype(BF16)
    gain_low = (gain_part - gain_high.astype(F32)).astype(BF16)
    first, second = attn_pair[:, :HALF_WIDTH], attn_pair[:, HALF_WIDTH:]
    first += side_by_side([(0, gain_high), (2, gain_low)], HALF_WIDTH)

    tokens, (first, near) = after(tokens, (first, near))
    far = other(tokens, "yl")
    along_z, along_x = from_both([first] * 4, "z", [second] * 4, "x", False)
    along_z, along_x, far, mlp_pair = lax.optimization_barrier(
        (jnp.stack(along_z), jnp.stack(along_x), far, mlp_pair)
    )
    mlp_w = lax.all_gather(mlp_pair, ("x", "z"), axis=0, tiled=True)
    token_pieces = [tokens, near, far, other(far, "core")]
    cotangent, far = after(cotangent, far)
    grad_far = other(cotangent, "yl")
    along_x, along_z = from_both([along_z] * 4, "x", [along_x] * 4, "z", True)

    positions = jnp.arange(length).astype(F32)
    freqs = rope_base ** (-(jnp.arange(HD // 2).astype(F32) * 2.0 / HD))
    angles = freqs[:, None] * positions[None, :]
    cosine, sine = jnp.cos(angles), jnp.sin(angles)

    gain_rows, attn_w, h_first, q, kt, v, attn, attnt, probs, *parts = attend(
        place, token_pieces, along_x, along_z, cosine, sine
    )
    grad_far, parts = after(grad_far, parts)
    grad_pieces = [cotangent, other(cotangent, "core"), grad_far, other(grad_far, "core")]
    middle_far = far_sum(parts[2], parts[3])
    middle = (
        tokens.astype(F32) + near_sum(parts[0], parts[1]) + other(middle_far, "yl").astype(F32)
    )
    normed2, factor2 = norm_rows(middle)
    h_own = (normed2 * gain_rows[1]).astype(BF16)

    h_pieces = [h_own, other(h_own, "core")]
    h_far = other(h_own, "yl")
    hidden_a, dgu_a, back_own, back_core, out_own, out_core = feed(
        place, mlp_w, h_pieces, grad_pieces[:2]
    )
    h_far, hidden_a = after(h_far, hidden_a)
    h_pieces += [h_far, other(h_far, "core")]
    hidden_b, dgu_b, back_chip, back_diag, out_chip, out_diag = feed(
        place, mlp_w, h_pieces[2:], grad_pieces[2:]
    )
    back_near = near_sum(back_own, back_core)
    out_near = near_sum(out_own, out_core)

    back_far = far_sum(back_chip, back_diag)
    hidden_b, back_far = after(hidden_b, back_far)
    mlp_grads = feed_grads(place, h_pieces, grad_pieces, dgu_a, dgu_b, hidden_a, hidden_b)
    mlp_grads, back_far = after(mlp_grads, other(back_far, "yl"))
    d_h2_own = back_near + back_far.astype(F32)
    early = scatter_rows(mlp_grads)
    out_far = far_sum(out_chip, out_diag)

    d_norm2, gain_two = norm_back(d_h2_own, normed2, factor2, gain_rows[1])
    d_middle = cotangent.astype(F32) + d_norm2
    d_out = d_middle.astype(BF16)
    d_out_far = other(d_out, "yl")
    d_out_far, out_near = after(d_out_far, out_near)
    out_pieces = [d_out, other(d_out, "core"), d_out_far, other(d_out_far, "core")]
    out_far, out_pieces = after(out_far, out_pieces)
    out_far = other(out_far, "yl")

    back = attend_back(
        place, cosine, sine, gain_two[None], out_pieces, token_pieces, attn_w,
        h_first, q, kt, v, attn, attnt, probs,
    )
    out_near, back = after(out_near, back)
    result = (middle + out_near + out_far.astype(F32)).astype(BF16)
    parts, late_parts = back[:4], back[4:]
    d_far = other(far_sum(parts[2], parts[3]), "yl")
    along_x, along_z = from_both(late_parts[:4], "x", late_parts[4:], "z", True)
    along_x, (d_far, result) = after(along_x, (d_far, result))
    middle_parts = late_middle(place, along_x, along_z)
    along_z, along_x = from_both(middle_parts[:4], "z", middle_parts[4:], "x", False)
    d_h1_own = near_sum(parts[0], parts[1]) + d_far.astype(F32)
    along_z, (d_h1_own, early) = after(along_z, (d_h1_own, early))
    late_keep, late_send = late_last(place, along_z, along_x)
    late = late_keep + other(late_send, "yh").astype(F32)

    normed1, factor1 = norm_rows(tokens.astype(F32))
    d_norm1, _ = norm_back(d_h1_own, normed1, factor1, gain_rows[0])
    input_grad = (d_middle + d_norm1).astype(BF16)

    out_at = heads_w + LATE_OUT
    grad_out = jnp.concatenate([late[:, heads_w:out_at], late[:, LATE_WIDTH : LATE_WIDTH + heads_w - LATE_OUT]], 1)
    gain_sum = late[:, out_at : out_at + 2].T
    for axis in ("core", "yl"):
        gain_sum = gain_sum + other(gain_sum, axis)
    grad_gains = lax.dynamic_slice(gain_sum, (0, block * gains_w), (2, gains_w))
    return (
        result,
        input_grad,
        late[:, :heads_w],
        late[:, 2 * LATE_WIDTH - heads_w :],
        grad_out.T,
        early[:, : 2 * hidden_w].reshape(-1, 2, hidden_w),
        early[:, 2 * hidden_w :].T,
        grad_gains,
    )


def solution(mesh):
    fine = Mesh(mesh.devices.reshape(4, 4, 2, 2, 2), ("x", "z", "yh", "yl", "core"))
    dp = ("x", "z", "yh")
    tensor = ("yl", "core")
    every = dp + tensor
    weights = (P(dp, tensor), P(dp, tensor), P(tensor, dp), P(dp, None, tensor), P(tensor, dp))
    rows = P(every, None)
    gains = P(None, every)
    return jax.shard_map(
        body,
        mesh=fine,
        in_specs=(rows, gains) + weights + (rows,),
        out_specs=(rows, rows) + weights + (gains,),
        check_vma=False,
    )
```

```python
import jax
import jax.numpy as jnp
from jax import lax
from jax.experimental import pallas as pl
from jax.experimental.pallas import tpu as pltpu
from jax.sharding import Mesh, PartitionSpec as P

HD = 96
F32 = jnp.float32
BF16 = jnp.bfloat16
norm_eps = 1e-05
rope_base = 100000.0
LOG2E = 1.4426950408889634
SCALE = HD ** (-0.5)
MIB = 1024 * 1024
SMALL = pl.CostEstimate(flops=1, bytes_accessed=1, transcendentals=0)

GAIN_AT, OUT_AT, QUERY_AT, KEYVAL_AT, REST_AT, ATTN_WIDTH = 0, 128, 256, 640, 1024, 1280
HALF_WIDTH = ATTN_WIDTH // 2
OUT_CUT = QUERY_AT - OUT_AT
LIMIT = 60


def dot_n(left, right):
    return jnp.dot(left, right, preferred_element_type=F32)


def dot_t(left, right):
    return lax.dot_general(left, right, (((1,), (1,)), ((), ())), preferred_element_type=F32)


def dot_tn(left, right):
    return lax.dot_general(left, right, (((0,), (0,)), ((), ())), preferred_element_type=F32)


def block_at(index, size):
    return pl.ds(pl.multiple_of(index * size, size), size)


def causal_mask(scores, size):
    key_at = lax.broadcasted_iota(jnp.int32, (size, size), 0)
    query_at = lax.broadcasted_iota(jnp.int32, (size, size), 1)
    tail = jnp.where(key_at <= query_at, scores[-size:], -1e30)
    if scores.shape[0] == size:
        return tail
    return jnp.concatenate([scores[:-size], tail], 0)


class Moves:
    def __init__(self, sems):
        self.sems = sems
        self.started = []

    def start(self, source, target):
        copy = pltpu.make_async_copy(source, target, self.sems.at[len(self.started)])
        copy.start()
        self.started.append(copy)
        return copy

    def wait(self):
        for copy in self.started:
            copy.wait()


def vmem(shape, dtype=BF16):
    return pltpu.VMEM(shape, dtype)


def like(shape, dtype=BF16):
    return jax.ShapeDtypeStruct(shape, dtype)


def whole():
    return pl.BlockSpec(memory_space=pltpu.VMEM)


def apart():
    return pl.BlockSpec(memory_space=pl.ANY)


def scalars():
    return pl.BlockSpec(memory_space=pltpu.SMEM)


def kernel_call(kernel, name, place, small, large, outs, small_outs, scratch, *copies):
    return pl.pallas_call(
        kernel,
        out_shape=list(small_outs) + list(outs),
        in_specs=[scalars()] + [whole()] * len(small) + [apart()] * len(large),
        out_specs=[whole()] * len(small_outs) + [apart()] * len(outs),
        scratch_shapes=list(scratch)
        + [pltpu.SemaphoreType.DMA((count,)) for count in copies],
        compiler_params=pltpu.CompilerParams(vmem_limit_bytes=LIMIT * MIB),
        cost_estimate=SMALL,
        name=name,
    )(place, *small, *large)


def probs_at(step, size):
    return step * (step + 1) // 2 * size, (step + 1) * size


def attend_kernel(place, cos_ref, sin_ref, t0, t1, t2, t3, a0, a1, a2, a3, b0, b1, b2, b3,
                  gains_ref, w_hbm, h_hbm, q_hbm, kt_hbm, v_hbm, attn_hbm, attnt_hbm, probs_hbm,
                  o0, o1, o2, o3,
                  t_ref, w_ref, h_ref, qt_ref, q_ref, kt_ref, k_ref, vt_ref, v_ref,
                  natural, attn_ref, attnt_ref, probs_ref, part_ref, in_sem, out_sem, probs_sem):
    block, ix, iz = place[0], place[1], place[2]
    half = HD // 2
    size = t_ref.shape[1]
    heads, _, length = qt_ref.shape
    group_size = heads // k_ref.shape[0]
    rows = a0.shape[1]
    fetch, store = Moves(in_sem), Moves(out_sem)
    came = []
    for far, (along_x, along_z) in enumerate(zip((a0, a1, a2, a3), (b0, b1, b2, b3))):
        for near in range(4):
            at_a = lax.rem(ix + far, 4) * 4 + lax.rem(iz + near, 4)
            at_b = lax.rem(ix + near, 4) * 4 + lax.rem(iz + far, 4)
            came.append(fetch.start(
                along_x.at[near], w_ref.at[block_at(at_a, rows), pl.ds(0, HALF_WIDTH)]))
            came.append(fetch.start(
                along_z.at[near], w_ref.at[block_at(at_b, rows), pl.ds(HALF_WIDTH, HALF_WIDTH)]))
    tokens_came = [
        fetch.start(piece, t_ref.at[i]) for i, piece in enumerate((t0, t1, t2, t3))
    ]
    for copy in came:
        copy.wait()
    store.start(w_ref, w_hbm)
    gains = w_ref[:, GAIN_AT:OUT_AT].astype(F32).T
    gain_row = gains[0:1] + gains[2:3]
    gains_ref[...] = gains[0:2] + gains[2:4]
    for step in range(4):
        at = block_at(lax.bitwise_xor(block, step), size)
        tokens_came[step].wait()
        value = t_ref[step].astype(F32)
        factor = lax.rsqrt(jnp.mean(value * value, -1, keepdims=True) + norm_eps)
        normed = (value * factor * gain_row).astype(BF16)
        h_ref[at, :] = normed
        cosine = cos_ref[:, at]
        sine = sin_ref[:, at]
        every = dot_n(normed, w_ref[:, QUERY_AT:REST_AT]).T
        query, keyval = every[: KEYVAL_AT - QUERY_AT], every[KEYVAL_AT - QUERY_AT :]

        def rotated(field):
            first, second = field[:half], field[half:]
            return jnp.concatenate(
                [first * cosine - second * sine, second * cosine + first * sine], 0
            )

        for head in range(query.shape[0] // HD):
            turned = rotated(query[head * HD : (head + 1) * HD])
            qt_ref[head, :, at] = turned.astype(BF16)
            q_ref[head, at, :] = turned.T.astype(BF16)
        for head in range(keyval.shape[0] // (2 * HD)):
            turned = rotated(keyval[2 * head * HD : (2 * head + 1) * HD])
            value_t = keyval[(2 * head + 1) * HD : (2 * head + 2) * HD]
            kt_ref[head, :, at] = turned.astype(BF16)
            k_ref[head, at, :] = turned.T.astype(BF16)
            vt_ref[head, :, at] = value_t.astype(BF16)
            v_ref[head, at, :] = value_t.T.astype(BF16)
    for source, target in ((h_ref, h_hbm), (q_ref, q_hbm), (kt_ref, kt_hbm), (v_ref, v_hbm)):
        store.start(source, target)

    def probs_copy(head):
        return pltpu.make_async_copy(probs_ref.at[head], probs_hbm.at[head], probs_sem.at[head])

    def one_head(head, carry):
        group = head // group_size
        for step in range(4):
            first, reach = probs_at(step, size)
            columns = slice(step * size, reach)
            scores = causal_mask(dot_n(k_ref[group, :reach, :], qt_ref[head, :, columns]), size)
            top = jnp.max(scores, 0, keepdims=True)
            expo = jnp.exp2((scores - top) * (SCALE * LOG2E))
            total = jnp.sum(expo, 0, keepdims=True)
            probs = (expo * (1.0 / total)).astype(BF16)
            probs_ref[head, first : first + reach, :] = probs
            mixed = dot_n(vt_ref[group, :, :reach], probs)
            attnt_ref[head, :, columns] = mixed.astype(BF16)
        probs_copy(head).start()
        return carry

    lax.fori_loop(0, heads, one_head, 0)
    store.start(attnt_ref, attnt_hbm)
    natural[...] = attnt_ref[...].reshape(heads * HD, length).T
    for step, out in ((1, o1), (3, o3), (2, o2), (0, o0)):
        at = block_at(lax.bitwise_xor(block, step), size)
        attn = natural[at, :]
        attn_ref[step * size : (step + 1) * size, :] = attn
        part = dot_t(attn[:, :OUT_CUT], w_ref[:, OUT_AT:QUERY_AT])
        part += dot_t(attn[:, OUT_CUT:], w_ref[:, REST_AT:])
        part_ref[step] = part.astype(BF16)
        store.start(part_ref.at[step], out)
    store.start(attn_ref, attn_hbm)
    store.wait()
    for head in range(heads):
        probs_copy(head).wait()


def attend(place, pieces, along_x, along_z, cosine, sine):
    width = pieces[0].shape[1]
    length = cosine.shape[1]
    size = length // 4
    heads = (KEYVAL_AT - QUERY_AT) // HD
    groups = (REST_AT - KEYVAL_AT) // (2 * HD)
    columns, rows = (heads, HD, length), (heads, length, HD)
    g_columns, g_rows = (groups, HD, length), (groups, length, HD)
    probs = (heads, sum(probs_at(3, size)), size)
    outs = [(width, ATTN_WIDTH), (length, width), rows, g_columns, g_rows,
            (length, heads * HD), columns, probs] + [(size, width)] * 4
    scratch = [(4, size, width), (width, ATTN_WIDTH), (length, width), columns, rows,
               g_columns, g_rows, g_columns, g_rows,
               (length, heads * HD), (length, heads * HD), columns, probs, (4, size, width)]
    return kernel_call(
        attend_kernel, "attend", place, (cosine, sine), (*pieces, *along_x, *along_z),
        [like(s) for s in outs], [like((2, width), F32)], [vmem(s) for s in scratch],
        36, 11, heads)


def attend_back_kernel(place, cos_ref, sin_ref,
                       o0, o1, o2, o3, w_hbm, h_hbm, q_hbm, kt_hbm, v_hbm, attn_hbm, attnt_hbm,
                       probs_hbm,
                       dqkv_hbm, x0, x1, x2, x3, y0, y1, y2, y3,
                       o_ref, w_ref, h_ref, q_ref, kt_ref, v_ref, attn_ref, attnt_ref, probs_ref,
                       do_ref, dot_ref, dqkv_ref, first_ref, second_ref,
                       delta_ref, dk_ref, dv_ref, turned_ref, in_sem, out_sem, probs_sem):
    block, ix, iz = place[0], place[1], place[2]
    heads, length, _ = q_ref.shape
    groups = v_ref.shape[0]
    group_size = heads // groups
    size = length // 4
    half = HD // 2
    width = w_ref.shape[0]
    heads_w = heads * HD
    fetch, store = Moves(in_sem), Moves(out_sem)
    rest_w = ATTN_WIDTH - REST_AT
    early = [
        fetch.start(w_hbm.at[:, pl.ds(OUT_AT, OUT_CUT)], w_ref.at[:, pl.ds(0, OUT_CUT)]),
        fetch.start(w_hbm.at[:, pl.ds(REST_AT, rest_w)], w_ref.at[:, pl.ds(OUT_CUT, rest_w)]),
    ]
    early += [
        fetch.start(piece, o_ref.at[pl.ds(i * size, size), :])
        for i, piece in enumerate((o0, o1, o2, o3))
    ]

    def probs_copy(head):
        return pltpu.make_async_copy(probs_hbm.at[head], probs_ref.at[head], probs_sem.at[head])

    middle = [
        fetch.start(source, target)
        for source, target in ((attnt_hbm, attnt_ref), (v_hbm, v_ref), (q_hbm, q_ref),
                               (kt_hbm, kt_ref))
    ]
    for head in range(heads):
        probs_copy(head).start()
    later = [fetch.start(attn_hbm, attn_ref), fetch.start(h_hbm, h_ref)]
    dk_ref[...] = jnp.zeros_like(dk_ref)
    dv_ref[...] = jnp.zeros_like(dv_ref)
    for copy in early[:2]:
        copy.wait()
    for step in range(4):
        at = block_at(lax.bitwise_xor(block, step), size)
        early[2 + step].wait()
        grad = dot_n(o_ref[step * size : (step + 1) * size, :], w_ref[...])
        grad_t = grad.T.astype(BF16)
        grad = grad.astype(BF16)
        for head in range(heads):
            dot_ref[head, :, at] = grad_t[head * HD : (head + 1) * HD]
            do_ref[head, at, :] = grad[:, head * HD : (head + 1) * HD]
    for copy in middle:
        copy.wait()
    delta_ref[...] = jnp.sum(
        attnt_ref[...].astype(F32) * dot_ref[...].astype(F32), 1, keepdims=True)

    def turned_back(field, cosine, sine):
        first, second = field[:half], field[half:]
        return jnp.concatenate(
            [first * cosine + second * sine, second * cosine - first * sine], 0)

    def one_head(head, carry):
        group = head // group_size
        probs_copy(head).wait()
        for step in range(4):
            first, reach = probs_at(step, size)
            columns = slice(step * size, reach)
            probs = probs_ref[head, first : first + reach, :]
            d_probs = dot_n(v_ref[group, :reach, :], dot_ref[head, :, columns])
            d_scores = (probs.astype(F32) * (d_probs - delta_ref[head, :, columns])).astype(BF16)
            dv_ref[group, :reach, :] += dot_n(probs, do_ref[head, columns, :])
            dk_ref[group, :reach, :] += dot_n(d_scores, q_ref[head, columns, :])
            d_query = dot_n(kt_ref[group, :, :reach], d_scores) * SCALE
            turned_ref[head, :, columns] = turned_back(
                d_query, cos_ref[:, columns], sin_ref[:, columns])
        return carry

    lax.fori_loop(0, heads, one_head, 0)
    for group in range(groups):
        turned_ref[heads + 2 * group] = turned_back(
            dk_ref[group].T * SCALE, cos_ref[...], sin_ref[...])
        turned_ref[heads + 2 * group + 1] = dv_ref[group].T
    dqkv_ref[...] = turned_ref[...].reshape((heads + 2 * groups) * HD, length).T.astype(BF16)
    store.start(dqkv_ref, dqkv_hbm)
    for copy in later:
        copy.wait()

    rows = width // 16
    part = dot_tn(h_ref[...], dqkv_ref[...]).astype(BF16)
    first_ref[:, :heads_w] = part[:, :heads_w]
    second_ref[:, LATE_WIDTH - heads_w :] = part[:, heads_w:]
    part = dot_tn(o_ref[...], attn_ref[...]).astype(BF16)
    first_ref[:, heads_w:] = part[:, :LATE_OUT]
    second_ref[:, : heads_w - LATE_OUT] = part[:, LATE_OUT:]
    for offset, (x_out, y_out) in enumerate(((x0, y0), (x1, y1), (x2, y2), (x3, y3))):
        to_x = lax.rem(ix + 4 - offset, 4)
        to_z = lax.rem(iz + 4 - offset, 4)
        store.start(first_ref.at[block_at(to_x, 4 * rows), :], x_out)
        for i in range(4):
            store.start(second_ref.at[block_at(i * 4 + to_z, rows), :], y_out.at[i])
    store.wait()


def attend_back(place, cosine, sine, pieces, weights, h_first, q, kt, v, attn, attnt, probs):
    size, width = pieces[0].shape
    heads, length, _ = q.shape
    groups = v.shape[0]
    every = heads + 2 * groups
    rows = width // 16
    outs = [(length, every * HD)] + [(4 * rows, LATE_WIDTH)] * 4 + [(4, rows, LATE_WIDTH)] * 4
    scratch = [
        (length, width), (width, heads * HD), (length, width),
        q.shape, kt.shape, v.shape, attn.shape, attnt.shape, probs.shape,
        (heads, length, HD), (heads, HD, length), (length, every * HD),
        (width, LATE_WIDTH), (width, LATE_WIDTH),
    ]
    wide = [(heads, 1, length), (groups, length, HD), (groups, length, HD), (every, HD, length)]
    return kernel_call(
        attend_back_kernel, "attend_back", place, (cosine, sine),
        (*pieces, weights, h_first, q, kt, v, attn, attnt, probs),
        [like(s) for s in outs], [],
        [vmem(s) for s in scratch] + [vmem(s, F32) for s in wide], 12, 21, heads)


def project_back_kernel(place, dqkv_hbm, w_hbm, c0, c1, c2, c3,
                        dqkv_ref, w_ref, part_ref, in_sem, out_sem):
    block = place[0]
    size = part_ref.shape[1]
    fetch, store = Moves(in_sem), Moves(out_sem)
    fetch.start(w_hbm.at[:, pl.ds(QUERY_AT, REST_AT - QUERY_AT)], w_ref)
    fetch.start(dqkv_hbm, dqkv_ref)
    fetch.wait()
    for step, out in ((3, c3), (2, c2), (1, c1), (0, c0)):
        at = block_at(lax.bitwise_xor(block, step), size)
        part_ref[step] = dot_t(dqkv_ref[at, :], w_ref[...]).astype(BF16)
        store.start(part_ref.at[step], out)
    store.wait()


def project_back(place, d_qkv, weights):
    length, every_w = d_qkv.shape
    width = weights.shape[0]
    size = length // 4
    return kernel_call(
        project_back_kernel, "project_back", place, (), (d_qkv, weights),
        [like((size, width))] * 4, [],
        [vmem(s) for s in (d_qkv.shape, (width, every_w), (4, size, width))], 2, 4)


def feed_kernel(place, h0, h1, g0, g1, w_hbm, hidden_hbm, dgu_hbm, b0, b1, r0, r1,
                w_ref, h_ref, g_ref, hidden_ref, dgu_ref, back_ref, out_ref, in_sem, out_sem):
    del place
    hidden_w = hidden_ref.shape[1]
    size = h_ref.shape[1]
    parts = [slice(i * hidden_w, (i + 1) * hidden_w) for i in range(3)]
    fetch, store = Moves(in_sem), Moves(out_sem)

    def weight(i):
        at = pl.ds(i * hidden_w, hidden_w)
        return fetch.start(w_hbm.at[:, at], w_ref.at[:, at])

    came = [fetch.start(h0, h_ref.at[0]), weight(0), weight(1), fetch.start(g0, g_ref.at[0]),
            weight(2), fetch.start(h1, h_ref.at[1]), fetch.start(g1, g_ref.at[1])]
    for i, (back, out) in enumerate(((b0, r0), (b1, r1))):
        rows = slice(i * size, (i + 1) * size)
        at = pl.ds(i * size, size)
        for copy in came[0:2] if i == 0 else came[5:7]:
            copy.wait()
        gate = dot_n(h_ref[i], w_ref[:, parts[0]])
        if i == 0:
            came[2].wait()
        up = dot_n(h_ref[i], w_ref[:, parts[1]])
        sig = 1.0 / (1.0 + jnp.exp2(gate * (-LOG2E)))
        silu = gate * sig
        hidden = (silu * up).astype(BF16)
        hidden_ref[rows, :] = hidden
        store.start(hidden_ref.at[at, :], hidden_hbm.at[at, :])
        if i == 0:
            came[3].wait()
            came[4].wait()
        d_hidden = dot_n(g_ref[i], w_ref[:, parts[2]])
        dgu_ref[rows, :hidden_w] = (
            d_hidden * up * (sig * (1.0 + gate * (1.0 - sig)))).astype(BF16)
        dgu_ref[rows, hidden_w:] = (d_hidden * silu).astype(BF16)
        store.start(dgu_ref.at[at, :], dgu_hbm.at[at, :])
        back_ref[i] = dot_t(dgu_ref[rows, :], w_ref[:, : 2 * hidden_w]).astype(BF16)
        store.start(back_ref.at[i], back)
        out_ref[i] = dot_t(hidden_ref[rows, :], w_ref[:, parts[2]]).astype(BF16)
        store.start(out_ref.at[i], out)
    store.wait()


def feed(place, weights, normed_pieces, grad_pieces):
    size, width = normed_pieces[0].shape
    hidden_w = weights.shape[1] // 3
    wide = [(2 * size, hidden_w), (2 * size, 2 * hidden_w)]
    return kernel_call(
        feed_kernel, "feed", place, (), (*normed_pieces, *grad_pieces, weights),
        [like(s) for s in wide + [(size, width)] * 4], [],
        [vmem(s) for s in [weights.shape] + [(2, size, width)] * 2 + wide + [(2, size, width)] * 2],
        7, 8)


def feed_grads_kernel(place, h0, h1, h2, h3, g0, g1, g2, g3, dgu_a, dgu_b, hidden_a, hidden_b,
                      out_hbm, h_ref, g_ref, dgu_ref, hidden_ref, out_ref, in_sem, out_sem):
    del place
    size = h0.shape[0]
    half, hidden_w = hidden_a.shape
    column = 512
    fetch, store = Moves(in_sem), Moves(out_sem)

    def rows_of(pieces, ref):
        return [
            fetch.start(piece, ref.at[pl.ds(i * size, size), :]) for i, piece in enumerate(pieces)
        ]

    def tiles_of(pieces, ref):
        tiles = []
        for tile in range(ref.shape[1] // column):
            at = pl.ds(tile * column, column)
            tiles.append([
                fetch.start(piece.at[:, at], ref.at[pl.ds(i * half, half), at])
                for i, piece in enumerate(pieces)
            ])
        return tiles

    h_came = rows_of((h0, h1, h2, h3), h_ref)
    dgu_came = tiles_of((dgu_a, dgu_b), dgu_ref)
    g_came = rows_of((g0, g1, g2, g3), g_ref)
    hidden_came = tiles_of((hidden_a, hidden_b), hidden_ref)
    at = 0
    for came, left, tiles, right in (
        (h_came, h_ref, dgu_came, dgu_ref), (g_came, g_ref, hidden_came, hidden_ref)
    ):
        for copy in came:
            copy.wait()
        for tile, copies in enumerate(tiles):
            for copy in copies:
                copy.wait()
            columns = pl.ds(at, column)
            out_ref[:, columns] = dot_tn(
                left[...], right[:, tile * column : (tile + 1) * column]).astype(BF16)
            store.start(out_ref.at[:, columns], out_hbm.at[:, columns])
            at += column
    store.wait()


def feed_grads(place, normed_pieces, grad_pieces, dgu_a, dgu_b, hidden_a, hidden_b):
    size, width = normed_pieces[0].shape
    half, hidden_w = hidden_a.shape
    scratch = [(4 * size, width)] * 2 + [(2 * half, 2 * hidden_w), (2 * half, hidden_w),
                                         (width, 3 * hidden_w)]
    return kernel_call(
        feed_grads_kernel, "feed_grads", place, (),
        (*normed_pieces, *grad_pieces, dgu_a, dgu_b, hidden_a, hidden_b),
        [like((width, 3 * hidden_w))], [], [vmem(s) for s in scratch], 20, 6)[0]


LATE_OUT, LATE_WIDTH = 192, 576


def late_middle_kernel(place, *refs):
    x_in, y_in, outs = refs[0:4], refs[4:8], refs[8:]
    ix, iz = place[1], place[2]
    rows = outs[0].shape[0]
    for offset in range(4):
        at = block_at(lax.rem(iz + 4 - offset, 4), rows)
        total = x_in[0][at, :].astype(F32)
        for ref in x_in[1:]:
            total += ref[at, :].astype(F32)
        outs[offset][...] = total.astype(BF16)
        to = lax.rem(ix + 4 - offset, 4)
        total = y_in[0][to].astype(F32)
        for ref in y_in[1:]:
            total += ref[to].astype(F32)
        outs[4 + offset][...] = total.astype(BF16)


def late_middle(place, along_x, along_z):
    _, rows, width = along_z[0].shape
    return pl.pallas_call(
        late_middle_kernel,
        out_shape=[like((rows, width))] * 8,
        in_specs=[scalars()] + [whole()] * 8,
        out_specs=[whole()] * 8,
        cost_estimate=SMALL,
        name="late_middle",
    )(place, *along_x, *along_z)


def late_last_kernel(place, *refs):
    x_in, y_in, keep_ref, send_ref = refs[0:4], refs[4:8], refs[8], refs[9]
    mine = place[3]
    rows = keep_ref.shape[0]
    for inputs, columns in ((x_in, slice(0, LATE_WIDTH)), (y_in, slice(LATE_WIDTH, 2 * LATE_WIDTH))):
        for ref, half in ((keep_ref, mine), (send_ref, 1 - mine)):
            at = block_at(half, rows)
            total = inputs[0][at, :].astype(F32)
            for other_ref in inputs[1:]:
                total += other_ref[at, :].astype(F32)
            ref[:, columns] = total.astype(ref.dtype)


def late_last(place, along_z, along_x):
    rows, width = along_x[0].shape
    return pl.pallas_call(
        late_last_kernel,
        out_shape=[
            jax.ShapeDtypeStruct((rows // 2, 2 * width), F32),
            jax.ShapeDtypeStruct((rows // 2, 2 * width), BF16),
        ],
        in_specs=[scalars()] + [whole()] * 8,
        out_specs=[whole()] * 2,
        cost_estimate=SMALL,
        name="late_last",
    )(place, *along_z, *along_x)


def norm_rows(values_in):
    factor = lax.rsqrt(jnp.mean(values_in * values_in, -1, keepdims=True) + norm_eps)
    return (values_in * factor, factor)


def norm_back(grad_in, normed, factor, gain_row):
    grad_normed = grad_in * gain_row
    inner = jnp.mean(grad_normed * normed, -1, keepdims=True)
    return factor * (grad_normed - normed * inner)


def from_offset(v, axis, offset, size):
    return lax.ppermute(v, axis, [((i + offset) % size, i) for i in range(size)])


def other(v, axis):
    return from_offset(v, axis, 1, 2)


def pair_rows(v, axis):
    it = other(v, axis)
    mine = jnp.arange(2)[:, None, None] == lax.axis_index(axis)
    return jnp.where(mine, v[None], it[None]).reshape(2 * v.shape[0], v.shape[1])


def side_by_side(parts, width):
    return sum(
        jnp.pad(part, ((0, 0), (at, width - at - part.shape[1]))) for at, part in parts
    )


def near_sum(own, core):
    return own.astype(F32) + other(core, "core").astype(F32)


def far_sum(chip, diagonal):
    return near_sum(chip, diagonal).astype(BF16)


def after(value, first):
    return lax.optimization_barrier((value, first))


def from_both(along_first, first_axis, along_second, second_axis, large, beside=()):
    near = [
        from_offset(part[i], axis, i, 4)
        for i in (1, 3)
        for part, axis in ((along_first, first_axis), (along_second, second_axis))
    ]
    opposite = along_first[2], along_second[2]
    if large:
        opposite, (near, beside) = after(opposite, (near, beside))
    far = [from_offset(opposite[0], first_axis, 2, 4), from_offset(opposite[1], second_axis, 2, 4)]
    near, far = after(near, far)
    first = [along_first[0], near[0], far[0], near[2]]
    second = [along_second[0], near[1], far[1], near[3]]
    return first, second, beside


def scatter_rows(v):
    two = lax.psum_scatter(v, ("x", "z"), scatter_dimension=0, tiled=True)
    rows = two.shape[0] // 2
    iyh = lax.axis_index("yh")
    keep = lax.dynamic_slice_in_dim(two, iyh * rows, rows, 0)
    send = lax.dynamic_slice_in_dim(two, (1 - iyh) * rows, rows, 0)
    return keep.astype(F32) + other(send, "yh").astype(F32)


def body(tokens, norm_gains, w_query, w_keyval, w_out, w_gateup, w_down, cotangent):
    D = tokens.shape[1]
    length = 4 * tokens.shape[0]
    hidden_w = w_down.shape[0]
    heads_w = w_query.shape[1]
    gains_w = norm_gains.shape[1]
    block = lax.axis_index("yl") * 2 + lax.axis_index("core")
    place = jnp.stack(
        [block, lax.axis_index("x"), lax.axis_index("z"), lax.axis_index("yh")]
    ).astype(jnp.int32)

    out_t = w_out.T
    attn_own = side_by_side(
        [
            (OUT_AT, out_t[:, :OUT_CUT]),
            (QUERY_AT, w_query),
            (KEYVAL_AT, w_keyval),
            (REST_AT, out_t[:, OUT_CUT:]),
        ],
        ATTN_WIDTH,
    )
    attn_pair = pair_rows(attn_own, "yh")
    mlp_own = (w_gateup[:, 0], w_gateup[:, 1], w_down.T)
    mlp_own = [(i * hidden_w, part) for i, part in enumerate(mlp_own)]
    mlp_pair = pair_rows(side_by_side(mlp_own, 3 * hidden_w), "yh")

    pair_w = 8 * gains_w
    gain_at = (lax.axis_index("yh") * 4 + block) * gains_w
    gain_part = lax.dynamic_update_slice(jnp.zeros((2, pair_w), F32), norm_gains, (0, gain_at))
    for axis in ("core", "yl", "yh"):
        gain_part = gain_part + other(gain_part, axis)
    gain_part = gain_part.T
    gain_high = lax.reduce_precision(gain_part, 8, 7)
    gain_low = (gain_part - gain_high).astype(BF16)
    gain_high = gain_high.astype(BF16)
    first, second = attn_pair[:, :HALF_WIDTH], attn_pair[:, HALF_WIDTH:]
    first += side_by_side([(0, gain_high), (2, gain_low)], HALF_WIDTH)

    first, mlp_pair = after(first, mlp_pair)
    along_z, along_x, _ = from_both([first] * 4, "z", [second] * 4, "x", False)
    along_z, along_x, mlp_pair, tokens = lax.optimization_barrier(
        (jnp.stack(along_z), jnp.stack(along_x), mlp_pair, tokens)
    )
    mlp_w = lax.all_gather(mlp_pair, ("x", "z"), axis=0, tiled=True)
    along_x, along_z, far = from_both(
        [along_z] * 4, "x", [along_x] * 4, "z", True, other(tokens, "yl")
    )
    token_pieces = [tokens, other(tokens, "core"), far, other(far, "core")]
    cotangent, far = after(cotangent, far)
    grad_far = other(cotangent, "yl")

    positions = jnp.arange(length).astype(F32)
    freqs = rope_base ** (-(jnp.arange(HD // 2).astype(F32) * 2.0 / HD))
    angles = freqs[:, None] * positions[None, :]
    cosine, sine = jnp.cos(angles), jnp.sin(angles)

    gain_rows, attn_w, h_first, q, kt, v, attn, attnt, probs, *parts = attend(
        place, token_pieces, along_x, along_z, cosine, sine
    )
    grad_far, parts = after(grad_far, parts)
    grad_pieces = [cotangent, other(cotangent, "core"), grad_far, other(grad_far, "core")]
    middle_far = far_sum(parts[2], parts[3])
    middle = (
        tokens.astype(F32) + near_sum(parts[0], parts[1]) + other(middle_far, "yl").astype(F32)
    )
    normed2, factor2 = norm_rows(middle)
    h_own = (normed2 * gain_rows[1]).astype(BF16)

    h_pieces = [h_own, other(h_own, "core")]
    h_far = other(h_own, "yl")
    hidden_a, dgu_a, back_own, back_core, out_own, out_core = feed(
        place, mlp_w, h_pieces, grad_pieces[:2]
    )
    h_far, hidden_a = after(h_far, hidden_a)
    h_pieces += [h_far, other(h_far, "core")]
    hidden_b, dgu_b, back_chip, back_diag, out_chip, out_diag = feed(
        place, mlp_w, h_pieces[2:], grad_pieces[2:]
    )
    back_near = near_sum(back_own, back_core)
    out_near = near_sum(out_own, out_core)

    back_far = far_sum(back_chip, back_diag)
    hidden_b, back_far = after(hidden_b, back_far)
    mlp_grads = feed_grads(place, h_pieces, grad_pieces, dgu_a, dgu_b, hidden_a, hidden_b)
    mlp_grads, back_far = after(mlp_grads, other(back_far, "yl"))
    d_h2_own = back_near + back_far.astype(F32)
    early = scatter_rows(mlp_grads)
    out_far = far_sum(out_chip, out_diag)

    d_norm2 = norm_back(d_h2_own, normed2, factor2, gain_rows[1])
    d_middle = cotangent.astype(F32) + d_norm2
    d_out = d_middle.astype(BF16)
    d_out_far = other(d_out, "yl")
    d_out_far, out_near = after(d_out_far, out_near)
    out_pieces = [d_out, other(d_out, "core"), d_out_far, other(d_out_far, "core")]
    out_far, out_pieces = after(out_far, out_pieces)
    out_far = other(out_far, "yl")

    back = attend_back(
        place, cosine, sine, out_pieces, attn_w, h_first, q, kt, v, attn, attnt, probs
    )
    d_qkv, *late_parts = back
    d_qkv, out_far = after(d_qkv, out_far)
    along_x, along_z, parts = from_both(
        late_parts[:4], "x", late_parts[4:], "z", True, project_back(place, d_qkv, attn_w)
    )
    d_far = other(far_sum(parts[2], parts[3]), "yl")
    result = (middle + out_near + out_far.astype(F32)).astype(BF16)
    along_x, result = after(along_x, result)
    middle_parts = late_middle(place, along_x, along_z)
    along_z, along_x, _ = from_both(middle_parts[:4], "z", middle_parts[4:], "x", False)
    d_h1_own = near_sum(parts[0], parts[1]) + d_far.astype(F32)
    along_z, (d_h1_own, early) = after(along_z, (d_h1_own, early))
    late_keep, late_send = late_last(place, along_z, along_x)
    late = late_keep + other(late_send, "yh").astype(F32)

    normed1, factor1 = norm_rows(tokens.astype(F32))
    d_norm1 = norm_back(d_h1_own, normed1, factor1, gain_rows[0])
    input_grad = (d_middle + d_norm1).astype(BF16)

    grad_query = late[:, :heads_w]
    grad_keyval = late[:, 2 * LATE_WIDTH - heads_w :]
    grad_out = late[:, heads_w : 2 * LATE_WIDTH - heads_w].T
    grad_gateup = early[:, : 2 * hidden_w].reshape(-1, 2, hidden_w)

    gain_sum = jnp.stack(
        [
            jnp.sum(grad_query * w_query.astype(F32) + grad_keyval * w_keyval.astype(F32), 1),
            jnp.sum(grad_gateup * w_gateup.astype(F32), (1, 2)),
        ]
    )
    for axis in ("core", "yl"):
        gain_sum = gain_sum + other(gain_sum, axis)
    grad_gains = lax.dynamic_slice(gain_sum, (0, block * gains_w), (2, gains_w)) / norm_gains
    return (
        result,
        input_grad,
        grad_query,
        grad_keyval,
        grad_out,
        grad_gateup,
        early[:, 2 * hidden_w :].T,
        grad_gains,
    )


def solution(mesh):
    fine = Mesh(mesh.devices.reshape(4, 4, 2, 2, 2), ("x", "z", "yh", "yl", "core"))
    dp = ("x", "z", "yh")
    tensor = ("yl", "core")
    every = dp + tensor
    weights = (P(dp, tensor), P(dp, tensor), P(tensor, dp), P(dp, None, tensor), P(tensor, dp))
    rows = P(every, None)
    gains = P(None, every)
    return jax.shard_map(
        body,
        mesh=fine,
        in_specs=(rows, gains) + weights + (rows,),
        out_specs=(rows, rows) + weights + (gains,),
        check_vma=False,
    )
```

```python
import jax
import jax.numpy as jnp
from jax import lax
from jax.experimental import pallas as pl
from jax.experimental.pallas import tpu as pltpu
from jax.sharding import Mesh, PartitionSpec as P

HD = 96
F32 = jnp.float32
BF16 = jnp.bfloat16
norm_eps = 1e-05
rope_base = 100000.0
LOG2E = 1.4426950408889634
SCALE = HD ** (-0.5)
MIB = 1024 * 1024
SMALL = pl.CostEstimate(flops=1, bytes_accessed=1, transcendentals=0)

GAIN_AT, OUT_AT, QUERY_AT, KEYVAL_AT, REST_AT, ATTN_WIDTH = 0, 128, 256, 640, 1024, 1280
HALF_WIDTH = ATTN_WIDTH // 2
OUT_CUT = QUERY_AT - OUT_AT
LIMIT = 39


def dot_n(left, right):
    return jnp.dot(left, right, preferred_element_type=F32)


def dot_t(left, right):
    return lax.dot_general(left, right, (((1,), (1,)), ((), ())), preferred_element_type=F32)


def dot_tn(left, right):
    return lax.dot_general(left, right, (((0,), (0,)), ((), ())), preferred_element_type=F32)


def dot_tt(left, right):
    return lax.dot_general(left, right, (((0,), (1,)), ((), ())), preferred_element_type=F32)


def block_at(index, size):
    return pl.ds(pl.multiple_of(index * size, size), size)


def causal_mask(scores, size):
    key_at = lax.broadcasted_iota(jnp.int32, (size, scores.shape[1]), 0)
    query_at = lax.broadcasted_iota(jnp.int32, (size, scores.shape[1]), 1) % size
    tail = jnp.where(key_at <= query_at, scores[-size:], -1e30)
    if scores.shape[0] == size:
        return tail
    return jnp.concatenate([scores[:-size], tail], 0)


class Moves:
    def __init__(self, sems):
        self.sems = sems
        self.started = []

    def start(self, source, target):
        copy = pltpu.make_async_copy(source, target, self.sems.at[len(self.started)])
        copy.start()
        self.started.append(copy)
        return copy

    def wait(self):
        for copy in self.started:
            copy.wait()


def vmem(shape, dtype=BF16):
    return pltpu.VMEM(shape, dtype)


def like(shape, dtype=BF16):
    return jax.ShapeDtypeStruct(shape, dtype)


def whole():
    return pl.BlockSpec(memory_space=pltpu.VMEM)


def apart():
    return pl.BlockSpec(memory_space=pl.ANY)


def scalars():
    return pl.BlockSpec(memory_space=pltpu.SMEM)


def kernel_call(kernel, name, place, small, large, outs, small_outs, scratch, *copies):
    return pl.pallas_call(
        kernel,
        out_shape=list(small_outs) + list(outs),
        in_specs=[scalars()] + [whole()] * len(small) + [apart()] * len(large),
        out_specs=[whole()] * len(small_outs) + [apart()] * len(outs),
        scratch_shapes=list(scratch)
        + [pltpu.SemaphoreType.DMA((count,)) for count in copies],
        compiler_params=pltpu.CompilerParams(vmem_limit_bytes=LIMIT * MIB),
        cost_estimate=SMALL,
        name=name,
    )(place, *small, *large)


def probs_at(step, size):
    return step * (step + 1) // 2 * size, (step + 1) * size


def head_rows(head):
    return slice(head * HD, (head + 1) * HD)


def attend_kernel(place, cos_ref, sin_ref, t0, t1, t2, t3, a0, a1, a2, a3, b0, b1, b2, b3,
                  gains_ref, w_hbm, h_hbm, qt_hbm, kt_hbm, vt_hbm, attn_hbm, probs_hbm,
                  o0, o1, o2, o3,
                  t_ref, w_ref, h_ref, qt_ref, kt_ref, vt_ref, attn_ref, probs_ref, part_ref, k_ref,
                  in_sem, out_sem, probs_sem):
    block, ix, iz = place[0], place[1], place[2]
    half = HD // 2
    size = t_ref.shape[1]
    heads = qt_ref.shape[0]
    group_size = heads // kt_ref.shape[0]
    rows = a0.shape[1]
    fetch, store = Moves(in_sem), Moves(out_sem)
    came = []
    for far, (along_x, along_z) in enumerate(zip((a0, a1, a2, a3), (b0, b1, b2, b3))):
        for near in range(4):
            at_a = lax.rem(ix + far, 4) * 4 + lax.rem(iz + near, 4)
            at_b = lax.rem(ix + near, 4) * 4 + lax.rem(iz + far, 4)
            came.append(fetch.start(
                along_x.at[near], w_ref.at[block_at(at_a, rows), pl.ds(0, HALF_WIDTH)]))
            came.append(fetch.start(
                along_z.at[near], w_ref.at[block_at(at_b, rows), pl.ds(HALF_WIDTH, HALF_WIDTH)]))
    tokens_came = [
        fetch.start(piece, t_ref.at[i]) for i, piece in enumerate((t0, t1, t2, t3))
    ]
    for copy in came:
        copy.wait()
    store.start(w_ref, w_hbm)
    gains = w_ref[:, GAIN_AT:OUT_AT].astype(F32).T
    gain_row = gains[0:1] + gains[2:3]
    gains_ref[...] = gains[0:2] + gains[2:4]
    for step in range(4):
        at = block_at(lax.bitwise_xor(block, step), size)
        tokens_came[step].wait()
        value = t_ref[step].astype(F32)
        factor = lax.rsqrt(jnp.mean(value * value, -1, keepdims=True) + norm_eps)
        normed = (value * factor * gain_row).astype(BF16)
        h_ref[at, :] = normed
        cosine = cos_ref[:, at]
        sine = sin_ref[:, at]
        every = dot_n(normed, w_ref[:, QUERY_AT:REST_AT]).T
        query, keyval = every[: KEYVAL_AT - QUERY_AT], every[KEYVAL_AT - QUERY_AT :]

        def rotated(field):
            first, second = field[:half], field[half:]
            return jnp.concatenate(
                [first * cosine - second * sine, second * cosine + first * sine], 0
            )

        for head in range(heads):
            qt_ref[head, :, at] = rotated(query[head_rows(head)]).astype(BF16)
        for group in range(heads // group_size):
            key = rotated(keyval[head_rows(2 * group)])
            kt_ref[group, :, at] = key.astype(BF16)
            k_ref[group, at, :] = key.T.astype(BF16)
            vt_ref[group, :, at] = keyval[head_rows(2 * group + 1)].astype(BF16)
    for source, target in ((h_ref, h_hbm), (qt_ref, qt_hbm), (kt_ref, kt_hbm), (vt_ref, vt_hbm)):
        store.start(source, target)

    def probs_copy(group):
        return pltpu.make_async_copy(
            probs_ref.at[group], probs_hbm.at[group], probs_sem.at[group])

    for group in range(heads // group_size):
        members = range(group * group_size, (group + 1) * group_size)
        for step in range(4):
            first, reach = probs_at(step, size)
            columns = slice(step * size, reach)
            query = jnp.concatenate([qt_ref[head, :, columns] for head in members], 1)
            scores = causal_mask(dot_n(k_ref[group, :reach, :], query), size)
            top = jnp.max(scores, 0, keepdims=True)
            expo = jnp.exp2((scores - top) * (SCALE * LOG2E))
            total = jnp.sum(expo, 0, keepdims=True)
            probs = (expo * (1.0 / total)).astype(BF16)
            probs_ref[group, first : first + reach, :] = probs
            mixed = dot_n(vt_ref[group, :, :reach], probs).astype(BF16)
            for i, head in enumerate(members):
                attn_ref[head_rows(head), columns] = mixed[:, i * size : (i + 1) * size]
        probs_copy(group).start()
    store.start(attn_ref, attn_hbm)
    for step, out in ((1, o1), (3, o3), (2, o2), (0, o0)):
        at = block_at(lax.bitwise_xor(block, step), size)
        part = dot_tt(attn_ref[:OUT_CUT, at], w_ref[:, OUT_AT:QUERY_AT])
        part += dot_tt(attn_ref[OUT_CUT:, at], w_ref[:, REST_AT:])
        part_ref[step] = part.astype(BF16)
        store.start(part_ref.at[step], out)
    store.wait()
    for group in range(heads // group_size):
        probs_copy(group).wait()


def attend(place, pieces, along_x, along_z, cosine, sine):
    size, width = pieces[0].shape
    length = 4 * size
    heads = (KEYVAL_AT - QUERY_AT) // HD
    groups = (REST_AT - KEYVAL_AT) // (2 * HD)
    columns, g_columns = (heads, HD, length), (groups, HD, length)
    probs = (groups, sum(probs_at(3, size)), heads // groups * size)
    kept = [(width, ATTN_WIDTH), (length, width), columns, g_columns, g_columns,
            (heads * HD, length), probs]
    return kernel_call(
        attend_kernel, "attend", place, (cosine, sine), (*pieces, *along_x, *along_z),
        [like(s) for s in kept + [(size, width)] * 4], [like((2, width), F32)],
        [vmem(s) for s in [(4, size, width)] + kept + [(4, size, width), (groups, length, HD)]],
        36, 10, groups)


def attend_back_kernel(place, cos_ref, sin_ref,
                       o0, o1, o2, o3, w_hbm, h_hbm, qt_hbm, kt_hbm, vt_hbm, attn_hbm, probs_hbm,
                       dqkv_hbm, x0, x1, x2, x3, y0, y1, y2, y3,
                       o_ref, w_ref, h_ref, qt_ref, kt_ref, vt_ref, attn_ref, probs_ref,
                       do_ref, dqkv_ref, first_ref, second_ref, v_ref, delta_ref, dk_ref, dv_ref,
                       in_sem, out_sem, probs_sem):
    block, ix, iz = place[0], place[1], place[2]
    heads, _, length = qt_ref.shape
    groups = kt_ref.shape[0]
    group_size = heads // groups
    size = length // 4
    half = HD // 2
    width = w_ref.shape[0]
    heads_w = heads * HD
    fetch, store = Moves(in_sem), Moves(out_sem)
    rest_w = ATTN_WIDTH - REST_AT
    early = [
        fetch.start(w_hbm.at[:, pl.ds(OUT_AT, OUT_CUT)], w_ref.at[:, pl.ds(0, OUT_CUT)]),
        fetch.start(w_hbm.at[:, pl.ds(REST_AT, rest_w)], w_ref.at[:, pl.ds(OUT_CUT, rest_w)]),
    ]
    early += [
        fetch.start(piece, o_ref.at[block_at(lax.bitwise_xor(block, i), size), :])
        for i, piece in enumerate((o0, o1, o2, o3))
    ]
    middle = [
        fetch.start(source, target)
        for source, target in ((attn_hbm, attn_ref), (vt_hbm, vt_ref), (qt_hbm, qt_ref),
                               (kt_hbm, kt_ref))
    ]

    def probs_copy(group):
        return pltpu.make_async_copy(
            probs_hbm.at[group], probs_ref.at[group], probs_sem.at[group])

    for group in range(groups):
        probs_copy(group).start()
    h_came = fetch.start(h_hbm, h_ref)
    for copy in early:
        copy.wait()
    do_ref[...] = dot_tt(w_ref[...], o_ref[...]).astype(BF16)
    for copy in middle:
        copy.wait()
    for group in range(groups):
        v_ref[group] = vt_ref[group].astype(F32).T.astype(BF16)
    for head in range(heads):
        rows = head_rows(head)
        delta_ref[head] = jnp.sum(
            attn_ref[rows, :].astype(F32) * do_ref[rows, :].astype(F32), 0, keepdims=True)

    def turned_back(field, cosine, sine):
        first, second = field[:half], field[half:]
        return jnp.concatenate(
            [first * cosine + second * sine, second * cosine - first * sine], 0).astype(BF16)

    for group in range(groups):
        members = range(group * group_size, (group + 1) * group_size)
        probs_copy(group).wait()
        for step in range(4):
            first, reach = probs_at(step, size)
            columns = slice(step * size, reach)
            probs = probs_ref[group, first : first + reach, :]
            query = jnp.concatenate([qt_ref[head, :, columns] for head in members], 1)
            d_out = jnp.concatenate([do_ref[head_rows(head), columns] for head in members], 1)
            delta = jnp.concatenate([delta_ref[head, :, columns] for head in members], 1)
            d_probs = dot_n(v_ref[group, :reach, :], d_out)
            d_scores = (probs.astype(F32) * (d_probs - delta)).astype(BF16)
            for ref, left, right in ((dv_ref, d_out, probs), (dk_ref, query, d_scores)):
                change = dot_t(left, right)
                if step > 0:
                    ref[group, :, : step * size] += change[:, : step * size]
                ref[group, :, columns] = change[:, columns]
            d_query = dot_n(kt_ref[group, :, :reach], d_scores) * SCALE
            for i, head in enumerate(members):
                dqkv_ref[head_rows(head), columns] = turned_back(
                    d_query[:, i * size : (i + 1) * size],
                    cos_ref[:, columns], sin_ref[:, columns])
        dqkv_ref[head_rows(heads + 2 * group), :] = turned_back(
            dk_ref[group] * SCALE, cos_ref[...], sin_ref[...])
        dqkv_ref[head_rows(heads + 2 * group + 1), :] = dv_ref[group].astype(BF16)
    store.start(dqkv_ref, dqkv_hbm)
    h_came.wait()

    rows = width // 16
    part = dot_tt(h_ref[...], dqkv_ref[...]).astype(BF16)
    first_ref[:, :heads_w] = part[:, :heads_w]
    second_ref[:, LATE_WIDTH - heads_w :] = part[:, heads_w:]
    part = dot_tt(o_ref[...], attn_ref[...]).astype(BF16)
    first_ref[:, heads_w:] = part[:, :LATE_OUT]
    second_ref[:, : heads_w - LATE_OUT] = part[:, LATE_OUT:]
    for offset, (x_out, y_out) in enumerate(((x0, y0), (x1, y1), (x2, y2), (x3, y3))):
        to_x = lax.rem(ix + 4 - offset, 4)
        to_z = lax.rem(iz + 4 - offset, 4)
        store.start(first_ref.at[block_at(to_x, 4 * rows), :], x_out)
        for i in range(4):
            store.start(second_ref.at[block_at(i * 4 + to_z, rows), :], y_out.at[i])
    store.wait()


def attend_back(place, cosine, sine, pieces, weights, h_first, qt, kt, vt, attn, probs):
    width = weights.shape[0]
    heads, _, length = qt.shape
    groups = kt.shape[0]
    every_w = (heads + 2 * groups) * HD
    rows = width // 16
    outs = [(every_w, length)] + [(4 * rows, LATE_WIDTH)] * 4 + [(4, rows, LATE_WIDTH)] * 4
    scratch = [
        (length, width), (width, heads * HD), (length, width),
        qt.shape, kt.shape, vt.shape, attn.shape, probs.shape,
        attn.shape, (every_w, length), (width, LATE_WIDTH), (width, LATE_WIDTH),
        (groups, length, HD),
    ]
    wide = [(heads, 1, length), kt.shape, kt.shape]
    return kernel_call(
        attend_back_kernel, "attend_back", place, (cosine, sine),
        (*pieces, weights, h_first, qt, kt, vt, attn, probs),
        [like(s) for s in outs], [],
        [vmem(s) for s in scratch] + [vmem(s, F32) for s in wide], 11, 21, groups)


def project_back_kernel(place, dqkv_hbm, w_hbm, c0, c1, c2, c3,
                        dqkv_ref, w_ref, part_ref, in_sem, out_sem):
    block = place[0]
    size = part_ref.shape[1]
    fetch, store = Moves(in_sem), Moves(out_sem)
    fetch.start(w_hbm.at[:, pl.ds(QUERY_AT, REST_AT - QUERY_AT)], w_ref)
    fetch.start(dqkv_hbm, dqkv_ref)
    fetch.wait()
    for step, out in ((3, c3), (2, c2), (1, c1), (0, c0)):
        at = block_at(lax.bitwise_xor(block, step), size)
        part_ref[step] = dot_tt(dqkv_ref[:, at], w_ref[...]).astype(BF16)
        store.start(part_ref.at[step], out)
    store.wait()


def project_back(place, d_qkv, weights):
    every_w, length = d_qkv.shape
    width = weights.shape[0]
    size = length // 4
    return kernel_call(
        project_back_kernel, "project_back", place, (), (d_qkv, weights),
        [like((size, width))] * 4, [],
        [vmem(s) for s in (d_qkv.shape, (width, every_w), (4, size, width))], 2, 4)


def feed_kernel(place, h0, h1, g0, g1, w_hbm, hidden_hbm, dgu_hbm, b0, b1, r0, r1,
                w_ref, h_ref, g_ref, hidden_ref, dgu_ref, back_ref, out_ref, in_sem, out_sem):
    del place
    hidden_w = hidden_ref.shape[1]
    size = h_ref.shape[1]
    parts = [slice(i * hidden_w, (i + 1) * hidden_w) for i in range(3)]
    fetch, store = Moves(in_sem), Moves(out_sem)

    def weight(i):
        at = pl.ds(i * hidden_w, hidden_w)
        return fetch.start(w_hbm.at[:, at], w_ref.at[:, at])

    came = [fetch.start(h0, h_ref.at[0]), weight(0), weight(1), fetch.start(g0, g_ref.at[0]),
            weight(2), fetch.start(h1, h_ref.at[1]), fetch.start(g1, g_ref.at[1])]
    for i, (back, out) in enumerate(((b0, r0), (b1, r1))):
        rows = slice(i * size, (i + 1) * size)
        at = pl.ds(i * size, size)
        for copy in came[0:2] if i == 0 else came[5:7]:
            copy.wait()
        gate = dot_n(h_ref[i], w_ref[:, parts[0]])
        if i == 0:
            came[2].wait()
        up = dot_n(h_ref[i], w_ref[:, parts[1]])
        sig = 1.0 / (1.0 + jnp.exp2(gate * (-LOG2E)))
        silu = gate * sig
        hidden = (silu * up).astype(BF16)
        hidden_ref[rows, :] = hidden
        store.start(hidden_ref.at[at, :], hidden_hbm.at[at, :])
        if i == 0:
            came[3].wait()
            came[4].wait()
        d_hidden = dot_n(g_ref[i], w_ref[:, parts[2]])
        dgu_ref[rows, :hidden_w] = (
            d_hidden * up * (sig * (1.0 + gate * (1.0 - sig)))).astype(BF16)
        dgu_ref[rows, hidden_w:] = (d_hidden * silu).astype(BF16)
        store.start(dgu_ref.at[at, :], dgu_hbm.at[at, :])
        back_ref[i] = dot_t(dgu_ref[rows, :], w_ref[:, : 2 * hidden_w]).astype(BF16)
        store.start(back_ref.at[i], back)
        out_ref[i] = dot_t(hidden_ref[rows, :], w_ref[:, parts[2]]).astype(BF16)
        store.start(out_ref.at[i], out)
    store.wait()


def feed(place, weights, normed_pieces, grad_pieces):
    size, width = normed_pieces[0].shape
    hidden_w = weights.shape[1] // 3
    wide = [(2 * size, hidden_w), (2 * size, 2 * hidden_w)]
    return kernel_call(
        feed_kernel, "feed", place, (), (*normed_pieces, *grad_pieces, weights),
        [like(s) for s in wide + [(size, width)] * 4], [],
        [vmem(s) for s in [weights.shape] + [(2, size, width)] * 2 + wide + [(2, size, width)] * 2],
        7, 8)


def feed_grads_kernel(place, h0, h1, h2, h3, g0, g1, g2, g3, dgu_a, dgu_b, hidden_a, hidden_b,
                      out_hbm, h_ref, g_ref, dgu_ref, hidden_ref, out_ref, in_sem, out_sem):
    del place
    size = h0.shape[0]
    half, hidden_w = hidden_a.shape
    column = 512
    fetch, store = Moves(in_sem), Moves(out_sem)

    def rows_of(pieces, ref):
        return [
            fetch.start(piece, ref.at[pl.ds(i * size, size), :]) for i, piece in enumerate(pieces)
        ]

    def tiles_of(pieces, ref):
        tiles = []
        for tile in range(ref.shape[1] // column):
            at = pl.ds(tile * column, column)
            tiles.append([
                fetch.start(piece.at[:, at], ref.at[pl.ds(i * half, half), at])
                for i, piece in enumerate(pieces)
            ])
        return tiles

    h_came = rows_of((h0, h1, h2, h3), h_ref)
    dgu_came = tiles_of((dgu_a, dgu_b), dgu_ref)
    g_came = rows_of((g0, g1, g2, g3), g_ref)
    hidden_came = tiles_of((hidden_a, hidden_b), hidden_ref)
    at = 0
    for came, left, tiles, right in (
        (h_came, h_ref, dgu_came, dgu_ref), (g_came, g_ref, hidden_came, hidden_ref)
    ):
        for copy in came:
            copy.wait()
        for tile, copies in enumerate(tiles):
            for copy in copies:
                copy.wait()
            columns = pl.ds(at, column)
            out_ref[:, columns] = dot_tn(
                left[...], right[:, tile * column : (tile + 1) * column]).astype(BF16)
            store.start(out_ref.at[:, columns], out_hbm.at[:, columns])
            at += column
    store.wait()


def feed_grads(place, normed_pieces, grad_pieces, dgu_a, dgu_b, hidden_a, hidden_b):
    size, width = normed_pieces[0].shape
    half, hidden_w = hidden_a.shape
    scratch = [(4 * size, width)] * 2 + [(2 * half, 2 * hidden_w), (2 * half, hidden_w),
                                         (width, 3 * hidden_w)]
    return kernel_call(
        feed_grads_kernel, "feed_grads", place, (),
        (*normed_pieces, *grad_pieces, dgu_a, dgu_b, hidden_a, hidden_b),
        [like((width, 3 * hidden_w))], [], [vmem(s) for s in scratch], 20, 6)[0]


LATE_OUT, LATE_WIDTH = 192, 576


def late_middle_kernel(place, *refs):
    x_in, y_in, outs = refs[0:4], refs[4:8], refs[8:]
    ix, iz = place[1], place[2]
    rows = outs[0].shape[0]
    for offset in range(4):
        at = block_at(lax.rem(iz + 4 - offset, 4), rows)
        total = x_in[0][at, :].astype(F32)
        for ref in x_in[1:]:
            total += ref[at, :].astype(F32)
        outs[offset][...] = total.astype(BF16)
        to = lax.rem(ix + 4 - offset, 4)
        total = y_in[0][to].astype(F32)
        for ref in y_in[1:]:
            total += ref[to].astype(F32)
        outs[4 + offset][...] = total.astype(BF16)


def late_middle(place, along_x, along_z):
    _, rows, width = along_z[0].shape
    return pl.pallas_call(
        late_middle_kernel,
        out_shape=[like((rows, width))] * 8,
        in_specs=[scalars()] + [whole()] * 8,
        out_specs=[whole()] * 8,
        cost_estimate=SMALL,
        name="late_middle",
    )(place, *along_x, *along_z)


def late_last_kernel(place, *refs):
    x_in, y_in, keep_ref, send_ref = refs[0:4], refs[4:8], refs[8], refs[9]
    mine = place[3]
    rows = keep_ref.shape[0]
    for inputs, columns in ((x_in, slice(0, LATE_WIDTH)), (y_in, slice(LATE_WIDTH, 2 * LATE_WIDTH))):
        for ref, half in ((keep_ref, mine), (send_ref, 1 - mine)):
            at = block_at(half, rows)
            total = inputs[0][at, :].astype(F32)
            for other_ref in inputs[1:]:
                total += other_ref[at, :].astype(F32)
            ref[:, columns] = total.astype(ref.dtype)


def late_last(place, along_z, along_x):
    rows, width = along_x[0].shape
    return pl.pallas_call(
        late_last_kernel,
        out_shape=[
            jax.ShapeDtypeStruct((rows // 2, 2 * width), F32),
            jax.ShapeDtypeStruct((rows // 2, 2 * width), BF16),
        ],
        in_specs=[scalars()] + [whole()] * 8,
        out_specs=[whole()] * 2,
        cost_estimate=SMALL,
        name="late_last",
    )(place, *along_z, *along_x)


def norm_rows(values_in):
    factor = lax.rsqrt(jnp.mean(values_in * values_in, -1, keepdims=True) + norm_eps)
    return (values_in * factor, factor)


def norm_back(grad_in, normed, factor, gain_row):
    grad_normed = grad_in * gain_row
    inner = jnp.mean(grad_normed * normed, -1, keepdims=True)
    return factor * (grad_normed - normed * inner)


def from_offset(v, axis, offset, size):
    return lax.ppermute(v, axis, [((i + offset) % size, i) for i in range(size)])


def other(v, axis):
    return from_offset(v, axis, 1, 2)


def pair_rows(v, axis):
    it = other(v, axis)
    mine = jnp.arange(2)[:, None, None] == lax.axis_index(axis)
    return jnp.where(mine, v[None], it[None]).reshape(2 * v.shape[0], v.shape[1])


def side_by_side(parts, width):
    return sum(
        jnp.pad(part, ((0, 0), (at, width - at - part.shape[1]))) for at, part in parts
    )


def near_sum(own, core):
    return own.astype(F32) + other(core, "core").astype(F32)


def far_sum(chip, diagonal):
    return near_sum(chip, diagonal).astype(BF16)


def after(value, first):
    return lax.optimization_barrier((value, first))


def from_ring(v, axis, offsets):
    return [from_offset(v, axis, i, 4) for i in offsets]


def stack_ring(v, received, offsets):
    parts = dict(zip(offsets, received))
    return jnp.stack([v] + [parts[i] for i in (1, 2, 3)])


def from_both(along_first, first_axis, along_second, second_axis, large, beside=()):
    near = [
        from_offset(part[i], axis, i, 4)
        for i in (1, 3)
        for part, axis in ((along_first, first_axis), (along_second, second_axis))
    ]
    opposite = along_first[2], along_second[2]
    if large:
        opposite, (near, beside) = after(opposite, (near, beside))
    far = [from_offset(opposite[0], first_axis, 2, 4), from_offset(opposite[1], second_axis, 2, 4)]
    near, far = after(near, far)
    first = [along_first[0], near[0], far[0], near[2]]
    second = [along_second[0], near[1], far[1], near[3]]
    return first, second, beside


def pair_sum(v, axis):
    rows = v.shape[0] // 2
    me = lax.axis_index(axis)
    keep = lax.dynamic_slice_in_dim(v, me * rows, rows, 0)
    send = lax.dynamic_slice_in_dim(v, (1 - me) * rows, rows, 0)
    return keep.astype(F32) + other(send, axis).astype(F32)


def body(tokens, norm_gains, w_query, w_keyval, w_out, w_gateup, w_down, cotangent):
    D = tokens.shape[1]
    length = 4 * tokens.shape[0]
    hidden_w = w_down.shape[0]
    heads_w = w_query.shape[1]
    gains_w = norm_gains.shape[1]
    block = lax.axis_index("yl") * 2 + lax.axis_index("core")
    place = jnp.stack(
        [block, lax.axis_index("x"), lax.axis_index("z"), lax.axis_index("yh")]
    ).astype(jnp.int32)

    out_t = w_out.T
    attn_own = side_by_side(
        [
            (OUT_AT, out_t[:, :OUT_CUT]),
            (QUERY_AT, w_query),
            (KEYVAL_AT, w_keyval),
            (REST_AT, out_t[:, OUT_CUT:]),
        ],
        ATTN_WIDTH,
    )
    attn_pair = pair_rows(attn_own, "yh")
    mlp_own = (w_gateup[:, 0], w_gateup[:, 1], w_down.T)
    mlp_own = [(i * hidden_w, part) for i, part in enumerate(mlp_own)]
    mlp_pair = pair_rows(side_by_side(mlp_own, 3 * hidden_w), "yh")

    pair_w = 8 * gains_w
    gain_at = (lax.axis_index("yh") * 4 + block) * gains_w
    gain_part = lax.dynamic_update_slice(jnp.zeros((2, pair_w), F32), norm_gains, (0, gain_at))
    for axis in ("core", "yl", "yh"):
        gain_part = gain_part + other(gain_part, axis)
    gain_part = gain_part.T
    gain_high = lax.reduce_precision(gain_part, 8, 7)
    gain_low = (gain_part - gain_high).astype(BF16)
    gain_high = gain_high.astype(BF16)
    first, second = attn_pair[:, :HALF_WIDTH], attn_pair[:, HALF_WIDTH:]
    first += side_by_side([(0, gain_high), (2, gain_low)], HALF_WIDTH)

    second_x = from_ring(second, "x", (1, 3, 2))
    second_x, first, mlp_pair, tokens = lax.optimization_barrier(
        (second_x, first, mlp_pair, tokens))
    second_own = stack_ring(second, second_x, (1, 3, 2))
    first_z = from_ring(first, "z", (1, 3, 2))
    second_near = from_ring(second_own, "z", (1, 3))
    far = other(tokens, "yl")
    first_z, second_near, mlp_pair, tokens = lax.optimization_barrier(
        (first_z, second_near, mlp_pair, tokens))
    mlp_w = lax.all_gather(mlp_pair, ("x", "z"), axis=0, tiled=True)
    first_own = stack_ring(first, first_z, (1, 3, 2))
    first_near = from_ring(first_own, "x", (1, 3))
    second_far = from_ring(second_own, "z", (2,))
    near = other(tokens, "core")
    first_near, second_far, far, near = lax.optimization_barrier(
        (first_near, second_far, far, near))
    first_own, first_near = after(first_own, first_near)
    first_far = from_ring(first_own, "x", (2,))
    along_x = [first_own, first_near[0], first_far[0], first_near[1]]
    along_z = [second_own, second_near[0], second_far[0], second_near[1]]
    token_pieces = [tokens, near, far, other(far, "core")]
    cotangent, far = after(cotangent, far)
    grad_far = other(cotangent, "yl")

    positions = jnp.arange(length).astype(F32)
    freqs = rope_base ** (-(jnp.arange(HD // 2).astype(F32) * 2.0 / HD))
    angles = freqs[:, None] * positions[None, :]
    cosine, sine = jnp.cos(angles), jnp.sin(angles)

    gain_rows, attn_w, h_first, qt, kt, vt, attn, probs, *parts = attend(
        place, token_pieces, along_x, along_z, cosine, sine
    )
    grad_far, parts = after(grad_far, parts)
    grad_pieces = [cotangent, other(cotangent, "core"), grad_far, other(grad_far, "core")]
    middle_far = far_sum(parts[2], parts[3])
    middle = (
        tokens.astype(F32) + near_sum(parts[0], parts[1]) + other(middle_far, "yl").astype(F32)
    )
    normed2, factor2 = norm_rows(middle)
    h_own = (normed2 * gain_rows[1]).astype(BF16)

    h_pieces = [h_own, other(h_own, "core")]
    h_far = other(h_own, "yl")
    hidden_a, dgu_a, back_own, back_core, out_own, out_core = feed(
        place, mlp_w, h_pieces, grad_pieces[:2]
    )
    h_far, hidden_a = after(h_far, hidden_a)
    h_pieces += [h_far, other(h_far, "core")]
    hidden_b, dgu_b, back_chip, back_diag, out_chip, out_diag = feed(
        place, mlp_w, h_pieces[2:], grad_pieces[2:]
    )
    back_near = near_sum(back_own, back_core)
    out_near = near_sum(out_own, out_core)

    back_far = far_sum(back_chip, back_diag)
    hidden_b, back_far = after(hidden_b, back_far)
    mlp_grads = feed_grads(place, h_pieces, grad_pieces, dgu_a, dgu_b, hidden_a, hidden_b)
    mlp_grads, back_far = after(mlp_grads, other(back_far, "yl"))
    d_h2_own = back_near + back_far.astype(F32)
    early = lax.psum_scatter(mlp_grads, ("x", "z"), scatter_dimension=0, tiled=True)
    out_far = far_sum(out_chip, out_diag)

    d_norm2 = norm_back(d_h2_own, normed2, factor2, gain_rows[1])
    d_middle = cotangent.astype(F32) + d_norm2
    d_out = d_middle.astype(BF16)
    d_out_far = other(d_out, "yl")
    d_out_far, out_near = after(d_out_far, out_near)
    out_pieces = [d_out, other(d_out, "core"), d_out_far, other(d_out_far, "core")]
    out_far, out_pieces = after(out_far, out_pieces)
    out_far = other(out_far, "yl")

    back = attend_back(
        place, cosine, sine, out_pieces, attn_w, h_first, qt, kt, vt, attn, probs
    )
    d_qkv, *late_parts = back
    d_qkv, out_far = after(d_qkv, out_far)
    along_x, along_z, parts = from_both(
        late_parts[:4], "x", late_parts[4:], "z", True, project_back(place, d_qkv, attn_w)
    )
    d_far = other(far_sum(parts[2], parts[3]), "yl")
    result = (middle + out_near + out_far.astype(F32)).astype(BF16)
    along_x, result = after(along_x, result)
    middle_parts = late_middle(place, along_x, along_z)
    along_z, along_x, early = from_both(
        middle_parts[:4], "z", middle_parts[4:], "x", True, early
    )
    early = pair_sum(early, "yh")
    d_h1_own = near_sum(parts[0], parts[1]) + d_far.astype(F32)
    along_z, (d_h1_own, early) = after(along_z, (d_h1_own, early))
    late_keep, late_send = late_last(place, along_z, along_x)
    late = late_keep + other(late_send, "yh").astype(F32)

    normed1, factor1 = norm_rows(tokens.astype(F32))
    d_norm1 = norm_back(d_h1_own, normed1, factor1, gain_rows[0])
    input_grad = (d_middle + d_norm1).astype(BF16)

    grad_query = late[:, :heads_w]
    grad_keyval = late[:, 2 * LATE_WIDTH - heads_w :]
    grad_out = late[:, heads_w : 2 * LATE_WIDTH - heads_w].T
    grad_gateup = early[:, : 2 * hidden_w].reshape(-1, 2, hidden_w)

    gain_sum = jnp.stack(
        [
            jnp.sum(grad_query * w_query.astype(F32) + grad_keyval * w_keyval.astype(F32), 1),
            jnp.sum(grad_gateup * w_gateup.astype(F32), (1, 2)),
        ]
    )
    gain_sum = gain_sum + sum(
        lax.ppermute(gain_sum, ("yl", "core"), [(i ^ step, i) for i in range(4)])
        for step in (1, 2, 3)
    )
    grad_gains = lax.dynamic_slice(gain_sum, (0, block * gains_w), (2, gains_w)) / norm_gains
    return (
        result,
        input_grad,
        grad_query,
        grad_keyval,
        grad_out,
        grad_gateup,
        early[:, 2 * hidden_w :].T,
        grad_gains,
    )


def solution(mesh):
    fine = Mesh(mesh.devices.reshape(4, 4, 2, 2, 2), ("x", "z", "yh", "yl", "core"))
    dp = ("x", "z", "yh")
    tensor = ("yl", "core")
    every = dp + tensor
    weights = (P(dp, tensor), P(dp, tensor), P(tensor, dp), P(dp, None, tensor), P(tensor, dp))
    rows = P(every, None)
    gains = P(None, every)
    return jax.shard_map(
        body,
        mesh=fine,
        in_specs=(rows, gains) + weights + (rows,),
        out_specs=(rows, rows) + weights + (gains,),
        check_vma=False,
    )
```

```python
import jax
import jax.numpy as jnp
from jax import lax
from jax.experimental import pallas as pl
from jax.experimental.pallas import tpu as pltpu
from jax.sharding import Mesh, PartitionSpec as P

HD = 96
F32 = jnp.float32
BF16 = jnp.bfloat16
norm_eps = 1e-05
rope_base = 100000.0
LOG2E = 1.4426950408889634
SCALE = HD ** (-0.5)
MIB = 1024 * 1024
SMALL = pl.CostEstimate(flops=1, bytes_accessed=1, transcendentals=0)

GAIN_AT, OUT_AT, QUERY_AT, KEYVAL_AT, REST_AT, ATTN_WIDTH = 0, 128, 256, 640, 1024, 1280
HALF_WIDTH = ATTN_WIDTH // 2
OUT_CUT = QUERY_AT - OUT_AT
LIMIT = 60


def dot_n(left, right):
    return jnp.dot(left, right, preferred_element_type=F32)


def dot_t(left, right):
    return lax.dot_general(left, right, (((1,), (1,)), ((), ())), preferred_element_type=F32)


def dot_tn(left, right):
    return lax.dot_general(left, right, (((0,), (0,)), ((), ())), preferred_element_type=F32)


def dot_tt(left, right):
    return lax.dot_general(left, right, (((0,), (1,)), ((), ())), preferred_element_type=F32)


def block_at(index, size):
    return pl.ds(pl.multiple_of(index * size, size), size)


def causal_mask(scores, size):
    key_at = lax.broadcasted_iota(jnp.int32, (size, scores.shape[1]), 0)
    query_at = lax.broadcasted_iota(jnp.int32, (size, scores.shape[1]), 1) % size
    tail = jnp.where(key_at <= query_at, scores[-size:], -1e30)
    if scores.shape[0] == size:
        return tail
    return jnp.concatenate([scores[:-size], tail], 0)


class Moves:
    def __init__(self, sems):
        self.sems = sems
        self.started = []

    def start(self, source, target):
        copy = pltpu.make_async_copy(source, target, self.sems.at[len(self.started)])
        copy.start()
        self.started.append(copy)
        return copy

    def wait(self):
        for copy in self.started:
            copy.wait()


def vmem(shape, dtype=BF16):
    return pltpu.VMEM(shape, dtype)


def like(shape, dtype=BF16):
    return jax.ShapeDtypeStruct(shape, dtype)


def whole():
    return pl.BlockSpec(memory_space=pltpu.VMEM)


def apart():
    return pl.BlockSpec(memory_space=pl.ANY)


def scalars():
    return pl.BlockSpec(memory_space=pltpu.SMEM)


def kernel_call(kernel, name, place, small, large, outs, small_outs, scratch, *copies):
    return pl.pallas_call(
        kernel,
        out_shape=list(small_outs) + list(outs),
        in_specs=[scalars()] + [whole()] * len(small) + [apart()] * len(large),
        out_specs=[whole()] * len(small_outs) + [apart()] * len(outs),
        scratch_shapes=list(scratch)
        + [pltpu.SemaphoreType.DMA((count,)) for count in copies],
        compiler_params=pltpu.CompilerParams(vmem_limit_bytes=LIMIT * MIB),
        cost_estimate=SMALL,
        name=name,
    )(place, *small, *large)


def probs_at(step, size):
    return step * (step + 1) // 2 * size, (step + 1) * size


def head_rows(head):
    return slice(head * HD, (head + 1) * HD)


def attend_kernel(place, cos_ref, sin_ref, t0, t1, t2, t3, a0, a1, a2, a3, b0, b1, b2, b3,
                  gains_ref, w_hbm, h_hbm, qt_hbm, kt_hbm, vt_hbm, attn_hbm, probs_hbm,
                  o0, o1, o2, o3,
                  t_ref, w_ref, h_ref, qt_ref, kt_ref, vt_ref, attn_ref, probs_ref, part_ref, k_ref,
                  in_sem, out_sem, probs_sem):
    block, ix, iz = place[0], place[1], place[2]
    half = HD // 2
    size = t_ref.shape[1]
    heads = qt_ref.shape[0]
    group_size = heads // kt_ref.shape[0]
    rows = a0.shape[1]
    fetch, store = Moves(in_sem), Moves(out_sem)
    came = []
    for far, (along_x, along_z) in enumerate(zip((a0, a1, a2, a3), (b0, b1, b2, b3))):
        for near in range(4):
            at_a = lax.rem(ix + far, 4) * 4 + lax.rem(iz + near, 4)
            at_b = lax.rem(ix + near, 4) * 4 + lax.rem(iz + far, 4)
            came.append(fetch.start(
                along_x.at[near], w_ref.at[block_at(at_a, rows), pl.ds(0, HALF_WIDTH)]))
            came.append(fetch.start(
                along_z.at[near], w_ref.at[block_at(at_b, rows), pl.ds(HALF_WIDTH, HALF_WIDTH)]))
    tokens_came = [
        fetch.start(piece, t_ref.at[i]) for i, piece in enumerate((t0, t1, t2, t3))
    ]
    for copy in came:
        copy.wait()
    store.start(w_ref, w_hbm)
    gains = w_ref[:, GAIN_AT:OUT_AT].astype(F32).T
    gain_row = gains[0:1] + gains[2:3]
    gains_ref[...] = gains[0:2] + gains[2:4]
    for step in range(4):
        at = block_at(lax.bitwise_xor(block, step), size)
        tokens_came[step].wait()
        value = t_ref[step].astype(F32)
        factor = lax.rsqrt(jnp.mean(value * value, -1, keepdims=True) + norm_eps)
        normed = (value * factor * gain_row).astype(BF16)
        h_ref[at, :] = normed
        cosine = cos_ref[:, at]
        sine = sin_ref[:, at]
        every = dot_n(normed, w_ref[:, QUERY_AT:REST_AT]).T
        query, keyval = every[: KEYVAL_AT - QUERY_AT], every[KEYVAL_AT - QUERY_AT :]

        def rotated(field):
            first, second = field[:half], field[half:]
            return jnp.concatenate(
                [first * cosine - second * sine, second * cosine + first * sine], 0
            )

        for head in range(heads):
            qt_ref[head, :, at] = rotated(query[head_rows(head)]).astype(BF16)
        for group in range(heads // group_size):
            key = rotated(keyval[head_rows(2 * group)])
            kt_ref[group, :, at] = key.astype(BF16)
            k_ref[group, at, :] = key.T.astype(BF16)
            vt_ref[group, :, at] = keyval[head_rows(2 * group + 1)].astype(BF16)
    for source, target in ((h_ref, h_hbm), (qt_ref, qt_hbm), (kt_ref, kt_hbm), (vt_ref, vt_hbm)):
        store.start(source, target)

    def probs_copy(group):
        return pltpu.make_async_copy(
            probs_ref.at[group], probs_hbm.at[group], probs_sem.at[group])

    for group in range(heads // group_size):
        members = range(group * group_size, (group + 1) * group_size)
        for step in range(4):
            first, reach = probs_at(step, size)
            columns = slice(step * size, reach)
            query = jnp.concatenate([qt_ref[head, :, columns] for head in members], 1)
            scores = causal_mask(dot_n(k_ref[group, :reach, :], query), size)
            top = jnp.max(scores, 0, keepdims=True)
            expo = jnp.exp2((scores - top) * (SCALE * LOG2E))
            total = jnp.sum(expo, 0, keepdims=True)
            probs = (expo * (1.0 / total)).astype(BF16)
            probs_ref[group, first : first + reach, :] = probs
            mixed = dot_n(vt_ref[group, :, :reach], probs).astype(BF16)
            for i, head in enumerate(members):
                attn_ref[head_rows(head), columns] = mixed[:, i * size : (i + 1) * size]
        probs_copy(group).start()
    store.start(attn_ref, attn_hbm)
    for step, out in ((1, o1), (3, o3), (2, o2), (0, o0)):
        at = block_at(lax.bitwise_xor(block, step), size)
        part = dot_tt(attn_ref[:OUT_CUT, at], w_ref[:, OUT_AT:QUERY_AT])
        part += dot_tt(attn_ref[OUT_CUT:, at], w_ref[:, REST_AT:])
        part_ref[step] = part.astype(BF16)
        store.start(part_ref.at[step], out)
    store.wait()
    for group in range(heads // group_size):
        probs_copy(group).wait()


def attend(place, pieces, along_x, along_z, cosine, sine):
    size, width = pieces[0].shape
    length = 4 * size
    heads = (KEYVAL_AT - QUERY_AT) // HD
    groups = (REST_AT - KEYVAL_AT) // (2 * HD)
    columns, g_columns = (heads, HD, length), (groups, HD, length)
    probs = (groups, sum(probs_at(3, size)), heads // groups * size)
    kept = [(width, ATTN_WIDTH), (length, width), columns, g_columns, g_columns,
            (heads * HD, length), probs]
    return kernel_call(
        attend_kernel, "attend", place, (cosine, sine), (*pieces, *along_x, *along_z),
        [like(s) for s in kept + [(size, width)] * 4], [like((2, width), F32)],
        [vmem(s) for s in [(4, size, width)] + kept + [(4, size, width), (groups, length, HD)]],
        36, 10, groups)


def attend_back_kernel(place, cos_ref, sin_ref,
                       o0, o1, o2, o3, w_hbm, h_hbm, qt_hbm, kt_hbm, vt_hbm, attn_hbm, probs_hbm,
                       dqkv_hbm, x0, x1, x2, x3, y0, y1, y2, y3,
                       o_ref, w_ref, h_ref, qt_ref, kt_ref, vt_ref, attn_ref, probs_ref,
                       do_ref, dqkv_ref, first_ref, second_ref, v_ref, delta_ref, dk_ref, dv_ref,
                       in_sem, out_sem, probs_sem):
    block, ix, iz = place[0], place[1], place[2]
    heads, _, length = qt_ref.shape
    groups = kt_ref.shape[0]
    group_size = heads // groups
    size = length // 4
    half = HD // 2
    width = w_ref.shape[0]
    heads_w = heads * HD
    fetch, store = Moves(in_sem), Moves(out_sem)
    rest_w = ATTN_WIDTH - REST_AT
    early = [
        fetch.start(w_hbm.at[:, pl.ds(OUT_AT, OUT_CUT)], w_ref.at[:, pl.ds(0, OUT_CUT)]),
        fetch.start(w_hbm.at[:, pl.ds(REST_AT, rest_w)], w_ref.at[:, pl.ds(OUT_CUT, rest_w)]),
    ]
    early += [
        fetch.start(piece, o_ref.at[block_at(lax.bitwise_xor(block, i), size), :])
        for i, piece in enumerate((o0, o1, o2, o3))
    ]
    middle = [
        fetch.start(source, target)
        for source, target in ((attn_hbm, attn_ref), (vt_hbm, vt_ref), (qt_hbm, qt_ref),
                               (kt_hbm, kt_ref))
    ]

    def probs_copy(group):
        return pltpu.make_async_copy(
            probs_hbm.at[group], probs_ref.at[group], probs_sem.at[group])

    for group in range(groups):
        probs_copy(group).start()
    h_came = fetch.start(h_hbm, h_ref)
    for copy in early:
        copy.wait()
    do_ref[...] = dot_tt(w_ref[...], o_ref[...]).astype(BF16)
    for copy in middle:
        copy.wait()
    for group in range(groups):
        v_ref[group] = vt_ref[group].astype(F32).T.astype(BF16)
    for head in range(heads):
        rows = head_rows(head)
        delta_ref[head] = jnp.sum(
            attn_ref[rows, :].astype(F32) * do_ref[rows, :].astype(F32), 0, keepdims=True)

    def turned_back(field, cosine, sine):
        first, second = field[:half], field[half:]
        return jnp.concatenate(
            [first * cosine + second * sine, second * cosine - first * sine], 0).astype(BF16)

    for group in range(groups):
        members = range(group * group_size, (group + 1) * group_size)
        probs_copy(group).wait()
        for step in range(4):
            first, reach = probs_at(step, size)
            columns = slice(step * size, reach)
            probs = probs_ref[group, first : first + reach, :]
            query = jnp.concatenate([qt_ref[head, :, columns] for head in members], 1)
            d_out = jnp.concatenate([do_ref[head_rows(head), columns] for head in members], 1)
            delta = jnp.concatenate([delta_ref[head, :, columns] for head in members], 1)
            d_probs = dot_n(v_ref[group, :reach, :], d_out)
            d_scores = (probs.astype(F32) * (d_probs - delta)).astype(BF16)
            for ref, left, right in ((dv_ref, d_out, probs), (dk_ref, query, d_scores)):
                change = dot_t(left, right)
                if step > 0:
                    ref[group, :, : step * size] += change[:, : step * size]
                ref[group, :, columns] = change[:, columns]
            d_query = dot_n(kt_ref[group, :, :reach], d_scores) * SCALE
            for i, head in enumerate(members):
                dqkv_ref[head_rows(head), columns] = turned_back(
                    d_query[:, i * size : (i + 1) * size],
                    cos_ref[:, columns], sin_ref[:, columns])
        dqkv_ref[head_rows(heads + 2 * group), :] = turned_back(
            dk_ref[group] * SCALE, cos_ref[...], sin_ref[...])
        dqkv_ref[head_rows(heads + 2 * group + 1), :] = dv_ref[group].astype(BF16)
    store.start(dqkv_ref, dqkv_hbm)
    h_came.wait()

    rows = width // 16
    part = dot_tt(h_ref[...], dqkv_ref[...]).astype(BF16)
    first_ref[:, :heads_w] = part[:, :heads_w]
    second_ref[:, LATE_WIDTH - heads_w :] = part[:, heads_w:]
    part = dot_tt(o_ref[...], attn_ref[...]).astype(BF16)
    first_ref[:, heads_w:] = part[:, :LATE_OUT]
    second_ref[:, : heads_w - LATE_OUT] = part[:, LATE_OUT:]
    for offset, (x_out, y_out) in enumerate(((x0, y0), (x1, y1), (x2, y2), (x3, y3))):
        to_x = lax.rem(ix + 4 - offset, 4)
        to_z = lax.rem(iz + 4 - offset, 4)
        store.start(first_ref.at[block_at(to_x, 4 * rows), :], x_out)
        for i in range(4):
            store.start(second_ref.at[block_at(i * 4 + to_z, rows), :], y_out.at[i])
    store.wait()


def attend_back(place, cosine, sine, pieces, weights, h_first, qt, kt, vt, attn, probs):
    width = weights.shape[0]
    heads, _, length = qt.shape
    groups = kt.shape[0]
    every_w = (heads + 2 * groups) * HD
    rows = width // 16
    outs = [(every_w, length)] + [(4 * rows, LATE_WIDTH)] * 4 + [(4, rows, LATE_WIDTH)] * 4
    scratch = [
        (length, width), (width, heads * HD), (length, width),
        qt.shape, kt.shape, vt.shape, attn.shape, probs.shape,
        attn.shape, (every_w, length), (width, LATE_WIDTH), (width, LATE_WIDTH),
        (groups, length, HD),
    ]
    wide = [(heads, 1, length), kt.shape, kt.shape]
    return kernel_call(
        attend_back_kernel, "attend_back", place, (cosine, sine),
        (*pieces, weights, h_first, qt, kt, vt, attn, probs),
        [like(s) for s in outs], [],
        [vmem(s) for s in scratch] + [vmem(s, F32) for s in wide], 11, 21, groups)


def project_back_kernel(place, dqkv_hbm, w_hbm, c0, c1, c2, c3,
                        dqkv_ref, w_ref, part_ref, in_sem, out_sem):
    block = place[0]
    size = part_ref.shape[1]
    fetch, store = Moves(in_sem), Moves(out_sem)
    fetch.start(w_hbm.at[:, pl.ds(QUERY_AT, REST_AT - QUERY_AT)], w_ref)
    fetch.start(dqkv_hbm, dqkv_ref)
    fetch.wait()
    for step, out in ((3, c3), (2, c2), (1, c1), (0, c0)):
        at = block_at(lax.bitwise_xor(block, step), size)
        part_ref[step] = dot_tt(dqkv_ref[:, at], w_ref[...]).astype(BF16)
        store.start(part_ref.at[step], out)
    store.wait()


def project_back(place, d_qkv, weights):
    every_w, length = d_qkv.shape
    width = weights.shape[0]
    size = length // 4
    return kernel_call(
        project_back_kernel, "project_back", place, (), (d_qkv, weights),
        [like((size, width))] * 4, [],
        [vmem(s) for s in (d_qkv.shape, (width, every_w), (4, size, width))], 2, 4)


def feed_kernel(place, h0, h1, g0, g1, w_hbm, hidden_hbm, dgu_hbm, b0, b1, r0, r1,
                w_ref, h_ref, g_ref, hidden_ref, dgu_ref, back_ref, out_ref, in_sem, out_sem):
    del place
    hidden_w = hidden_ref.shape[1]
    size = h_ref.shape[1]
    parts = [slice(i * hidden_w, (i + 1) * hidden_w) for i in range(3)]
    fetch, store = Moves(in_sem), Moves(out_sem)

    def weight(i):
        at = pl.ds(i * hidden_w, hidden_w)
        return fetch.start(w_hbm.at[:, at], w_ref.at[:, at])

    came = [fetch.start(h0, h_ref.at[0]), weight(0), weight(1), fetch.start(g0, g_ref.at[0]),
            weight(2), fetch.start(h1, h_ref.at[1]), fetch.start(g1, g_ref.at[1])]
    for i, (back, out) in enumerate(((b0, r0), (b1, r1))):
        rows = slice(i * size, (i + 1) * size)
        at = pl.ds(i * size, size)
        for copy in came[0:2] if i == 0 else came[5:7]:
            copy.wait()
        gate = dot_n(h_ref[i], w_ref[:, parts[0]])
        if i == 0:
            came[2].wait()
        up = dot_n(h_ref[i], w_ref[:, parts[1]])
        sig = 1.0 / (1.0 + jnp.exp2(gate * (-LOG2E)))
        silu = gate * sig
        hidden = (silu * up).astype(BF16)
        hidden_ref[rows, :] = hidden
        store.start(hidden_ref.at[at, :], hidden_hbm.at[at, :])
        if i == 0:
            came[3].wait()
            came[4].wait()
        d_hidden = dot_n(g_ref[i], w_ref[:, parts[2]])
        dgu_ref[rows, :hidden_w] = (
            d_hidden * up * (sig * (1.0 + gate * (1.0 - sig)))).astype(BF16)
        dgu_ref[rows, hidden_w:] = (d_hidden * silu).astype(BF16)
        store.start(dgu_ref.at[at, :], dgu_hbm.at[at, :])
        back_ref[i] = dot_t(dgu_ref[rows, :], w_ref[:, : 2 * hidden_w]).astype(BF16)
        store.start(back_ref.at[i], back)
        out_ref[i] = dot_t(hidden_ref[rows, :], w_ref[:, parts[2]]).astype(BF16)
        store.start(out_ref.at[i], out)
    store.wait()


def feed(place, weights, normed_pieces, grad_pieces):
    size, width = normed_pieces[0].shape
    hidden_w = weights.shape[1] // 3
    wide = [(2 * size, hidden_w), (2 * size, 2 * hidden_w)]
    return kernel_call(
        feed_kernel, "feed", place, (), (*normed_pieces, *grad_pieces, weights),
        [like(s) for s in wide + [(size, width)] * 4], [],
        [vmem(s) for s in [weights.shape] + [(2, size, width)] * 2 + wide + [(2, size, width)] * 2],
        7, 8)


def feed_grads_kernel(place, h0, h1, h2, h3, g0, g1, g2, g3, dgu_a, dgu_b, hidden_a, hidden_b,
                      out_hbm, h_ref, g_ref, dgu_ref, hidden_ref, out_ref, in_sem, out_sem):
    del place
    size = h0.shape[0]
    half, hidden_w = hidden_a.shape
    column = 512
    fetch, store = Moves(in_sem), Moves(out_sem)

    def rows_of(pieces, ref):
        return [
            fetch.start(piece, ref.at[pl.ds(i * size, size), :]) for i, piece in enumerate(pieces)
        ]

    def tiles_of(pieces, ref):
        tiles = []
        for tile in range(ref.shape[1] // column):
            at = pl.ds(tile * column, column)
            tiles.append([
                fetch.start(piece.at[:, at], ref.at[pl.ds(i * half, half), at])
                for i, piece in enumerate(pieces)
            ])
        return tiles

    h_came = rows_of((h0, h1, h2, h3), h_ref)
    dgu_came = tiles_of((dgu_a, dgu_b), dgu_ref)
    g_came = rows_of((g0, g1, g2, g3), g_ref)
    hidden_came = tiles_of((hidden_a, hidden_b), hidden_ref)
    at = 0
    for came, left, tiles, right in (
        (h_came, h_ref, dgu_came, dgu_ref), (g_came, g_ref, hidden_came, hidden_ref)
    ):
        for copy in came:
            copy.wait()
        for tile, copies in enumerate(tiles):
            for copy in copies:
                copy.wait()
            columns = pl.ds(at, column)
            out_ref[:, columns] = dot_tn(
                left[...], right[:, tile * column : (tile + 1) * column]).astype(BF16)
            store.start(out_ref.at[:, columns], out_hbm.at[:, columns])
            at += column
    store.wait()


def feed_grads(place, normed_pieces, grad_pieces, dgu_a, dgu_b, hidden_a, hidden_b):
    size, width = normed_pieces[0].shape
    half, hidden_w = hidden_a.shape
    scratch = [(4 * size, width)] * 2 + [(2 * half, 2 * hidden_w), (2 * half, hidden_w),
                                         (width, 3 * hidden_w)]
    return kernel_call(
        feed_grads_kernel, "feed_grads", place, (),
        (*normed_pieces, *grad_pieces, dgu_a, dgu_b, hidden_a, hidden_b),
        [like((width, 3 * hidden_w))], [], [vmem(s) for s in scratch], 20, 6)[0]


LATE_OUT, LATE_WIDTH = 192, 576


def late_middle_kernel(place, *refs):
    x_in, y_in, outs = refs[0:4], refs[4:8], refs[8:]
    ix, iz = place[1], place[2]
    rows = outs[0].shape[0]
    for offset in range(4):
        at = block_at(lax.rem(iz + 4 - offset, 4), rows)
        total = x_in[0][at, :].astype(F32)
        for ref in x_in[1:]:
            total += ref[at, :].astype(F32)
        outs[offset][...] = total.astype(BF16)
        to = lax.rem(ix + 4 - offset, 4)
        total = y_in[0][to].astype(F32)
        for ref in y_in[1:]:
            total += ref[to].astype(F32)
        outs[4 + offset][...] = total.astype(BF16)


def late_middle(place, along_x, along_z):
    _, rows, width = along_z[0].shape
    return pl.pallas_call(
        late_middle_kernel,
        out_shape=[like((rows, width))] * 8,
        in_specs=[scalars()] + [whole()] * 8,
        out_specs=[whole()] * 8,
        compiler_params=pltpu.CompilerParams(vmem_limit_bytes=16 * MIB),
        cost_estimate=SMALL,
        name="late_middle",
    )(place, *along_x, *along_z)


def late_last_kernel(place, *refs):
    x_in, y_in, keep_ref, send_ref = refs[0:4], refs[4:8], refs[8], refs[9]
    mine = place[3]
    rows = keep_ref.shape[0]
    for inputs, columns in ((x_in, slice(0, LATE_WIDTH)), (y_in, slice(LATE_WIDTH, 2 * LATE_WIDTH))):
        for ref, half in ((keep_ref, mine), (send_ref, 1 - mine)):
            at = block_at(half, rows)
            total = inputs[0][at, :].astype(F32)
            for other_ref in inputs[1:]:
                total += other_ref[at, :].astype(F32)
            ref[:, columns] = total.astype(ref.dtype)


def late_last(place, along_z, along_x):
    rows, width = along_x[0].shape
    return pl.pallas_call(
        late_last_kernel,
        out_shape=[
            jax.ShapeDtypeStruct((rows // 2, 2 * width), F32),
            jax.ShapeDtypeStruct((rows // 2, 2 * width), BF16),
        ],
        in_specs=[scalars()] + [whole()] * 8,
        out_specs=[whole()] * 2,
        compiler_params=pltpu.CompilerParams(vmem_limit_bytes=16 * MIB),
        cost_estimate=SMALL,
        name="late_last",
    )(place, *along_z, *along_x)


def norm_rows(values_in):
    factor = lax.rsqrt(jnp.mean(values_in * values_in, -1, keepdims=True) + norm_eps)
    return (values_in * factor, factor)


def norm_back(grad_in, normed, factor, gain_row):
    grad_normed = grad_in * gain_row
    inner = jnp.mean(grad_normed * normed, -1, keepdims=True)
    return factor * (grad_normed - normed * inner)


def from_offset(v, axis, offset, size):
    return lax.ppermute(v, axis, [((i + offset) % size, i) for i in range(size)])


def other(v, axis):
    return from_offset(v, axis, 1, 2)


def pair_rows(v, axis):
    it = other(v, axis)
    mine = jnp.arange(2)[:, None, None] == lax.axis_index(axis)
    return jnp.where(mine, v[None], it[None]).reshape(2 * v.shape[0], v.shape[1])


def side_by_side(parts, width):
    return sum(
        jnp.pad(part, ((0, 0), (at, width - at - part.shape[1]))) for at, part in parts
    )


def near_sum(own, core):
    return own.astype(F32) + other(core, "core").astype(F32)


def far_sum(chip, diagonal):
    return near_sum(chip, diagonal).astype(BF16)


def after(value, first):
    return lax.optimization_barrier((value, first))


def from_both(along_first, first_axis, along_second, second_axis, large, beside=()):
    near = [
        from_offset(part[i], axis, i, 4)
        for i in (1, 3)
        for part, axis in ((along_first, first_axis), (along_second, second_axis))
    ]
    opposite = along_first[2], along_second[2]
    if large:
        opposite, (near, beside) = after(opposite, (near, beside))
    far = [from_offset(opposite[0], first_axis, 2, 4), from_offset(opposite[1], second_axis, 2, 4)]
    near, far = after(near, far)
    first = [along_first[0], near[0], far[0], near[2]]
    second = [along_second[0], near[1], far[1], near[3]]
    return first, second, beside


def pair_sum(v, axis):
    rows = v.shape[0] // 2
    me = lax.axis_index(axis)
    keep = lax.dynamic_slice_in_dim(v, me * rows, rows, 0)
    send = lax.dynamic_slice_in_dim(v, (1 - me) * rows, rows, 0)
    return keep.astype(F32) + other(send, axis).astype(F32)


def body(tokens, norm_gains, w_query, w_keyval, w_out, w_gateup, w_down, cotangent):
    D = tokens.shape[1]
    length = 4 * tokens.shape[0]
    hidden_w = w_down.shape[0]
    heads_w = w_query.shape[1]
    gains_w = norm_gains.shape[1]
    block = lax.axis_index("yl") * 2 + lax.axis_index("core")
    place = jnp.stack(
        [block, lax.axis_index("x"), lax.axis_index("z"), lax.axis_index("yh")]
    ).astype(jnp.int32)

    out_t = w_out.T
    attn_own = side_by_side(
        [
            (OUT_AT, out_t[:, :OUT_CUT]),
            (QUERY_AT, w_query),
            (KEYVAL_AT, w_keyval),
            (REST_AT, out_t[:, OUT_CUT:]),
        ],
        ATTN_WIDTH,
    )
    attn_pair = pair_rows(attn_own, "yh")
    pair_w = 8 * gains_w
    gain_at = (lax.axis_index("yh") * 4 + block) * gains_w
    gain_part = lax.dynamic_update_slice(jnp.zeros((2, pair_w), F32), norm_gains, (0, gain_at))
    for axis in ("core", "yl", "yh"):
        gain_part = gain_part + other(gain_part, axis)
    mlp_own, gain_part = after((w_gateup[:, 0], w_gateup[:, 1], w_down.T), gain_part)
    mlp_own = [(i * hidden_w, part) for i, part in enumerate(mlp_own)]
    mlp_pair = pair_rows(side_by_side(mlp_own, 3 * hidden_w), "yh")
    gain_part = gain_part.T
    gain_high = lax.reduce_precision(gain_part, 8, 7)
    gain_low = (gain_part - gain_high).astype(BF16)
    gain_high = gain_high.astype(BF16)
    first, second = attn_pair[:, :HALF_WIDTH], attn_pair[:, HALF_WIDTH:]
    first += side_by_side([(0, gain_high), (2, gain_low)], HALF_WIDTH)

    along_z, along_x, _ = from_both([first] * 4, "z", [second] * 4, "x", False)
    along_z, along_x, mlp_pair, tokens = lax.optimization_barrier(
        (jnp.stack(along_z), jnp.stack(along_x), mlp_pair, tokens)
    )
    mlp_w = lax.all_gather(mlp_pair, ("x", "z"), axis=0, tiled=True)
    along_x, along_z, far = from_both(
        [along_z] * 4, "x", [along_x] * 4, "z", True, other(tokens, "yl")
    )
    token_pieces = [tokens, other(tokens, "core"), far, other(far, "core")]
    cotangent, far = after(cotangent, far)
    grad_far = other(cotangent, "yl")

    positions = jnp.arange(length).astype(F32)
    freqs = rope_base ** (-(jnp.arange(HD // 2).astype(F32) * 2.0 / HD))
    angles = freqs[:, None] * positions[None, :]
    cosine, sine = jnp.cos(angles), jnp.sin(angles)

    gain_rows, attn_w, h_first, qt, kt, vt, attn, probs, *parts = attend(
        place, token_pieces, along_x, along_z, cosine, sine
    )
    grad_far, parts = after(grad_far, parts)
    grad_pieces = [cotangent, other(cotangent, "core"), grad_far, other(grad_far, "core")]
    middle_far = far_sum(parts[2], parts[3])
    middle = (
        tokens.astype(F32) + near_sum(parts[0], parts[1]) + other(middle_far, "yl").astype(F32)
    )
    normed2, factor2 = norm_rows(middle)
    h_own = (normed2 * gain_rows[1]).astype(BF16)

    h_pieces = [h_own, other(h_own, "core")]
    h_far = other(h_own, "yl")
    hidden_a, dgu_a, back_own, back_core, out_own, out_core = feed(
        place, mlp_w, h_pieces, grad_pieces[:2]
    )
    h_far, hidden_a = after(h_far, hidden_a)
    h_pieces += [h_far, other(h_far, "core")]
    hidden_b, dgu_b, back_chip, back_diag, out_chip, out_diag = feed(
        place, mlp_w, h_pieces[2:], grad_pieces[2:]
    )
    back_near = near_sum(back_own, back_core)
    out_near = near_sum(out_own, out_core)

    back_far = far_sum(back_chip, back_diag)
    hidden_b, (back_far, back_near) = after(hidden_b, (back_far, back_near))
    mlp_grads = feed_grads(place, h_pieces, grad_pieces, dgu_a, dgu_b, hidden_a, hidden_b)
    mlp_grads, back_far = after(mlp_grads, other(back_far, "yl"))
    d_h2_own = back_near + back_far.astype(F32)
    early = lax.psum_scatter(mlp_grads, ("x", "z"), scatter_dimension=0, tiled=True)
    out_far = far_sum(out_chip, out_diag)

    d_norm2 = norm_back(d_h2_own, normed2, factor2, gain_rows[1])
    d_middle = cotangent.astype(F32) + d_norm2
    d_out = d_middle.astype(BF16)
    d_out_far = other(d_out, "yl")
    d_out_far, out_near = after(d_out_far, out_near)
    out_pieces = [d_out, other(d_out, "core"), d_out_far, other(d_out_far, "core")]
    out_far, out_pieces = after(out_far, out_pieces)
    out_far = other(out_far, "yl")

    back = attend_back(
        place, cosine, sine, out_pieces, attn_w, h_first, qt, kt, vt, attn, probs
    )
    d_qkv, *late_parts = back
    d_qkv, out_far = after(d_qkv, out_far)
    along_x, along_z, parts = from_both(
        late_parts[:4], "x", late_parts[4:], "z", True, project_back(place, d_qkv, attn_w)
    )
    d_far = other(far_sum(parts[2], parts[3]), "yl")
    result = (middle + out_near + out_far.astype(F32)).astype(BF16)
    along_x, result = after(along_x, result)
    middle_parts = late_middle(place, along_x, along_z)
    along_z, along_x, early = from_both(
        middle_parts[:4], "z", middle_parts[4:], "x", True, early
    )
    early = pair_sum(early, "yh")
    d_h1_own = near_sum(parts[0], parts[1]) + d_far.astype(F32)
    along_z, (d_h1_own, early) = after(along_z, (d_h1_own, early))
    late_keep, late_send = late_last(place, along_z, along_x)
    late = late_keep + other(late_send, "yh").astype(F32)

    normed1, factor1 = norm_rows(tokens.astype(F32))
    d_norm1 = norm_back(d_h1_own, normed1, factor1, gain_rows[0])
    input_grad = (d_middle + d_norm1).astype(BF16)

    grad_query = late[:, :heads_w]
    grad_keyval = late[:, 2 * LATE_WIDTH - heads_w :]
    grad_out = late[:, heads_w : 2 * LATE_WIDTH - heads_w].T
    grad_gateup = early[:, : 2 * hidden_w].reshape(-1, 2, hidden_w)

    gain_sum = jnp.stack(
        [
            jnp.sum(grad_query * w_query.astype(F32) + grad_keyval * w_keyval.astype(F32), 1),
            jnp.sum(grad_gateup * w_gateup.astype(F32), (1, 2)),
        ]
    )
    gain_sum = gain_sum + sum(
        lax.ppermute(gain_sum, ("yl", "core"), [(i ^ step, i) for i in range(4)])
        for step in (1, 2, 3)
    )
    grad_gains = lax.dynamic_slice(gain_sum, (0, block * gains_w), (2, gains_w)) / norm_gains
    return (
        result,
        input_grad,
        grad_query,
        grad_keyval,
        grad_out,
        grad_gateup,
        early[:, 2 * hidden_w :].T,
        grad_gains,
    )


def solution(mesh):
    fine = Mesh(mesh.devices.reshape(4, 4, 2, 2, 2), ("x", "z", "yh", "yl", "core"))
    dp = ("x", "z", "yh")
    tensor = ("yl", "core")
    every = dp + tensor
    weights = (P(dp, tensor), P(dp, tensor), P(tensor, dp), P(dp, None, tensor), P(tensor, dp))
    rows = P(every, None)
    gains = P(None, every)
    return jax.shard_map(
        body,
        mesh=fine,
        in_specs=(rows, gains) + weights + (rows,),
        out_specs=(rows, rows) + weights + (gains,),
        check_vma=False,
    )
```

```python
import jax
import jax.numpy as jnp
from jax import lax
from jax.experimental import pallas as pl
from jax.experimental.pallas import tpu as pltpu
from jax.sharding import Mesh, PartitionSpec as P

HD = 96
F32 = jnp.float32
BF16 = jnp.bfloat16
norm_eps = 1e-05
rope_base = 100000.0
LOG2E = 1.4426950408889634
SCALE = HD ** (-0.5)
MIB = 1024 * 1024
SMALL = pl.CostEstimate(flops=1, bytes_accessed=1, transcendentals=0)

GAIN_AT, QUERY_AT, KEYVAL_AT, OUT_AT, ATTN_WIDTH = 0, 128, 512, 896, 1280
LIMIT = 60


def dot_n(left, right):
    return jnp.dot(left, right, preferred_element_type=F32)


def dot_t(left, right):
    return lax.dot_general(left, right, (((1,), (1,)), ((), ())), preferred_element_type=F32)


def dot_tn(left, right):
    return lax.dot_general(left, right, (((0,), (0,)), ((), ())), preferred_element_type=F32)


def dot_tt(left, right):
    return lax.dot_general(left, right, (((0,), (1,)), ((), ())), preferred_element_type=F32)


def block_at(index, size):
    return pl.ds(pl.multiple_of(index * size, size), size)


def causal_mask(scores, size):
    key_at = lax.broadcasted_iota(jnp.int32, (size, scores.shape[1]), 0)
    query_at = lax.broadcasted_iota(jnp.int32, (size, scores.shape[1]), 1) % size
    tail = jnp.where(key_at <= query_at, scores[-size:], -1e30)
    if scores.shape[0] == size:
        return tail
    return jnp.concatenate([scores[:-size], tail], 0)


class Moves:
    def __init__(self, sems):
        self.sems = sems
        self.started = []

    def start(self, source, target):
        copy = pltpu.make_async_copy(source, target, self.sems.at[len(self.started)])
        copy.start()
        self.started.append(copy)
        return copy

    def wait(self):
        for copy in self.started:
            copy.wait()


def vmem(shape, dtype=BF16):
    return pltpu.VMEM(shape, dtype)


def like(shape, dtype=BF16):
    return jax.ShapeDtypeStruct(shape, dtype)


def whole():
    return pl.BlockSpec(memory_space=pltpu.VMEM)


def apart():
    return pl.BlockSpec(memory_space=pl.ANY)


def scalars():
    return pl.BlockSpec(memory_space=pltpu.SMEM)


def kernel_call(kernel, name, place, small, large, outs, small_outs, scratch, *copies):
    return pl.pallas_call(
        kernel,
        out_shape=list(small_outs) + list(outs),
        in_specs=[scalars()] + [whole()] * len(small) + [apart()] * len(large),
        out_specs=[whole()] * len(small_outs) + [apart()] * len(outs),
        scratch_shapes=list(scratch)
        + [pltpu.SemaphoreType.DMA((count,)) for count in copies],
        compiler_params=pltpu.CompilerParams(vmem_limit_bytes=LIMIT * MIB),
        cost_estimate=SMALL,
        name=name,
    )(place, *small, *large)


def probs_at(step, size):
    return step * (step + 1) // 2 * size, (step + 1) * size


def head_rows(head):
    return slice(head * HD, (head + 1) * HD)


def attend_kernel(place, cos_ref, sin_ref, t0, t1, t2, t3, w_hbm, gains_ref, h_hbm, qt_hbm, kt_hbm, vt_hbm, attn_hbm, probs_hbm,
                  o0, o1, o2, o3, t_ref, w_ref, h_ref, qt_ref, kt_ref, vt_ref, attn_ref, probs_ref, part_ref, k_ref,
                  in_sem, out_sem, probs_sem):
    block = place[0]
    half = HD // 2
    size = t_ref.shape[1]
    heads = qt_ref.shape[0]
    group_size = heads // kt_ref.shape[0]
    fetch, store = Moves(in_sem), Moves(out_sem)
    parts = pl.ds(0, OUT_AT), pl.ds(OUT_AT, ATTN_WIDTH - OUT_AT)
    w_came = [fetch.start(w_hbm.at[:, parts[0]], w_ref.at[:, parts[0]])]
    tokens_came = [
        fetch.start(piece, t_ref.at[i]) for i, piece in enumerate((t0, t1, t2, t3))
    ]
    w_came.append(fetch.start(w_hbm.at[:, parts[1]], w_ref.at[:, parts[1]]))
    w_came[0].wait()
    gains = w_ref[:, GAIN_AT:QUERY_AT].astype(F32).T
    gain_row = gains[0:1] + gains[2:3]
    gains_ref[...] = gains[0:2] + gains[2:4]
    for step in range(4):
        at = block_at(lax.bitwise_xor(block, step), size)
        tokens_came[step].wait()
        value = t_ref[step].astype(F32)
        factor = lax.rsqrt(jnp.mean(value * value, -1, keepdims=True) + norm_eps)
        normed = (value * factor * gain_row).astype(BF16)
        h_ref[at, :] = normed
        cosine = cos_ref[:, at]
        sine = sin_ref[:, at]
        every = dot_n(normed, w_ref[:, QUERY_AT:OUT_AT]).T
        query, keyval = every[: KEYVAL_AT - QUERY_AT], every[KEYVAL_AT - QUERY_AT :]

        def rotated(field):
            first, second = field[:half], field[half:]
            return jnp.concatenate(
                [first * cosine - second * sine, second * cosine + first * sine], 0
            )

        for head in range(heads):
            qt_ref[head, :, at] = rotated(query[head_rows(head)]).astype(BF16)
        for group in range(heads // group_size):
            key = rotated(keyval[head_rows(2 * group)])
            kt_ref[group, :, at] = key.astype(BF16)
            k_ref[group, at, :] = key.T.astype(BF16)
            vt_ref[group, :, at] = keyval[head_rows(2 * group + 1)].astype(BF16)
    for source, target in ((h_ref, h_hbm), (qt_ref, qt_hbm), (kt_ref, kt_hbm), (vt_ref, vt_hbm)):
        store.start(source, target)

    def probs_copy(group):
        return pltpu.make_async_copy(
            probs_ref.at[group], probs_hbm.at[group], probs_sem.at[group])

    for group in range(heads // group_size):
        members = range(group * group_size, (group + 1) * group_size)
        for step in range(4):
            first, reach = probs_at(step, size)
            columns = slice(step * size, reach)
            query = jnp.concatenate([qt_ref[head, :, columns] for head in members], 1)
            scores = causal_mask(dot_n(k_ref[group, :reach, :], query), size)
            top = jnp.max(scores, 0, keepdims=True)
            expo = jnp.exp2((scores - top) * (SCALE * LOG2E))
            total = jnp.sum(expo, 0, keepdims=True)
            probs = (expo * (1.0 / total)).astype(BF16)
            probs_ref[group, first : first + reach, :] = probs
            mixed = dot_n(vt_ref[group, :, :reach], probs).astype(BF16)
            for i, head in enumerate(members):
                attn_ref[head_rows(head), columns] = mixed[:, i * size : (i + 1) * size]
        probs_copy(group).start()
    store.start(attn_ref, attn_hbm)
    w_came[1].wait()
    for step, out in ((1, o1), (3, o3), (2, o2), (0, o0)):
        at = block_at(lax.bitwise_xor(block, step), size)
        part_ref[step] = dot_tt(attn_ref[:, at], w_ref[:, OUT_AT:]).astype(BF16)
        store.start(part_ref.at[step], out)
    store.wait()
    for group in range(heads // group_size):
        probs_copy(group).wait()


def attend(place, pieces, weights, cosine, sine):
    size, width = pieces[0].shape
    length = 4 * size
    heads = (KEYVAL_AT - QUERY_AT) // HD
    groups = (OUT_AT - KEYVAL_AT) // (2 * HD)
    columns, g_columns = (heads, HD, length), (groups, HD, length)
    probs = (groups, sum(probs_at(3, size)), heads // groups * size)
    kept = [(length, width), columns, g_columns, g_columns, (heads * HD, length), probs]
    return kernel_call(
        attend_kernel, "attend", place, (cosine, sine), (*pieces, weights),
        [like(s) for s in kept + [(size, width)] * 4], [like((2, width), F32)],
        [vmem(s) for s in [(4, size, width), weights.shape] + kept
         + [(4, size, width), (groups, length, HD)]],
        6, 9, groups)


def attend_back_kernel(place, cos_ref, sin_ref,
                       o0, o1, o2, o3, w_hbm, h_hbm, qt_hbm, kt_hbm, vt_hbm, attn_hbm, probs_hbm,
                       dqkv_hbm, x0, x1, x2, x3, y0, y1, y2, y3,
                       o_ref, w_ref, h_ref, qt_ref, kt_ref, vt_ref, attn_ref, probs_ref,
                       do_ref, dqkv_ref, first_ref, second_ref, v_ref, delta_ref, dk_ref, dv_ref,
                       in_sem, out_sem, probs_sem):
    block, ix, iz = place[0], place[1], place[2]
    heads, _, length = qt_ref.shape
    groups = kt_ref.shape[0]
    group_size = heads // groups
    size = length // 4
    half = HD // 2
    width = w_ref.shape[0]
    heads_w = heads * HD
    fetch, store = Moves(in_sem), Moves(out_sem)
    early = [fetch.start(w_hbm.at[:, pl.ds(OUT_AT, ATTN_WIDTH - OUT_AT)], w_ref)]
    early += [
        fetch.start(piece, o_ref.at[block_at(lax.bitwise_xor(block, i), size), :])
        for i, piece in enumerate((o0, o1, o2, o3))
    ]
    middle = [
        fetch.start(source, target)
        for source, target in ((attn_hbm, attn_ref), (vt_hbm, vt_ref), (qt_hbm, qt_ref),
                               (kt_hbm, kt_ref))
    ]

    def probs_copy(group):
        return pltpu.make_async_copy(
            probs_hbm.at[group], probs_ref.at[group], probs_sem.at[group])

    for group in range(groups):
        probs_copy(group).start()
    h_came = fetch.start(h_hbm, h_ref)
    for copy in early:
        copy.wait()
    do_ref[...] = dot_tt(w_ref[...], o_ref[...]).astype(BF16)
    for copy in middle:
        copy.wait()
    for group in range(groups):
        v_ref[group] = vt_ref[group].astype(F32).T.astype(BF16)
    for head in range(heads):
        rows = head_rows(head)
        delta_ref[head] = jnp.sum(
            attn_ref[rows, :].astype(F32) * do_ref[rows, :].astype(F32), 0, keepdims=True)

    def turned_back(field, cosine, sine):
        first, second = field[:half], field[half:]
        return jnp.concatenate(
            [first * cosine + second * sine, second * cosine - first * sine], 0).astype(BF16)

    for group in range(groups):
        members = range(group * group_size, (group + 1) * group_size)
        probs_copy(group).wait()
        for step in range(4):
            first, reach = probs_at(step, size)
            columns = slice(step * size, reach)
            probs = probs_ref[group, first : first + reach, :]
            query = jnp.concatenate([qt_ref[head, :, columns] for head in members], 1)
            d_out = jnp.concatenate([do_ref[head_rows(head), columns] for head in members], 1)
            delta = jnp.concatenate([delta_ref[head, :, columns] for head in members], 1)
            d_probs = dot_n(v_ref[group, :reach, :], d_out)
            d_scores = (probs.astype(F32) * (d_probs - delta)).astype(BF16)
            for ref, left, right in ((dv_ref, d_out, probs), (dk_ref, query, d_scores)):
                change = dot_t(left, right)
                if step > 0:
                    ref[group, :, : step * size] += change[:, : step * size]
                ref[group, :, columns] = change[:, columns]
            d_query = dot_n(kt_ref[group, :, :reach], d_scores) * SCALE
            for i, head in enumerate(members):
                dqkv_ref[head_rows(head), columns] = turned_back(
                    d_query[:, i * size : (i + 1) * size],
                    cos_ref[:, columns], sin_ref[:, columns])
        dqkv_ref[head_rows(heads + 2 * group), :] = turned_back(
            dk_ref[group] * SCALE, cos_ref[...], sin_ref[...])
        dqkv_ref[head_rows(heads + 2 * group + 1), :] = dv_ref[group].astype(BF16)
    store.start(dqkv_ref, dqkv_hbm)
    h_came.wait()

    rows = width // 16
    part = dot_tt(h_ref[...], dqkv_ref[...]).astype(BF16)
    first_ref[:, :heads_w] = part[:, :heads_w]
    second_ref[:, LATE_WIDTH - heads_w :] = part[:, heads_w:]
    part = dot_tt(o_ref[...], attn_ref[...]).astype(BF16)
    first_ref[:, heads_w:] = part[:, :LATE_OUT]
    second_ref[:, : heads_w - LATE_OUT] = part[:, LATE_OUT:]
    for offset, (x_out, y_out) in enumerate(((x0, y0), (x1, y1), (x2, y2), (x3, y3))):
        to_x = lax.rem(ix + 4 - offset, 4)
        to_z = lax.rem(iz + 4 - offset, 4)
        store.start(first_ref.at[block_at(to_x, 4 * rows), :], x_out)
        for i in range(4):
            store.start(second_ref.at[block_at(i * 4 + to_z, rows), :], y_out.at[i])
    store.wait()


def attend_back(place, cosine, sine, pieces, weights, h_first, qt, kt, vt, attn, probs):
    width = weights.shape[0]
    heads, _, length = qt.shape
    groups = kt.shape[0]
    every_w = (heads + 2 * groups) * HD
    rows = width // 16
    outs = [(every_w, length)] + [(4 * rows, LATE_WIDTH)] * 4 + [(4, rows, LATE_WIDTH)] * 4
    scratch = [
        (length, width), (width, heads * HD), (length, width),
        qt.shape, kt.shape, vt.shape, attn.shape, probs.shape,
        attn.shape, (every_w, length), (width, LATE_WIDTH), (width, LATE_WIDTH),
        (groups, length, HD),
    ]
    wide = [(heads, 1, length), kt.shape, kt.shape]
    return kernel_call(
        attend_back_kernel, "attend_back", place, (cosine, sine),
        (*pieces, weights, h_first, qt, kt, vt, attn, probs),
        [like(s) for s in outs], [],
        [vmem(s) for s in scratch] + [vmem(s, F32) for s in wide], 10, 21, groups)


def project_back_kernel(place, dqkv_hbm, w_hbm, c0, c1, c2, c3,
                        dqkv_ref, w_ref, part_ref, in_sem, out_sem):
    block = place[0]
    size = part_ref.shape[1]
    fetch, store = Moves(in_sem), Moves(out_sem)
    fetch.start(w_hbm.at[:, pl.ds(QUERY_AT, OUT_AT - QUERY_AT)], w_ref)
    fetch.start(dqkv_hbm, dqkv_ref)
    fetch.wait()
    for step, out in ((3, c3), (2, c2), (1, c1), (0, c0)):
        at = block_at(lax.bitwise_xor(block, step), size)
        part_ref[step] = dot_tt(dqkv_ref[:, at], w_ref[...]).astype(BF16)
        store.start(part_ref.at[step], out)
    store.wait()


def project_back(place, d_qkv, weights):
    every_w, length = d_qkv.shape
    width = weights.shape[0]
    size = length // 4
    return kernel_call(
        project_back_kernel, "project_back", place, (), (d_qkv, weights),
        [like((size, width))] * 4, [],
        [vmem(s) for s in (d_qkv.shape, (width, every_w), (4, size, width))], 2, 4)


def feed_kernel(place, h0, h1, g0, g1, a0, a1, a2, a3, b0, b1, b2, b3,
                hidden_hbm, dgu_hbm, back0, back1, out0, out1,
                w_ref, h_ref, g_ref, hidden_ref, dgu_ref, back_ref, out_ref, in_sem, out_sem):
    ix, iz = place[1], place[2]
    hidden_w = hidden_ref.shape[1]
    size = h_ref.shape[1]
    _, rows, half = a0.shape
    parts = [slice(i * hidden_w, (i + 1) * hidden_w) for i in range(3)]
    fetch, store = Moves(in_sem), Moves(out_sem)

    def weights(first, width):
        copies = []
        for far in range(4):
            for near in range(4):
                if first < half:
                    at = lax.rem(ix + far, 4) * 4 + lax.rem(iz + near, 4)
                    source = (a0, a1, a2, a3)[far].at[near, :, pl.ds(first, width)]
                else:
                    at = lax.rem(ix + near, 4) * 4 + lax.rem(iz + far, 4)
                    source = (b0, b1, b2, b3)[far].at[near, :, pl.ds(first - half, width)]
                copies.append(
                    fetch.start(source, w_ref.at[block_at(at, rows), pl.ds(first, width)]))
        return copies

    came = [[fetch.start(h0, h_ref.at[0])] + weights(0, hidden_w)]
    came.append(weights(hidden_w, half - hidden_w) + weights(half, 2 * hidden_w - half))
    came.append([fetch.start(g0, g_ref.at[0])] + weights(2 * hidden_w, hidden_w))
    came.append([fetch.start(h1, h_ref.at[1]), fetch.start(g1, g_ref.at[1])])

    def wait(group):
        for copy in came[group]:
            copy.wait()

    for i, (back, out) in enumerate(((back0, out0), (back1, out1))):
        at = pl.ds(i * size, size)
        rows_at = slice(i * size, (i + 1) * size)
        wait(3 if i else 0)
        gate = dot_n(h_ref[i], w_ref[:, parts[0]])
        if i == 0:
            wait(1)
        up = dot_n(h_ref[i], w_ref[:, parts[1]])
        sig = 1.0 / (1.0 + jnp.exp2(gate * (-LOG2E)))
        silu = gate * sig
        hidden = (silu * up).astype(BF16)
        hidden_ref[rows_at, :] = hidden
        store.start(hidden_ref.at[at, :], hidden_hbm.at[at, :])
        if i == 0:
            wait(2)
        d_hidden = dot_n(g_ref[i], w_ref[:, parts[2]])
        dgu_ref[rows_at, :hidden_w] = (
            d_hidden * up * (sig * (1.0 + gate * (1.0 - sig)))).astype(BF16)
        dgu_ref[rows_at, hidden_w:] = (d_hidden * silu).astype(BF16)
        store.start(dgu_ref.at[at, :], dgu_hbm.at[at, :])
        back_ref[i] = dot_t(dgu_ref[rows_at, :], w_ref[:, : 2 * hidden_w]).astype(BF16)
        store.start(back_ref.at[i], back)
        out_ref[i] = dot_t(hidden_ref[rows_at, :], w_ref[:, parts[2]]).astype(BF16)
        store.start(out_ref.at[i], out)
    store.wait()


def feed(place, along_x, along_z, normed_pieces, grad_pieces):
    size, width = normed_pieces[0].shape
    hidden_w = 2 * along_x[0].shape[2] // 3
    wide = [(2 * size, hidden_w), (2 * size, 2 * hidden_w)]
    return kernel_call(
        feed_kernel, "feed", place, (), (*normed_pieces, *grad_pieces, *along_x, *along_z),
        [like(s) for s in wide + [(size, width)] * 4], [],
        [vmem(s) for s in [(width, 3 * hidden_w)] + [(2, size, width)] * 2 + wide
         + [(2, size, width)] * 2],
        68, 8)


def feed_grads_kernel(place, h0, h1, h2, h3, g0, g1, g2, g3, dgu_a, dgu_b, hidden_a, hidden_b,
                      out_hbm, h_ref, g_ref, dgu_ref, hidden_ref, out_ref, in_sem, out_sem):
    del place
    size = h0.shape[0]
    half, hidden_w = hidden_a.shape
    column = 512
    fetch, store = Moves(in_sem), Moves(out_sem)

    def rows_of(pieces, ref):
        return [
            fetch.start(piece, ref.at[pl.ds(i * size, size), :]) for i, piece in enumerate(pieces)
        ]

    def tiles_of(pieces, ref):
        tiles = []
        for tile in range(ref.shape[1] // column):
            at = pl.ds(tile * column, column)
            tiles.append([
                fetch.start(piece.at[:, at], ref.at[pl.ds(i * half, half), at])
                for i, piece in enumerate(pieces)
            ])
        return tiles

    h_came = rows_of((h0, h1, h2, h3), h_ref)
    dgu_came = tiles_of((dgu_a, dgu_b), dgu_ref)
    g_came = rows_of((g0, g1, g2, g3), g_ref)
    hidden_came = tiles_of((hidden_a, hidden_b), hidden_ref)
    at = 0
    for came, left, tiles, right in (
        (h_came, h_ref, dgu_came, dgu_ref), (g_came, g_ref, hidden_came, hidden_ref)
    ):
        for copy in came:
            copy.wait()
        for tile, copies in enumerate(tiles):
            for copy in copies:
                copy.wait()
            columns = pl.ds(at, column)
            out_ref[:, columns] = dot_tn(
                left[...], right[:, tile * column : (tile + 1) * column]).astype(BF16)
            store.start(out_ref.at[:, columns], out_hbm.at[:, columns])
            at += column
    store.wait()


def feed_grads(place, normed_pieces, grad_pieces, dgu_a, dgu_b, hidden_a, hidden_b):
    size, width = normed_pieces[0].shape
    half, hidden_w = hidden_a.shape
    scratch = [(4 * size, width)] * 2 + [(2 * half, 2 * hidden_w), (2 * half, hidden_w),
                                         (width, 3 * hidden_w)]
    return kernel_call(
        feed_grads_kernel, "feed_grads", place, (),
        (*normed_pieces, *grad_pieces, dgu_a, dgu_b, hidden_a, hidden_b),
        [like((width, 3 * hidden_w))], [], [vmem(s) for s in scratch], 20, 6)[0]


LATE_OUT, LATE_WIDTH = 192, 576


def late_middle_kernel(place, *refs):
    x_in, y_in, outs = refs[0:4], refs[4:8], refs[8:]
    ix, iz = place[1], place[2]
    rows = outs[0].shape[0]
    for offset in range(4):
        at = block_at(lax.rem(iz + 4 - offset, 4), rows)
        total = x_in[0][at, :].astype(F32)
        for ref in x_in[1:]:
            total += ref[at, :].astype(F32)
        outs[offset][...] = total.astype(BF16)
        to = lax.rem(ix + 4 - offset, 4)
        total = y_in[0][to].astype(F32)
        for ref in y_in[1:]:
            total += ref[to].astype(F32)
        outs[4 + offset][...] = total.astype(BF16)


def late_middle(place, along_x, along_z):
    _, rows, width = along_z[0].shape
    return pl.pallas_call(
        late_middle_kernel,
        out_shape=[like((rows, width))] * 8,
        in_specs=[scalars()] + [whole()] * 8,
        out_specs=[whole()] * 8,
        compiler_params=pltpu.CompilerParams(vmem_limit_bytes=16 * MIB),
        cost_estimate=SMALL,
        name="late_middle",
    )(place, *along_x, *along_z)


def late_last_kernel(place, *refs):
    x_in, y_in, keep_ref, send_ref = refs[0:4], refs[4:8], refs[8], refs[9]
    mine = place[3]
    rows = keep_ref.shape[0]
    for inputs, columns in ((x_in, slice(0, LATE_WIDTH)), (y_in, slice(LATE_WIDTH, 2 * LATE_WIDTH))):
        for ref, half in ((keep_ref, mine), (send_ref, 1 - mine)):
            at = block_at(half, rows)
            total = inputs[0][at, :].astype(F32)
            for other_ref in inputs[1:]:
                total += other_ref[at, :].astype(F32)
            ref[:, columns] = total.astype(ref.dtype)


def late_last(place, along_z, along_x):
    rows, width = along_x[0].shape
    return pl.pallas_call(
        late_last_kernel,
        out_shape=[
            jax.ShapeDtypeStruct((rows // 2, 2 * width), F32),
            jax.ShapeDtypeStruct((rows // 2, 2 * width), BF16),
        ],
        in_specs=[scalars()] + [whole()] * 8,
        out_specs=[whole()] * 2,
        compiler_params=pltpu.CompilerParams(vmem_limit_bytes=16 * MIB),
        cost_estimate=SMALL,
        name="late_last",
    )(place, *along_z, *along_x)


def norm_rows(values_in):
    factor = lax.rsqrt(jnp.mean(values_in * values_in, -1, keepdims=True) + norm_eps)
    return (values_in * factor, factor)


def norm_back(grad_in, normed, factor, gain_row):
    grad_normed = grad_in * gain_row
    inner = jnp.mean(grad_normed * normed, -1, keepdims=True)
    return factor * (grad_normed - normed * inner)


def from_offset(v, axis, offset, size):
    return lax.ppermute(v, axis, [((i + offset) % size, i) for i in range(size)])


def other(v, axis):
    return from_offset(v, axis, 1, 2)


def pair_rows(v, axis):
    it = other(v, axis)
    mine = jnp.arange(2)[:, None, None] == lax.axis_index(axis)
    return jnp.where(mine, v[None], it[None]).reshape(2 * v.shape[0], v.shape[1])


def side_by_side(parts, width):
    return sum(
        jnp.pad(part, ((0, 0), (at, width - at - part.shape[1]))) for at, part in parts
    )


def near_sum(own, core):
    return own.astype(F32) + other(core, "core").astype(F32)


def far_sum(chip, diagonal):
    return near_sum(chip, diagonal).astype(BF16)


def after(value, first):
    return lax.optimization_barrier((value, first))


def from_both(along_first, first_axis, along_second, second_axis, large, beside=()):
    near = [
        from_offset(part[i], axis, i, 4)
        for i in (1, 3)
        for part, axis in ((along_first, first_axis), (along_second, second_axis))
    ]
    opposite = along_first[2], along_second[2]
    if large:
        opposite, (near, beside) = after(opposite, (near, beside))
    far = [from_offset(opposite[0], first_axis, 2, 4), from_offset(opposite[1], second_axis, 2, 4)]
    near, far = after(near, far)
    first = [along_first[0], near[0], far[0], near[2]]
    second = [along_second[0], near[1], far[1], near[3]]
    return first, second, beside


def pair_sum(v, axis):
    rows = v.shape[0] // 2
    me = lax.axis_index(axis)
    keep = lax.dynamic_slice_in_dim(v, me * rows, rows, 0)
    send = lax.dynamic_slice_in_dim(v, (1 - me) * rows, rows, 0)
    return keep.astype(F32) + other(send, axis).astype(F32)


def body(tokens, norm_gains, w_query, w_keyval, w_out, w_gateup, w_down, cotangent):
    D = tokens.shape[1]
    length = 4 * tokens.shape[0]
    hidden_w = w_down.shape[0]
    heads_w = w_query.shape[1]
    gains_w = norm_gains.shape[1]
    block = lax.axis_index("yl") * 2 + lax.axis_index("core")
    place = jnp.stack(
        [block, lax.axis_index("x"), lax.axis_index("z"), lax.axis_index("yh")]
    ).astype(jnp.int32)

    attn_own = side_by_side(
        [(QUERY_AT, w_query), (KEYVAL_AT, w_keyval), (OUT_AT, w_out.T)], ATTN_WIDTH
    )
    attn_pair = pair_rows(attn_own, "yh")

    pair_w = 8 * gains_w
    gain_at = (lax.axis_index("yh") * 4 + block) * gains_w
    gain_part = lax.dynamic_update_slice(jnp.zeros((2, pair_w), F32), norm_gains, (0, gain_at))
    for axis in ("core", "yl", "yh"):
        gain_part = gain_part + other(gain_part, axis)
    mlp_own, gain_part = after((w_gateup[:, 0], w_gateup[:, 1], w_down.T), gain_part)
    gain_part = gain_part.T
    gain_high = lax.reduce_precision(gain_part, 8, 7)
    gain_low = (gain_part - gain_high).astype(BF16)
    gain_high = gain_high.astype(BF16)
    attn_pair += side_by_side([(0, gain_high), (2, gain_low)], ATTN_WIDTH)
    attn_w = lax.all_gather(attn_pair, ("x", "z"), axis=0, tiled=True)

    mlp_own = [(i * hidden_w, part) for i, part in enumerate(mlp_own)]
    mlp_pair = pair_rows(side_by_side(mlp_own, 3 * hidden_w), "yh")
    half = 3 * hidden_w // 2
    along_z, along_x, _ = from_both(
        [mlp_pair[:, :half]] * 4, "z", [mlp_pair[:, half:]] * 4, "x", False
    )
    along_z, along_x, tokens = lax.optimization_barrier(
        (jnp.stack(along_z), jnp.stack(along_x), tokens)
    )
    along_x, along_z, far = from_both(
        [along_z] * 4, "x", [along_x] * 4, "z", True, other(tokens, "yl")
    )
    token_pieces = [tokens, other(tokens, "core"), far, other(far, "core")]
    cotangent, far = after(cotangent, far)
    grad_far = other(cotangent, "yl")

    positions = jnp.arange(length).astype(F32)
    freqs = rope_base ** (-(jnp.arange(HD // 2).astype(F32) * 2.0 / HD))
    angles = freqs[:, None] * positions[None, :]
    cosine, sine = jnp.cos(angles), jnp.sin(angles)

    gain_rows, h_first, qt, kt, vt, attn, probs, *parts = attend(
        place, token_pieces, attn_w, cosine, sine
    )
    grad_far, parts = after(grad_far, parts)
    grad_pieces = [cotangent, other(cotangent, "core"), grad_far, other(grad_far, "core")]
    diagonal, (along_x, along_z) = after(other(parts[3], "core"), (along_x, along_z))
    middle_far = (parts[2].astype(F32) + diagonal.astype(F32)).astype(BF16)
    middle = (
        tokens.astype(F32) + near_sum(parts[0], parts[1]) + other(middle_far, "yl").astype(F32)
    )
    normed2, factor2 = norm_rows(middle)
    h_own = (normed2 * gain_rows[1]).astype(BF16)

    h_pieces = [h_own, other(h_own, "core")]
    h_far = other(h_own, "yl")
    hidden_a, dgu_a, back_own, back_core, out_own, out_core = feed(
        place, along_x, along_z, h_pieces, grad_pieces[:2]
    )
    h_far, hidden_a = after(h_far, hidden_a)
    h_pieces += [h_far, other(h_far, "core")]
    hidden_b, dgu_b, back_chip, back_diag, out_chip, out_diag = feed(
        place, along_x, along_z, h_pieces[2:], grad_pieces[2:]
    )
    back_near = near_sum(back_own, back_core)
    out_near = near_sum(out_own, out_core)

    back_far = far_sum(back_chip, back_diag)
    hidden_b, (back_far, back_near) = after(hidden_b, (back_far, back_near))
    mlp_grads = feed_grads(place, h_pieces, grad_pieces, dgu_a, dgu_b, hidden_a, hidden_b)
    mlp_grads, back_far = after(mlp_grads, other(back_far, "yl"))
    d_h2_own = back_near + back_far.astype(F32)
    early = lax.psum_scatter(mlp_grads, ("x", "z"), scatter_dimension=0, tiled=True)
    out_far = far_sum(out_chip, out_diag)

    d_norm2 = norm_back(d_h2_own, normed2, factor2, gain_rows[1])
    d_middle = cotangent.astype(F32) + d_norm2
    d_out = d_middle.astype(BF16)
    d_out_far = other(d_out, "yl")
    d_out_far, out_near = after(d_out_far, out_near)
    out_pieces = [d_out, other(d_out, "core"), d_out_far, other(d_out_far, "core")]
    out_far, out_pieces = after(out_far, out_pieces)
    out_far = other(out_far, "yl")

    back = attend_back(
        place, cosine, sine, out_pieces, attn_w, h_first, qt, kt, vt, attn, probs
    )
    d_qkv, *late_parts = back
    d_qkv, out_far = after(d_qkv, out_far)
    along_x, along_z, parts = from_both(
        late_parts[:4], "x", late_parts[4:], "z", True, project_back(place, d_qkv, attn_w)
    )
    d_far = other(far_sum(parts[2], parts[3]), "yl")
    result = (middle + out_near + out_far.astype(F32)).astype(BF16)
    along_x, result = after(along_x, result)
    middle_parts = late_middle(place, along_x, along_z)
    along_z, along_x, early = from_both(
        middle_parts[:4], "z", middle_parts[4:], "x", True, early
    )
    early = pair_sum(early, "yh")
    d_h1_own = near_sum(parts[0], parts[1]) + d_far.astype(F32)
    along_z, (d_h1_own, early) = after(along_z, (d_h1_own, early))
    late_keep, late_send = late_last(place, along_z, along_x)
    late = late_keep + other(late_send, "yh").astype(F32)

    normed1, factor1 = norm_rows(tokens.astype(F32))
    d_norm1 = norm_back(d_h1_own, normed1, factor1, gain_rows[0])
    input_grad = (d_middle + d_norm1).astype(BF16)

    grad_query = late[:, :heads_w]
    grad_keyval = late[:, 2 * LATE_WIDTH - heads_w :]
    grad_out = late[:, heads_w : 2 * LATE_WIDTH - heads_w].T
    grad_gateup = early[:, : 2 * hidden_w].reshape(-1, 2, hidden_w)

    gain_sum = jnp.stack(
        [
            jnp.sum(grad_query * w_query.astype(F32) + grad_keyval * w_keyval.astype(F32), 1),
            jnp.sum(grad_gateup * w_gateup.astype(F32), (1, 2)),
        ]
    )
    gain_sum = gain_sum + sum(
        lax.ppermute(gain_sum, ("yl", "core"), [(i ^ step, i) for i in range(4)])
        for step in (1, 2, 3)
    )
    grad_gains = lax.dynamic_slice(gain_sum, (0, block * gains_w), (2, gains_w)) / norm_gains
    return (
        result,
        input_grad,
        grad_query,
        grad_keyval,
        grad_out,
        grad_gateup,
        early[:, 2 * hidden_w :].T,
        grad_gains,
    )


def solution(mesh):
    fine = Mesh(mesh.devices.reshape(4, 4, 2, 2, 2), ("x", "z", "yh", "yl", "core"))
    dp = ("x", "z", "yh")
    tensor = ("yl", "core")
    every = dp + tensor
    weights = (P(dp, tensor), P(dp, tensor), P(tensor, dp), P(dp, None, tensor), P(tensor, dp))
    rows = P(every, None)
    gains = P(None, every)
    return jax.shard_map(
        body,
        mesh=fine,
        in_specs=(rows, gains) + weights + (rows,),
        out_specs=(rows, rows) + weights + (gains,),
        check_vma=False,
    )
```

```python
import jax
import jax.numpy as jnp
from jax import lax
from jax.experimental import pallas as pl
from jax.experimental.pallas import tpu as pltpu
from jax.sharding import Mesh, PartitionSpec as P

HD = 96
F32 = jnp.float32
BF16 = jnp.bfloat16
norm_eps = 1e-05
rope_base = 100000.0
LOG2E = 1.4426950408889634
SCALE = HD ** (-0.5)
MIB = 1024 * 1024
SMALL = pl.CostEstimate(flops=1, bytes_accessed=1, transcendentals=0)

GAIN_AT, OUT_AT, QUERY_AT, KEYVAL_AT, REST_AT, ATTN_WIDTH = 0, 128, 256, 640, 1024, 1280
HALF_WIDTH = ATTN_WIDTH // 2
OUT_CUT = QUERY_AT - OUT_AT
LIMIT = 60


def dot_n(left, right):
    return jnp.dot(left, right, preferred_element_type=F32)


def dot_t(left, right):
    return lax.dot_general(left, right, (((1,), (1,)), ((), ())), preferred_element_type=F32)


def dot_tn(left, right):
    return lax.dot_general(left, right, (((0,), (0,)), ((), ())), preferred_element_type=F32)


def dot_tt(left, right):
    return lax.dot_general(left, right, (((0,), (1,)), ((), ())), preferred_element_type=F32)


def block_at(index, size):
    return pl.ds(pl.multiple_of(index * size, size), size)


def causal_mask(scores, size):
    key_at = lax.broadcasted_iota(jnp.int32, (size, scores.shape[1]), 0)
    query_at = lax.broadcasted_iota(jnp.int32, (size, scores.shape[1]), 1) % size
    tail = jnp.where(key_at <= query_at, scores[-size:], -1e30)
    if scores.shape[0] == size:
        return tail
    return jnp.concatenate([scores[:-size], tail], 0)


class Moves:
    def __init__(self, sems):
        self.sems = sems
        self.started = []

    def start(self, source, target):
        copy = pltpu.make_async_copy(source, target, self.sems.at[len(self.started)])
        copy.start()
        self.started.append(copy)
        return copy

    def wait(self):
        for copy in self.started:
            copy.wait()


def vmem(shape, dtype=BF16):
    return pltpu.VMEM(shape, dtype)


def like(shape, dtype=BF16):
    return jax.ShapeDtypeStruct(shape, dtype)


def whole():
    return pl.BlockSpec(memory_space=pltpu.VMEM)


def apart():
    return pl.BlockSpec(memory_space=pl.ANY)


def scalars():
    return pl.BlockSpec(memory_space=pltpu.SMEM)


def kernel_call(kernel, name, place, small, large, outs, small_outs, scratch, *copies):
    return pl.pallas_call(
        kernel,
        out_shape=list(small_outs) + list(outs),
        in_specs=[scalars()] + [whole()] * len(small) + [apart()] * len(large),
        out_specs=[whole()] * len(small_outs) + [apart()] * len(outs),
        scratch_shapes=list(scratch)
        + [pltpu.SemaphoreType.DMA((count,)) for count in copies],
        compiler_params=pltpu.CompilerParams(vmem_limit_bytes=LIMIT * MIB),
        cost_estimate=SMALL,
        name=name,
    )(place, *small, *large)


def probs_at(step, size):
    return step * (step + 1) // 2 * size, (step + 1) * size


def head_rows(head):
    return slice(head * HD, (head + 1) * HD)


def attend_kernel(place, cos_ref, sin_ref, t0, t1, t2, t3, a0, a1, a2, a3, b0, b1, b2, b3,
                  gains_ref, w_hbm, h_hbm, qt_hbm, kt_hbm, vt_hbm, attn_hbm, probs_hbm,
                  o0, o1, o2, o3,
                  t_ref, w_ref, h_ref, qt_ref, kt_ref, vt_ref, attn_ref, probs_ref, part_ref, k_ref,
                  in_sem, out_sem, probs_sem):
    block, ix, iz = place[0], place[1], place[2]
    half = HD // 2
    size = t_ref.shape[1]
    heads = qt_ref.shape[0]
    group_size = heads // kt_ref.shape[0]
    rows = a0.shape[1]
    fetch, store = Moves(in_sem), Moves(out_sem)
    gains_came, came = [], []
    for far, (along_x, along_z) in enumerate(zip((a0, a1, a2, a3), (b0, b1, b2, b3))):
        for near in range(4):
            at_a = block_at(lax.rem(ix + far, 4) * 4 + lax.rem(iz + near, 4), rows)
            at_b = block_at(lax.rem(ix + near, 4) * 4 + lax.rem(iz + far, 4), rows)
            for source, first, width, target, copies in (
                (along_x, 0, OUT_AT, at_a, gains_came),
                (along_x, OUT_AT, HALF_WIDTH - OUT_AT, at_a, came),
                (along_z, HALF_WIDTH, HALF_WIDTH, at_b, came),
            ):
                copies.append((
                    source.at[near, :, pl.ds(first % HALF_WIDTH, width)],
                    w_ref.at[target, pl.ds(first, width)],
                ))
    gains_came = [fetch.start(*copy) for copy in gains_came]
    tokens_came = [
        fetch.start(piece, t_ref.at[i]) for i, piece in enumerate((t0, t1, t2, t3))
    ]
    came = [fetch.start(*copy) for copy in came]
    for copy in gains_came:
        copy.wait()
    gains = w_ref[:, GAIN_AT:OUT_AT].astype(F32).T
    gain_row = gains[0:1] + gains[2:3]
    gains_ref[...] = gains[0:2] + gains[2:4]
    for step in range(4):
        tokens_came[step].wait()
        value = t_ref[step].astype(F32)
        factor = lax.rsqrt(jnp.mean(value * value, -1, keepdims=True) + norm_eps)
        h_ref[block_at(lax.bitwise_xor(block, step), size), :] = (
            value * factor * gain_row).astype(BF16)
    for copy in came:
        copy.wait()
    store.start(w_ref, w_hbm)
    for step in range(4):
        at = slice(step * size, (step + 1) * size)
        normed = h_ref[at, :]
        cosine = cos_ref[:, at]
        sine = sin_ref[:, at]
        every = dot_n(normed, w_ref[:, QUERY_AT:REST_AT]).T
        query, keyval = every[: KEYVAL_AT - QUERY_AT], every[KEYVAL_AT - QUERY_AT :]

        def rotated(field):
            first, second = field[:half], field[half:]
            return jnp.concatenate(
                [first * cosine - second * sine, second * cosine + first * sine], 0
            )

        for head in range(heads):
            qt_ref[head, :, at] = rotated(query[head_rows(head)]).astype(BF16)
        for group in range(heads // group_size):
            key = rotated(keyval[head_rows(2 * group)])
            kt_ref[group, :, at] = key.astype(BF16)
            k_ref[group, at, :] = key.T.astype(BF16)
            vt_ref[group, :, at] = keyval[head_rows(2 * group + 1)].astype(BF16)
    for source, target in ((h_ref, h_hbm), (qt_ref, qt_hbm), (kt_ref, kt_hbm), (vt_ref, vt_hbm)):
        store.start(source, target)

    def probs_copy(group):
        return pltpu.make_async_copy(
            probs_ref.at[group], probs_hbm.at[group], probs_sem.at[group])

    for group in range(heads // group_size):
        members = range(group * group_size, (group + 1) * group_size)
        for step in range(4):
            first, reach = probs_at(step, size)
            columns = slice(step * size, reach)
            query = jnp.concatenate([qt_ref[head, :, columns] for head in members], 1)
            scores = causal_mask(dot_n(k_ref[group, :reach, :], query), size)
            top = jnp.max(scores, 0, keepdims=True)
            expo = jnp.exp2((scores - top) * (SCALE * LOG2E))
            total = jnp.sum(expo, 0, keepdims=True)
            probs = (expo * (1.0 / total)).astype(BF16)
            probs_ref[group, first : first + reach, :] = probs
            mixed = dot_n(vt_ref[group, :, :reach], probs).astype(BF16)
            for i, head in enumerate(members):
                attn_ref[head_rows(head), columns] = mixed[:, i * size : (i + 1) * size]
        probs_copy(group).start()
    store.start(attn_ref, attn_hbm)
    for step, out in ((1, o1), (3, o3), (2, o2), (0, o0)):
        at = block_at(lax.bitwise_xor(block, step), size)
        part = dot_tt(attn_ref[:OUT_CUT, at], w_ref[:, OUT_AT:QUERY_AT])
        part += dot_tt(attn_ref[OUT_CUT:, at], w_ref[:, REST_AT:])
        part_ref[step] = part.astype(BF16)
        store.start(part_ref.at[step], out)
    store.wait()
    for group in range(heads // group_size):
        probs_copy(group).wait()


def attend(place, pieces, along_x, along_z, cosine, sine):
    size, width = pieces[0].shape
    length = 4 * size
    heads = (KEYVAL_AT - QUERY_AT) // HD
    groups = (REST_AT - KEYVAL_AT) // (2 * HD)
    columns, g_columns = (heads, HD, length), (groups, HD, length)
    probs = (groups, sum(probs_at(3, size)), heads // groups * size)
    kept = [(width, ATTN_WIDTH), (length, width), columns, g_columns, g_columns,
            (heads * HD, length), probs]
    return kernel_call(
        attend_kernel, "attend", place, (cosine, sine), (*pieces, *along_x, *along_z),
        [like(s) for s in kept + [(size, width)] * 4], [like((2, width), F32)],
        [vmem(s) for s in [(4, size, width)] + kept + [(4, size, width), (groups, length, HD)]],
        52, 10, groups)


def attend_back_kernel(place, cos_ref, sin_ref,
                       o0, o1, o2, o3, w_hbm, h_hbm, qt_hbm, kt_hbm, vt_hbm, attn_hbm, probs_hbm,
                       dqkv_hbm, x0, x1, x2, x3, y0, y1, y2, y3,
                       o_ref, w_ref, h_ref, qt_ref, kt_ref, vt_ref, attn_ref, probs_ref,
                       do_ref, dqkv_ref, first_ref, second_ref, v_ref, delta_ref, dk_ref, dv_ref,
                       in_sem, out_sem, probs_sem):
    block, ix, iz = place[0], place[1], place[2]
    heads, _, length = qt_ref.shape
    groups = kt_ref.shape[0]
    group_size = heads // groups
    size = length // 4
    half = HD // 2
    width = w_ref.shape[0]
    heads_w = heads * HD
    fetch, store = Moves(in_sem), Moves(out_sem)
    rest_w = ATTN_WIDTH - REST_AT
    early = [
        fetch.start(w_hbm.at[:, pl.ds(OUT_AT, OUT_CUT)], w_ref.at[:, pl.ds(0, OUT_CUT)]),
        fetch.start(w_hbm.at[:, pl.ds(REST_AT, rest_w)], w_ref.at[:, pl.ds(OUT_CUT, rest_w)]),
    ]
    early += [
        fetch.start(piece, o_ref.at[block_at(lax.bitwise_xor(block, i), size), :])
        for i, piece in enumerate((o0, o1, o2, o3))
    ]
    middle = [
        fetch.start(source, target)
        for source, target in ((attn_hbm, attn_ref), (vt_hbm, vt_ref), (qt_hbm, qt_ref),
                               (kt_hbm, kt_ref))
    ]

    def probs_copy(group):
        return pltpu.make_async_copy(
            probs_hbm.at[group], probs_ref.at[group], probs_sem.at[group])

    for group in range(groups):
        probs_copy(group).start()
    h_came = fetch.start(h_hbm, h_ref)
    for copy in early:
        copy.wait()
    do_ref[...] = dot_tt(w_ref[...], o_ref[...]).astype(BF16)
    for copy in middle:
        copy.wait()
    for group in range(groups):
        v_ref[group] = vt_ref[group].astype(F32).T.astype(BF16)
    for head in range(heads):
        rows = head_rows(head)
        delta_ref[head] = jnp.sum(
            attn_ref[rows, :].astype(F32) * do_ref[rows, :].astype(F32), 0, keepdims=True)

    def turned_back(field, cosine, sine):
        first, second = field[:half], field[half:]
        return jnp.concatenate(
            [first * cosine + second * sine, second * cosine - first * sine], 0).astype(BF16)

    for group in range(groups):
        members = range(group * group_size, (group + 1) * group_size)
        probs_copy(group).wait()
        for step in range(4):
            first, reach = probs_at(step, size)
            columns = slice(step * size, reach)
            probs = probs_ref[group, first : first + reach, :]
            query = jnp.concatenate([qt_ref[head, :, columns] for head in members], 1)
            d_out = jnp.concatenate([do_ref[head_rows(head), columns] for head in members], 1)
            delta = jnp.concatenate([delta_ref[head, :, columns] for head in members], 1)
            d_probs = dot_n(v_ref[group, :reach, :], d_out)
            d_scores = (probs.astype(F32) * (d_probs - delta)).astype(BF16)
            for ref, left, right in ((dv_ref, d_out, probs), (dk_ref, query, d_scores)):
                change = dot_t(left, right)
                if step > 0:
                    ref[group, :, : step * size] += change[:, : step * size]
                ref[group, :, columns] = change[:, columns]
            d_query = dot_n(kt_ref[group, :, :reach], d_scores) * SCALE
            for i, head in enumerate(members):
                dqkv_ref[head_rows(head), columns] = turned_back(
                    d_query[:, i * size : (i + 1) * size],
                    cos_ref[:, columns], sin_ref[:, columns])
        dqkv_ref[head_rows(heads + 2 * group), :] = turned_back(
            dk_ref[group] * SCALE, cos_ref[...], sin_ref[...])
        dqkv_ref[head_rows(heads + 2 * group + 1), :] = dv_ref[group].astype(BF16)
    store.start(dqkv_ref, dqkv_hbm)
    h_came.wait()

    rows = width // 16
    part = dot_tt(h_ref[...], dqkv_ref[...]).astype(BF16)
    first_ref[:, :heads_w] = part[:, :heads_w]
    second_ref[:, LATE_WIDTH - heads_w :] = part[:, heads_w:]
    part = dot_tt(o_ref[...], attn_ref[...]).astype(BF16)
    first_ref[:, heads_w:] = part[:, :LATE_OUT]
    second_ref[:, : heads_w - LATE_OUT] = part[:, LATE_OUT:]
    for offset, (x_out, y_out) in enumerate(((x0, y0), (x1, y1), (x2, y2), (x3, y3))):
        to_x = lax.rem(ix + 4 - offset, 4)
        to_z = lax.rem(iz + 4 - offset, 4)
        store.start(first_ref.at[block_at(to_x, 4 * rows), :], x_out)
        for i in range(4):
            store.start(second_ref.at[block_at(i * 4 + to_z, rows), :], y_out.at[i])
    store.wait()


def attend_back(place, cosine, sine, pieces, weights, h_first, qt, kt, vt, attn, probs):
    width = weights.shape[0]
    heads, _, length = qt.shape
    groups = kt.shape[0]
    every_w = (heads + 2 * groups) * HD
    rows = width // 16
    outs = [(every_w, length)] + [(4 * rows, LATE_WIDTH)] * 4 + [(4, rows, LATE_WIDTH)] * 4
    scratch = [
        (length, width), (width, heads * HD), (length, width),
        qt.shape, kt.shape, vt.shape, attn.shape, probs.shape,
        attn.shape, (every_w, length), (width, LATE_WIDTH), (width, LATE_WIDTH),
        (groups, length, HD),
    ]
    wide = [(heads, 1, length), kt.shape, kt.shape]
    return kernel_call(
        attend_back_kernel, "attend_back", place, (cosine, sine),
        (*pieces, weights, h_first, qt, kt, vt, attn, probs),
        [like(s) for s in outs], [],
        [vmem(s) for s in scratch] + [vmem(s, F32) for s in wide], 11, 21, groups)


def project_back_kernel(place, dqkv_hbm, w_hbm, c0, c1, c2, c3,
                        dqkv_ref, w_ref, part_ref, in_sem, out_sem):
    block = place[0]
    size = part_ref.shape[1]
    fetch, store = Moves(in_sem), Moves(out_sem)
    fetch.start(w_hbm.at[:, pl.ds(QUERY_AT, REST_AT - QUERY_AT)], w_ref)
    fetch.start(dqkv_hbm, dqkv_ref)
    fetch.wait()
    for step, out in ((3, c3), (2, c2), (1, c1), (0, c0)):
        at = block_at(lax.bitwise_xor(block, step), size)
        part_ref[step] = dot_tt(dqkv_ref[:, at], w_ref[...]).astype(BF16)
        store.start(part_ref.at[step], out)
    store.wait()


def project_back(place, d_qkv, weights):
    every_w, length = d_qkv.shape
    width = weights.shape[0]
    size = length // 4
    return kernel_call(
        project_back_kernel, "project_back", place, (), (d_qkv, weights),
        [like((size, width))] * 4, [],
        [vmem(s) for s in (d_qkv.shape, (width, every_w), (4, size, width))], 2, 4)


def feed_kernel(place, h0, h1, g0, g1, w_hbm, hidden_hbm, dgu_hbm, b0, b1, r0, r1,
                w_ref, h_ref, g_ref, hidden_ref, dgu_ref, back_ref, out_ref, in_sem, out_sem):
    del place
    hidden_w = hidden_ref.shape[1]
    size = h_ref.shape[1]
    parts = [slice(i * hidden_w, (i + 1) * hidden_w) for i in range(3)]
    fetch, store = Moves(in_sem), Moves(out_sem)

    def weight(i):
        at = pl.ds(i * hidden_w, hidden_w)
        return fetch.start(w_hbm.at[:, at], w_ref.at[:, at])

    came = [fetch.start(h0, h_ref.at[0]), weight(0), weight(1), fetch.start(g0, g_ref.at[0]),
            weight(2), fetch.start(h1, h_ref.at[1]), fetch.start(g1, g_ref.at[1])]
    for i, (back, out) in enumerate(((b0, r0), (b1, r1))):
        rows = slice(i * size, (i + 1) * size)
        at = pl.ds(i * size, size)
        for copy in came[0:2] if i == 0 else came[5:7]:
            copy.wait()
        gate = dot_n(h_ref[i], w_ref[:, parts[0]])
        if i == 0:
            came[2].wait()
        up = dot_n(h_ref[i], w_ref[:, parts[1]])
        sig = 1.0 / (1.0 + jnp.exp2(gate * (-LOG2E)))
        silu = gate * sig
        hidden = (silu * up).astype(BF16)
        hidden_ref[rows, :] = hidden
        store.start(hidden_ref.at[at, :], hidden_hbm.at[at, :])
        if i == 0:
            came[3].wait()
            came[4].wait()
        d_hidden = dot_n(g_ref[i], w_ref[:, parts[2]])
        dgu_ref[rows, :hidden_w] = (
            d_hidden * up * (sig * (1.0 + gate * (1.0 - sig)))).astype(BF16)
        dgu_ref[rows, hidden_w:] = (d_hidden * silu).astype(BF16)
        store.start(dgu_ref.at[at, :], dgu_hbm.at[at, :])
        back_ref[i] = dot_t(dgu_ref[rows, :], w_ref[:, : 2 * hidden_w]).astype(BF16)
        store.start(back_ref.at[i], back)
        out_ref[i] = dot_t(hidden_ref[rows, :], w_ref[:, parts[2]]).astype(BF16)
        store.start(out_ref.at[i], out)
    store.wait()


def feed(place, weights, normed_pieces, grad_pieces):
    size, width = normed_pieces[0].shape
    hidden_w = weights.shape[1] // 3
    wide = [(2 * size, hidden_w), (2 * size, 2 * hidden_w)]
    return kernel_call(
        feed_kernel, "feed", place, (), (*normed_pieces, *grad_pieces, weights),
        [like(s) for s in wide + [(size, width)] * 4], [],
        [vmem(s) for s in [weights.shape] + [(2, size, width)] * 2 + wide + [(2, size, width)] * 2],
        7, 8)


def feed_grads_kernel(place, h0, h1, h2, h3, g0, g1, g2, g3, dgu_a, dgu_b, hidden_a, hidden_b,
                      out_hbm, h_ref, g_ref, dgu_ref, hidden_ref, out_ref, in_sem, out_sem):
    del place
    size = h0.shape[0]
    half, hidden_w = hidden_a.shape
    column = 512
    fetch, store = Moves(in_sem), Moves(out_sem)

    def rows_of(pieces, ref):
        return [
            fetch.start(piece, ref.at[pl.ds(i * size, size), :]) for i, piece in enumerate(pieces)
        ]

    def tiles_of(pieces, ref):
        tiles = []
        for tile in range(ref.shape[1] // column):
            at = pl.ds(tile * column, column)
            tiles.append([
                fetch.start(piece.at[:, at], ref.at[pl.ds(i * half, half), at])
                for i, piece in enumerate(pieces)
            ])
        return tiles

    h_came = rows_of((h0, h1, h2, h3), h_ref)
    dgu_came = tiles_of((dgu_a, dgu_b), dgu_ref)
    g_came = rows_of((g0, g1, g2, g3), g_ref)
    hidden_came = tiles_of((hidden_a, hidden_b), hidden_ref)
    at = 0
    for came, left, tiles, right in (
        (h_came, h_ref, dgu_came, dgu_ref), (g_came, g_ref, hidden_came, hidden_ref)
    ):
        for copy in came:
            copy.wait()
        for tile, copies in enumerate(tiles):
            for copy in copies:
                copy.wait()
            columns = pl.ds(at, column)
            out_ref[:, columns] = dot_tn(
                left[...], right[:, tile * column : (tile + 1) * column]).astype(BF16)
            store.start(out_ref.at[:, columns], out_hbm.at[:, columns])
            at += column
    store.wait()


def feed_grads(place, normed_pieces, grad_pieces, dgu_a, dgu_b, hidden_a, hidden_b):
    size, width = normed_pieces[0].shape
    half, hidden_w = hidden_a.shape
    scratch = [(4 * size, width)] * 2 + [(2 * half, 2 * hidden_w), (2 * half, hidden_w),
                                         (width, 3 * hidden_w)]
    return kernel_call(
        feed_grads_kernel, "feed_grads", place, (),
        (*normed_pieces, *grad_pieces, dgu_a, dgu_b, hidden_a, hidden_b),
        [like((width, 3 * hidden_w))], [], [vmem(s) for s in scratch], 20, 6)[0]


LATE_OUT, LATE_WIDTH = 192, 576


def late_middle_kernel(place, *refs):
    x_in, y_in, outs = refs[0:4], refs[4:8], refs[8:]
    ix, iz = place[1], place[2]
    rows = outs[0].shape[0]
    for offset in range(4):
        at = block_at(lax.rem(iz + 4 - offset, 4), rows)
        total = x_in[0][at, :].astype(F32)
        for ref in x_in[1:]:
            total += ref[at, :].astype(F32)
        outs[offset][...] = total.astype(BF16)
        to = lax.rem(ix + 4 - offset, 4)
        total = y_in[0][to].astype(F32)
        for ref in y_in[1:]:
            total += ref[to].astype(F32)
        outs[4 + offset][...] = total.astype(BF16)


def late_middle(place, along_x, along_z):
    _, rows, width = along_z[0].shape
    return pl.pallas_call(
        late_middle_kernel,
        out_shape=[like((rows, width))] * 8,
        in_specs=[scalars()] + [whole()] * 8,
        out_specs=[whole()] * 8,
        compiler_params=pltpu.CompilerParams(vmem_limit_bytes=16 * MIB),
        cost_estimate=SMALL,
        name="late_middle",
    )(place, *along_x, *along_z)


def late_last_kernel(place, *refs):
    x_in, y_in, keep_ref, send_ref = refs[0:4], refs[4:8], refs[8], refs[9]
    mine = place[3]
    rows = keep_ref.shape[0]
    for inputs, columns in ((x_in, slice(0, LATE_WIDTH)), (y_in, slice(LATE_WIDTH, 2 * LATE_WIDTH))):
        for ref, half in ((keep_ref, mine), (send_ref, 1 - mine)):
            at = block_at(half, rows)
            total = inputs[0][at, :].astype(F32)
            for other_ref in inputs[1:]:
                total += other_ref[at, :].astype(F32)
            ref[:, columns] = total.astype(ref.dtype)


def late_last(place, along_z, along_x):
    rows, width = along_x[0].shape
    return pl.pallas_call(
        late_last_kernel,
        out_shape=[
            jax.ShapeDtypeStruct((rows // 2, 2 * width), F32),
            jax.ShapeDtypeStruct((rows // 2, 2 * width), BF16),
        ],
        in_specs=[scalars()] + [whole()] * 8,
        out_specs=[whole()] * 2,
        compiler_params=pltpu.CompilerParams(vmem_limit_bytes=16 * MIB),
        cost_estimate=SMALL,
        name="late_last",
    )(place, *along_z, *along_x)


def norm_rows(values_in):
    factor = lax.rsqrt(jnp.mean(values_in * values_in, -1, keepdims=True) + norm_eps)
    return (values_in * factor, factor)


def norm_back(grad_in, normed, factor, gain_row):
    grad_normed = grad_in * gain_row
    inner = jnp.mean(grad_normed * normed, -1, keepdims=True)
    return factor * (grad_normed - normed * inner)


def from_offset(v, axis, offset, size):
    return lax.ppermute(v, axis, [((i + offset) % size, i) for i in range(size)])


def other(v, axis):
    return from_offset(v, axis, 1, 2)


def pair_rows(v, axis):
    it = other(v, axis)
    mine = jnp.arange(2)[:, None, None] == lax.axis_index(axis)
    return jnp.where(mine, v[None], it[None]).reshape(2 * v.shape[0], v.shape[1])


def side_by_side(parts, width):
    return sum(
        jnp.pad(part, ((0, 0), (at, width - at - part.shape[1]))) for at, part in parts
    )


def near_sum(own, core):
    return own.astype(F32) + other(core, "core").astype(F32)


def far_sum(chip, diagonal):
    return near_sum(chip, diagonal).astype(BF16)


def after(value, first):
    return lax.optimization_barrier((value, first))


def from_both(along_first, first_axis, along_second, second_axis, large, beside=()):
    near = [
        from_offset(part[i], axis, i, 4)
        for i in (1, 3)
        for part, axis in ((along_first, first_axis), (along_second, second_axis))
    ]
    opposite = along_first[2], along_second[2]
    if large:
        opposite, (near, beside) = after(opposite, (near, beside))
    far = [from_offset(opposite[0], first_axis, 2, 4), from_offset(opposite[1], second_axis, 2, 4)]
    near, far = after(near, far)
    first = [along_first[0], near[0], far[0], near[2]]
    second = [along_second[0], near[1], far[1], near[3]]
    return first, second, beside


def pair_sum(v, axis):
    rows = v.shape[0] // 2
    me = lax.axis_index(axis)
    keep = lax.dynamic_slice_in_dim(v, me * rows, rows, 0)
    send = lax.dynamic_slice_in_dim(v, (1 - me) * rows, rows, 0)
    return keep.astype(F32) + other(send, axis).astype(F32)


def body(tokens, norm_gains, w_query, w_keyval, w_out, w_gateup, w_down, cotangent):
    D = tokens.shape[1]
    length = 4 * tokens.shape[0]
    hidden_w = w_down.shape[0]
    heads_w = w_query.shape[1]
    gains_w = norm_gains.shape[1]
    block = lax.axis_index("yl") * 2 + lax.axis_index("core")
    place = jnp.stack(
        [block, lax.axis_index("x"), lax.axis_index("z"), lax.axis_index("yh")]
    ).astype(jnp.int32)

    out_t = w_out.T
    attn_own = side_by_side(
        [
            (OUT_AT, out_t[:, :OUT_CUT]),
            (QUERY_AT, w_query),
            (KEYVAL_AT, w_keyval),
            (REST_AT, out_t[:, OUT_CUT:]),
        ],
        ATTN_WIDTH,
    )
    attn_pair = pair_rows(attn_own, "yh")
    pair_w = 8 * gains_w
    gain_at = (lax.axis_index("yh") * 4 + block) * gains_w
    gain_part = lax.dynamic_update_slice(jnp.zeros((2, pair_w), F32), norm_gains, (0, gain_at))
    for axis in ("core", "yl", "yh"):
        gain_part = gain_part + other(gain_part, axis)
    (gate_up, down, tokens), gain_part = after((w_gateup, w_down, tokens), gain_part)
    mlp_own = (gate_up[:, 0], gate_up[:, 1], down.T)
    mlp_own = [(i * hidden_w, part) for i, part in enumerate(mlp_own)]
    mlp_pair = pair_rows(side_by_side(mlp_own, 3 * hidden_w), "yh")
    gain_part = gain_part.T
    gain_high = lax.reduce_precision(gain_part, 8, 7)
    gain_low = (gain_part - gain_high).astype(BF16)
    gain_high = gain_high.astype(BF16)
    first, second = attn_pair[:, :HALF_WIDTH], attn_pair[:, HALF_WIDTH:]
    first += side_by_side([(0, gain_high), (2, gain_low)], HALF_WIDTH)

    along_z, along_x, _ = from_both([first] * 4, "z", [second] * 4, "x", False)
    far = other(tokens, "yl")
    along_z, along_x, mlp_pair, far = lax.optimization_barrier(
        (jnp.stack(along_z), jnp.stack(along_x), mlp_pair, far)
    )
    mlp_w = lax.all_gather(mlp_pair, ("x", "z"), axis=0, tiled=True)
    along_x, along_z, _ = from_both([along_z] * 4, "x", [along_x] * 4, "z", False)
    token_pieces = [tokens, other(tokens, "core"), far, other(far, "core")]
    cotangent, far = after(cotangent, far)
    grad_far = other(cotangent, "yl")

    positions = jnp.arange(length).astype(F32)
    freqs = rope_base ** (-(jnp.arange(HD // 2).astype(F32) * 2.0 / HD))
    angles = freqs[:, None] * positions[None, :]
    cosine, sine = jnp.cos(angles), jnp.sin(angles)

    gain_rows, attn_w, h_first, qt, kt, vt, attn, probs, *parts = attend(
        place, token_pieces, along_x, along_z, cosine, sine
    )
    grad_far, parts = after(grad_far, parts)
    grad_pieces = [cotangent, other(cotangent, "core"), grad_far, other(grad_far, "core")]
    middle_far = far_sum(parts[2], parts[3])
    middle = (
        tokens.astype(F32) + near_sum(parts[0], parts[1]) + other(middle_far, "yl").astype(F32)
    )
    normed2, factor2 = norm_rows(middle)
    h_own = (normed2 * gain_rows[1]).astype(BF16)

    h_pieces = [h_own, other(h_own, "core")]
    h_far = other(h_own, "yl")
    hidden_a, dgu_a, back_own, back_core, out_own, out_core = feed(
        place, mlp_w, h_pieces, grad_pieces[:2]
    )
    h_far, hidden_a = after(h_far, hidden_a)
    h_pieces += [h_far, other(h_far, "core")]
    hidden_b, dgu_b, back_chip, back_diag, out_chip, out_diag = feed(
        place, mlp_w, h_pieces[2:], grad_pieces[2:]
    )
    back_core = other(back_core, "core")
    out_near = near_sum(out_own, out_core)

    back_far = far_sum(back_chip, back_diag)
    hidden_b, (back_far, back_core) = after(hidden_b, (back_far, back_core))
    mlp_grads = feed_grads(place, h_pieces, grad_pieces, dgu_a, dgu_b, hidden_a, hidden_b)
    mlp_grads, back_far = after(mlp_grads, other(back_far, "yl"))
    d_h2_own = back_own.astype(F32) + back_core.astype(F32) + back_far.astype(F32)
    early = lax.psum_scatter(mlp_grads, ("x", "z"), scatter_dimension=0, tiled=True)
    out_far = far_sum(out_chip, out_diag)

    d_norm2 = norm_back(d_h2_own, normed2, factor2, gain_rows[1])
    d_middle = cotangent.astype(F32) + d_norm2
    d_out = d_middle.astype(BF16)
    d_out_far = other(d_out, "yl")
    d_out_far, out_near = after(d_out_far, out_near)
    out_pieces = [d_out, other(d_out, "core"), d_out_far, other(d_out_far, "core")]
    out_far, out_pieces = after(out_far, out_pieces)
    out_far = other(out_far, "yl")

    back = attend_back(
        place, cosine, sine, out_pieces, attn_w, h_first, qt, kt, vt, attn, probs
    )
    d_qkv, *late_parts = back
    d_qkv, out_far = after(d_qkv, out_far)
    along_x, along_z, parts = from_both(
        late_parts[:4], "x", late_parts[4:], "z", True, project_back(place, d_qkv, attn_w)
    )
    d_far = other(far_sum(parts[2], parts[3]), "yl")
    result = (middle + out_near + out_far.astype(F32)).astype(BF16)
    along_x, result = after(along_x, result)
    middle_parts = late_middle(place, along_x, along_z)
    along_z, along_x, early = from_both(
        middle_parts[:4], "z", middle_parts[4:], "x", True, early
    )
    early = pair_sum(early, "yh")
    d_h1_own = near_sum(parts[0], parts[1]) + d_far.astype(F32)
    along_z, (d_h1_own, early) = after(along_z, (d_h1_own, early))
    late_keep, late_send = late_last(place, along_z, along_x)
    late = late_keep + other(late_send, "yh").astype(F32)

    normed1, factor1 = norm_rows(tokens.astype(F32))
    d_norm1 = norm_back(d_h1_own, normed1, factor1, gain_rows[0])
    input_grad = (d_middle + d_norm1).astype(BF16)

    grad_query = late[:, :heads_w]
    grad_keyval = late[:, 2 * LATE_WIDTH - heads_w :]
    grad_out = late[:, heads_w : 2 * LATE_WIDTH - heads_w].T
    grad_gateup = early[:, : 2 * hidden_w].reshape(-1, 2, hidden_w)

    gain_sum = jnp.stack(
        [
            jnp.sum(grad_query * w_query.astype(F32) + grad_keyval * w_keyval.astype(F32), 1),
            jnp.sum(grad_gateup * w_gateup.astype(F32), (1, 2)),
        ]
    )
    gain_sum = gain_sum + sum(
        lax.ppermute(gain_sum, ("yl", "core"), [(i ^ step, i) for i in range(4)])
        for step in (1, 2, 3)
    )
    grad_gains = lax.dynamic_slice(gain_sum, (0, block * gains_w), (2, gains_w)) / norm_gains
    return (
        result,
        input_grad,
        grad_query,
        grad_keyval,
        grad_out,
        grad_gateup,
        early[:, 2 * hidden_w :].T,
        grad_gains,
    )


def solution(mesh):
    fine = Mesh(mesh.devices.reshape(4, 4, 2, 2, 2), ("x", "z", "yh", "yl", "core"))
    dp = ("x", "z", "yh")
    tensor = ("yl", "core")
    every = dp + tensor
    weights = (P(dp, tensor), P(dp, tensor), P(tensor, dp), P(dp, None, tensor), P(tensor, dp))
    rows = P(every, None)
    gains = P(None, every)
    return jax.shard_map(
        body,
        mesh=fine,
        in_specs=(rows, gains) + weights + (rows,),
        out_specs=(rows, rows) + weights + (gains,),
        check_vma=False,
    )
```

```python
import jax
import jax.numpy as jnp
from jax import lax
from jax.experimental import pallas as pl
from jax.experimental.pallas import tpu as pltpu
from jax.sharding import Mesh, PartitionSpec as P

HD = 96
F32 = jnp.float32
BF16 = jnp.bfloat16
norm_eps = 1e-05
rope_base = 100000.0
LOG2E = 1.4426950408889634
SCALE = HD ** (-0.5)
MIB = 1024 * 1024
SMALL = pl.CostEstimate(flops=1, bytes_accessed=1, transcendentals=0)

QUERY_AT, KEYVAL_AT, OUT_AT, ATTN_WIDTH = 0, 384, 768, 1152
GAIN_WIDTH = 128
LIMIT = 60


def dot_n(left, right):
    return jnp.dot(left, right, preferred_element_type=F32)


def dot_t(left, right):
    return lax.dot_general(left, right, (((1,), (1,)), ((), ())), preferred_element_type=F32)


def dot_tn(left, right):
    return lax.dot_general(left, right, (((0,), (0,)), ((), ())), preferred_element_type=F32)


def dot_tt(left, right):
    return lax.dot_general(left, right, (((0,), (1,)), ((), ())), preferred_element_type=F32)


def block_at(index, size):
    return pl.ds(pl.multiple_of(index * size, size), size)


def causal_mask(scores, size):
    key_at = lax.broadcasted_iota(jnp.int32, (size, scores.shape[1]), 0)
    query_at = lax.broadcasted_iota(jnp.int32, (size, scores.shape[1]), 1) % size
    tail = jnp.where(key_at <= query_at, scores[-size:], -1e30)
    if scores.shape[0] == size:
        return tail
    return jnp.concatenate([scores[:-size], tail], 0)


class Moves:
    def __init__(self, sems):
        self.sems = sems
        self.started = []

    def start(self, source, target):
        copy = pltpu.make_async_copy(source, target, self.sems.at[len(self.started)])
        copy.start()
        self.started.append(copy)
        return copy

    def wait(self):
        for copy in self.started:
            copy.wait()


def vmem(shape, dtype=BF16):
    return pltpu.VMEM(shape, dtype)


def like(shape, dtype=BF16):
    return jax.ShapeDtypeStruct(shape, dtype)


def whole():
    return pl.BlockSpec(memory_space=pltpu.VMEM)


def apart():
    return pl.BlockSpec(memory_space=pl.ANY)


def scalars():
    return pl.BlockSpec(memory_space=pltpu.SMEM)


def kernel_call(kernel, name, place, small, large, outs, small_outs, scratch, *copies):
    return pl.pallas_call(
        kernel,
        out_shape=list(small_outs) + list(outs),
        in_specs=[scalars()] + [whole()] * len(small) + [apart()] * len(large),
        out_specs=[whole()] * len(small_outs) + [apart()] * len(outs),
        scratch_shapes=list(scratch)
        + [pltpu.SemaphoreType.DMA((count,)) for count in copies],
        compiler_params=pltpu.CompilerParams(vmem_limit_bytes=LIMIT * MIB),
        cost_estimate=SMALL,
        name=name,
    )(place, *small, *large)


def probs_at(step, size):
    return step * (step + 1) // 2 * size, (step + 1) * size


def head_rows(head):
    return slice(head * HD, (head + 1) * HD)


def attend_kernel(place, cos_ref, sin_ref, t0, t1, t2, t3, c0, c1, c2, c3, w_hbm, gains_ref, h_hbm, qt_hbm, kt_hbm, vt_hbm, attn_hbm, probs_hbm,
                  o0, o1, o2, o3, t_ref, c_ref, w_ref, h_ref, qt_ref, kt_ref, vt_ref, attn_ref, probs_ref, part_ref, k_ref,
                  in_sem, out_sem, probs_sem):
    block, ix, iz = place[0], place[1], place[2]
    half = HD // 2
    size = t_ref.shape[1]
    heads = qt_ref.shape[0]
    group_size = heads // kt_ref.shape[0]
    rows = c0.shape[1]
    fetch, store = Moves(in_sem), Moves(out_sem)
    gains_came = [
        fetch.start(
            piece.at[near],
            c_ref.at[block_at(lax.rem(ix + far, 4) * 4 + lax.rem(iz + near, 4), rows), :])
        for far, piece in enumerate((c0, c1, c2, c3)) for near in range(4)
    ]
    tokens_came = [
        fetch.start(piece, t_ref.at[i]) for i, piece in enumerate((t0, t1, t2, t3))
    ]
    parts = pl.ds(0, OUT_AT), pl.ds(OUT_AT, ATTN_WIDTH - OUT_AT)
    w_came = [fetch.start(w_hbm.at[:, part], w_ref.at[:, part]) for part in parts]
    for copy in gains_came:
        copy.wait()
    gains = c_ref[...].astype(F32).T
    gain_row = gains[0:1] + gains[2:3]
    gains_ref[...] = gains[0:2] + gains[2:4]
    for step in range(4):
        tokens_came[step].wait()
        value = t_ref[step].astype(F32)
        factor = lax.rsqrt(jnp.mean(value * value, -1, keepdims=True) + norm_eps)
        h_ref[block_at(lax.bitwise_xor(block, step), size), :] = (
            value * factor * gain_row).astype(BF16)
    w_came[0].wait()
    for step in range(4):
        at = slice(step * size, (step + 1) * size)
        normed = h_ref[at, :]
        cosine = cos_ref[:, at]
        sine = sin_ref[:, at]
        every = dot_n(normed, w_ref[:, QUERY_AT:OUT_AT]).T
        query, keyval = every[: KEYVAL_AT - QUERY_AT], every[KEYVAL_AT - QUERY_AT :]

        def rotated(field):
            first, second = field[:half], field[half:]
            return jnp.concatenate(
                [first * cosine - second * sine, second * cosine + first * sine], 0
            )

        for head in range(heads):
            qt_ref[head, :, at] = rotated(query[head_rows(head)]).astype(BF16)
        for group in range(heads // group_size):
            key = rotated(keyval[head_rows(2 * group)])
            kt_ref[group, :, at] = key.astype(BF16)
            k_ref[group, at, :] = key.T.astype(BF16)
            vt_ref[group, :, at] = keyval[head_rows(2 * group + 1)].astype(BF16)
    for source, target in ((h_ref, h_hbm), (qt_ref, qt_hbm), (kt_ref, kt_hbm), (vt_ref, vt_hbm)):
        store.start(source, target)

    def probs_copy(group):
        return pltpu.make_async_copy(
            probs_ref.at[group], probs_hbm.at[group], probs_sem.at[group])

    for group in range(heads // group_size):
        members = range(group * group_size, (group + 1) * group_size)
        for step in range(4):
            first, reach = probs_at(step, size)
            columns = slice(step * size, reach)
            query = jnp.concatenate([qt_ref[head, :, columns] for head in members], 1)
            scores = causal_mask(dot_n(k_ref[group, :reach, :], query), size)
            top = jnp.max(scores, 0, keepdims=True)
            expo = jnp.exp2((scores - top) * (SCALE * LOG2E))
            total = jnp.sum(expo, 0, keepdims=True)
            probs = (expo * (1.0 / total)).astype(BF16)
            probs_ref[group, first : first + reach, :] = probs
            mixed = dot_n(vt_ref[group, :, :reach], probs).astype(BF16)
            for i, head in enumerate(members):
                attn_ref[head_rows(head), columns] = mixed[:, i * size : (i + 1) * size]
        probs_copy(group).start()
    store.start(attn_ref, attn_hbm)
    w_came[1].wait()
    for step, out in ((1, o1), (3, o3), (2, o2), (0, o0)):
        at = block_at(lax.bitwise_xor(block, step), size)
        part_ref[step] = dot_tt(attn_ref[:, at], w_ref[:, OUT_AT:]).astype(BF16)
        store.start(part_ref.at[step], out)
    store.wait()
    for group in range(heads // group_size):
        probs_copy(group).wait()


def attend(place, pieces, gain_pieces, weights, cosine, sine):
    size, width = pieces[0].shape
    length = 4 * size
    heads = (KEYVAL_AT - QUERY_AT) // HD
    groups = (OUT_AT - KEYVAL_AT) // (2 * HD)
    columns, g_columns = (heads, HD, length), (groups, HD, length)
    probs = (groups, sum(probs_at(3, size)), heads // groups * size)
    kept = [(length, width), columns, g_columns, g_columns, (heads * HD, length), probs]
    return kernel_call(
        attend_kernel, "attend", place, (cosine, sine), (*pieces, *gain_pieces, weights),
        [like(s) for s in kept + [(size, width)] * 4], [like((2, width), F32)],
        [vmem(s) for s in [(4, size, width), (width, GAIN_WIDTH), weights.shape] + kept
         + [(4, size, width), (groups, length, HD)]],
        22, 9, groups)


def attend_back_kernel(place, cos_ref, sin_ref,
                       o0, o1, o2, o3, w_hbm, h_hbm, qt_hbm, kt_hbm, vt_hbm, attn_hbm, probs_hbm,
                       dqkv_hbm, x0, x1, x2, x3, y0, y1, y2, y3,
                       o_ref, w_ref, h_ref, qt_ref, kt_ref, vt_ref, attn_ref, probs_ref,
                       do_ref, dqkv_ref, first_ref, second_ref, v_ref, delta_ref, dk_ref, dv_ref,
                       in_sem, out_sem, probs_sem):
    block, ix, iz = place[0], place[1], place[2]
    heads, _, length = qt_ref.shape
    groups = kt_ref.shape[0]
    group_size = heads // groups
    size = length // 4
    half = HD // 2
    width = w_ref.shape[0]
    heads_w = heads * HD
    fetch, store = Moves(in_sem), Moves(out_sem)
    early = [fetch.start(w_hbm.at[:, pl.ds(OUT_AT, ATTN_WIDTH - OUT_AT)], w_ref)]
    early += [
        fetch.start(piece, o_ref.at[block_at(lax.bitwise_xor(block, i), size), :])
        for i, piece in enumerate((o0, o1, o2, o3))
    ]
    middle = [
        fetch.start(source, target)
        for source, target in ((attn_hbm, attn_ref), (vt_hbm, vt_ref), (qt_hbm, qt_ref),
                               (kt_hbm, kt_ref))
    ]

    def probs_copy(group):
        return pltpu.make_async_copy(
            probs_hbm.at[group], probs_ref.at[group], probs_sem.at[group])

    for group in range(groups):
        probs_copy(group).start()
    h_came = fetch.start(h_hbm, h_ref)
    for copy in early:
        copy.wait()
    do_ref[...] = dot_tt(w_ref[...], o_ref[...]).astype(BF16)
    for copy in middle:
        copy.wait()
    for group in range(groups):
        v_ref[group] = vt_ref[group].astype(F32).T.astype(BF16)
    for head in range(heads):
        rows = head_rows(head)
        delta_ref[head] = jnp.sum(
            attn_ref[rows, :].astype(F32) * do_ref[rows, :].astype(F32), 0, keepdims=True)

    def turned_back(field, cosine, sine):
        first, second = field[:half], field[half:]
        return jnp.concatenate(
            [first * cosine + second * sine, second * cosine - first * sine], 0).astype(BF16)

    for group in range(groups):
        members = range(group * group_size, (group + 1) * group_size)
        probs_copy(group).wait()
        for step in range(4):
            first, reach = probs_at(step, size)
            columns = slice(step * size, reach)
            probs = probs_ref[group, first : first + reach, :]
            query = jnp.concatenate([qt_ref[head, :, columns] for head in members], 1)
            d_out = jnp.concatenate([do_ref[head_rows(head), columns] for head in members], 1)
            delta = jnp.concatenate([delta_ref[head, :, columns] for head in members], 1)
            d_probs = dot_n(v_ref[group, :reach, :], d_out)
            d_scores = (probs.astype(F32) * (d_probs - delta)).astype(BF16)
            for ref, left, right in ((dv_ref, d_out, probs), (dk_ref, query, d_scores)):
                change = dot_t(left, right)
                if step > 0:
                    ref[group, :, : step * size] += change[:, : step * size]
                ref[group, :, columns] = change[:, columns]
            d_query = dot_n(kt_ref[group, :, :reach], d_scores) * SCALE
            for i, head in enumerate(members):
                dqkv_ref[head_rows(head), columns] = turned_back(
                    d_query[:, i * size : (i + 1) * size],
                    cos_ref[:, columns], sin_ref[:, columns])
        dqkv_ref[head_rows(heads + 2 * group), :] = turned_back(
            dk_ref[group] * SCALE, cos_ref[...], sin_ref[...])
        dqkv_ref[head_rows(heads + 2 * group + 1), :] = dv_ref[group].astype(BF16)
    store.start(dqkv_ref, dqkv_hbm)
    h_came.wait()

    rows = width // 16
    part = dot_tt(h_ref[...], dqkv_ref[...]).astype(BF16)
    first_ref[:, :heads_w] = part[:, :heads_w]
    second_ref[:, LATE_WIDTH - heads_w :] = part[:, heads_w:]
    part = dot_tt(o_ref[...], attn_ref[...]).astype(BF16)
    first_ref[:, heads_w:] = part[:, :LATE_OUT]
    second_ref[:, : heads_w - LATE_OUT] = part[:, LATE_OUT:]
    for offset, (x_out, y_out) in enumerate(((x0, y0), (x1, y1), (x2, y2), (x3, y3))):
        to_x = lax.rem(ix + 4 - offset, 4)
        to_z = lax.rem(iz + 4 - offset, 4)
        store.start(first_ref.at[block_at(to_x, 4 * rows), :], x_out)
        for i in range(4):
            store.start(second_ref.at[block_at(i * 4 + to_z, rows), :], y_out.at[i])
    store.wait()


def attend_back(place, cosine, sine, pieces, weights, h_first, qt, kt, vt, attn, probs):
    width = weights.shape[0]
    heads, _, length = qt.shape
    groups = kt.shape[0]
    every_w = (heads + 2 * groups) * HD
    rows = width // 16
    outs = [(every_w, length)] + [(4 * rows, LATE_WIDTH)] * 4 + [(4, rows, LATE_WIDTH)] * 4
    scratch = [
        (length, width), (width, heads * HD), (length, width),
        qt.shape, kt.shape, vt.shape, attn.shape, probs.shape,
        attn.shape, (every_w, length), (width, LATE_WIDTH), (width, LATE_WIDTH),
        (groups, length, HD),
    ]
    wide = [(heads, 1, length), kt.shape, kt.shape]
    return kernel_call(
        attend_back_kernel, "attend_back", place, (cosine, sine),
        (*pieces, weights, h_first, qt, kt, vt, attn, probs),
        [like(s) for s in outs], [],
        [vmem(s) for s in scratch] + [vmem(s, F32) for s in wide], 10, 21, groups)


def project_back_kernel(place, dqkv_hbm, w_hbm, c0, c1, c2, c3,
                        dqkv_ref, w_ref, part_ref, in_sem, out_sem):
    block = place[0]
    size = part_ref.shape[1]
    fetch, store = Moves(in_sem), Moves(out_sem)
    fetch.start(w_hbm.at[:, pl.ds(QUERY_AT, OUT_AT - QUERY_AT)], w_ref)
    fetch.start(dqkv_hbm, dqkv_ref)
    fetch.wait()
    for step, out in ((3, c3), (2, c2), (1, c1), (0, c0)):
        at = block_at(lax.bitwise_xor(block, step), size)
        part_ref[step] = dot_tt(dqkv_ref[:, at], w_ref[...]).astype(BF16)
        store.start(part_ref.at[step], out)
    store.wait()


def project_back(place, d_qkv, weights):
    every_w, length = d_qkv.shape
    width = weights.shape[0]
    size = length // 4
    return kernel_call(
        project_back_kernel, "project_back", place, (), (d_qkv, weights),
        [like((size, width))] * 4, [],
        [vmem(s) for s in (d_qkv.shape, (width, every_w), (4, size, width))], 2, 4)


def feed_kernel(place, h0, h1, g0, g1, a0, a1, a2, a3, b0, b1, b2, b3,
                hidden_hbm, dgu_hbm, back0, back1, out0, out1,
                w_ref, h_ref, g_ref, hidden_ref, dgu_ref, back_ref, out_ref, in_sem, out_sem):
    ix, iz = place[1], place[2]
    hidden_w = hidden_ref.shape[1]
    size = h_ref.shape[1]
    _, rows, half = b0.shape
    parts = [slice(i * hidden_w, (i + 1) * hidden_w) for i in range(3)]
    fetch, store = Moves(in_sem), Moves(out_sem)

    def weights(first, width):
        copies = []
        for far in range(4):
            for near in range(4):
                if first < half:
                    at = lax.rem(ix + far, 4) * 4 + lax.rem(iz + near, 4)
                    source = (a0, a1, a2, a3)[far].at[near, :, pl.ds(GAIN_WIDTH + first, width)]
                else:
                    at = lax.rem(ix + near, 4) * 4 + lax.rem(iz + far, 4)
                    source = (b0, b1, b2, b3)[far].at[near, :, pl.ds(first - half, width)]
                copies.append(
                    fetch.start(source, w_ref.at[block_at(at, rows), pl.ds(first, width)]))
        return copies

    came = [[fetch.start(h0, h_ref.at[0])] + weights(0, hidden_w)]
    came.append(weights(hidden_w, half - hidden_w) + weights(half, 2 * hidden_w - half))
    came.append([fetch.start(g0, g_ref.at[0])] + weights(2 * hidden_w, hidden_w))
    came.append([fetch.start(h1, h_ref.at[1]), fetch.start(g1, g_ref.at[1])])

    def wait(group):
        for copy in came[group]:
            copy.wait()

    for i, (back, out) in enumerate(((back0, out0), (back1, out1))):
        at = pl.ds(i * size, size)
        rows_at = slice(i * size, (i + 1) * size)
        wait(3 if i else 0)
        gate = dot_n(h_ref[i], w_ref[:, parts[0]])
        if i == 0:
            wait(1)
        up = dot_n(h_ref[i], w_ref[:, parts[1]])
        sig = 1.0 / (1.0 + jnp.exp2(gate * (-LOG2E)))
        silu = gate * sig
        hidden = (silu * up).astype(BF16)
        hidden_ref[rows_at, :] = hidden
        store.start(hidden_ref.at[at, :], hidden_hbm.at[at, :])
        if i == 0:
            wait(2)
        d_hidden = dot_n(g_ref[i], w_ref[:, parts[2]])
        dgu_ref[rows_at, :hidden_w] = (
            d_hidden * up * (sig * (1.0 + gate * (1.0 - sig)))).astype(BF16)
        dgu_ref[rows_at, hidden_w:] = (d_hidden * silu).astype(BF16)
        store.start(dgu_ref.at[at, :], dgu_hbm.at[at, :])
        back_ref[i] = dot_t(dgu_ref[rows_at, :], w_ref[:, : 2 * hidden_w]).astype(BF16)
        store.start(back_ref.at[i], back)
        out_ref[i] = dot_t(hidden_ref[rows_at, :], w_ref[:, parts[2]]).astype(BF16)
        store.start(out_ref.at[i], out)
    store.wait()


def feed(place, along_x, along_z, normed_pieces, grad_pieces):
    size, width = normed_pieces[0].shape
    hidden_w = 2 * along_z[0].shape[2] // 3
    wide = [(2 * size, hidden_w), (2 * size, 2 * hidden_w)]
    return kernel_call(
        feed_kernel, "feed", place, (), (*normed_pieces, *grad_pieces, *along_x, *along_z),
        [like(s) for s in wide + [(size, width)] * 4], [],
        [vmem(s) for s in [(width, 3 * hidden_w)] + [(2, size, width)] * 2 + wide
         + [(2, size, width)] * 2],
        68, 8)


def feed_grads_kernel(place, h0, h1, h2, h3, g0, g1, g2, g3, dgu_a, dgu_b, hidden_a, hidden_b,
                      out_hbm, h_ref, g_ref, dgu_ref, hidden_ref, out_ref, in_sem, out_sem):
    del place
    size = h0.shape[0]
    half, hidden_w = hidden_a.shape
    column = 512
    fetch, store = Moves(in_sem), Moves(out_sem)

    def rows_of(pieces, ref):
        return [
            fetch.start(piece, ref.at[pl.ds(i * size, size), :]) for i, piece in enumerate(pieces)
        ]

    def tiles_of(pieces, ref):
        tiles = []
        for tile in range(ref.shape[1] // column):
            at = pl.ds(tile * column, column)
            tiles.append([
                fetch.start(piece.at[:, at], ref.at[pl.ds(i * half, half), at])
                for i, piece in enumerate(pieces)
            ])
        return tiles

    h_came = rows_of((h0, h1, h2, h3), h_ref)
    dgu_came = tiles_of((dgu_a, dgu_b), dgu_ref)
    g_came = rows_of((g0, g1, g2, g3), g_ref)
    hidden_came = tiles_of((hidden_a, hidden_b), hidden_ref)
    at = 0
    for came, left, tiles, right in (
        (h_came, h_ref, dgu_came, dgu_ref), (g_came, g_ref, hidden_came, hidden_ref)
    ):
        for copy in came:
            copy.wait()
        for tile, copies in enumerate(tiles):
            for copy in copies:
                copy.wait()
            columns = pl.ds(at, column)
            out_ref[:, columns] = dot_tn(
                left[...], right[:, tile * column : (tile + 1) * column]).astype(BF16)
            store.start(out_ref.at[:, columns], out_hbm.at[:, columns])
            at += column
    store.wait()


def feed_grads(place, normed_pieces, grad_pieces, dgu_a, dgu_b, hidden_a, hidden_b):
    size, width = normed_pieces[0].shape
    half, hidden_w = hidden_a.shape
    scratch = [(4 * size, width)] * 2 + [(2 * half, 2 * hidden_w), (2 * half, hidden_w),
                                         (width, 3 * hidden_w)]
    return kernel_call(
        feed_grads_kernel, "feed_grads", place, (),
        (*normed_pieces, *grad_pieces, dgu_a, dgu_b, hidden_a, hidden_b),
        [like((width, 3 * hidden_w))], [], [vmem(s) for s in scratch], 20, 6)[0]


LATE_OUT, LATE_WIDTH = 192, 576


def late_middle_kernel(place, *refs):
    x_in, y_in, outs = refs[0:4], refs[4:8], refs[8:]
    ix, iz = place[1], place[2]
    rows = outs[0].shape[0]
    for offset in range(4):
        at = block_at(lax.rem(iz + 4 - offset, 4), rows)
        total = x_in[0][at, :].astype(F32)
        for ref in x_in[1:]:
            total += ref[at, :].astype(F32)
        outs[offset][...] = total.astype(BF16)
        to = lax.rem(ix + 4 - offset, 4)
        total = y_in[0][to].astype(F32)
        for ref in y_in[1:]:
            total += ref[to].astype(F32)
        outs[4 + offset][...] = total.astype(BF16)


def late_middle(place, along_x, along_z):
    _, rows, width = along_z[0].shape
    return pl.pallas_call(
        late_middle_kernel,
        out_shape=[like((rows, width))] * 8,
        in_specs=[scalars()] + [whole()] * 8,
        out_specs=[whole()] * 8,
        compiler_params=pltpu.CompilerParams(vmem_limit_bytes=16 * MIB),
        cost_estimate=SMALL,
        name="late_middle",
    )(place, *along_x, *along_z)


def late_last_kernel(place, *refs):
    x_in, y_in, keep_ref, send_ref = refs[0:4], refs[4:8], refs[8], refs[9]
    mine = place[3]
    rows = keep_ref.shape[0]
    for inputs, columns in ((x_in, slice(0, LATE_WIDTH)), (y_in, slice(LATE_WIDTH, 2 * LATE_WIDTH))):
        for ref, half in ((keep_ref, mine), (send_ref, 1 - mine)):
            at = block_at(half, rows)
            total = inputs[0][at, :].astype(F32)
            for other_ref in inputs[1:]:
                total += other_ref[at, :].astype(F32)
            ref[:, columns] = total.astype(ref.dtype)


def late_last(place, along_z, along_x):
    rows, width = along_x[0].shape
    return pl.pallas_call(
        late_last_kernel,
        out_shape=[
            jax.ShapeDtypeStruct((rows // 2, 2 * width), F32),
            jax.ShapeDtypeStruct((rows // 2, 2 * width), BF16),
        ],
        in_specs=[scalars()] + [whole()] * 8,
        out_specs=[whole()] * 2,
        compiler_params=pltpu.CompilerParams(vmem_limit_bytes=16 * MIB),
        cost_estimate=SMALL,
        name="late_last",
    )(place, *along_z, *along_x)


def norm_rows(values_in):
    factor = lax.rsqrt(jnp.mean(values_in * values_in, -1, keepdims=True) + norm_eps)
    return (values_in * factor, factor)


def norm_back(grad_in, normed, factor, gain_row):
    grad_normed = grad_in * gain_row
    inner = jnp.mean(grad_normed * normed, -1, keepdims=True)
    return factor * (grad_normed - normed * inner)


def from_offset(v, axis, offset, size):
    return lax.ppermute(v, axis, [((i + offset) % size, i) for i in range(size)])


def other(v, axis):
    return from_offset(v, axis, 1, 2)


def pair_rows(v, axis):
    it = other(v, axis)
    mine = jnp.arange(2)[:, None, None] == lax.axis_index(axis)
    return jnp.where(mine, v[None], it[None]).reshape(2 * v.shape[0], v.shape[1])


def side_by_side(parts, width):
    return sum(
        jnp.pad(part, ((0, 0), (at, width - at - part.shape[1]))) for at, part in parts
    )


def near_sum(own, core):
    return own.astype(F32) + other(core, "core").astype(F32)


def far_sum(chip, diagonal):
    return near_sum(chip, diagonal).astype(BF16)


def after(value, first):
    return lax.optimization_barrier((value, first))


def from_both(along_first, first_axis, along_second, second_axis, large, beside=()):
    near = [
        from_offset(part[i], axis, i, 4)
        for i in (1, 3)
        for part, axis in ((along_first, first_axis), (along_second, second_axis))
    ]
    opposite = along_first[2], along_second[2]
    if large:
        opposite, (near, beside) = after(opposite, (near, beside))
    far = [from_offset(opposite[0], first_axis, 2, 4), from_offset(opposite[1], second_axis, 2, 4)]
    near, far = after(near, far)
    first = [along_first[0], near[0], far[0], near[2]]
    second = [along_second[0], near[1], far[1], near[3]]
    return first, second, beside


def pair_sum(v, axis):
    rows = v.shape[0] // 2
    me = lax.axis_index(axis)
    keep = lax.dynamic_slice_in_dim(v, me * rows, rows, 0)
    send = lax.dynamic_slice_in_dim(v, (1 - me) * rows, rows, 0)
    return keep.astype(F32) + other(send, axis).astype(F32)


def body(tokens, norm_gains, w_query, w_keyval, w_out, w_gateup, w_down, cotangent):
    D = tokens.shape[1]
    length = 4 * tokens.shape[0]
    hidden_w = w_down.shape[0]
    heads_w = w_query.shape[1]
    gains_w = norm_gains.shape[1]
    block = lax.axis_index("yl") * 2 + lax.axis_index("core")
    place = jnp.stack(
        [block, lax.axis_index("x"), lax.axis_index("z"), lax.axis_index("yh")]
    ).astype(jnp.int32)

    attn_own = side_by_side(
        [(QUERY_AT, w_query), (KEYVAL_AT, w_keyval), (OUT_AT, w_out.T)], ATTN_WIDTH
    )
    attn_pair = pair_rows(attn_own, "yh")

    attn_w = lax.all_gather(attn_pair, ("x", "z"), axis=0, tiled=True)

    gain_part = lax.dynamic_update_slice(
        jnp.zeros((2, 4 * gains_w), F32), norm_gains, (0, block * gains_w))
    for axis in ("core", "yl"):
        gain_part = gain_part + other(gain_part, axis)
    (gate_up, down, tokens), gain_part = after((w_gateup, w_down, tokens), gain_part)
    gain_part = gain_part.T
    gain_high = lax.reduce_precision(gain_part, 8, 7)
    gain_low = (gain_part - gain_high).astype(BF16)
    mlp_own = [(0, gain_high.astype(BF16)), (2, gain_low)] + [
        (GAIN_WIDTH + i * hidden_w, part)
        for i, part in enumerate((gate_up[:, 0], gate_up[:, 1], down.T))
    ]
    width = GAIN_WIDTH + 3 * hidden_w
    mlp_pair = pair_rows(side_by_side(mlp_own, width), "yh")
    half = GAIN_WIDTH + 3 * hidden_w // 2
    first, second = mlp_pair[:, :half], mlp_pair[:, half:]
    along_z, along_x, _ = from_both([first] * 4, "z", [second] * 4, "x", False)
    mlp_z, mlp_x = after(jnp.stack(along_z), jnp.stack(along_x))
    gain_own = mlp_z[:, :, :GAIN_WIDTH]
    gain_pieces = [gain_own] + [from_offset(gain_own, "x", i, 4) for i in (1, 2, 3)]

    far = other(tokens, "yl")
    token_pieces = [tokens, other(tokens, "core"), far, other(far, "core")]
    cotangent, far = after(cotangent, far)
    grad_far = other(cotangent, "yl")
    positions = jnp.arange(length).astype(F32)
    freqs = rope_base ** (-(jnp.arange(HD // 2).astype(F32) * 2.0 / HD))
    angles = freqs[:, None] * positions[None, :]
    cosine, sine = jnp.cos(angles), jnp.sin(angles)

    (mlp_z, mlp_x), (attn_w, gain_pieces, token_pieces, cosine, sine) = after(
        (mlp_z, mlp_x), (attn_w, gain_pieces, token_pieces, cosine, sine))
    mlp_near = [
        from_offset(v, axis, i, 4) for i in (1, 3) for v, axis in ((mlp_z, "x"), (mlp_x, "z"))]

    gain_rows, h_first, qt, kt, vt, attn, probs, *parts = attend(
        place, token_pieces, gain_pieces, attn_w, cosine, sine
    )
    grad_far, parts = after(grad_far, parts)
    grad_pieces = [cotangent, other(cotangent, "core"), grad_far, other(grad_far, "core")]
    diagonal, mlp_near = after(other(parts[3], "core"), mlp_near)
    middle_far = (parts[2].astype(F32) + diagonal.astype(F32)).astype(BF16)
    mlp_z, mlp_x = after((mlp_z, mlp_x), mlp_near)[0]
    along_x = [mlp_z, mlp_near[0], from_offset(mlp_z, "x", 2, 4), mlp_near[2]]
    along_z = [mlp_x, mlp_near[1], from_offset(mlp_x, "z", 2, 4), mlp_near[3]]
    middle = (
        tokens.astype(F32) + near_sum(parts[0], parts[1]) + other(middle_far, "yl").astype(F32)
    )
    normed2, factor2 = norm_rows(middle)
    h_own = (normed2 * gain_rows[1]).astype(BF16)

    h_pieces = [h_own, other(h_own, "core")]
    h_far = other(h_own, "yl")
    hidden_a, dgu_a, back_own, back_core, out_own, out_core = feed(
        place, along_x, along_z, h_pieces, grad_pieces[:2]
    )
    h_far, hidden_a = after(h_far, hidden_a)
    h_pieces += [h_far, other(h_far, "core")]
    hidden_b, dgu_b, back_chip, back_diag, out_chip, out_diag = feed(
        place, along_x, along_z, h_pieces[2:], grad_pieces[2:]
    )
    back_core = other(back_core, "core")
    out_near = near_sum(out_own, out_core)

    back_far = far_sum(back_chip, back_diag)
    hidden_b, (back_far, back_core) = after(hidden_b, (back_far, back_core))
    mlp_grads = feed_grads(place, h_pieces, grad_pieces, dgu_a, dgu_b, hidden_a, hidden_b)
    mlp_grads, back_far = after(mlp_grads, other(back_far, "yl"))
    d_h2_own = back_own.astype(F32) + back_core.astype(F32) + back_far.astype(F32)
    early = lax.psum_scatter(mlp_grads, ("x", "z"), scatter_dimension=0, tiled=True)
    out_far = far_sum(out_chip, out_diag)

    d_norm2 = norm_back(d_h2_own, normed2, factor2, gain_rows[1])
    d_middle = cotangent.astype(F32) + d_norm2
    d_out = d_middle.astype(BF16)
    d_out_far = other(d_out, "yl")
    d_out_far, out_near = after(d_out_far, out_near)
    out_pieces = [d_out, other(d_out, "core"), d_out_far, other(d_out_far, "core")]
    out_far, out_pieces = after(out_far, out_pieces)
    out_far = other(out_far, "yl")

    back = attend_back(
        place, cosine, sine, out_pieces, attn_w, h_first, qt, kt, vt, attn, probs
    )
    d_qkv, *late_parts = back
    d_qkv, out_far = after(d_qkv, out_far)
    along_x, along_z, parts = from_both(
        late_parts[:4], "x", late_parts[4:], "z", True, project_back(place, d_qkv, attn_w)
    )
    d_far = other(far_sum(parts[2], parts[3]), "yl")
    result = (middle + out_near + out_far.astype(F32)).astype(BF16)
    along_x, result = after(along_x, result)
    middle_parts = late_middle(place, along_x, along_z)
    along_z, along_x, early = from_both(
        middle_parts[:4], "z", middle_parts[4:], "x", True, early
    )
    early = pair_sum(early, "yh")
    d_h1_own = near_sum(parts[0], parts[1]) + d_far.astype(F32)
    along_z, (d_h1_own, early) = after(along_z, (d_h1_own, early))
    late_keep, late_send = late_last(place, along_z, along_x)
    late = late_keep + other(late_send, "yh").astype(F32)

    normed1, factor1 = norm_rows(tokens.astype(F32))
    d_norm1 = norm_back(d_h1_own, normed1, factor1, gain_rows[0])
    input_grad = (d_middle + d_norm1).astype(BF16)

    grad_query = late[:, :heads_w]
    grad_keyval = late[:, 2 * LATE_WIDTH - heads_w :]
    grad_out = late[:, heads_w : 2 * LATE_WIDTH - heads_w].T
    grad_gateup = early[:, : 2 * hidden_w].reshape(-1, 2, hidden_w)

    gain_sum = jnp.stack(
        [
            jnp.sum(grad_query * w_query.astype(F32) + grad_keyval * w_keyval.astype(F32), 1),
            jnp.sum(grad_gateup * w_gateup.astype(F32), (1, 2)),
        ]
    )
    gain_sum = gain_sum + sum(
        lax.ppermute(gain_sum, ("yl", "core"), [(i ^ step, i) for i in range(4)])
        for step in (1, 2, 3)
    )
    grad_gains = lax.dynamic_slice(gain_sum, (0, block * gains_w), (2, gains_w)) / norm_gains
    return (
        result,
        input_grad,
        grad_query,
        grad_keyval,
        grad_out,
        grad_gateup,
        early[:, 2 * hidden_w :].T,
        grad_gains,
    )


def solution(mesh):
    fine = Mesh(mesh.devices.reshape(4, 4, 2, 2, 2), ("x", "z", "yh", "yl", "core"))
    dp = ("x", "z", "yh")
    tensor = ("yl", "core")
    every = dp + tensor
    weights = (P(dp, tensor), P(dp, tensor), P(tensor, dp), P(dp, None, tensor), P(tensor, dp))
    rows = P(every, None)
    gains = P(None, every)
    return jax.shard_map(
        body,
        mesh=fine,
        in_specs=(rows, gains) + weights + (rows,),
        out_specs=(rows, rows) + weights + (gains,),
        check_vma=False,
    )
```

```python
import jax
import jax.numpy as jnp
from jax import lax
from jax.experimental import pallas as pl
from jax.experimental.pallas import tpu as pltpu
from jax.sharding import Mesh, PartitionSpec as P

HD = 96
F32 = jnp.float32
BF16 = jnp.bfloat16
norm_eps = 1e-05
rope_base = 100000.0
LOG2E = 1.4426950408889634
SCALE = HD ** (-0.5)
MIB = 1024 * 1024
SMALL = pl.CostEstimate(flops=1, bytes_accessed=1, transcendentals=0)

GAIN_AT, OUT_AT, QUERY_AT, KEYVAL_AT, REST_AT, ATTN_WIDTH = 0, 128, 256, 640, 1024, 1280
HALF_WIDTH = ATTN_WIDTH // 2
OUT_CUT = QUERY_AT - OUT_AT
LIMIT = 60


def dot_n(left, right):
    return jnp.dot(left, right, preferred_element_type=F32)


def dot_t(left, right):
    return lax.dot_general(left, right, (((1,), (1,)), ((), ())), preferred_element_type=F32)


def dot_tn(left, right):
    return lax.dot_general(left, right, (((0,), (0,)), ((), ())), preferred_element_type=F32)


def dot_tt(left, right):
    return lax.dot_general(left, right, (((0,), (1,)), ((), ())), preferred_element_type=F32)


def block_at(index, size):
    return pl.ds(pl.multiple_of(index * size, size), size)


def causal_mask(scores, size):
    key_at = lax.broadcasted_iota(jnp.int32, (size, scores.shape[1]), 0)
    query_at = lax.broadcasted_iota(jnp.int32, (size, scores.shape[1]), 1) % size
    tail = jnp.where(key_at <= query_at, scores[-size:], -1e30)
    if scores.shape[0] == size:
        return tail
    return jnp.concatenate([scores[:-size], tail], 0)


class Moves:
    def __init__(self, sems):
        self.sems = sems
        self.started = []

    def start(self, source, target):
        copy = pltpu.make_async_copy(source, target, self.sems.at[len(self.started)])
        copy.start()
        self.started.append(copy)
        return copy

    def wait(self):
        for copy in self.started:
            copy.wait()


def vmem(shape, dtype=BF16):
    return pltpu.VMEM(shape, dtype)


def like(shape, dtype=BF16):
    return jax.ShapeDtypeStruct(shape, dtype)


def whole():
    return pl.BlockSpec(memory_space=pltpu.VMEM)


def apart():
    return pl.BlockSpec(memory_space=pl.ANY)


def scalars():
    return pl.BlockSpec(memory_space=pltpu.SMEM)


def kernel_call(kernel, name, place, small, large, outs, small_outs, scratch, *copies):
    return pl.pallas_call(
        kernel,
        out_shape=list(small_outs) + list(outs),
        in_specs=[scalars()] + [whole()] * len(small) + [apart()] * len(large),
        out_specs=[whole()] * len(small_outs) + [apart()] * len(outs),
        scratch_shapes=list(scratch)
        + [pltpu.SemaphoreType.DMA((count,)) for count in copies],
        compiler_params=pltpu.CompilerParams(vmem_limit_bytes=LIMIT * MIB),
        cost_estimate=SMALL,
        name=name,
    )(place, *small, *large)


def probs_at(step, size):
    return step * (step + 1) // 2 * size, (step + 1) * size


def head_rows(head):
    return slice(head * HD, (head + 1) * HD)


def attend_kernel(place, cos_ref, sin_ref, t0, t1, t2, t3, a0, a1, a2, a3, b0, b1, b2, b3,
                  gains_ref, w_hbm, h_hbm, qt_hbm, kt_hbm, vt_hbm, attn_hbm, probs_hbm,
                  o0, o1, o2, o3,
                  t_ref, w_ref, h_ref, qt_ref, kt_ref, vt_ref, attn_ref, probs_ref, part_ref, k_ref,
                  in_sem, out_sem, probs_sem):
    block, ix, iz = place[0], place[1], place[2]
    half = HD // 2
    size = t_ref.shape[1]
    heads = qt_ref.shape[0]
    group_size = heads // kt_ref.shape[0]
    rows = a0.shape[1]
    fetch, store = Moves(in_sem), Moves(out_sem)
    gains_came, came = [], []
    for far, (along_x, along_z) in enumerate(zip((a0, a1, a2, a3), (b0, b1, b2, b3))):
        for near in range(4):
            at_a = block_at(lax.rem(ix + far, 4) * 4 + lax.rem(iz + near, 4), rows)
            at_b = block_at(lax.rem(ix + near, 4) * 4 + lax.rem(iz + far, 4), rows)
            for source, first, width, target, copies in (
                (along_x, 0, OUT_AT, at_a, gains_came),
                (along_x, OUT_AT, HALF_WIDTH - OUT_AT, at_a, came),
                (along_z, HALF_WIDTH, HALF_WIDTH, at_b, came),
            ):
                copies.append((
                    source.at[near, :, pl.ds(first % HALF_WIDTH, width)],
                    w_ref.at[target, pl.ds(first, width)],
                ))
    gains_came = [fetch.start(*copy) for copy in gains_came]
    tokens_came = [
        fetch.start(piece, t_ref.at[i]) for i, piece in enumerate((t0, t1, t2, t3))
    ]
    came = [fetch.start(*copy) for copy in came]
    for copy in gains_came:
        copy.wait()
    gains = w_ref[:, GAIN_AT:OUT_AT].astype(F32).T
    gain_row = gains[0:1] + gains[2:3]
    gains_ref[...] = gains[0:2] + gains[2:4]
    for step in range(4):
        tokens_came[step].wait()
        value = t_ref[step].astype(F32)
        factor = lax.rsqrt(jnp.mean(value * value, -1, keepdims=True) + norm_eps)
        h_ref[block_at(lax.bitwise_xor(block, step), size), :] = (
            value * factor * gain_row).astype(BF16)
    for copy in came:
        copy.wait()
    store.start(w_ref, w_hbm)
    for step in range(4):
        at = slice(step * size, (step + 1) * size)
        normed = h_ref[at, :]
        cosine = cos_ref[:, at]
        sine = sin_ref[:, at]
        every = dot_n(normed, w_ref[:, QUERY_AT:REST_AT]).T
        query, keyval = every[: KEYVAL_AT - QUERY_AT], every[KEYVAL_AT - QUERY_AT :]

        def rotated(field):
            first, second = field[:half], field[half:]
            return jnp.concatenate(
                [first * cosine - second * sine, second * cosine + first * sine], 0
            )

        for head in range(heads):
            qt_ref[head, :, at] = rotated(query[head_rows(head)]).astype(BF16)
        for group in range(heads // group_size):
            key = rotated(keyval[head_rows(2 * group)])
            kt_ref[group, :, at] = key.astype(BF16)
            k_ref[group, at, :] = key.T.astype(BF16)
            vt_ref[group, :, at] = keyval[head_rows(2 * group + 1)].astype(BF16)
    for source, target in ((h_ref, h_hbm), (qt_ref, qt_hbm), (kt_ref, kt_hbm), (vt_ref, vt_hbm)):
        store.start(source, target)

    def probs_copy(group):
        return pltpu.make_async_copy(
            probs_ref.at[group], probs_hbm.at[group], probs_sem.at[group])

    for group in range(heads // group_size):
        members = range(group * group_size, (group + 1) * group_size)
        for step in range(4):
            first, reach = probs_at(step, size)
            columns = slice(step * size, reach)
            query = jnp.concatenate([qt_ref[head, :, columns] for head in members], 1)
            scores = causal_mask(dot_n(k_ref[group, :reach, :], query), size)
            top = jnp.max(scores, 0, keepdims=True)
            expo = jnp.exp2((scores - top) * (SCALE * LOG2E))
            total = jnp.sum(expo, 0, keepdims=True)
            probs = (expo * (1.0 / total)).astype(BF16)
            probs_ref[group, first : first + reach, :] = probs
            mixed = dot_n(vt_ref[group, :, :reach], probs).astype(BF16)
            for i, head in enumerate(members):
                attn_ref[head_rows(head), columns] = mixed[:, i * size : (i + 1) * size]
        probs_copy(group).start()
    store.start(attn_ref, attn_hbm)
    for step, out in ((1, o1), (3, o3), (2, o2), (0, o0)):
        at = block_at(lax.bitwise_xor(block, step), size)
        part = dot_tt(attn_ref[:OUT_CUT, at], w_ref[:, OUT_AT:QUERY_AT])
        part += dot_tt(attn_ref[OUT_CUT:, at], w_ref[:, REST_AT:])
        part_ref[step] = part.astype(BF16)
        store.start(part_ref.at[step], out)
    store.wait()
    for group in range(heads // group_size):
        probs_copy(group).wait()


def attend(place, pieces, along_x, along_z, cosine, sine):
    size, width = pieces[0].shape
    length = 4 * size
    heads = (KEYVAL_AT - QUERY_AT) // HD
    groups = (REST_AT - KEYVAL_AT) // (2 * HD)
    columns, g_columns = (heads, HD, length), (groups, HD, length)
    probs = (groups, sum(probs_at(3, size)), heads // groups * size)
    kept = [(width, ATTN_WIDTH), (length, width), columns, g_columns, g_columns,
            (heads * HD, length), probs]
    return kernel_call(
        attend_kernel, "attend", place, (cosine, sine), (*pieces, *along_x, *along_z),
        [like(s) for s in kept + [(size, width)] * 4], [like((2, width), F32)],
        [vmem(s) for s in [(4, size, width)] + kept + [(4, size, width), (groups, length, HD)]],
        52, 10, groups)


def attend_back_kernel(place, cos_ref, sin_ref,
                       o0, o1, o2, o3, w_hbm, h_hbm, qt_hbm, kt_hbm, vt_hbm, attn_hbm, probs_hbm,
                       keep_hbm, send_hbm, y0, y1, y2, y3, c0, c1, c2, c3,
                       o_ref, w_ref, h_ref, qt_ref, kt_ref, vt_ref, attn_ref, probs_ref,
                       do_ref, dqkv_ref, first_ref, second_ref, v_ref, proj_ref, part_ref, delta_ref, dk_ref, dv_ref,
                       in_sem, out_sem, probs_sem):
    block, iz, mine = place[0], place[2], place[3]
    heads, _, length = qt_ref.shape
    groups = kt_ref.shape[0]
    group_size = heads // groups
    size = length // 4
    half = HD // 2
    width = w_ref.shape[0]
    heads_w = heads * HD
    fetch, store = Moves(in_sem), Moves(out_sem)
    rest_w = ATTN_WIDTH - REST_AT
    early = [
        fetch.start(w_hbm.at[:, pl.ds(OUT_AT, OUT_CUT)], w_ref.at[:, pl.ds(0, OUT_CUT)]),
        fetch.start(w_hbm.at[:, pl.ds(REST_AT, rest_w)], w_ref.at[:, pl.ds(OUT_CUT, rest_w)]),
    ]
    early += [
        fetch.start(piece, o_ref.at[block_at(lax.bitwise_xor(block, i), size), :])
        for i, piece in enumerate((o0, o1, o2, o3))
    ]
    middle = [
        fetch.start(source, target)
        for source, target in ((attn_hbm, attn_ref), (vt_hbm, vt_ref), (qt_hbm, qt_ref),
                               (kt_hbm, kt_ref))
    ]

    def probs_copy(group):
        return pltpu.make_async_copy(
            probs_hbm.at[group], probs_ref.at[group], probs_sem.at[group])

    for group in range(groups):
        probs_copy(group).start()
    h_came = fetch.start(h_hbm, h_ref)
    proj_came = fetch.start(w_hbm.at[:, pl.ds(QUERY_AT, REST_AT - QUERY_AT)], proj_ref)
    for copy in early:
        copy.wait()
    do_ref[...] = dot_tt(w_ref[...], o_ref[...]).astype(BF16)
    for copy in middle:
        copy.wait()
    for group in range(groups):
        v_ref[group] = vt_ref[group].astype(F32).T.astype(BF16)
    for head in range(heads):
        rows = head_rows(head)
        delta_ref[head] = jnp.sum(
            attn_ref[rows, :].astype(F32) * do_ref[rows, :].astype(F32), 0, keepdims=True)

    def turned_back(field, cosine, sine):
        first, second = field[:half], field[half:]
        return jnp.concatenate(
            [first * cosine + second * sine, second * cosine - first * sine], 0).astype(BF16)

    for group in range(groups):
        members = range(group * group_size, (group + 1) * group_size)
        probs_copy(group).wait()
        for step in range(4):
            first, reach = probs_at(step, size)
            columns = slice(step * size, reach)
            probs = probs_ref[group, first : first + reach, :]
            query = jnp.concatenate([qt_ref[head, :, columns] for head in members], 1)
            d_out = jnp.concatenate([do_ref[head_rows(head), columns] for head in members], 1)
            delta = jnp.concatenate([delta_ref[head, :, columns] for head in members], 1)
            d_probs = dot_n(v_ref[group, :reach, :], d_out)
            d_scores = (probs.astype(F32) * (d_probs - delta)).astype(BF16)
            for ref, left, right in ((dv_ref, d_out, probs), (dk_ref, query, d_scores)):
                change = dot_t(left, right)
                if step > 0:
                    ref[group, :, : step * size] += change[:, : step * size]
                ref[group, :, columns] = change[:, columns]
            d_query = dot_n(kt_ref[group, :, :reach], d_scores) * SCALE
            for i, head in enumerate(members):
                dqkv_ref[head_rows(head), columns] = turned_back(
                    d_query[:, i * size : (i + 1) * size],
                    cos_ref[:, columns], sin_ref[:, columns])
        dqkv_ref[head_rows(heads + 2 * group), :] = turned_back(
            dk_ref[group] * SCALE, cos_ref[...], sin_ref[...])
        dqkv_ref[head_rows(heads + 2 * group + 1), :] = dv_ref[group].astype(BF16)
    h_came.wait()

    rows = width // 16
    part = dot_tt(h_ref[...], dqkv_ref[...]).astype(BF16)
    first_ref[:, :heads_w] = part[:, :heads_w]
    second_ref[...] = part[:, heads_w:]
    first_ref[:, heads_w:] = dot_tt(o_ref[...], attn_ref[...]).astype(BF16)
    for i in range(16):
        for half, out in ((mine, keep_hbm), (1 - mine, send_hbm)):
            store.start(first_ref.at[block_at(2 * i + half, rows // 2), :], out.at[i])
    for offset, out in enumerate((y0, y1, y2, y3)):
        to_z = lax.rem(iz + 4 - offset, 4)
        for i in range(4):
            store.start(second_ref.at[block_at(i * 4 + to_z, rows), :], out.at[i])

    proj_came.wait()
    for step, out in ((1, c1), (3, c3), (2, c2), (0, c0)):
        at = block_at(lax.bitwise_xor(block, step), size)
        part_ref[step] = dot_tt(dqkv_ref[:, at], proj_ref[...]).astype(BF16)
        store.start(part_ref.at[step], out)
    store.wait()


def attend_back(place, cosine, sine, pieces, weights, h_first, qt, kt, vt, attn, probs):
    width = weights.shape[0]
    heads, _, length = qt.shape
    groups = kt.shape[0]
    every_w = (heads + 2 * groups) * HD
    rows = width // 16
    heads_w = heads * HD
    outs = [(16, rows // 2, 2 * heads_w)] * 2 + [(4, rows, every_w - heads_w)] * 4
    outs += [pieces[0].shape] * 4
    scratch = [
        (length, width), (width, heads * HD), (length, width),
        qt.shape, kt.shape, vt.shape, attn.shape, probs.shape,
        attn.shape, (every_w, length), (width, 2 * heads_w), (width, every_w - heads_w),
        (groups, length, HD), (width, every_w), (4, *pieces[0].shape),
    ]
    wide = [(heads, 1, length), kt.shape, kt.shape]
    return kernel_call(
        attend_back_kernel, "attend_back", place, (cosine, sine),
        (*pieces, weights, h_first, qt, kt, vt, attn, probs),
        [like(s) for s in outs], [],
        [vmem(s) for s in scratch] + [vmem(s, F32) for s in wide], 12, 52, groups)


def feed_kernel(place, h0, h1, g0, g1, w_hbm, hidden_hbm, dgu_hbm, b0, b1, r0, r1,
                w_ref, h_ref, g_ref, hidden_ref, dgu_ref, back_ref, out_ref, in_sem, out_sem):
    del place
    hidden_w = hidden_ref.shape[1]
    size = h_ref.shape[1]
    parts = [slice(i * hidden_w, (i + 1) * hidden_w) for i in range(3)]
    fetch, store = Moves(in_sem), Moves(out_sem)

    def weight(i):
        at = pl.ds(i * hidden_w, hidden_w)
        return fetch.start(w_hbm.at[:, at], w_ref.at[:, at])

    came = [fetch.start(h0, h_ref.at[0]), weight(0), weight(1), fetch.start(g0, g_ref.at[0]),
            weight(2), fetch.start(h1, h_ref.at[1]), fetch.start(g1, g_ref.at[1])]
    for i, (back, out) in enumerate(((b0, r0), (b1, r1))):
        rows = slice(i * size, (i + 1) * size)
        at = pl.ds(i * size, size)
        for copy in came[0:2] if i == 0 else came[5:7]:
            copy.wait()
        gate = dot_n(h_ref[i], w_ref[:, parts[0]])
        if i == 0:
            came[2].wait()
        up = dot_n(h_ref[i], w_ref[:, parts[1]])
        sig = 1.0 / (1.0 + jnp.exp2(gate * (-LOG2E)))
        silu = gate * sig
        hidden = (silu * up).astype(BF16)
        hidden_ref[rows, :] = hidden
        store.start(hidden_ref.at[at, :], hidden_hbm.at[at, :])
        if i == 0:
            came[3].wait()
            came[4].wait()
        d_hidden = dot_n(g_ref[i], w_ref[:, parts[2]])
        dgu_ref[rows, :hidden_w] = (
            d_hidden * up * (sig * (1.0 + gate * (1.0 - sig)))).astype(BF16)
        dgu_ref[rows, hidden_w:] = (d_hidden * silu).astype(BF16)
        store.start(dgu_ref.at[at, :], dgu_hbm.at[at, :])
        back_ref[i] = dot_t(dgu_ref[rows, :], w_ref[:, : 2 * hidden_w]).astype(BF16)
        store.start(back_ref.at[i], back)
        out_ref[i] = dot_t(hidden_ref[rows, :], w_ref[:, parts[2]]).astype(BF16)
        store.start(out_ref.at[i], out)
    store.wait()


def feed(place, weights, normed_pieces, grad_pieces):
    size, width = normed_pieces[0].shape
    hidden_w = weights.shape[1] // 3
    wide = [(2 * size, hidden_w), (2 * size, 2 * hidden_w)]
    return kernel_call(
        feed_kernel, "feed", place, (), (*normed_pieces, *grad_pieces, weights),
        [like(s) for s in wide + [(size, width)] * 4], [],
        [vmem(s) for s in [weights.shape] + [(2, size, width)] * 2 + wide + [(2, size, width)] * 2],
        7, 8)


def feed_grads_kernel(place, h0, h1, h2, h3, g0, g1, g2, g3, dgu_a, dgu_b, hidden_a, hidden_b,
                      out_hbm, h_ref, g_ref, dgu_ref, hidden_ref, out_ref, in_sem, out_sem):
    del place
    size = h0.shape[0]
    half, hidden_w = hidden_a.shape
    column = 512
    fetch, store = Moves(in_sem), Moves(out_sem)

    def rows_of(pieces, ref):
        return [
            fetch.start(piece, ref.at[pl.ds(i * size, size), :]) for i, piece in enumerate(pieces)
        ]

    def tiles_of(pieces, ref):
        tiles = []
        for tile in range(ref.shape[1] // column):
            at = pl.ds(tile * column, column)
            tiles.append([
                fetch.start(piece.at[:, at], ref.at[pl.ds(i * half, half), at])
                for i, piece in enumerate(pieces)
            ])
        return tiles

    h_came = rows_of((h0, h1, h2, h3), h_ref)
    dgu_came = tiles_of((dgu_a, dgu_b), dgu_ref)
    g_came = rows_of((g0, g1, g2, g3), g_ref)
    hidden_came = tiles_of((hidden_a, hidden_b), hidden_ref)
    at = 0
    for came, left, tiles, right in (
        (h_came, h_ref, dgu_came, dgu_ref), (g_came, g_ref, hidden_came, hidden_ref)
    ):
        for copy in came:
            copy.wait()
        for tile, copies in enumerate(tiles):
            for copy in copies:
                copy.wait()
            columns = pl.ds(at, column)
            out_ref[:, columns] = dot_tn(
                left[...], right[:, tile * column : (tile + 1) * column]).astype(BF16)
            store.start(out_ref.at[:, columns], out_hbm.at[:, columns])
            at += column
    store.wait()


def feed_grads(place, normed_pieces, grad_pieces, dgu_a, dgu_b, hidden_a, hidden_b):
    size, width = normed_pieces[0].shape
    half, hidden_w = hidden_a.shape
    scratch = [(4 * size, width)] * 2 + [(2 * half, 2 * hidden_w), (2 * half, hidden_w),
                                         (width, 3 * hidden_w)]
    return kernel_call(
        feed_grads_kernel, "feed_grads", place, (),
        (*normed_pieces, *grad_pieces, dgu_a, dgu_b, hidden_a, hidden_b),
        [like((width, 3 * hidden_w))], [], [vmem(s) for s in scratch], 20, 6)[0]


def late_middle_kernel(place, keep_ref, came_ref, y0, y1, y2, y3, *outs):
    ix = place[1]
    _, rows, width = keep_ref.shape
    for offset, out in enumerate(outs):
        to = lax.rem(ix + 4 - offset, 4)
        at = pl.ds(to * 4, 4)
        total = keep_ref[at].astype(F32) + came_ref[at].astype(F32)
        out[: 4 * rows, :] = total.reshape(4 * rows, width).astype(BF16)
        total = y0[to].astype(F32)
        for ref in (y1, y2, y3):
            total += ref[to].astype(F32)
        for half in range(2):
            out[4 * rows :, half * width // 2 : (half + 1) * width // 2] = (
                total[half * rows : (half + 1) * rows].astype(BF16))


def late_middle(place, keep, came, along_z):
    _, rows, width = keep.shape
    return pl.pallas_call(
        late_middle_kernel,
        out_shape=[like((5 * rows, width))] * 4,
        in_specs=[scalars()] + [whole()] * 6,
        out_specs=[whole()] * 4,
        compiler_params=pltpu.CompilerParams(vmem_limit_bytes=16 * MIB),
        cost_estimate=SMALL,
        name="late_middle",
    )(place, keep, came, *along_z)


def late_last_kernel(place, *refs):
    inputs, outs, (keep_ref, send_ref) = refs[0:4], refs[4:8], refs[8:10]
    iz, mine = place[2], place[3]
    rows, width = keep_ref.shape

    def total(row_at, column_at):
        return sum(ref[row_at, column_at].astype(F32) for ref in inputs)

    for offset, out in enumerate(outs):
        to = lax.rem(iz + 4 - offset, 4)
        out[...] = total(block_at(to, rows), slice(None)).astype(out.dtype)
    last = slice(4 * rows, 5 * rows)
    keep_ref[...] = total(last, block_at(mine, width))
    send_ref[...] = total(last, block_at(1 - mine, width)).astype(BF16)


def late_last(place, along_x):
    rows, width = along_x[0].shape[0] // 5, along_x[0].shape[1]
    outs = [like((rows, width), F32)] + [like((rows, width))] * 3
    outs += [like((rows, width // 2), F32), like((rows, width // 2))]
    return pl.pallas_call(
        late_last_kernel,
        out_shape=outs,
        in_specs=[scalars()] + [whole()] * 4,
        out_specs=[whole()] * 6,
        compiler_params=pltpu.CompilerParams(vmem_limit_bytes=16 * MIB),
        cost_estimate=SMALL,
        name="late_last",
    )(place, *along_x)


def norm_rows(values_in):
    factor = lax.rsqrt(jnp.mean(values_in * values_in, -1, keepdims=True) + norm_eps)
    return (values_in * factor, factor)


def norm_back(grad_in, normed, factor, gain_row):
    grad_normed = grad_in * gain_row
    inner = jnp.mean(grad_normed * normed, -1, keepdims=True)
    return factor * (grad_normed - normed * inner)


def from_offset(v, axis, offset, size):
    return lax.ppermute(v, axis, [((i + offset) % size, i) for i in range(size)])


def other(v, axis):
    return from_offset(v, axis, 1, 2)


def pair_rows(v, axis):
    it = other(v, axis)
    mine = jnp.arange(2)[:, None, None] == lax.axis_index(axis)
    return jnp.where(mine, v[None], it[None]).reshape(2 * v.shape[0], v.shape[1])


def side_by_side(parts, width):
    return sum(
        jnp.pad(part, ((0, 0), (at, width - at - part.shape[1]))) for at, part in parts
    )


def near_sum(own, core):
    return own.astype(F32) + other(core, "core").astype(F32)


def far_sum(chip, diagonal):
    return near_sum(chip, diagonal).astype(BF16)


def after(value, first):
    return lax.optimization_barrier((value, first))


def from_both(along_first, first_axis, along_second, second_axis, large, beside=()):
    near = [
        from_offset(part[i], axis, i, 4)
        for i in (1, 3)
        for part, axis in ((along_first, first_axis), (along_second, second_axis))
    ]
    opposite = along_first[2], along_second[2]
    if large:
        opposite, (near, beside) = after(opposite, (near, beside))
    far = [from_offset(opposite[0], first_axis, 2, 4), from_offset(opposite[1], second_axis, 2, 4)]
    near, far = after(near, far)
    first = [along_first[0], near[0], far[0], near[2]]
    second = [along_second[0], near[1], far[1], near[3]]
    return first, second, beside


def pair_sum(v, axis):
    rows = v.shape[0] // 2
    me = lax.axis_index(axis)
    keep = lax.dynamic_slice_in_dim(v, me * rows, rows, 0)
    send = lax.dynamic_slice_in_dim(v, (1 - me) * rows, rows, 0)
    return keep.astype(F32) + other(send, axis).astype(F32)


def body(tokens, norm_gains, w_query, w_keyval, w_out, w_gateup, w_down, cotangent):
    D = tokens.shape[1]
    length = 4 * tokens.shape[0]
    hidden_w = w_down.shape[0]
    heads_w = w_query.shape[1]
    gains_w = norm_gains.shape[1]
    block = lax.axis_index("yl") * 2 + lax.axis_index("core")
    place = jnp.stack(
        [block, lax.axis_index("x"), lax.axis_index("z"), lax.axis_index("yh")]
    ).astype(jnp.int32)

    out_t = w_out.T
    attn_own = side_by_side(
        [
            (OUT_AT, out_t[:, :OUT_CUT]),
            (QUERY_AT, w_query),
            (KEYVAL_AT, w_keyval),
            (REST_AT, out_t[:, OUT_CUT:]),
        ],
        ATTN_WIDTH,
    )
    attn_pair = pair_rows(attn_own, "yh")
    pair_w = 8 * gains_w
    gain_at = (lax.axis_index("yh") * 4 + block) * gains_w
    gain_part = lax.dynamic_update_slice(jnp.zeros((2, pair_w), F32), norm_gains, (0, gain_at))
    for axis in ("core", "yl", "yh"):
        gain_part = gain_part + other(gain_part, axis)
    (gate_up, down), gain_part = after((w_gateup, w_down), gain_part)
    mlp_own = (gate_up[:, 0], gate_up[:, 1], down.T)
    mlp_own = [(i * hidden_w, part) for i, part in enumerate(mlp_own)]
    mlp_pair = pair_rows(side_by_side(mlp_own, 3 * hidden_w), "yh")
    tokens, mlp_pair = after(tokens, mlp_pair)
    gain_part = gain_part.T
    gain_high = lax.reduce_precision(gain_part, 8, 7)
    gain_low = (gain_part - gain_high).astype(BF16)
    gain_high = gain_high.astype(BF16)
    first, second = attn_pair[:, :HALF_WIDTH], attn_pair[:, HALF_WIDTH:]
    first += side_by_side([(0, gain_high), (2, gain_low)], HALF_WIDTH)

    along_z, along_x, _ = from_both([first] * 4, "z", [second] * 4, "x", False)
    far = other(tokens, "yl")
    along_z, along_x, mlp_pair, far = lax.optimization_barrier(
        (jnp.stack(along_z), jnp.stack(along_x), mlp_pair, far)
    )
    mlp_w = lax.all_gather(mlp_pair, ("x", "z"), axis=0, tiled=True)
    along_x, along_z, _ = from_both([along_z] * 4, "x", [along_x] * 4, "z", False)
    token_pieces = [tokens, other(tokens, "core"), far, other(far, "core")]
    cotangent, far = after(cotangent, far)
    grad_far = other(cotangent, "yl")

    positions = jnp.arange(length).astype(F32)
    freqs = rope_base ** (-(jnp.arange(HD // 2).astype(F32) * 2.0 / HD))
    angles = freqs[:, None] * positions[None, :]
    cosine, sine = jnp.cos(angles), jnp.sin(angles)

    gain_rows, attn_w, h_first, qt, kt, vt, attn, probs, *parts = attend(
        place, token_pieces, along_x, along_z, cosine, sine
    )
    grad_far, parts = after(grad_far, parts)
    grad_pieces = [cotangent, other(cotangent, "core"), grad_far, other(grad_far, "core")]
    middle_far = far_sum(parts[2], parts[3])
    middle = (
        tokens.astype(F32) + near_sum(parts[0], parts[1]) + other(middle_far, "yl").astype(F32)
    )
    normed2, factor2 = norm_rows(middle)
    h_own = (normed2 * gain_rows[1]).astype(BF16)

    h_pieces = [h_own, other(h_own, "core")]
    h_far = other(h_own, "yl")
    hidden_a, dgu_a, back_own, back_core, out_own, out_core = feed(
        place, mlp_w, h_pieces, grad_pieces[:2]
    )
    h_far, hidden_a = after(h_far, hidden_a)
    h_pieces += [h_far, other(h_far, "core")]
    hidden_b, dgu_b, back_chip, back_diag, out_chip, out_diag = feed(
        place, mlp_w, h_pieces[2:], grad_pieces[2:]
    )
    back_core = other(back_core, "core")
    out_near = near_sum(out_own, out_core)

    back_far = far_sum(back_chip, back_diag)
    hidden_b, (back_far, back_core) = after(hidden_b, (back_far, back_core))
    mlp_grads = feed_grads(place, h_pieces, grad_pieces, dgu_a, dgu_b, hidden_a, hidden_b)
    mlp_grads, back_far = after(mlp_grads, other(back_far, "yl"))
    d_h2_own = back_own.astype(F32) + back_core.astype(F32) + back_far.astype(F32)
    early = lax.psum_scatter(mlp_grads, ("x", "z"), scatter_dimension=0, tiled=True)
    out_far = far_sum(out_chip, out_diag)

    d_norm2 = norm_back(d_h2_own, normed2, factor2, gain_rows[1])
    d_middle = cotangent.astype(F32) + d_norm2
    d_out = d_middle.astype(BF16)
    d_out_far = other(d_out, "yl")
    d_out_far, out_near = after(d_out_far, out_near)
    out_pieces = [d_out, other(d_out, "core"), d_out_far, other(d_out_far, "core")]
    out_far, out_pieces = after(out_far, out_pieces)
    out_far = other(out_far, "yl")

    back = attend_back(
        place, cosine, sine, out_pieces, attn_w, h_first, qt, kt, vt, attn, probs
    )
    back, out_far = after(back, out_far)
    late_parts, parts = back[:6], back[6:]
    keep, send, *along_z = late_parts
    came = other(send, "yh")
    along_z[1:] = [from_offset(along_z[i], "z", i, 4) for i in (1, 2, 3)]
    (came, along_z), d_far = after((came, along_z), far_sum(parts[2], parts[3]))
    along_x = list(late_middle(place, keep, came, along_z))
    along_x[1:] = [from_offset(along_x[i], "x", i, 4) for i in (1, 2, 3)]
    (along_x[1], along_x[3]), early = after((along_x[1], along_x[3]), early)
    early = pair_sum(early, "yh")
    d_far = other(d_far, "yl")
    result = (middle + out_near + out_far.astype(F32)).astype(BF16)
    d_h1_own = near_sum(parts[0], parts[1]) + d_far.astype(F32)
    along_x, (early, d_h1_own) = after(along_x, (early, d_h1_own))
    late, *send_z, late_keyval, send_pair = late_last(place, along_x)
    send_z = [from_offset(v, "z", i + 1, 4) for i, v in enumerate(send_z)]
    send_z, send_pair = after(send_z, other(send_pair, "yh"))
    late = late + sum(v.astype(F32) for v in send_z)
    grad_keyval = late_keyval + send_pair.astype(F32)

    normed1, factor1 = norm_rows(tokens.astype(F32))
    d_norm1 = norm_back(d_h1_own, normed1, factor1, gain_rows[0])
    input_grad = (d_middle + d_norm1).astype(BF16)

    grad_query = late[:, :heads_w]
    grad_out = late[:, heads_w:].T
    grad_gateup = early[:, : 2 * hidden_w].reshape(-1, 2, hidden_w)

    gain_sum = jnp.stack(
        [
            jnp.sum(grad_query * w_query.astype(F32) + grad_keyval * w_keyval.astype(F32), 1),
            jnp.sum(grad_gateup * w_gateup.astype(F32), (1, 2)),
        ]
    )
    gain_sum = gain_sum + sum(
        lax.ppermute(gain_sum, ("yl", "core"), [(i ^ step, i) for i in range(4)])
        for step in (1, 2, 3)
    )
    grad_gains = lax.dynamic_slice(gain_sum, (0, block * gains_w), (2, gains_w)) / norm_gains
    return (
        result,
        input_grad,
        grad_query,
        grad_keyval,
        grad_out,
        grad_gateup,
        early[:, 2 * hidden_w :].T,
        grad_gains,
    )


def solution(mesh):
    fine = Mesh(mesh.devices.reshape(4, 4, 2, 2, 2), ("x", "z", "yh", "yl", "core"))
    dp = ("x", "z", "yh")
    tensor = ("yl", "core")
    every = dp + tensor
    weights = (P(dp, tensor), P(dp, tensor), P(tensor, dp), P(dp, None, tensor), P(tensor, dp))
    rows = P(every, None)
    gains = P(None, every)
    return jax.shard_map(
        body,
        mesh=fine,
        in_specs=(rows, gains) + weights + (rows,),
        out_specs=(rows, rows) + weights + (gains,),
        check_vma=False,
    )
```

```python
import jax
import jax.numpy as jnp
from jax import lax
from jax.experimental import pallas as pl
from jax.experimental.pallas import tpu as pltpu
from jax.sharding import Mesh, PartitionSpec as P

HD = 96
F32 = jnp.float32
BF16 = jnp.bfloat16
norm_eps = 1e-05
rope_base = 100000.0
LOG2E = 1.4426950408889634
SCALE = HD ** (-0.5)
MIB = 1024 * 1024
SMALL = pl.CostEstimate(flops=1, bytes_accessed=1, transcendentals=0)

GAIN_AT, OUT_AT, QUERY_AT, KEYVAL_AT, REST_AT, ATTN_WIDTH = 0, 128, 256, 640, 1024, 1280
HALF_WIDTH = ATTN_WIDTH // 2
OUT_CUT = QUERY_AT - OUT_AT
LIMIT = 56


def dot_n(left, right):
    return jnp.dot(left, right, preferred_element_type=F32)


def dot_t(left, right):
    return lax.dot_general(left, right, (((1,), (1,)), ((), ())), preferred_element_type=F32)


def dot_tn(left, right):
    return lax.dot_general(left, right, (((0,), (0,)), ((), ())), preferred_element_type=F32)


def dot_tt(left, right):
    return lax.dot_general(left, right, (((0,), (1,)), ((), ())), preferred_element_type=F32)


def block_at(index, size):
    return pl.ds(pl.multiple_of(index * size, size), size)


def causal_mask(scores, size):
    key_at = lax.broadcasted_iota(jnp.int32, (size, scores.shape[1]), 0)
    query_at = lax.broadcasted_iota(jnp.int32, (size, scores.shape[1]), 1) % size
    tail = jnp.where(key_at <= query_at, scores[-size:], -1e30)
    if scores.shape[0] == size:
        return tail
    return jnp.concatenate([scores[:-size], tail], 0)


class Moves:
    def __init__(self, sems):
        self.sems = sems
        self.started = []

    def start(self, source, target):
        copy = pltpu.make_async_copy(source, target, self.sems.at[len(self.started)])
        copy.start()
        self.started.append(copy)
        return copy

    def wait(self):
        for copy in self.started:
            copy.wait()


def vmem(shape, dtype=BF16):
    return pltpu.VMEM(shape, dtype)


def like(shape, dtype=BF16):
    return jax.ShapeDtypeStruct(shape, dtype)


def whole():
    return pl.BlockSpec(memory_space=pltpu.VMEM)


def apart():
    return pl.BlockSpec(memory_space=pl.ANY)


def scalars():
    return pl.BlockSpec(memory_space=pltpu.SMEM)


def kernel_call(kernel, name, place, small, large, outs, small_outs, scratch, *copies):
    return pl.pallas_call(
        kernel,
        out_shape=list(small_outs) + list(outs),
        in_specs=[scalars()] + [whole()] * len(small) + [apart()] * len(large),
        out_specs=[whole()] * len(small_outs) + [apart()] * len(outs),
        scratch_shapes=list(scratch)
        + [pltpu.SemaphoreType.DMA((count,)) for count in copies],
        compiler_params=pltpu.CompilerParams(vmem_limit_bytes=LIMIT * MIB),
        cost_estimate=SMALL,
        name=name,
    )(place, *small, *large)


def probs_at(step, size):
    return step * (step + 1) // 2 * size, (step + 1) * size


def head_rows(head):
    return slice(head * HD, (head + 1) * HD)


def attend_kernel(place, cos_ref, sin_ref, t0, t1, t2, t3, a0, a1, a2, a3, b0, b1, b2, b3,
                  gains_ref, w_hbm, h_hbm, qt_hbm, kt_hbm, vt_hbm, attn_hbm, probs_hbm,
                  o0, o1, o2, o3,
                  t_ref, w_ref, h_ref, qt_ref, kt_ref, vt_ref, attn_ref, probs_ref, part_ref, k_ref,
                  in_sem, out_sem, probs_sem):
    block, ix, iz = place[0], place[1], place[2]
    half = HD // 2
    size = t_ref.shape[1]
    heads = qt_ref.shape[0]
    group_size = heads // kt_ref.shape[0]
    rows = a0.shape[1]
    fetch, store = Moves(in_sem), Moves(out_sem)
    gains_came, came = [], []
    for far, (along_x, along_z) in enumerate(zip((a0, a1, a2, a3), (b0, b1, b2, b3))):
        for near in range(4):
            at_a = block_at(lax.rem(ix + far, 4) * 4 + lax.rem(iz + near, 4), rows)
            at_b = block_at(lax.rem(ix + near, 4) * 4 + lax.rem(iz + far, 4), rows)
            for source, first, width, target, copies in (
                (along_x, 0, OUT_AT, at_a, gains_came),
                (along_x, OUT_AT, HALF_WIDTH - OUT_AT, at_a, came),
                (along_z, HALF_WIDTH, HALF_WIDTH, at_b, came),
            ):
                copies.append((
                    source.at[near, :, pl.ds(first % HALF_WIDTH, width)],
                    w_ref.at[target, pl.ds(first, width)],
                ))
    gains_came = [fetch.start(*copy) for copy in gains_came]
    tokens_came = [
        fetch.start(piece, t_ref.at[i]) for i, piece in enumerate((t0, t1, t2, t3))
    ]
    came = [fetch.start(*copy) for copy in came]
    for copy in gains_came:
        copy.wait()
    gains = w_ref[:, GAIN_AT:OUT_AT].astype(F32).T
    gain_row = gains[0:1] + gains[2:3]
    gains_ref[...] = gains[0:2] + gains[2:4]
    for step in range(4):
        tokens_came[step].wait()
        value = t_ref[step].astype(F32)
        factor = lax.rsqrt(jnp.mean(value * value, -1, keepdims=True) + norm_eps)
        h_ref[block_at(lax.bitwise_xor(block, step), size), :] = (
            value * factor * gain_row).astype(BF16)
    for copy in came:
        copy.wait()
    store.start(w_ref, w_hbm)
    for step in range(4):
        at = slice(step * size, (step + 1) * size)
        normed = h_ref[at, :]
        cosine = cos_ref[:, at]
        sine = sin_ref[:, at]
        every = dot_n(normed, w_ref[:, QUERY_AT:REST_AT]).T
        query, keyval = every[: KEYVAL_AT - QUERY_AT], every[KEYVAL_AT - QUERY_AT :]

        def rotated(field):
            first, second = field[:half], field[half:]
            return jnp.concatenate(
                [first * cosine - second * sine, second * cosine + first * sine], 0
            )

        for head in range(heads):
            qt_ref[head, :, at] = rotated(query[head_rows(head)]).astype(BF16)
        for group in range(heads // group_size):
            key = rotated(keyval[head_rows(2 * group)])
            kt_ref[group, :, at] = key.astype(BF16)
            k_ref[group, at, :] = key.T.astype(BF16)
            vt_ref[group, :, at] = keyval[head_rows(2 * group + 1)].astype(BF16)
    for source, target in ((h_ref, h_hbm), (qt_ref, qt_hbm), (kt_ref, kt_hbm), (vt_ref, vt_hbm)):
        store.start(source, target)

    def probs_copy(group):
        return pltpu.make_async_copy(
            probs_ref.at[group], probs_hbm.at[group], probs_sem.at[group])

    for group in range(heads // group_size):
        members = range(group * group_size, (group + 1) * group_size)
        for step in range(4):
            first, reach = probs_at(step, size)
            columns = slice(step * size, reach)
            query = jnp.concatenate([qt_ref[head, :, columns] for head in members], 1)
            scores = causal_mask(dot_n(k_ref[group, :reach, :], query), size)
            top = jnp.max(scores, 0, keepdims=True)
            expo = jnp.exp2((scores - top) * (SCALE * LOG2E))
            total = jnp.sum(expo, 0, keepdims=True)
            probs = (expo * (1.0 / total)).astype(BF16)
            probs_ref[group, first : first + reach, :] = probs
            mixed = dot_n(vt_ref[group, :, :reach], probs).astype(BF16)
            for i, head in enumerate(members):
                attn_ref[head_rows(head), columns] = mixed[:, i * size : (i + 1) * size]
        probs_copy(group).start()
    store.start(attn_ref, attn_hbm)
    for step, out in ((1, o1), (3, o3), (2, o2), (0, o0)):
        at = block_at(lax.bitwise_xor(block, step), size)
        part = dot_tt(attn_ref[:OUT_CUT, at], w_ref[:, OUT_AT:QUERY_AT])
        part += dot_tt(attn_ref[OUT_CUT:, at], w_ref[:, REST_AT:])
        part_ref[step] = part.astype(BF16)
        store.start(part_ref.at[step], out)
    store.wait()
    for group in range(heads // group_size):
        probs_copy(group).wait()


def attend(place, pieces, along_x, along_z, cosine, sine):
    size, width = pieces[0].shape
    length = 4 * size
    heads = (KEYVAL_AT - QUERY_AT) // HD
    groups = (REST_AT - KEYVAL_AT) // (2 * HD)
    columns, g_columns = (heads, HD, length), (groups, HD, length)
    probs = (groups, sum(probs_at(3, size)), heads // groups * size)
    kept = [(width, ATTN_WIDTH), (length, width), columns, g_columns, g_columns,
            (heads * HD, length), probs]
    return kernel_call(
        attend_kernel, "attend", place, (cosine, sine), (*pieces, *along_x, *along_z),
        [like(s) for s in kept + [(size, width)] * 4], [like((2, width), F32)],
        [vmem(s) for s in [(4, size, width)] + kept + [(4, size, width), (groups, length, HD)]],
        52, 10, groups)


def attend_back_kernel(place, cos_ref, sin_ref,
                       o0, o1, o2, o3, w_hbm, h_hbm, qt_hbm, kt_hbm, vt_hbm, attn_hbm, probs_hbm,
                       dqkv_hbm, x0, x1, x2, x3, y0, y1, y2, y3,
                       o_ref, w_ref, h_ref, qt_ref, kt_ref, vt_ref, attn_ref, probs_ref,
                       do_ref, dqkv_ref, first_ref, second_ref, v_ref, delta_ref, dk_ref, dv_ref,
                       in_sem, out_sem, probs_sem):
    block, ix, iz = place[0], place[1], place[2]
    heads, _, length = qt_ref.shape
    groups = kt_ref.shape[0]
    group_size = heads // groups
    size = length // 4
    half = HD // 2
    width = w_ref.shape[0]
    heads_w = heads * HD
    fetch, store = Moves(in_sem), Moves(out_sem)
    rest_w = ATTN_WIDTH - REST_AT
    early = [
        fetch.start(w_hbm.at[:, pl.ds(OUT_AT, OUT_CUT)], w_ref.at[:, pl.ds(0, OUT_CUT)]),
        fetch.start(w_hbm.at[:, pl.ds(REST_AT, rest_w)], w_ref.at[:, pl.ds(OUT_CUT, rest_w)]),
    ]
    early += [
        fetch.start(piece, o_ref.at[block_at(lax.bitwise_xor(block, i), size), :])
        for i, piece in enumerate((o0, o1, o2, o3))
    ]
    middle = [
        fetch.start(source, target)
        for source, target in ((attn_hbm, attn_ref), (vt_hbm, vt_ref), (qt_hbm, qt_ref),
                               (kt_hbm, kt_ref))
    ]

    def probs_copy(group):
        return pltpu.make_async_copy(
            probs_hbm.at[group], probs_ref.at[group], probs_sem.at[group])

    for group in range(groups):
        probs_copy(group).start()
    h_came = fetch.start(h_hbm, h_ref)
    for copy in early:
        copy.wait()
    do_ref[...] = dot_tt(w_ref[...], o_ref[...]).astype(BF16)
    for copy in middle:
        copy.wait()
    for group in range(groups):
        v_ref[group] = vt_ref[group].astype(F32).T.astype(BF16)
    for head in range(heads):
        rows = head_rows(head)
        delta_ref[head] = jnp.sum(
            attn_ref[rows, :].astype(F32) * do_ref[rows, :].astype(F32), 0, keepdims=True)

    def turned_back(field, cosine, sine):
        first, second = field[:half], field[half:]
        return jnp.concatenate(
            [first * cosine + second * sine, second * cosine - first * sine], 0).astype(BF16)

    for group in range(groups):
        members = range(group * group_size, (group + 1) * group_size)
        probs_copy(group).wait()
        for step in range(4):
            first, reach = probs_at(step, size)
            columns = slice(step * size, reach)
            probs = probs_ref[group, first : first + reach, :]
            query = jnp.concatenate([qt_ref[head, :, columns] for head in members], 1)
            d_out = jnp.concatenate([do_ref[head_rows(head), columns] for head in members], 1)
            delta = jnp.concatenate([delta_ref[head, :, columns] for head in members], 1)
            d_probs = dot_n(v_ref[group, :reach, :], d_out)
            d_scores = (probs.astype(F32) * (d_probs - delta)).astype(BF16)
            for ref, left, right in ((dv_ref, d_out, probs), (dk_ref, query, d_scores)):
                change = dot_t(left, right)
                if step > 0:
                    ref[group, :, : step * size] += change[:, : step * size]
                ref[group, :, columns] = change[:, columns]
            d_query = dot_n(kt_ref[group, :, :reach], d_scores) * SCALE
            for i, head in enumerate(members):
                dqkv_ref[head_rows(head), columns] = turned_back(
                    d_query[:, i * size : (i + 1) * size],
                    cos_ref[:, columns], sin_ref[:, columns])
        dqkv_ref[head_rows(heads + 2 * group), :] = turned_back(
            dk_ref[group] * SCALE, cos_ref[...], sin_ref[...])
        dqkv_ref[head_rows(heads + 2 * group + 1), :] = dv_ref[group].astype(BF16)
    store.start(dqkv_ref, dqkv_hbm)
    h_came.wait()

    rows = width // 16
    part = dot_tt(h_ref[...], dqkv_ref[...]).astype(BF16)
    first_ref[:, :heads_w] = part[:, :heads_w]
    second_ref[:, LATE_WIDTH - heads_w :] = part[:, heads_w:]
    part = dot_tt(o_ref[...], attn_ref[...]).astype(BF16)
    first_ref[:, heads_w:] = part[:, :LATE_OUT]
    second_ref[:, : heads_w - LATE_OUT] = part[:, LATE_OUT:]
    for offset, (x_out, y_out) in enumerate(((x0, y0), (x1, y1), (x2, y2), (x3, y3))):
        to_x = lax.rem(ix + 4 - offset, 4)
        to_z = lax.rem(iz + 4 - offset, 4)
        store.start(first_ref.at[block_at(to_x, 4 * rows), :], x_out)
        for i in range(4):
            store.start(second_ref.at[block_at(i * 4 + to_z, rows), :], y_out.at[i])
    store.wait()


def attend_back(place, cosine, sine, pieces, weights, h_first, qt, kt, vt, attn, probs):
    width = weights.shape[0]
    heads, _, length = qt.shape
    groups = kt.shape[0]
    every_w = (heads + 2 * groups) * HD
    rows = width // 16
    outs = [(every_w, length)] + [(4 * rows, LATE_WIDTH)] * 4 + [(4, rows, LATE_WIDTH)] * 4
    scratch = [
        (length, width), (width, heads * HD), (length, width),
        qt.shape, kt.shape, vt.shape, attn.shape, probs.shape,
        attn.shape, (every_w, length), (width, LATE_WIDTH), (width, LATE_WIDTH),
        (groups, length, HD),
    ]
    wide = [(heads, 1, length), kt.shape, kt.shape]
    return kernel_call(
        attend_back_kernel, "attend_back", place, (cosine, sine),
        (*pieces, weights, h_first, qt, kt, vt, attn, probs),
        [like(s) for s in outs], [],
        [vmem(s) for s in scratch] + [vmem(s, F32) for s in wide], 11, 21, groups)


def project_back_kernel(place, dqkv_hbm, w_hbm, c0, c1, c2, c3,
                        dqkv_ref, w_ref, part_ref, in_sem, out_sem):
    block = place[0]
    size = part_ref.shape[1]
    fetch, store = Moves(in_sem), Moves(out_sem)
    fetch.start(w_hbm.at[:, pl.ds(QUERY_AT, REST_AT - QUERY_AT)], w_ref)
    fetch.start(dqkv_hbm, dqkv_ref)
    fetch.wait()
    for step, out in ((3, c3), (2, c2), (1, c1), (0, c0)):
        at = block_at(lax.bitwise_xor(block, step), size)
        part_ref[step] = dot_tt(dqkv_ref[:, at], w_ref[...]).astype(BF16)
        store.start(part_ref.at[step], out)
    store.wait()


def project_back(place, d_qkv, weights):
    every_w, length = d_qkv.shape
    width = weights.shape[0]
    size = length // 4
    return kernel_call(
        project_back_kernel, "project_back", place, (), (d_qkv, weights),
        [like((size, width))] * 4, [],
        [vmem(s) for s in (d_qkv.shape, (width, every_w), (4, size, width))], 2, 4)


def feed_kernel(place, h0, h1, g0, g1, w_hbm, hidden_hbm, dgu_hbm, b0, b1, r0, r1,
                w_ref, h_ref, g_ref, hidden_ref, dgu_ref, back_ref, out_ref, in_sem, out_sem):
    del place
    hidden_w = hidden_ref.shape[1]
    size = h_ref.shape[1]
    parts = [slice(i * hidden_w, (i + 1) * hidden_w) for i in range(3)]
    fetch, store = Moves(in_sem), Moves(out_sem)

    def weight(i):
        at = pl.ds(i * hidden_w, hidden_w)
        return fetch.start(w_hbm.at[:, at], w_ref.at[:, at])

    came = [fetch.start(h0, h_ref.at[0]), weight(0), weight(1), fetch.start(g0, g_ref.at[0]),
            weight(2), fetch.start(h1, h_ref.at[1]), fetch.start(g1, g_ref.at[1])]
    for i, (back, out) in enumerate(((b0, r0), (b1, r1))):
        rows = slice(i * size, (i + 1) * size)
        at = pl.ds(i * size, size)
        for copy in came[0:2] if i == 0 else came[5:7]:
            copy.wait()
        gate = dot_n(h_ref[i], w_ref[:, parts[0]])
        if i == 0:
            came[2].wait()
        up = dot_n(h_ref[i], w_ref[:, parts[1]])
        sig = 1.0 / (1.0 + jnp.exp2(gate * (-LOG2E)))
        silu = gate * sig
        hidden = (silu * up).astype(BF16)
        hidden_ref[rows, :] = hidden
        store.start(hidden_ref.at[at, :], hidden_hbm.at[at, :])
        if i == 0:
            came[3].wait()
            came[4].wait()
        d_hidden = dot_n(g_ref[i], w_ref[:, parts[2]])
        dgu_ref[rows, :hidden_w] = (
            d_hidden * up * (sig * (1.0 + gate * (1.0 - sig)))).astype(BF16)
        dgu_ref[rows, hidden_w:] = (d_hidden * silu).astype(BF16)
        store.start(dgu_ref.at[at, :], dgu_hbm.at[at, :])
        back_ref[i] = dot_t(dgu_ref[rows, :], w_ref[:, : 2 * hidden_w]).astype(BF16)
        store.start(back_ref.at[i], back)
        out_ref[i] = dot_t(hidden_ref[rows, :], w_ref[:, parts[2]]).astype(BF16)
        store.start(out_ref.at[i], out)
    store.wait()


def feed(place, weights, normed_pieces, grad_pieces):
    size, width = normed_pieces[0].shape
    hidden_w = weights.shape[1] // 3
    wide = [(2 * size, hidden_w), (2 * size, 2 * hidden_w)]
    return kernel_call(
        feed_kernel, "feed", place, (), (*normed_pieces, *grad_pieces, weights),
        [like(s) for s in wide + [(size, width)] * 4], [],
        [vmem(s) for s in [weights.shape] + [(2, size, width)] * 2 + wide + [(2, size, width)] * 2],
        7, 8)


def feed_grads_kernel(place, h0, h1, h2, h3, g0, g1, g2, g3, dgu_a, dgu_b, hidden_a, hidden_b,
                      out_hbm, h_ref, g_ref, dgu_ref, hidden_ref, out_ref, in_sem, out_sem):
    del place
    size = h0.shape[0]
    half, hidden_w = hidden_a.shape
    column = 512
    fetch, store = Moves(in_sem), Moves(out_sem)

    def rows_of(pieces, ref):
        return [
            fetch.start(piece, ref.at[pl.ds(i * size, size), :]) for i, piece in enumerate(pieces)
        ]

    def tiles_of(pieces, ref):
        tiles = []
        for tile in range(ref.shape[1] // column):
            at = pl.ds(tile * column, column)
            tiles.append([
                fetch.start(piece.at[:, at], ref.at[pl.ds(i * half, half), at])
                for i, piece in enumerate(pieces)
            ])
        return tiles

    h_came = rows_of((h0, h1, h2, h3), h_ref)
    dgu_came = tiles_of((dgu_a, dgu_b), dgu_ref)
    g_came = rows_of((g0, g1, g2, g3), g_ref)
    hidden_came = tiles_of((hidden_a, hidden_b), hidden_ref)
    at = 0
    for came, left, tiles, right in (
        (h_came, h_ref, dgu_came, dgu_ref), (g_came, g_ref, hidden_came, hidden_ref)
    ):
        for copy in came:
            copy.wait()
        for tile, copies in enumerate(tiles):
            for copy in copies:
                copy.wait()
            columns = pl.ds(at, column)
            out_ref[:, columns] = dot_tn(
                left[...], right[:, tile * column : (tile + 1) * column]).astype(BF16)
            store.start(out_ref.at[:, columns], out_hbm.at[:, columns])
            at += column
    store.wait()


def feed_grads(place, normed_pieces, grad_pieces, dgu_a, dgu_b, hidden_a, hidden_b):
    size, width = normed_pieces[0].shape
    half, hidden_w = hidden_a.shape
    scratch = [(4 * size, width)] * 2 + [(2 * half, 2 * hidden_w), (2 * half, hidden_w),
                                         (width, 3 * hidden_w)]
    return kernel_call(
        feed_grads_kernel, "feed_grads", place, (),
        (*normed_pieces, *grad_pieces, dgu_a, dgu_b, hidden_a, hidden_b),
        [like((width, 3 * hidden_w))], [], [vmem(s) for s in scratch], 20, 6)[0]


LATE_OUT, LATE_WIDTH = 192, 576


def late_middle_kernel(place, *refs):
    x_in, y_in, outs = refs[0:4], refs[4:8], refs[8:]
    ix, iz = place[1], place[2]
    rows = outs[0].shape[0]
    for offset in range(4):
        at = block_at(lax.rem(iz + 4 - offset, 4), rows)
        total = x_in[0][at, :].astype(F32)
        for ref in x_in[1:]:
            total += ref[at, :].astype(F32)
        outs[offset][...] = total.astype(BF16)
        to = lax.rem(ix + 4 - offset, 4)
        total = y_in[0][to].astype(F32)
        for ref in y_in[1:]:
            total += ref[to].astype(F32)
        outs[4 + offset][...] = total.astype(BF16)


def late_middle(place, along_x, along_z):
    _, rows, width = along_z[0].shape
    return pl.pallas_call(
        late_middle_kernel,
        out_shape=[like((rows, width))] * 8,
        in_specs=[scalars()] + [whole()] * 8,
        out_specs=[whole()] * 8,
        compiler_params=pltpu.CompilerParams(vmem_limit_bytes=16 * MIB),
        cost_estimate=SMALL,
        name="late_middle",
    )(place, *along_x, *along_z)


def late_last_kernel(place, *refs):
    x_in, y_in, keep_ref, send_ref = refs[0:4], refs[4:8], refs[8], refs[9]
    mine = place[3]
    rows = keep_ref.shape[0]
    for inputs, columns in ((x_in, slice(0, LATE_WIDTH)), (y_in, slice(LATE_WIDTH, 2 * LATE_WIDTH))):
        for ref, half in ((keep_ref, mine), (send_ref, 1 - mine)):
            at = block_at(half, rows)
            total = inputs[0][at, :].astype(F32)
            for other_ref in inputs[1:]:
                total += other_ref[at, :].astype(F32)
            ref[:, columns] = total.astype(ref.dtype)


def late_last(place, along_z, along_x):
    rows, width = along_x[0].shape
    return pl.pallas_call(
        late_last_kernel,
        out_shape=[
            jax.ShapeDtypeStruct((rows // 2, 2 * width), F32),
            jax.ShapeDtypeStruct((rows // 2, 2 * width), BF16),
        ],
        in_specs=[scalars()] + [whole()] * 8,
        out_specs=[whole()] * 2,
        compiler_params=pltpu.CompilerParams(vmem_limit_bytes=16 * MIB),
        cost_estimate=SMALL,
        name="late_last",
    )(place, *along_z, *along_x)


def norm_rows(values_in):
    factor = lax.rsqrt(jnp.mean(values_in * values_in, -1, keepdims=True) + norm_eps)
    return (values_in * factor, factor)


def norm_back(grad_in, normed, factor, gain_row):
    grad_normed = grad_in * gain_row
    inner = jnp.mean(grad_normed * normed, -1, keepdims=True)
    return factor * (grad_normed - normed * inner)


def from_offset(v, axis, offset, size):
    return lax.ppermute(v, axis, [((i + offset) % size, i) for i in range(size)])


def other(v, axis):
    return from_offset(v, axis, 1, 2)


def pair_rows(v, axis):
    it = other(v, axis)
    mine = jnp.arange(2)[:, None, None] == lax.axis_index(axis)
    return jnp.where(mine, v[None], it[None]).reshape(2 * v.shape[0], v.shape[1])


def side_by_side(parts, width):
    return sum(
        jnp.pad(part, ((0, 0), (at, width - at - part.shape[1]))) for at, part in parts
    )


def near_sum(own, core):
    return own.astype(F32) + other(core, "core").astype(F32)


def far_sum(chip, diagonal):
    return near_sum(chip, diagonal).astype(BF16)


def after(value, first):
    return lax.optimization_barrier((value, first))


def from_both(along_first, first_axis, along_second, second_axis, large, beside=()):
    near = [
        from_offset(part[i], axis, i, 4)
        for i in (1, 3)
        for part, axis in ((along_first, first_axis), (along_second, second_axis))
    ]
    opposite = along_first[2], along_second[2]
    if large:
        opposite, (near, beside) = after(opposite, (near, beside))
    far = [from_offset(opposite[0], first_axis, 2, 4), from_offset(opposite[1], second_axis, 2, 4)]
    near, far = after(near, far)
    first = [along_first[0], near[0], far[0], near[2]]
    second = [along_second[0], near[1], far[1], near[3]]
    return first, second, beside


def pair_sum(v, axis):
    rows = v.shape[0] // 2
    me = lax.axis_index(axis)
    keep = lax.dynamic_slice_in_dim(v, me * rows, rows, 0)
    send = lax.dynamic_slice_in_dim(v, (1 - me) * rows, rows, 0)
    return keep.astype(F32) + other(send, axis).astype(F32)


def body(tokens, norm_gains, w_query, w_keyval, w_out, w_gateup, w_down, cotangent):
    D = tokens.shape[1]
    length = 4 * tokens.shape[0]
    hidden_w = w_down.shape[0]
    heads_w = w_query.shape[1]
    gains_w = norm_gains.shape[1]
    block = lax.axis_index("yl") * 2 + lax.axis_index("core")
    place = jnp.stack(
        [block, lax.axis_index("x"), lax.axis_index("z"), lax.axis_index("yh")]
    ).astype(jnp.int32)

    out_t = w_out.T
    attn_own = side_by_side(
        [
            (OUT_AT, out_t[:, :OUT_CUT]),
            (QUERY_AT, w_query),
            (KEYVAL_AT, w_keyval),
            (REST_AT, out_t[:, OUT_CUT:]),
        ],
        ATTN_WIDTH,
    )
    attn_pair = pair_rows(attn_own, "yh")
    pair_w = 8 * gains_w
    gain_at = (lax.axis_index("yh") * 4 + block) * gains_w
    gain_part = lax.dynamic_update_slice(jnp.zeros((2, pair_w), F32), norm_gains, (0, gain_at))
    for axis in ("core", "yl", "yh"):
        gain_part = gain_part + other(gain_part, axis)
    (gate_up, down), gain_part = after((w_gateup, w_down), gain_part)
    mlp_own = (gate_up[:, 0], gate_up[:, 1], down.T)
    mlp_own = [(i * hidden_w, part) for i, part in enumerate(mlp_own)]
    mlp_pair = pair_rows(side_by_side(mlp_own, 3 * hidden_w), "yh")
    gain_part = gain_part.T
    gain_high = lax.reduce_precision(gain_part, 8, 7)
    gain_low = (gain_part - gain_high).astype(BF16)
    gain_high = gain_high.astype(BF16)
    first, second = attn_pair[:, :HALF_WIDTH], attn_pair[:, HALF_WIDTH:]
    first += side_by_side([(0, gain_high), (2, gain_low)], HALF_WIDTH)

    along_z, along_x, _ = from_both([first] * 4, "z", [second] * 4, "x", False)
    along_z, along_x, mlp_pair, tokens = lax.optimization_barrier(
        (jnp.stack(along_z), jnp.stack(along_x), mlp_pair, tokens)
    )
    mlp_w = lax.all_gather(mlp_pair, ("x", "z"), axis=0, tiled=True)
    along_x, along_z, far = from_both(
        [along_z] * 4, "x", [along_x] * 4, "z", True, other(tokens, "yl")
    )
    token_pieces = [tokens, other(tokens, "core"), far, other(far, "core")]
    cotangent, far = after(cotangent, far)
    grad_far = other(cotangent, "yl")

    positions = jnp.arange(length).astype(F32)
    freqs = rope_base ** (-(jnp.arange(HD // 2).astype(F32) * 2.0 / HD))
    angles = freqs[:, None] * positions[None, :]
    cosine, sine = jnp.cos(angles), jnp.sin(angles)

    gain_rows, attn_w, h_first, qt, kt, vt, attn, probs, *parts = attend(
        place, token_pieces, along_x, along_z, cosine, sine
    )
    grad_far, parts = after(grad_far, parts)
    grad_pieces = [cotangent, other(cotangent, "core"), grad_far, other(grad_far, "core")]
    middle_far = far_sum(parts[2], parts[3])
    middle = (
        tokens.astype(F32) + near_sum(parts[0], parts[1]) + other(middle_far, "yl").astype(F32)
    )
    normed2, factor2 = norm_rows(middle)
    h_own = (normed2 * gain_rows[1]).astype(BF16)

    h_pieces = [h_own, other(h_own, "core")]
    h_far = other(h_own, "yl")
    hidden_a, dgu_a, back_own, back_core, out_own, out_core = feed(
        place, mlp_w, h_pieces, grad_pieces[:2]
    )
    h_far, hidden_a = after(h_far, hidden_a)
    h_pieces += [h_far, other(h_far, "core")]
    hidden_b, dgu_b, back_chip, back_diag, out_chip, out_diag = feed(
        place, mlp_w, h_pieces[2:], grad_pieces[2:]
    )
    back_core = other(back_core, "core")
    out_near = near_sum(out_own, out_core)

    back_far = far_sum(back_chip, back_diag)
    hidden_b, (back_far, back_core) = after(hidden_b, (back_far, back_core))
    mlp_grads = feed_grads(place, h_pieces, grad_pieces, dgu_a, dgu_b, hidden_a, hidden_b)
    mlp_grads, back_far = after(mlp_grads, other(back_far, "yl"))
    d_h2_own = back_own.astype(F32) + back_core.astype(F32) + back_far.astype(F32)
    early = lax.psum_scatter(mlp_grads, ("x", "z"), scatter_dimension=0, tiled=True)
    out_far = far_sum(out_chip, out_diag)

    d_norm2 = norm_back(d_h2_own, normed2, factor2, gain_rows[1])
    d_middle = cotangent.astype(F32) + d_norm2
    d_out = d_middle.astype(BF16)
    d_out_far = other(d_out, "yl")
    d_out_far, out_near = after(d_out_far, out_near)
    out_pieces = [d_out, other(d_out, "core"), d_out_far, other(d_out_far, "core")]
    out_far, out_pieces = after(out_far, out_pieces)
    out_far = other(out_far, "yl")

    back = attend_back(
        place, cosine, sine, out_pieces, attn_w, h_first, qt, kt, vt, attn, probs
    )
    d_qkv, *late_parts = back
    d_qkv, out_far = after(d_qkv, out_far)
    along_x, along_z, parts = from_both(
        late_parts[:4], "x", late_parts[4:], "z", True, project_back(place, d_qkv, attn_w)
    )
    d_far = other(far_sum(parts[2], parts[3]), "yl")
    result = (middle + out_near + out_far.astype(F32)).astype(BF16)
    along_x, result = after(along_x, result)
    middle_parts = late_middle(place, along_x, along_z)
    along_z, along_x, early = from_both(
        middle_parts[:4], "z", middle_parts[4:], "x", True, early
    )
    early = pair_sum(early, "yh")
    d_h1_own = near_sum(parts[0], parts[1]) + d_far.astype(F32)
    along_z, (d_h1_own, early) = after(along_z, (d_h1_own, early))
    late_keep, late_send = late_last(place, along_z, along_x)
    late = late_keep + other(late_send, "yh").astype(F32)

    normed1, factor1 = norm_rows(tokens.astype(F32))
    d_norm1 = norm_back(d_h1_own, normed1, factor1, gain_rows[0])
    input_grad = (d_middle + d_norm1).astype(BF16)

    grad_query = late[:, :heads_w]
    grad_keyval = late[:, 2 * LATE_WIDTH - heads_w :]
    grad_out = late[:, heads_w : 2 * LATE_WIDTH - heads_w].T
    grad_gateup = early[:, : 2 * hidden_w].reshape(-1, 2, hidden_w)

    gain_sum = jnp.stack(
        [
            jnp.sum(grad_query * w_query.astype(F32) + grad_keyval * w_keyval.astype(F32), 1),
            jnp.sum(grad_gateup * w_gateup.astype(F32), (1, 2)),
        ]
    )
    gain_sum = gain_sum + sum(
        lax.ppermute(gain_sum, ("yl", "core"), [(i ^ step, i) for i in range(4)])
        for step in (1, 2, 3)
    )
    grad_gains = lax.dynamic_slice(gain_sum, (0, block * gains_w), (2, gains_w)) / norm_gains
    return (
        result,
        input_grad,
        grad_query,
        grad_keyval,
        grad_out,
        grad_gateup,
        early[:, 2 * hidden_w :].T,
        grad_gains,
    )


def solution(mesh):
    fine = Mesh(mesh.devices.reshape(4, 4, 2, 2, 2), ("x", "z", "yh", "yl", "core"))
    dp = ("x", "z", "yh")
    tensor = ("yl", "core")
    every = dp + tensor
    weights = (P(dp, tensor), P(dp, tensor), P(tensor, dp), P(dp, None, tensor), P(tensor, dp))
    rows = P(every, None)
    gains = P(None, every)
    return jax.shard_map(
        body,
        mesh=fine,
        in_specs=(rows, gains) + weights + (rows,),
        out_specs=(rows, rows) + weights + (gains,),
        check_vma=False,
    )
```

```python
import jax
import jax.numpy as jnp
from jax import lax
from jax.experimental import pallas as pl
from jax.experimental.pallas import tpu as pltpu
from jax.sharding import Mesh, PartitionSpec as P

HD = 96
F32 = jnp.float32
BF16 = jnp.bfloat16
norm_eps = 1e-05
rope_base = 100000.0
LOG2E = 1.4426950408889634
SCALE = HD ** (-0.5)
MIB = 1024 * 1024
SMALL = pl.CostEstimate(flops=1, bytes_accessed=1, transcendentals=0)

GAIN_AT, OUT_AT, QUERY_AT, KEYVAL_AT, REST_AT, ATTN_WIDTH = 0, 128, 256, 640, 1024, 1280
HALF_WIDTH = ATTN_WIDTH // 2
OUT_CUT = QUERY_AT - OUT_AT
LIMIT = 56


def dot_n(left, right):
    return jnp.dot(left, right, preferred_element_type=F32)


def dot_t(left, right):
    return lax.dot_general(left, right, (((1,), (1,)), ((), ())), preferred_element_type=F32)


def dot_tn(left, right):
    return lax.dot_general(left, right, (((0,), (0,)), ((), ())), preferred_element_type=F32)


def dot_tt(left, right):
    return lax.dot_general(left, right, (((0,), (1,)), ((), ())), preferred_element_type=F32)


def block_at(index, size):
    return pl.ds(pl.multiple_of(index * size, size), size)


def causal_mask(scores, size):
    key_at = lax.broadcasted_iota(jnp.int32, (size, scores.shape[1]), 0)
    query_at = lax.broadcasted_iota(jnp.int32, (size, scores.shape[1]), 1) % size
    tail = jnp.where(key_at <= query_at, scores[-size:], -1e30)
    if scores.shape[0] == size:
        return tail
    return jnp.concatenate([scores[:-size], tail], 0)


class Moves:
    def __init__(self, sems):
        self.sems = sems
        self.started = []

    def start(self, source, target):
        copy = pltpu.make_async_copy(source, target, self.sems.at[len(self.started)])
        copy.start()
        self.started.append(copy)
        return copy

    def wait(self):
        for copy in self.started:
            copy.wait()


def vmem(shape, dtype=BF16):
    return pltpu.VMEM(shape, dtype)


def like(shape, dtype=BF16):
    return jax.ShapeDtypeStruct(shape, dtype)


def whole():
    return pl.BlockSpec(memory_space=pltpu.VMEM)


def apart():
    return pl.BlockSpec(memory_space=pl.ANY)


def scalars():
    return pl.BlockSpec(memory_space=pltpu.SMEM)


def kernel_call(kernel, name, place, small, large, outs, small_outs, scratch, *copies):
    return pl.pallas_call(
        kernel,
        out_shape=list(small_outs) + list(outs),
        in_specs=[scalars()] + [whole()] * len(small) + [apart()] * len(large),
        out_specs=[whole()] * len(small_outs) + [apart()] * len(outs),
        scratch_shapes=list(scratch)
        + [pltpu.SemaphoreType.DMA((count,)) for count in copies],
        compiler_params=pltpu.CompilerParams(vmem_limit_bytes=LIMIT * MIB),
        cost_estimate=SMALL,
        name=name,
    )(place, *small, *large)


def probs_at(step, size):
    return step * (step + 1) // 2 * size, (step + 1) * size


def head_rows(head):
    return slice(head * HD, (head + 1) * HD)


def attend_kernel(place, cos_ref, sin_ref, t0, t1, t2, t3, a0, a1, a2, a3, b0, b1, b2, b3,
                  gains_ref, w_hbm, h_hbm, qt_hbm, kt_hbm, vt_hbm, attn_hbm, probs_hbm,
                  o0, o1, o2, o3,
                  t_ref, w_ref, h_ref, qt_ref, kt_ref, vt_ref, attn_ref, probs_ref, part_ref, k_ref,
                  in_sem, out_sem, probs_sem):
    block, ix, iz = place[0], place[1], place[2]
    half = HD // 2
    size = t_ref.shape[1]
    heads = qt_ref.shape[0]
    group_size = heads // kt_ref.shape[0]
    rows = a0.shape[1]
    fetch, store = Moves(in_sem), Moves(out_sem)
    gains_came, came = [], []
    for far, (along_x, along_z) in enumerate(zip((a0, a1, a2, a3), (b0, b1, b2, b3))):
        for near in range(4):
            at_a = block_at(lax.rem(ix + far, 4) * 4 + lax.rem(iz + near, 4), rows)
            at_b = block_at(lax.rem(ix + near, 4) * 4 + lax.rem(iz + far, 4), rows)
            for source, first, width, target, copies in (
                (along_x, 0, OUT_AT, at_a, gains_came),
                (along_x, OUT_AT, HALF_WIDTH - OUT_AT, at_a, came),
                (along_z, HALF_WIDTH, HALF_WIDTH, at_b, came),
            ):
                copies.append((
                    source.at[near, :, pl.ds(first % HALF_WIDTH, width)],
                    w_ref.at[target, pl.ds(first, width)],
                ))
    gains_came = [fetch.start(*copy) for copy in gains_came]
    tokens_came = [
        fetch.start(piece, t_ref.at[i]) for i, piece in enumerate((t0, t1, t2, t3))
    ]
    came = [fetch.start(*copy) for copy in came]
    for copy in gains_came:
        copy.wait()
    gains = w_ref[:, GAIN_AT:OUT_AT].astype(F32).T
    gain_row = gains[0:1] + gains[2:3]
    gains_ref[...] = gains[0:2] + gains[2:4]
    for step in range(4):
        tokens_came[step].wait()
        value = t_ref[step].astype(F32)
        factor = lax.rsqrt(jnp.mean(value * value, -1, keepdims=True) + norm_eps)
        h_ref[block_at(lax.bitwise_xor(block, step), size), :] = (
            value * factor * gain_row).astype(BF16)
    for copy in came:
        copy.wait()
    store.start(w_ref, w_hbm)
    for step in range(4):
        at = slice(step * size, (step + 1) * size)
        normed = h_ref[at, :]
        cosine = cos_ref[:, at]
        sine = sin_ref[:, at]
        every = dot_n(normed, w_ref[:, QUERY_AT:REST_AT]).T
        query, keyval = every[: KEYVAL_AT - QUERY_AT], every[KEYVAL_AT - QUERY_AT :]

        def rotated(field):
            first, second = field[:half], field[half:]
            return jnp.concatenate(
                [first * cosine - second * sine, second * cosine + first * sine], 0
            )

        for head in range(heads):
            qt_ref[head, :, at] = rotated(query[head_rows(head)]).astype(BF16)
        for group in range(heads // group_size):
            key = rotated(keyval[head_rows(2 * group)])
            kt_ref[group, :, at] = key.astype(BF16)
            k_ref[group, at, :] = key.T.astype(BF16)
            vt_ref[group, :, at] = keyval[head_rows(2 * group + 1)].astype(BF16)
    for source, target in ((h_ref, h_hbm), (qt_ref, qt_hbm), (kt_ref, kt_hbm), (vt_ref, vt_hbm)):
        store.start(source, target)

    def probs_copy(group):
        return pltpu.make_async_copy(
            probs_ref.at[group], probs_hbm.at[group], probs_sem.at[group])

    for group in range(heads // group_size):
        members = range(group * group_size, (group + 1) * group_size)
        for step in range(4):
            first, reach = probs_at(step, size)
            columns = slice(step * size, reach)
            query = jnp.concatenate([qt_ref[head, :, columns] for head in members], 1)
            scores = causal_mask(dot_n(k_ref[group, :reach, :], query), size)
            top = jnp.max(scores, 0, keepdims=True)
            expo = jnp.exp2((scores - top) * (SCALE * LOG2E))
            total = jnp.sum(expo, 0, keepdims=True)
            probs = (expo * (1.0 / total)).astype(BF16)
            probs_ref[group, first : first + reach, :] = probs
            mixed = dot_n(vt_ref[group, :, :reach], probs).astype(BF16)
            for i, head in enumerate(members):
                attn_ref[head_rows(head), columns] = mixed[:, i * size : (i + 1) * size]
        probs_copy(group).start()
    store.start(attn_ref, attn_hbm)
    for step, out in ((1, o1), (3, o3), (2, o2), (0, o0)):
        at = block_at(lax.bitwise_xor(block, step), size)
        part = dot_tt(attn_ref[:OUT_CUT, at], w_ref[:, OUT_AT:QUERY_AT])
        part += dot_tt(attn_ref[OUT_CUT:, at], w_ref[:, REST_AT:])
        part_ref[step] = part.astype(BF16)
        store.start(part_ref.at[step], out)
    store.wait()
    for group in range(heads // group_size):
        probs_copy(group).wait()


def attend(place, pieces, along_x, along_z, cosine, sine):
    size, width = pieces[0].shape
    length = 4 * size
    heads = (KEYVAL_AT - QUERY_AT) // HD
    groups = (REST_AT - KEYVAL_AT) // (2 * HD)
    columns, g_columns = (heads, HD, length), (groups, HD, length)
    probs = (groups, sum(probs_at(3, size)), heads // groups * size)
    kept = [(width, ATTN_WIDTH), (length, width), columns, g_columns, g_columns,
            (heads * HD, length), probs]
    return kernel_call(
        attend_kernel, "attend", place, (cosine, sine), (*pieces, *along_x, *along_z),
        [like(s) for s in kept + [(size, width)] * 4], [like((2, width), F32)],
        [vmem(s) for s in [(4, size, width)] + kept + [(4, size, width), (groups, length, HD)]],
        52, 10, groups)


def attend_back_kernel(place, cos_ref, sin_ref,
                       o0, o1, o2, o3, w_hbm, h_hbm, qt_hbm, kt_hbm, vt_hbm, attn_hbm, probs_hbm,
                       dqkv_hbm, x0, x1, x2, x3, y0, y1, y2, y3,
                       o_ref, w_ref, h_ref, qt_ref, kt_ref, vt_ref, attn_ref, probs_ref,
                       do_ref, dqkv_ref, first_ref, second_ref, v_ref, delta_ref, dk_ref, dv_ref,
                       in_sem, out_sem, probs_sem):
    block, ix, iz = place[0], place[1], place[2]
    heads, _, length = qt_ref.shape
    groups = kt_ref.shape[0]
    group_size = heads // groups
    size = length // 4
    half = HD // 2
    width = w_ref.shape[0]
    heads_w = heads * HD
    fetch, store = Moves(in_sem), Moves(out_sem)
    rest_w = ATTN_WIDTH - REST_AT
    early = [
        fetch.start(w_hbm.at[:, pl.ds(OUT_AT, OUT_CUT)], w_ref.at[:, pl.ds(0, OUT_CUT)]),
        fetch.start(w_hbm.at[:, pl.ds(REST_AT, rest_w)], w_ref.at[:, pl.ds(OUT_CUT, rest_w)]),
    ]
    early += [
        fetch.start(piece, o_ref.at[block_at(lax.bitwise_xor(block, i), size), :])
        for i, piece in enumerate((o0, o1, o2, o3))
    ]
    middle = [
        fetch.start(source, target)
        for source, target in ((attn_hbm, attn_ref), (vt_hbm, vt_ref), (qt_hbm, qt_ref),
                               (kt_hbm, kt_ref))
    ]

    def probs_copy(group):
        return pltpu.make_async_copy(
            probs_hbm.at[group], probs_ref.at[group], probs_sem.at[group])

    for group in range(groups):
        probs_copy(group).start()
    h_came = fetch.start(h_hbm, h_ref)
    for copy in early:
        copy.wait()
    do_ref[...] = dot_tt(w_ref[...], o_ref[...]).astype(BF16)
    for copy in middle:
        copy.wait()
    for group in range(groups):
        v_ref[group] = vt_ref[group].astype(F32).T.astype(BF16)
    for head in range(heads):
        rows = head_rows(head)
        delta_ref[head] = jnp.sum(
            attn_ref[rows, :].astype(F32) * do_ref[rows, :].astype(F32), 0, keepdims=True)

    def turned_back(field, cosine, sine):
        first, second = field[:half], field[half:]
        return jnp.concatenate(
            [first * cosine + second * sine, second * cosine - first * sine], 0).astype(BF16)

    for group in range(groups):
        members = range(group * group_size, (group + 1) * group_size)
        probs_copy(group).wait()
        for step in range(4):
            first, reach = probs_at(step, size)
            columns = slice(step * size, reach)
            probs = probs_ref[group, first : first + reach, :]
            query = jnp.concatenate([qt_ref[head, :, columns] for head in members], 1)
            d_out = jnp.concatenate([do_ref[head_rows(head), columns] for head in members], 1)
            delta = jnp.concatenate([delta_ref[head, :, columns] for head in members], 1)
            d_probs = dot_n(v_ref[group, :reach, :], d_out)
            d_scores = (probs.astype(F32) * (d_probs - delta)).astype(BF16)
            for ref, left, right in ((dv_ref, d_out, probs), (dk_ref, query, d_scores)):
                change = dot_t(left, right)
                if step > 0:
                    ref[group, :, : step * size] += change[:, : step * size]
                ref[group, :, columns] = change[:, columns]
            d_query = dot_n(kt_ref[group, :, :reach], d_scores) * SCALE
            for i, head in enumerate(members):
                dqkv_ref[head_rows(head), columns] = turned_back(
                    d_query[:, i * size : (i + 1) * size],
                    cos_ref[:, columns], sin_ref[:, columns])
        dqkv_ref[head_rows(heads + 2 * group), :] = turned_back(
            dk_ref[group] * SCALE, cos_ref[...], sin_ref[...])
        dqkv_ref[head_rows(heads + 2 * group + 1), :] = dv_ref[group].astype(BF16)
    store.start(dqkv_ref, dqkv_hbm)
    h_came.wait()

    rows = width // 16
    part = dot_tt(h_ref[...], dqkv_ref[...]).astype(BF16)
    first_ref[:, :heads_w] = part[:, :heads_w]
    second_ref[:, LATE_WIDTH - heads_w :] = part[:, heads_w:]
    part = dot_tt(o_ref[...], attn_ref[...]).astype(BF16)
    first_ref[:, heads_w:] = part[:, :LATE_OUT]
    second_ref[:, : heads_w - LATE_OUT] = part[:, LATE_OUT:]
    for offset, (x_out, y_out) in enumerate(((x0, y0), (x1, y1), (x2, y2), (x3, y3))):
        to_x = lax.rem(ix + 4 - offset, 4)
        to_z = lax.rem(iz + 4 - offset, 4)
        store.start(first_ref.at[block_at(to_x, 4 * rows), :], x_out)
        for i in range(4):
            store.start(second_ref.at[block_at(i * 4 + to_z, rows), :], y_out.at[i])
    store.wait()


def attend_back(place, cosine, sine, pieces, weights, h_first, qt, kt, vt, attn, probs):
    width = weights.shape[0]
    heads, _, length = qt.shape
    groups = kt.shape[0]
    every_w = (heads + 2 * groups) * HD
    rows = width // 16
    outs = [(every_w, length)] + [(4 * rows, LATE_WIDTH)] * 4 + [(4, rows, LATE_WIDTH)] * 4
    scratch = [
        (length, width), (width, heads * HD), (length, width),
        qt.shape, kt.shape, vt.shape, attn.shape, probs.shape,
        attn.shape, (every_w, length), (width, LATE_WIDTH), (width, LATE_WIDTH),
        (groups, length, HD),
    ]
    wide = [(heads, 1, length), kt.shape, kt.shape]
    return kernel_call(
        attend_back_kernel, "attend_back", place, (cosine, sine),
        (*pieces, weights, h_first, qt, kt, vt, attn, probs),
        [like(s) for s in outs], [],
        [vmem(s) for s in scratch] + [vmem(s, F32) for s in wide], 11, 21, groups)


def project_back_kernel(place, dqkv_hbm, w_hbm, c0, c1, c2, c3,
                        dqkv_ref, w_ref, part_ref, in_sem, out_sem):
    block = place[0]
    size = part_ref.shape[1]
    fetch, store = Moves(in_sem), Moves(out_sem)
    fetch.start(w_hbm.at[:, pl.ds(QUERY_AT, REST_AT - QUERY_AT)], w_ref)
    fetch.start(dqkv_hbm, dqkv_ref)
    fetch.wait()
    for step, out in ((3, c3), (2, c2), (1, c1), (0, c0)):
        at = block_at(lax.bitwise_xor(block, step), size)
        part_ref[step] = dot_tt(dqkv_ref[:, at], w_ref[...]).astype(BF16)
        store.start(part_ref.at[step], out)
    store.wait()


def project_back(place, d_qkv, weights):
    every_w, length = d_qkv.shape
    width = weights.shape[0]
    size = length // 4
    return kernel_call(
        project_back_kernel, "project_back", place, (), (d_qkv, weights),
        [like((size, width))] * 4, [],
        [vmem(s) for s in (d_qkv.shape, (width, every_w), (4, size, width))], 2, 4)


def feed_kernel(place, h0, h1, g0, g1, w_hbm, hidden_hbm, dgu_hbm, b0, b1, r0, r1,
                w_ref, h_ref, g_ref, hidden_ref, dgu_ref, back_ref, out_ref, in_sem, out_sem):
    del place
    hidden_w = hidden_ref.shape[1]
    size = h_ref.shape[1]
    parts = [slice(i * hidden_w, (i + 1) * hidden_w) for i in range(3)]
    fetch, store = Moves(in_sem), Moves(out_sem)

    def weight(i):
        at = pl.ds(i * hidden_w, hidden_w)
        return fetch.start(w_hbm.at[:, at], w_ref.at[:, at])

    came = [fetch.start(h0, h_ref.at[0]), weight(0), weight(1), fetch.start(g0, g_ref.at[0]),
            weight(2), fetch.start(h1, h_ref.at[1]), fetch.start(g1, g_ref.at[1])]
    for i, (back, out) in enumerate(((b0, r0), (b1, r1))):
        rows = slice(i * size, (i + 1) * size)
        at = pl.ds(i * size, size)
        for copy in came[0:2] if i == 0 else came[5:7]:
            copy.wait()
        gate = dot_n(h_ref[i], w_ref[:, parts[0]])
        if i == 0:
            came[2].wait()
        up = dot_n(h_ref[i], w_ref[:, parts[1]])
        sig = 1.0 / (1.0 + jnp.exp2(gate * (-LOG2E)))
        silu = gate * sig
        hidden = (silu * up).astype(BF16)
        hidden_ref[rows, :] = hidden
        store.start(hidden_ref.at[at, :], hidden_hbm.at[at, :])
        if i == 0:
            came[3].wait()
            came[4].wait()
        d_hidden = dot_n(g_ref[i], w_ref[:, parts[2]])
        dgu_ref[rows, :hidden_w] = (
            d_hidden * up * (sig * (1.0 + gate * (1.0 - sig)))).astype(BF16)
        dgu_ref[rows, hidden_w:] = (d_hidden * silu).astype(BF16)
        store.start(dgu_ref.at[at, :], dgu_hbm.at[at, :])
        back_ref[i] = dot_t(dgu_ref[rows, :], w_ref[:, : 2 * hidden_w]).astype(BF16)
        store.start(back_ref.at[i], back)
        out_ref[i] = dot_t(hidden_ref[rows, :], w_ref[:, parts[2]]).astype(BF16)
        store.start(out_ref.at[i], out)
    store.wait()


def feed(place, weights, normed_pieces, grad_pieces):
    size, width = normed_pieces[0].shape
    hidden_w = weights.shape[1] // 3
    wide = [(2 * size, hidden_w), (2 * size, 2 * hidden_w)]
    return kernel_call(
        feed_kernel, "feed", place, (), (*normed_pieces, *grad_pieces, weights),
        [like(s) for s in wide + [(size, width)] * 4], [],
        [vmem(s) for s in [weights.shape] + [(2, size, width)] * 2 + wide + [(2, size, width)] * 2],
        7, 8)


def feed_grads_kernel(place, h0, h1, h2, h3, g0, g1, g2, g3, dgu_a, dgu_b, hidden_a, hidden_b,
                      out_hbm, h_ref, g_ref, dgu_ref, hidden_ref, out_ref, in_sem, out_sem):
    del place
    size = h0.shape[0]
    half, hidden_w = hidden_a.shape
    column = 512
    fetch, store = Moves(in_sem), Moves(out_sem)

    def rows_of(pieces, ref):
        return [
            fetch.start(piece, ref.at[pl.ds(i * size, size), :]) for i, piece in enumerate(pieces)
        ]

    def tiles_of(pieces, ref):
        tiles = []
        for tile in range(ref.shape[1] // column):
            at = pl.ds(tile * column, column)
            tiles.append([
                fetch.start(piece.at[:, at], ref.at[pl.ds(i * half, half), at])
                for i, piece in enumerate(pieces)
            ])
        return tiles

    h_came = rows_of((h0, h1, h2, h3), h_ref)
    dgu_came = tiles_of((dgu_a, dgu_b), dgu_ref)
    g_came = rows_of((g0, g1, g2, g3), g_ref)
    hidden_came = tiles_of((hidden_a, hidden_b), hidden_ref)
    at = 0
    for came, left, tiles, right in (
        (h_came, h_ref, dgu_came, dgu_ref), (g_came, g_ref, hidden_came, hidden_ref)
    ):
        for copy in came:
            copy.wait()
        for tile, copies in enumerate(tiles):
            for copy in copies:
                copy.wait()
            columns = pl.ds(at, column)
            out_ref[:, columns] = dot_tn(
                left[...], right[:, tile * column : (tile + 1) * column]).astype(BF16)
            store.start(out_ref.at[:, columns], out_hbm.at[:, columns])
            at += column
    store.wait()


def feed_grads(place, normed_pieces, grad_pieces, dgu_a, dgu_b, hidden_a, hidden_b):
    size, width = normed_pieces[0].shape
    half, hidden_w = hidden_a.shape
    scratch = [(4 * size, width)] * 2 + [(2 * half, 2 * hidden_w), (2 * half, hidden_w),
                                         (width, 3 * hidden_w)]
    return kernel_call(
        feed_grads_kernel, "feed_grads", place, (),
        (*normed_pieces, *grad_pieces, dgu_a, dgu_b, hidden_a, hidden_b),
        [like((width, 3 * hidden_w))], [], [vmem(s) for s in scratch], 20, 6)[0]


LATE_OUT, LATE_WIDTH = 192, 576


def late_middle_kernel(place, *refs):
    x_in, y_in, outs = refs[0:4], refs[4:8], refs[8:]
    ix, iz = place[1], place[2]
    rows = outs[0].shape[0]
    for offset in range(4):
        at = block_at(lax.rem(iz + 4 - offset, 4), rows)
        total = x_in[0][at, :].astype(F32)
        for ref in x_in[1:]:
            total += ref[at, :].astype(F32)
        outs[offset][...] = total.astype(BF16)
        to = lax.rem(ix + 4 - offset, 4)
        total = y_in[0][to].astype(F32)
        for ref in y_in[1:]:
            total += ref[to].astype(F32)
        outs[4 + offset][...] = total.astype(BF16)


def late_middle(place, along_x, along_z):
    _, rows, width = along_z[0].shape
    return pl.pallas_call(
        late_middle_kernel,
        out_shape=[like((rows, width))] * 8,
        in_specs=[scalars()] + [whole()] * 8,
        out_specs=[whole()] * 8,
        compiler_params=pltpu.CompilerParams(vmem_limit_bytes=16 * MIB),
        cost_estimate=SMALL,
        name="late_middle",
    )(place, *along_x, *along_z)


def late_last_kernel(place, *refs):
    x_in, y_in, keep_ref, send_ref = refs[0:4], refs[4:8], refs[8], refs[9]
    mine = place[3]
    rows = keep_ref.shape[0]
    for inputs, columns in ((x_in, slice(0, LATE_WIDTH)), (y_in, slice(LATE_WIDTH, 2 * LATE_WIDTH))):
        for ref, half in ((keep_ref, mine), (send_ref, 1 - mine)):
            at = block_at(half, rows)
            total = inputs[0][at, :].astype(F32)
            for other_ref in inputs[1:]:
                total += other_ref[at, :].astype(F32)
            ref[:, columns] = total.astype(ref.dtype)


def late_last(place, along_z, along_x):
    rows, width = along_x[0].shape
    return pl.pallas_call(
        late_last_kernel,
        out_shape=[
            jax.ShapeDtypeStruct((rows // 2, 2 * width), F32),
            jax.ShapeDtypeStruct((rows // 2, 2 * width), BF16),
        ],
        in_specs=[scalars()] + [whole()] * 8,
        out_specs=[whole()] * 2,
        compiler_params=pltpu.CompilerParams(vmem_limit_bytes=16 * MIB),
        cost_estimate=SMALL,
        name="late_last",
    )(place, *along_z, *along_x)


def feed_norm_back_kernel(own, core, far, middle, cotangent, gain, d_middle, d_out):
    grad = own[...].astype(F32) + core[...].astype(F32) + far[...].astype(F32)
    value = middle[...]
    factor = lax.rsqrt(jnp.mean(value * value, -1, keepdims=True) + norm_eps)
    normed = value * factor
    grad = grad * gain[...]
    inner = jnp.mean(grad * normed, -1, keepdims=True)
    total = cotangent[...].astype(F32) + factor * (grad - normed * inner)
    d_middle[...] = total
    d_out[...] = total.astype(BF16)


def feed_norm_back(own, core, far, middle, cotangent, gain_row):
    size, width = middle.shape
    rows = pl.BlockSpec((size // 4, width), lambda i: (i, 0))
    return pl.pallas_call(
        feed_norm_back_kernel,
        grid=(4,),
        out_shape=[like((size, width), F32), like((size, width))],
        in_specs=[rows] * 5 + [pl.BlockSpec((1, width), lambda i: (0, 0))],
        out_specs=[rows] * 2,
        compiler_params=pltpu.CompilerParams(vmem_limit_bytes=16 * MIB),
        cost_estimate=SMALL,
        name="feed_norm_back",
    )(own, core, far, middle, cotangent, gain_row)


def norm_rows(values_in):
    factor = lax.rsqrt(jnp.mean(values_in * values_in, -1, keepdims=True) + norm_eps)
    return (values_in * factor, factor)


def norm_back(grad_in, normed, factor, gain_row):
    grad_normed = grad_in * gain_row
    inner = jnp.mean(grad_normed * normed, -1, keepdims=True)
    return factor * (grad_normed - normed * inner)


def from_offset(v, axis, offset, size):
    return lax.ppermute(v, axis, [((i + offset) % size, i) for i in range(size)])


def other(v, axis):
    return from_offset(v, axis, 1, 2)


def pair_rows(v, axis):
    it = other(v, axis)
    mine = jnp.arange(2)[:, None, None] == lax.axis_index(axis)
    return jnp.where(mine, v[None], it[None]).reshape(2 * v.shape[0], v.shape[1])


def side_by_side(parts, width):
    return sum(
        jnp.pad(part, ((0, 0), (at, width - at - part.shape[1]))) for at, part in parts
    )


def near_sum(own, core):
    return own.astype(F32) + other(core, "core").astype(F32)


def far_sum(chip, diagonal):
    return near_sum(chip, diagonal).astype(BF16)


def after(value, first):
    return lax.optimization_barrier((value, first))


def from_both(along_first, first_axis, along_second, second_axis, large, beside=()):
    near = [
        from_offset(part[i], axis, i, 4)
        for i in (1, 3)
        for part, axis in ((along_first, first_axis), (along_second, second_axis))
    ]
    opposite = along_first[2], along_second[2]
    if large:
        opposite, (near, beside) = after(opposite, (near, beside))
    far = [from_offset(opposite[0], first_axis, 2, 4), from_offset(opposite[1], second_axis, 2, 4)]
    near, far = after(near, far)
    first = [along_first[0], near[0], far[0], near[2]]
    second = [along_second[0], near[1], far[1], near[3]]
    return first, second, beside


def pair_sum(v, axis):
    rows = v.shape[0] // 2
    me = lax.axis_index(axis)
    keep = lax.dynamic_slice_in_dim(v, me * rows, rows, 0)
    send = lax.dynamic_slice_in_dim(v, (1 - me) * rows, rows, 0)
    return keep.astype(F32) + other(send, axis).astype(F32)


def body(tokens, norm_gains, w_query, w_keyval, w_out, w_gateup, w_down, cotangent):
    D = tokens.shape[1]
    length = 4 * tokens.shape[0]
    hidden_w = w_down.shape[0]
    heads_w = w_query.shape[1]
    gains_w = norm_gains.shape[1]
    block = lax.axis_index("yl") * 2 + lax.axis_index("core")
    place = jnp.stack(
        [block, lax.axis_index("x"), lax.axis_index("z"), lax.axis_index("yh")]
    ).astype(jnp.int32)

    out_t = w_out.T
    attn_own = side_by_side(
        [
            (OUT_AT, out_t[:, :OUT_CUT]),
            (QUERY_AT, w_query),
            (KEYVAL_AT, w_keyval),
            (REST_AT, out_t[:, OUT_CUT:]),
        ],
        ATTN_WIDTH,
    )
    attn_pair = pair_rows(attn_own, "yh")
    pair_w = 8 * gains_w
    gain_at = (lax.axis_index("yh") * 4 + block) * gains_w
    gain_part = lax.dynamic_update_slice(jnp.zeros((2, pair_w), F32), norm_gains, (0, gain_at))
    for axis in ("core", "yl", "yh"):
        gain_part = gain_part + other(gain_part, axis)
    (gate_up, down), gain_part = after((w_gateup, w_down), gain_part)
    mlp_own = (gate_up[:, 0], gate_up[:, 1], down.T)
    mlp_own = [(i * hidden_w, part) for i, part in enumerate(mlp_own)]
    mlp_pair = pair_rows(side_by_side(mlp_own, 3 * hidden_w), "yh")
    gain_part = gain_part.T
    gain_high = lax.reduce_precision(gain_part, 8, 7)
    gain_low = (gain_part - gain_high).astype(BF16)
    gain_high = gain_high.astype(BF16)
    first, second = attn_pair[:, :HALF_WIDTH], attn_pair[:, HALF_WIDTH:]
    first += side_by_side([(0, gain_high), (2, gain_low)], HALF_WIDTH)

    along_z, along_x, _ = from_both([first] * 4, "z", [second] * 4, "x", False)
    along_z, along_x, mlp_pair, tokens = lax.optimization_barrier(
        (jnp.stack(along_z), jnp.stack(along_x), mlp_pair, tokens)
    )
    mlp_w = lax.all_gather(mlp_pair, ("x", "z"), axis=0, tiled=True)
    along_x, along_z, far = from_both(
        [along_z] * 4, "x", [along_x] * 4, "z", True, other(tokens, "yl")
    )
    token_pieces = [tokens, other(tokens, "core"), far, other(far, "core")]
    cotangent, far = after(cotangent, far)
    grad_far = other(cotangent, "yl")

    positions = jnp.arange(length).astype(F32)
    freqs = rope_base ** (-(jnp.arange(HD // 2).astype(F32) * 2.0 / HD))
    angles = freqs[:, None] * positions[None, :]
    cosine, sine = jnp.cos(angles), jnp.sin(angles)

    gain_rows, attn_w, h_first, qt, kt, vt, attn, probs, *parts = attend(
        place, token_pieces, along_x, along_z, cosine, sine
    )
    grad_far, parts = after(grad_far, parts)
    grad_pieces = [cotangent, other(cotangent, "core"), grad_far, other(grad_far, "core")]
    middle_far = far_sum(parts[2], parts[3])
    middle = (
        tokens.astype(F32) + near_sum(parts[0], parts[1]) + other(middle_far, "yl").astype(F32)
    )
    normed2, factor2 = norm_rows(middle)
    h_own = (normed2 * gain_rows[1]).astype(BF16)

    h_pieces = [h_own, other(h_own, "core")]
    h_far = other(h_own, "yl")
    hidden_a, dgu_a, back_own, back_core, out_own, out_core = feed(
        place, mlp_w, h_pieces, grad_pieces[:2]
    )
    h_far, hidden_a = after(h_far, hidden_a)
    h_pieces += [h_far, other(h_far, "core")]
    hidden_b, dgu_b, back_chip, back_diag, out_chip, out_diag = feed(
        place, mlp_w, h_pieces[2:], grad_pieces[2:]
    )
    back_core = other(back_core, "core")
    out_near = near_sum(out_own, out_core)

    back_far = far_sum(back_chip, back_diag)
    hidden_b, (back_far, back_core) = after(hidden_b, (back_far, back_core))
    mlp_grads = feed_grads(place, h_pieces, grad_pieces, dgu_a, dgu_b, hidden_a, hidden_b)
    mlp_grads, back_far = after(mlp_grads, other(back_far, "yl"))
    early = lax.psum_scatter(mlp_grads, ("x", "z"), scatter_dimension=0, tiled=True)
    out_far = far_sum(out_chip, out_diag)

    d_middle, d_out = feed_norm_back(
        back_own, back_core, back_far, middle, cotangent, gain_rows[1:2])
    d_out_far = other(d_out, "yl")
    d_out_far, out_near = after(d_out_far, out_near)
    out_pieces = [d_out, other(d_out, "core"), d_out_far, other(d_out_far, "core")]
    out_far, out_pieces = after(out_far, out_pieces)
    out_far = other(out_far, "yl")

    back = attend_back(
        place, cosine, sine, out_pieces, attn_w, h_first, qt, kt, vt, attn, probs
    )
    d_qkv, *late_parts = back
    d_qkv, out_far = after(d_qkv, out_far)
    along_x, along_z, parts = from_both(
        late_parts[:4], "x", late_parts[4:], "z", True, project_back(place, d_qkv, attn_w)
    )
    d_far = other(far_sum(parts[2], parts[3]), "yl")
    result = (middle + out_near + out_far.astype(F32)).astype(BF16)
    along_x, result = after(along_x, result)
    middle_parts = late_middle(place, along_x, along_z)
    along_z, along_x, early = from_both(
        middle_parts[:4], "z", middle_parts[4:], "x", True, early
    )
    early = pair_sum(early, "yh")
    d_h1_own = near_sum(parts[0], parts[1]) + d_far.astype(F32)
    along_z, (d_h1_own, early) = after(along_z, (d_h1_own, early))
    late_keep, late_send = late_last(place, along_z, along_x)
    late = late_keep + other(late_send, "yh").astype(F32)

    normed1, factor1 = norm_rows(tokens.astype(F32))
    d_norm1 = norm_back(d_h1_own, normed1, factor1, gain_rows[0])
    input_grad = (d_middle + d_norm1).astype(BF16)

    grad_query = late[:, :heads_w]
    grad_keyval = late[:, 2 * LATE_WIDTH - heads_w :]
    grad_out = late[:, heads_w : 2 * LATE_WIDTH - heads_w].T
    grad_gateup = early[:, : 2 * hidden_w].reshape(-1, 2, hidden_w)

    gain_sum = jnp.stack(
        [
            jnp.sum(grad_query * w_query.astype(F32) + grad_keyval * w_keyval.astype(F32), 1),
            jnp.sum(grad_gateup * w_gateup.astype(F32), (1, 2)),
        ]
    )
    gain_sum = gain_sum + sum(
        lax.ppermute(gain_sum, ("yl", "core"), [(i ^ step, i) for i in range(4)])
        for step in (1, 2, 3)
    )
    grad_gains = lax.dynamic_slice(gain_sum, (0, block * gains_w), (2, gains_w)) / norm_gains
    return (
        result,
        input_grad,
        grad_query,
        grad_keyval,
        grad_out,
        grad_gateup,
        early[:, 2 * hidden_w :].T,
        grad_gains,
    )


def solution(mesh):
    fine = Mesh(mesh.devices.reshape(4, 4, 2, 2, 2), ("x", "z", "yh", "yl", "core"))
    dp = ("x", "z", "yh")
    tensor = ("yl", "core")
    every = dp + tensor
    weights = (P(dp, tensor), P(dp, tensor), P(tensor, dp), P(dp, None, tensor), P(tensor, dp))
    rows = P(every, None)
    gains = P(None, every)
    return jax.shard_map(
        body,
        mesh=fine,
        in_specs=(rows, gains) + weights + (rows,),
        out_specs=(rows, rows) + weights + (gains,),
        check_vma=False,
    )
```

```python
import jax
import jax.numpy as jnp
from jax import lax
from jax.experimental import pallas as pl
from jax.experimental.pallas import tpu as pltpu
from jax.sharding import Mesh, PartitionSpec as P

HD = 96
F32 = jnp.float32
BF16 = jnp.bfloat16
norm_eps = 1e-05
rope_base = 100000.0
LOG2E = 1.4426950408889634
SCALE = HD ** (-0.5)
MIB = 1024 * 1024
SMALL = pl.CostEstimate(flops=1, bytes_accessed=1, transcendentals=0)

GAIN_AT, OUT_AT, QUERY_AT, KEYVAL_AT, REST_AT, ATTN_WIDTH = 0, 128, 256, 640, 1024, 1280
HALF_WIDTH = ATTN_WIDTH // 2
OUT_CUT = QUERY_AT - OUT_AT
LIMIT = 56


def dot_n(left, right):
    return jnp.dot(left, right, preferred_element_type=F32)


def dot_t(left, right):
    return lax.dot_general(left, right, (((1,), (1,)), ((), ())), preferred_element_type=F32)


def dot_tn(left, right):
    return lax.dot_general(left, right, (((0,), (0,)), ((), ())), preferred_element_type=F32)


def dot_tt(left, right):
    return lax.dot_general(left, right, (((0,), (1,)), ((), ())), preferred_element_type=F32)


def block_at(index, size):
    return pl.ds(pl.multiple_of(index * size, size), size)


def causal_mask(scores, size):
    key_at = lax.broadcasted_iota(jnp.int32, (size, scores.shape[1]), 0)
    query_at = lax.broadcasted_iota(jnp.int32, (size, scores.shape[1]), 1) % size
    tail = jnp.where(key_at <= query_at, scores[-size:], -1e30)
    if scores.shape[0] == size:
        return tail
    return jnp.concatenate([scores[:-size], tail], 0)


class Moves:
    def __init__(self, sems):
        self.sems = sems
        self.started = []

    def start(self, source, target):
        copy = pltpu.make_async_copy(source, target, self.sems.at[len(self.started)])
        copy.start()
        self.started.append(copy)
        return copy

    def wait(self):
        for copy in self.started:
            copy.wait()


def vmem(shape, dtype=BF16):
    return pltpu.VMEM(shape, dtype)


def like(shape, dtype=BF16):
    return jax.ShapeDtypeStruct(shape, dtype)


def whole():
    return pl.BlockSpec(memory_space=pltpu.VMEM)


def apart():
    return pl.BlockSpec(memory_space=pl.ANY)


def scalars():
    return pl.BlockSpec(memory_space=pltpu.SMEM)


def kernel_call(kernel, name, place, small, large, outs, small_outs, scratch, *copies):
    return pl.pallas_call(
        kernel,
        out_shape=list(small_outs) + list(outs),
        in_specs=[scalars()] + [whole()] * len(small) + [apart()] * len(large),
        out_specs=[whole()] * len(small_outs) + [apart()] * len(outs),
        scratch_shapes=list(scratch)
        + [pltpu.SemaphoreType.DMA((count,)) for count in copies],
        compiler_params=pltpu.CompilerParams(vmem_limit_bytes=LIMIT * MIB),
        cost_estimate=SMALL,
        name=name,
    )(place, *small, *large)


def probs_at(step, size):
    return step * (step + 1) // 2 * size, (step + 1) * size


def head_rows(head):
    return slice(head * HD, (head + 1) * HD)


def attend_kernel(place, cos_ref, sin_ref, t0, t1, t2, t3, a0, a1, a2, a3, b0, b1, b2, b3,
                  gains_ref, w_hbm, h_hbm, qt_hbm, kt_hbm, vt_hbm, attn_hbm, probs_hbm,
                  o0, o1, o2, o3,
                  t_ref, w_ref, h_ref, qt_ref, kt_ref, vt_ref, attn_ref, probs_ref, part_ref, k_ref,
                  in_sem, out_sem, probs_sem):
    block, ix, iz = place[0], place[1], place[2]
    half = HD // 2
    size = t_ref.shape[1]
    heads = qt_ref.shape[0]
    group_size = heads // kt_ref.shape[0]
    rows = a0.shape[1]
    fetch, store = Moves(in_sem), Moves(out_sem)
    gains_came, came = [], []
    for far, (along_x, along_z) in enumerate(zip((a0, a1, a2, a3), (b0, b1, b2, b3))):
        for near in range(4):
            at_a = block_at(lax.rem(ix + far, 4) * 4 + lax.rem(iz + near, 4), rows)
            at_b = block_at(lax.rem(ix + near, 4) * 4 + lax.rem(iz + far, 4), rows)
            for source, first, width, target, copies in (
                (along_x, 0, OUT_AT, at_a, gains_came),
                (along_x, OUT_AT, HALF_WIDTH - OUT_AT, at_a, came),
                (along_z, HALF_WIDTH, HALF_WIDTH, at_b, came),
            ):
                copies.append((
                    source.at[near, :, pl.ds(first % HALF_WIDTH, width)],
                    w_ref.at[target, pl.ds(first, width)],
                ))
    gains_came = [fetch.start(*copy) for copy in gains_came]
    tokens_came = [
        fetch.start(piece, t_ref.at[i]) for i, piece in enumerate((t0, t1, t2, t3))
    ]
    came = [fetch.start(*copy) for copy in came]
    for copy in gains_came:
        copy.wait()
    gains = w_ref[:, GAIN_AT:OUT_AT].astype(F32).T
    gain_row = gains[0:1] + gains[2:3]
    gains_ref[...] = gains[0:2] + gains[2:4]
    for step in range(4):
        tokens_came[step].wait()
        value = t_ref[step].astype(F32)
        factor = lax.rsqrt(jnp.mean(value * value, -1, keepdims=True) + norm_eps)
        h_ref[block_at(lax.bitwise_xor(block, step), size), :] = (
            value * factor * gain_row).astype(BF16)
    for copy in came:
        copy.wait()
    store.start(w_ref, w_hbm)
    for step in range(4):
        at = slice(step * size, (step + 1) * size)
        normed = h_ref[at, :]
        cosine = cos_ref[:, at]
        sine = sin_ref[:, at]
        every = dot_n(normed, w_ref[:, QUERY_AT:REST_AT]).T
        query, keyval = every[: KEYVAL_AT - QUERY_AT], every[KEYVAL_AT - QUERY_AT :]

        def rotated(field):
            first, second = field[:half], field[half:]
            return jnp.concatenate(
                [first * cosine - second * sine, second * cosine + first * sine], 0
            )

        for head in range(heads):
            qt_ref[head, :, at] = rotated(query[head_rows(head)]).astype(BF16)
        for group in range(heads // group_size):
            key = rotated(keyval[head_rows(2 * group)])
            kt_ref[group, :, at] = key.astype(BF16)
            k_ref[group, at, :] = key.T.astype(BF16)
            vt_ref[group, :, at] = keyval[head_rows(2 * group + 1)].astype(BF16)
    for source, target in ((h_ref, h_hbm), (qt_ref, qt_hbm), (kt_ref, kt_hbm), (vt_ref, vt_hbm)):
        store.start(source, target)

    def probs_copy(group):
        return pltpu.make_async_copy(
            probs_ref.at[group], probs_hbm.at[group], probs_sem.at[group])

    for group in range(heads // group_size):
        members = range(group * group_size, (group + 1) * group_size)
        for step in range(4):
            first, reach = probs_at(step, size)
            columns = slice(step * size, reach)
            query = jnp.concatenate([qt_ref[head, :, columns] for head in members], 1)
            scores = causal_mask(dot_n(k_ref[group, :reach, :], query), size)
            top = jnp.max(scores, 0, keepdims=True)
            expo = jnp.exp2((scores - top) * (SCALE * LOG2E))
            total = jnp.sum(expo, 0, keepdims=True)
            probs = (expo * (1.0 / total)).astype(BF16)
            probs_ref[group, first : first + reach, :] = probs
            mixed = dot_n(vt_ref[group, :, :reach], probs).astype(BF16)
            for i, head in enumerate(members):
                attn_ref[head_rows(head), columns] = mixed[:, i * size : (i + 1) * size]
        probs_copy(group).start()
    store.start(attn_ref, attn_hbm)
    for step, out in ((1, o1), (3, o3), (2, o2), (0, o0)):
        at = block_at(lax.bitwise_xor(block, step), size)
        part = dot_tt(attn_ref[:OUT_CUT, at], w_ref[:, OUT_AT:QUERY_AT])
        part += dot_tt(attn_ref[OUT_CUT:, at], w_ref[:, REST_AT:])
        part_ref[step] = part.astype(BF16)
        store.start(part_ref.at[step], out)
    store.wait()
    for group in range(heads // group_size):
        probs_copy(group).wait()


def attend(place, pieces, along_x, along_z, cosine, sine):
    size, width = pieces[0].shape
    length = 4 * size
    heads = (KEYVAL_AT - QUERY_AT) // HD
    groups = (REST_AT - KEYVAL_AT) // (2 * HD)
    columns, g_columns = (heads, HD, length), (groups, HD, length)
    probs = (groups, sum(probs_at(3, size)), heads // groups * size)
    kept = [(width, ATTN_WIDTH), (length, width), columns, g_columns, g_columns,
            (heads * HD, length), probs]
    return kernel_call(
        attend_kernel, "attend", place, (cosine, sine), (*pieces, *along_x, *along_z),
        [like(s) for s in kept + [(size, width)] * 4], [like((2, width), F32)],
        [vmem(s) for s in [(4, size, width)] + kept + [(4, size, width), (groups, length, HD)]],
        52, 10, groups)


def attend_back_kernel(place, cos_ref, sin_ref,
                       o0, o1, o2, o3, w_hbm, h_hbm, qt_hbm, kt_hbm, vt_hbm, attn_hbm, probs_hbm,
                       dqkv_hbm, x0, x1, x2, x3, y0, y1, y2, y3,
                       o_ref, w_ref, h_ref, qt_ref, kt_ref, vt_ref, attn_ref, probs_ref,
                       do_ref, dqkv_ref, first_ref, second_ref, v_ref, delta_ref, dk_ref, dv_ref,
                       in_sem, out_sem, probs_sem):
    block, ix, iz = place[0], place[1], place[2]
    heads, _, length = qt_ref.shape
    groups = kt_ref.shape[0]
    group_size = heads // groups
    size = length // 4
    half = HD // 2
    width = w_ref.shape[0]
    heads_w = heads * HD
    fetch, store = Moves(in_sem), Moves(out_sem)
    rest_w = ATTN_WIDTH - REST_AT
    early = [
        fetch.start(w_hbm.at[:, pl.ds(OUT_AT, OUT_CUT)], w_ref.at[:, pl.ds(0, OUT_CUT)]),
        fetch.start(w_hbm.at[:, pl.ds(REST_AT, rest_w)], w_ref.at[:, pl.ds(OUT_CUT, rest_w)]),
    ]
    early += [
        fetch.start(piece, o_ref.at[block_at(lax.bitwise_xor(block, i), size), :])
        for i, piece in enumerate((o0, o1, o2, o3))
    ]
    middle = [
        fetch.start(source, target)
        for source, target in ((attn_hbm, attn_ref), (vt_hbm, vt_ref), (qt_hbm, qt_ref),
                               (kt_hbm, kt_ref))
    ]

    def probs_copy(group):
        return pltpu.make_async_copy(
            probs_hbm.at[group], probs_ref.at[group], probs_sem.at[group])

    for group in range(groups):
        probs_copy(group).start()
    h_came = fetch.start(h_hbm, h_ref)
    for copy in early:
        copy.wait()
    do_ref[...] = dot_tt(w_ref[...], o_ref[...]).astype(BF16)
    for copy in middle:
        copy.wait()
    for group in range(groups):
        v_ref[group] = vt_ref[group].astype(F32).T.astype(BF16)
    for head in range(heads):
        rows = head_rows(head)
        delta_ref[head] = jnp.sum(
            attn_ref[rows, :].astype(F32) * do_ref[rows, :].astype(F32), 0, keepdims=True)

    def turned_back(field, cosine, sine):
        first, second = field[:half], field[half:]
        return jnp.concatenate(
            [first * cosine + second * sine, second * cosine - first * sine], 0).astype(BF16)

    for group in range(groups):
        members = range(group * group_size, (group + 1) * group_size)
        probs_copy(group).wait()
        for step in range(4):
            first, reach = probs_at(step, size)
            columns = slice(step * size, reach)
            probs = probs_ref[group, first : first + reach, :]
            query = jnp.concatenate([qt_ref[head, :, columns] for head in members], 1)
            d_out = jnp.concatenate([do_ref[head_rows(head), columns] for head in members], 1)
            delta = jnp.concatenate([delta_ref[head, :, columns] for head in members], 1)
            d_probs = dot_n(v_ref[group, :reach, :], d_out)
            d_scores = (probs.astype(F32) * (d_probs - delta)).astype(BF16)
            for ref, left, right in ((dv_ref, d_out, probs), (dk_ref, query, d_scores)):
                change = dot_t(left, right)
                if step > 0:
                    ref[group, :, : step * size] += change[:, : step * size]
                ref[group, :, columns] = change[:, columns]
            d_query = dot_n(kt_ref[group, :, :reach], d_scores) * SCALE
            for i, head in enumerate(members):
                dqkv_ref[head_rows(head), columns] = turned_back(
                    d_query[:, i * size : (i + 1) * size],
                    cos_ref[:, columns], sin_ref[:, columns])
        dqkv_ref[head_rows(heads + 2 * group), :] = turned_back(
            dk_ref[group] * SCALE, cos_ref[...], sin_ref[...])
        dqkv_ref[head_rows(heads + 2 * group + 1), :] = dv_ref[group].astype(BF16)
    store.start(dqkv_ref, dqkv_hbm)
    h_came.wait()

    rows = width // 16
    part = dot_tt(h_ref[...], dqkv_ref[...]).astype(BF16)
    first_ref[:, :heads_w] = part[:, :heads_w]
    second_ref[:, LATE_WIDTH - heads_w :] = part[:, heads_w:]
    part = dot_tt(o_ref[...], attn_ref[...]).astype(BF16)
    first_ref[:, heads_w:] = part[:, :LATE_OUT]
    second_ref[:, : heads_w - LATE_OUT] = part[:, LATE_OUT:]
    for offset, (x_out, y_out) in enumerate(((x0, y0), (x1, y1), (x2, y2), (x3, y3))):
        to_x = lax.rem(ix + 4 - offset, 4)
        to_z = lax.rem(iz + 4 - offset, 4)
        store.start(first_ref.at[block_at(to_x, 4 * rows), :], x_out)
        for i in range(4):
            store.start(second_ref.at[block_at(i * 4 + to_z, rows), :], y_out.at[i])
    store.wait()


def attend_back(place, cosine, sine, pieces, weights, h_first, qt, kt, vt, attn, probs):
    width = weights.shape[0]
    heads, _, length = qt.shape
    groups = kt.shape[0]
    every_w = (heads + 2 * groups) * HD
    rows = width // 16
    outs = [(every_w, length)] + [(4 * rows, LATE_WIDTH)] * 4 + [(4, rows, LATE_WIDTH)] * 4
    scratch = [
        (length, width), (width, heads * HD), (length, width),
        qt.shape, kt.shape, vt.shape, attn.shape, probs.shape,
        attn.shape, (every_w, length), (width, LATE_WIDTH), (width, LATE_WIDTH),
        (groups, length, HD),
    ]
    wide = [(heads, 1, length), kt.shape, kt.shape]
    return kernel_call(
        attend_back_kernel, "attend_back", place, (cosine, sine),
        (*pieces, weights, h_first, qt, kt, vt, attn, probs),
        [like(s) for s in outs], [],
        [vmem(s) for s in scratch] + [vmem(s, F32) for s in wide], 11, 21, groups)


def project_back_kernel(place, dqkv_hbm, w_hbm, c0, c1, c2, c3,
                        dqkv_ref, w_ref, part_ref, in_sem, out_sem):
    block = place[0]
    size = part_ref.shape[1]
    fetch, store = Moves(in_sem), Moves(out_sem)
    fetch.start(w_hbm.at[:, pl.ds(QUERY_AT, REST_AT - QUERY_AT)], w_ref)
    fetch.start(dqkv_hbm, dqkv_ref)
    fetch.wait()
    for step, out in ((3, c3), (2, c2), (1, c1), (0, c0)):
        at = block_at(lax.bitwise_xor(block, step), size)
        part_ref[step] = dot_tt(dqkv_ref[:, at], w_ref[...]).astype(BF16)
        store.start(part_ref.at[step], out)
    store.wait()


def project_back(place, d_qkv, weights):
    every_w, length = d_qkv.shape
    width = weights.shape[0]
    size = length // 4
    return kernel_call(
        project_back_kernel, "project_back", place, (), (d_qkv, weights),
        [like((size, width))] * 4, [],
        [vmem(s) for s in (d_qkv.shape, (width, every_w), (4, size, width))], 2, 4)


def feed_kernel(place, h0, h1, g0, g1, w_hbm, hidden_hbm, dgu_hbm, b0, b1, r0, r1,
                w_ref, h_ref, g_ref, hidden_ref, dgu_ref, back_ref, out_ref, in_sem, out_sem):
    del place
    hidden_w = hidden_ref.shape[1]
    size = h_ref.shape[1]
    parts = [slice(i * hidden_w, (i + 1) * hidden_w) for i in range(3)]
    fetch, store = Moves(in_sem), Moves(out_sem)

    def weight(i):
        at = pl.ds(i * hidden_w, hidden_w)
        return fetch.start(w_hbm.at[:, at], w_ref.at[:, at])

    came = [fetch.start(h0, h_ref.at[0]), weight(0), weight(1), fetch.start(g0, g_ref.at[0]),
            weight(2), fetch.start(h1, h_ref.at[1]), fetch.start(g1, g_ref.at[1])]
    for i, (back, out) in enumerate(((b0, r0), (b1, r1))):
        rows = slice(i * size, (i + 1) * size)
        at = pl.ds(i * size, size)
        for copy in came[0:2] if i == 0 else came[5:7]:
            copy.wait()
        gate = dot_n(h_ref[i], w_ref[:, parts[0]])
        if i == 0:
            came[2].wait()
        up = dot_n(h_ref[i], w_ref[:, parts[1]])
        sig = 1.0 / (1.0 + jnp.exp2(gate * (-LOG2E)))
        silu = gate * sig
        hidden = (silu * up).astype(BF16)
        hidden_ref[rows, :] = hidden
        store.start(hidden_ref.at[at, :], hidden_hbm.at[at, :])
        if i == 0:
            came[3].wait()
            came[4].wait()
        d_hidden = dot_n(g_ref[i], w_ref[:, parts[2]])
        dgu_ref[rows, :hidden_w] = (
            d_hidden * up * (sig * (1.0 + gate * (1.0 - sig)))).astype(BF16)
        dgu_ref[rows, hidden_w:] = (d_hidden * silu).astype(BF16)
        store.start(dgu_ref.at[at, :], dgu_hbm.at[at, :])
        back_ref[i] = dot_t(dgu_ref[rows, :], w_ref[:, : 2 * hidden_w]).astype(BF16)
        store.start(back_ref.at[i], back)
        out_ref[i] = dot_t(hidden_ref[rows, :], w_ref[:, parts[2]]).astype(BF16)
        store.start(out_ref.at[i], out)
    store.wait()


def feed(place, weights, normed_pieces, grad_pieces):
    size, width = normed_pieces[0].shape
    hidden_w = weights.shape[1] // 3
    wide = [(2 * size, hidden_w), (2 * size, 2 * hidden_w)]
    return kernel_call(
        feed_kernel, "feed", place, (), (*normed_pieces, *grad_pieces, weights),
        [like(s) for s in wide + [(size, width)] * 4], [],
        [vmem(s) for s in [weights.shape] + [(2, size, width)] * 2 + wide + [(2, size, width)] * 2],
        7, 8)


def feed_grads_kernel(place, h0, h1, h2, h3, g0, g1, g2, g3, dgu_a, dgu_b, hidden_a, hidden_b,
                      out_hbm, h_ref, g_ref, dgu_ref, hidden_ref, out_ref, in_sem, out_sem):
    del place
    size = h0.shape[0]
    half, hidden_w = hidden_a.shape
    column = 512
    fetch, store = Moves(in_sem), Moves(out_sem)

    def rows_of(pieces, ref):
        return [
            fetch.start(piece, ref.at[pl.ds(i * size, size), :]) for i, piece in enumerate(pieces)
        ]

    def tiles_of(pieces, ref):
        tiles = []
        for tile in range(ref.shape[1] // column):
            at = pl.ds(tile * column, column)
            tiles.append([
                fetch.start(piece.at[:, at], ref.at[pl.ds(i * half, half), at])
                for i, piece in enumerate(pieces)
            ])
        return tiles

    h_came = rows_of((h0, h1, h2, h3), h_ref)
    dgu_came = tiles_of((dgu_a, dgu_b), dgu_ref)
    g_came = rows_of((g0, g1, g2, g3), g_ref)
    hidden_came = tiles_of((hidden_a, hidden_b), hidden_ref)
    at = 0
    for came, left, tiles, right in (
        (h_came, h_ref, dgu_came, dgu_ref), (g_came, g_ref, hidden_came, hidden_ref)
    ):
        for copy in came:
            copy.wait()
        for tile, copies in enumerate(tiles):
            for copy in copies:
                copy.wait()
            columns = pl.ds(at, column)
            out_ref[:, columns] = dot_tn(
                left[...], right[:, tile * column : (tile + 1) * column]).astype(BF16)
            store.start(out_ref.at[:, columns], out_hbm.at[:, columns])
            at += column
    store.wait()


def feed_grads(place, normed_pieces, grad_pieces, dgu_a, dgu_b, hidden_a, hidden_b):
    size, width = normed_pieces[0].shape
    half, hidden_w = hidden_a.shape
    scratch = [(4 * size, width)] * 2 + [(2 * half, 2 * hidden_w), (2 * half, hidden_w),
                                         (width, 3 * hidden_w)]
    return kernel_call(
        feed_grads_kernel, "feed_grads", place, (),
        (*normed_pieces, *grad_pieces, dgu_a, dgu_b, hidden_a, hidden_b),
        [like((width, 3 * hidden_w))], [], [vmem(s) for s in scratch], 20, 6)[0]


LATE_OUT, LATE_WIDTH = 192, 576


def late_middle_kernel(place, *refs):
    x_in, y_in, outs = refs[0:4], refs[4:8], refs[8:]
    ix, iz = place[1], place[2]
    rows = outs[0].shape[0]
    for offset in range(4):
        at = block_at(lax.rem(iz + 4 - offset, 4), rows)
        total = x_in[0][at, :].astype(F32)
        for ref in x_in[1:]:
            total += ref[at, :].astype(F32)
        outs[offset][...] = total.astype(BF16)
        to = lax.rem(ix + 4 - offset, 4)
        total = y_in[0][to].astype(F32)
        for ref in y_in[1:]:
            total += ref[to].astype(F32)
        outs[4 + offset][...] = total.astype(BF16)


def late_middle(place, along_x, along_z):
    _, rows, width = along_z[0].shape
    return pl.pallas_call(
        late_middle_kernel,
        out_shape=[like((rows, width))] * 8,
        in_specs=[scalars()] + [whole()] * 8,
        out_specs=[whole()] * 8,
        compiler_params=pltpu.CompilerParams(vmem_limit_bytes=16 * MIB),
        cost_estimate=SMALL,
        name="late_middle",
    )(place, *along_x, *along_z)


def late_last_kernel(place, *refs):
    x_in, y_in, keep_ref, send_ref = refs[0:4], refs[4:8], refs[8], refs[9]
    mine = place[3]
    rows = keep_ref.shape[0]
    for inputs, columns in ((x_in, slice(0, LATE_WIDTH)), (y_in, slice(LATE_WIDTH, 2 * LATE_WIDTH))):
        for ref, half in ((keep_ref, mine), (send_ref, 1 - mine)):
            at = block_at(half, rows)
            total = inputs[0][at, :].astype(F32)
            for other_ref in inputs[1:]:
                total += other_ref[at, :].astype(F32)
            ref[:, columns] = total.astype(ref.dtype)


def late_last(place, along_z, along_x):
    rows, width = along_x[0].shape
    return pl.pallas_call(
        late_last_kernel,
        out_shape=[
            jax.ShapeDtypeStruct((rows // 2, 2 * width), F32),
            jax.ShapeDtypeStruct((rows // 2, 2 * width), BF16),
        ],
        in_specs=[scalars()] + [whole()] * 8,
        out_specs=[whole()] * 2,
        compiler_params=pltpu.CompilerParams(vmem_limit_bytes=16 * MIB),
        cost_estimate=SMALL,
        name="late_last",
    )(place, *along_z, *along_x)


def feed_norm_back_kernel(own, core, far, middle, cotangent, gain, d_middle, d_out):
    grad = own[...].astype(F32) + core[...].astype(F32) + far[...].astype(F32)
    value = middle[...]
    factor = lax.rsqrt(jnp.mean(value * value, -1, keepdims=True) + norm_eps)
    normed = value * factor
    grad = grad * gain[...]
    inner = jnp.mean(grad * normed, -1, keepdims=True)
    total = cotangent[...].astype(F32) + factor * (grad - normed * inner)
    d_middle[...] = total
    d_out[...] = total.astype(BF16)


def feed_norm_back(own, core, far, middle, cotangent, gain_row):
    size, width = middle.shape
    rows = pl.BlockSpec((size // 4, width), lambda i: (i, 0))
    return pl.pallas_call(
        feed_norm_back_kernel,
        grid=(4,),
        out_shape=[like((size, width), F32), like((size, width))],
        in_specs=[rows] * 5 + [pl.BlockSpec((1, width), lambda i: (0, 0))],
        out_specs=[rows] * 2,
        compiler_params=pltpu.CompilerParams(vmem_limit_bytes=16 * MIB),
        cost_estimate=SMALL,
        name="feed_norm_back",
    )(own, core, far, middle, cotangent, gain_row)


def norm_rows(values_in):
    factor = lax.rsqrt(jnp.mean(values_in * values_in, -1, keepdims=True) + norm_eps)
    return (values_in * factor, factor)


def norm_back(grad_in, normed, factor, gain_row):
    grad_normed = grad_in * gain_row
    inner = jnp.mean(grad_normed * normed, -1, keepdims=True)
    return factor * (grad_normed - normed * inner)


def from_offset(v, axis, offset, size):
    return lax.ppermute(v, axis, [((i + offset) % size, i) for i in range(size)])


def other(v, axis):
    return from_offset(v, axis, 1, 2)


def pair_rows(v, axis):
    it = other(v, axis)
    mine = jnp.arange(2)[:, None, None] == lax.axis_index(axis)
    return jnp.where(mine, v[None], it[None]).reshape(2 * v.shape[0], v.shape[1])


def side_by_side(parts, width):
    return sum(
        jnp.pad(part, ((0, 0), (at, width - at - part.shape[1]))) for at, part in parts
    )


def near_sum(own, core):
    return own.astype(F32) + other(core, "core").astype(F32)


def far_sum(chip, diagonal):
    return near_sum(chip, diagonal).astype(BF16)


def after(value, first):
    return lax.optimization_barrier((value, first))


def from_both(along_first, first_axis, along_second, second_axis, large, beside=()):
    near = [
        from_offset(part[i], axis, i, 4)
        for i in (1, 3)
        for part, axis in ((along_first, first_axis), (along_second, second_axis))
    ]
    opposite = along_first[2], along_second[2]
    if large:
        opposite, (near, beside) = after(opposite, (near, beside))
    far = [from_offset(opposite[0], first_axis, 2, 4), from_offset(opposite[1], second_axis, 2, 4)]
    near, far = after(near, far)
    first = [along_first[0], near[0], far[0], near[2]]
    second = [along_second[0], near[1], far[1], near[3]]
    return first, second, beside


def pair_sum(v, axis):
    rows = v.shape[0] // 2
    me = lax.axis_index(axis)
    keep = lax.dynamic_slice_in_dim(v, me * rows, rows, 0)
    send = lax.dynamic_slice_in_dim(v, (1 - me) * rows, rows, 0)
    return keep.astype(F32) + other(send, axis).astype(F32)


def body(tokens, norm_gains, w_query, w_keyval, w_out, w_gateup, w_down, cotangent):
    D = tokens.shape[1]
    length = 4 * tokens.shape[0]
    hidden_w = w_down.shape[0]
    heads_w = w_query.shape[1]
    gains_w = norm_gains.shape[1]
    block = lax.axis_index("yl") * 2 + lax.axis_index("core")
    place = jnp.stack(
        [block, lax.axis_index("x"), lax.axis_index("z"), lax.axis_index("yh")]
    ).astype(jnp.int32)

    out_t = w_out.T
    attn_own = side_by_side(
        [
            (OUT_AT, out_t[:, :OUT_CUT]),
            (QUERY_AT, w_query),
            (KEYVAL_AT, w_keyval),
            (REST_AT, out_t[:, OUT_CUT:]),
        ],
        ATTN_WIDTH,
    )
    attn_pair = pair_rows(attn_own, "yh")
    pair_w = 8 * gains_w
    gain_at = (lax.axis_index("yh") * 4 + block) * gains_w
    gain_part = lax.dynamic_update_slice(jnp.zeros((2, pair_w), F32), norm_gains, (0, gain_at))
    for axis in ("core", "yl", "yh"):
        gain_part = gain_part + other(gain_part, axis)
    (gate_up, down), gain_part = after((w_gateup, w_down), gain_part)
    mlp_own = (gate_up[:, 0], gate_up[:, 1], down.T)
    mlp_own = [(i * hidden_w, part) for i, part in enumerate(mlp_own)]
    mlp_pair = pair_rows(side_by_side(mlp_own, 3 * hidden_w), "yh")
    gain_part = gain_part.T
    gain_high = lax.reduce_precision(gain_part, 8, 7)
    gain_low = (gain_part - gain_high).astype(BF16)
    gain_high = gain_high.astype(BF16)
    first, second = attn_pair[:, :HALF_WIDTH], attn_pair[:, HALF_WIDTH:]
    first += side_by_side([(0, gain_high), (2, gain_low)], HALF_WIDTH)

    mlp_pair, first = after(mlp_pair, first)
    mlp_w = lax.all_gather(mlp_pair, ("x", "z"), axis=0, tiled=True)
    along_z, along_x, _ = from_both([first] * 4, "z", [second] * 4, "x", False)
    along_z, along_x, tokens = lax.optimization_barrier(
        (jnp.stack(along_z), jnp.stack(along_x), tokens)
    )
    along_x, along_z, far = from_both(
        [along_z] * 4, "x", [along_x] * 4, "z", True, other(tokens, "yl")
    )
    token_pieces = [tokens, other(tokens, "core"), far, other(far, "core")]
    cotangent, far = after(cotangent, far)
    grad_far = other(cotangent, "yl")

    positions = jnp.arange(length).astype(F32)
    freqs = rope_base ** (-(jnp.arange(HD // 2).astype(F32) * 2.0 / HD))
    angles = freqs[:, None] * positions[None, :]
    cosine, sine = jnp.cos(angles), jnp.sin(angles)

    gain_rows, attn_w, h_first, qt, kt, vt, attn, probs, *parts = attend(
        place, token_pieces, along_x, along_z, cosine, sine
    )
    grad_far, parts = after(grad_far, parts)
    grad_pieces = [cotangent, other(cotangent, "core"), grad_far, other(grad_far, "core")]
    middle_far = far_sum(parts[2], parts[3])
    middle = (
        tokens.astype(F32) + near_sum(parts[0], parts[1]) + other(middle_far, "yl").astype(F32)
    )
    normed2, factor2 = norm_rows(middle)
    h_own = (normed2 * gain_rows[1]).astype(BF16)

    h_pieces = [h_own, other(h_own, "core")]
    h_far = other(h_own, "yl")
    hidden_a, dgu_a, back_own, back_core, out_own, out_core = feed(
        place, mlp_w, h_pieces, grad_pieces[:2]
    )
    h_far, hidden_a = after(h_far, hidden_a)
    h_pieces += [h_far, other(h_far, "core")]
    hidden_b, dgu_b, back_chip, back_diag, out_chip, out_diag = feed(
        place, mlp_w, h_pieces[2:], grad_pieces[2:]
    )
    back_core = other(back_core, "core")
    out_near = near_sum(out_own, out_core)

    back_far = far_sum(back_chip, back_diag)
    hidden_b, (back_far, back_core) = after(hidden_b, (back_far, back_core))
    mlp_grads = feed_grads(place, h_pieces, grad_pieces, dgu_a, dgu_b, hidden_a, hidden_b)
    mlp_grads, back_far = after(mlp_grads, other(back_far, "yl"))
    early = lax.psum_scatter(mlp_grads, ("x", "z"), scatter_dimension=0, tiled=True)
    out_far = far_sum(out_chip, out_diag)

    d_middle, d_out = feed_norm_back(
        back_own, back_core, back_far, middle, cotangent, gain_rows[1:2])
    d_out_far = other(d_out, "yl")
    d_out_far, out_near = after(d_out_far, out_near)
    out_pieces = [d_out, other(d_out, "core"), d_out_far, other(d_out_far, "core")]
    out_far, out_pieces = after(out_far, out_pieces)
    out_far = other(out_far, "yl")

    back = attend_back(
        place, cosine, sine, out_pieces, attn_w, h_first, qt, kt, vt, attn, probs
    )
    d_qkv, *late_parts = back
    d_qkv, out_far = after(d_qkv, out_far)
    along_x, along_z, parts = from_both(
        late_parts[:4], "x", late_parts[4:], "z", True, project_back(place, d_qkv, attn_w)
    )
    d_far = other(far_sum(parts[2], parts[3]), "yl")
    result = (middle + out_near + out_far.astype(F32)).astype(BF16)
    along_x, result = after(along_x, result)
    middle_parts = late_middle(place, along_x, along_z)
    along_z, along_x, early = from_both(
        middle_parts[:4], "z", middle_parts[4:], "x", True, early
    )
    early = pair_sum(early, "yh")
    d_h1_own = near_sum(parts[0], parts[1]) + d_far.astype(F32)
    along_z, (d_h1_own, early) = after(along_z, (d_h1_own, early))
    late_keep, late_send = late_last(place, along_z, along_x)
    late = late_keep + other(late_send, "yh").astype(F32)

    normed1, factor1 = norm_rows(tokens.astype(F32))
    d_norm1 = norm_back(d_h1_own, normed1, factor1, gain_rows[0])
    input_grad = (d_middle + d_norm1).astype(BF16)

    grad_query = late[:, :heads_w]
    grad_keyval = late[:, 2 * LATE_WIDTH - heads_w :]
    grad_out = late[:, heads_w : 2 * LATE_WIDTH - heads_w].T
    grad_gateup = early[:, : 2 * hidden_w].reshape(-1, 2, hidden_w)

    gain_sum = jnp.stack(
        [
            jnp.sum(grad_query * w_query.astype(F32) + grad_keyval * w_keyval.astype(F32), 1),
            jnp.sum(grad_gateup * w_gateup.astype(F32), (1, 2)),
        ]
    )
    gain_sum = gain_sum + sum(
        lax.ppermute(gain_sum, ("yl", "core"), [(i ^ step, i) for i in range(4)])
        for step in (1, 2, 3)
    )
    grad_gains = lax.dynamic_slice(gain_sum, (0, block * gains_w), (2, gains_w)) / norm_gains
    return (
        result,
        input_grad,
        grad_query,
        grad_keyval,
        grad_out,
        grad_gateup,
        early[:, 2 * hidden_w :].T,
        grad_gains,
    )


def solution(mesh):
    fine = Mesh(mesh.devices.reshape(4, 4, 2, 2, 2), ("x", "z", "yh", "yl", "core"))
    dp = ("x", "z", "yh")
    tensor = ("yl", "core")
    every = dp + tensor
    weights = (P(dp, tensor), P(dp, tensor), P(tensor, dp), P(dp, None, tensor), P(tensor, dp))
    rows = P(every, None)
    gains = P(None, every)
    return jax.shard_map(
        body,
        mesh=fine,
        in_specs=(rows, gains) + weights + (rows,),
        out_specs=(rows, rows) + weights + (gains,),
        check_vma=False,
    )
```
